128 devices in a mesh: ctx: 16 (over x, y_lo, core), mp: 8 (over z, y_hi).
Axes of the slice: x: 4, y: 4 (y_hi: 2, y_lo: 2; y = y_hi * 2 + y_lo), z: 4, core: 2. Of those that a mesh axis runs over, the one named last changes fastest.
Arguments:
- layer_input: bfloat16 [16384, 1024], P(('ctx', 'mp')), may hold values from -6 to 6
- positions: int32 [16384], P('ctx'), may hold values from 0 to 24575, as said below
- expert_ids: int32 [16384, 8], P(('ctx', 'mp')), may hold values from 0 to 31, all different within a row; in each aligned block of 128 rows (0 to 127, 128 to 255, ...) at most 36 rows name the same one
- attn_gain: bfloat16 [1024], P('ctx'), may hold values from 0.5 to 1.5
- w_query: bfloat16 [1024, 1024], P('ctx', 'mp'), may hold values from -0.75 to 0.75
- w_key: bfloat16 [1024, 512], P('ctx', 'mp'), may hold values from -0.75 to 0.75
- w_value: bfloat16 [1024, 512], P('ctx', 'mp'), may hold values from -0.1875 to 0.1875
- w_attn_out: bfloat16 [1024, 1024], P('mp', 'ctx'), may hold values from -4 to 4
- ffn_gain: bfloat16 [1024], P('ctx'), may hold values from 0.5 to 1.5
- router: bfloat16 [1024, 32], P('ctx'), may hold values from -0.09375 to 0.09375
- w_in: bfloat16 [32, 1024, 1024], P('mp', 'ctx'), may hold values from -0.1875 to 0.1875
- w_out: bfloat16 [32, 512, 1024], P('mp', None, 'ctx'), may hold values from -4 to 4
- cotangent: bfloat16 [16384, 1024], P(('ctx', 'mp')), may hold values from -6 to 6
Outputs:
- activations: bfloat16 [16384, 1024], P(('ctx', 'mp'))
- input_grad: bfloat16 [16384, 1024], P(('ctx', 'mp'))
- attn_gain_grad: float32 [1024], P(('ctx', 'mp'))
- query_grad: float32 [1024, 1024], P('ctx', 'mp')
- key_grad: float32 [1024, 512], P('ctx', 'mp')
- value_grad: float32 [1024, 512], P('ctx', 'mp')
- attn_out_grad: float32 [1024, 1024], P('mp', 'ctx')
- ffn_gain_grad: float32 [1024], P(('ctx', 'mp'))
- router_grad: float32 [1024, 32], P(('ctx', 'mp'))
- expert_in_grad: float32 [32, 1024, 1024], P('mp', 'ctx')
- expert_out_grad: float32 [32, 512, 1024], P('mp', None, 'ctx')
The draws below stay inside these ranges and needn't reach their ends.
Inputs may be any that keep to these rules, and one draw needn't show every extreme that they name: `expert_ids`: each row names 8 different experts. Among the rows of one device (aligned blocks of 128 rows, in order) no expert is named more than 36 times, a bound that some block reaches. `positions`: the first position is 0 and each next one is larger by 1 or 2; exactly 8192 of these steps are 2.
All inputs are finite; a program needn't handle non-finite values.
Results may differ from the reference program's by a relative error of at most 0.038.
Values may be sent and summed in bfloat16 or wider, within the bound.
A program may use at most 128 MiB of HBM per device.

```python
import math
import jax
import jax.numpy as jnp
import numpy as np
from jax import lax

D = 1024
HEAD_DIM = 64
GROUP = 2
FF = 512
TOP = 8
TOK_DEV = 128
KV_HEADS = 8
HEADS = 16
EXPERTS = 32
CAP = 36
TOKENS = 16384


def draw_positions(key, part):
    key = jax.random.fold_in(key, 7)
    order = jax.random.permutation(key, TOKENS - 1)
    step_sizes = 1 + (order < TOKENS // 2).astype(jnp.int32)
    return jnp.concatenate([jnp.zeros((1,), jnp.int32), jnp.cumsum(step_sizes).astype(jnp.int32)])


def block_levels(rng, extent, split, smallest, high):
    level, own = 1.0, jax.random.fold_in(rng, 6)
    for axis_at, blocks in split:
        draws = jnp.exp(jax.random.uniform(jax.random.fold_in(own, axis_at), (blocks,), jnp.float32, smallest / len(split), high / len(split)))
        level = level * jnp.repeat(draws, extent[axis_at] // blocks).reshape([-1 if axis == axis_at else 1 for axis in range(len(extent))])
    return level


def routed_block(rng, own, number, rows, count, top, bound, skew):
    ranking = jax.random.permutation(rng, count)
    heavy_load, ordinary = portions_of(count, rows * top, bound, skew, True), portions_of(count, rows * top, bound, skew, False)
    places = jnp.arange(count)

    def named(lengths, turn):
        used = int((lengths > 0).sum())
        fixed = max(1, used // 4)
        shifted = fixed + (places - fixed + turn * (used - fixed)) % max(1, count - fixed)
        return jnp.zeros((count,), jnp.int32).at[ranking[jnp.where(places < fixed, places, shifted)]].set(jnp.asarray(lengths, jnp.int32))

    lengths = jnp.where(number % 4 == 0, named(heavy_load, number // 4), named(ordinary, number - number // 4 - 1))
    mixed = jax.random.permutation(jax.random.fold_in(own, 3), count)
    donor, sink = mixed[0:count // 2 * 2:2], mixed[1:count // 2 * 2:2]
    slack = jnp.minimum(lengths[donor] - 1, bound - lengths[sink]) // 2
    slack = jnp.where((donor == ranking[0]) | (sink == ranking[0]) | (lengths[sink] == 0), 0, jnp.maximum(slack, 0))
    shifted = jax.random.randint(jax.random.fold_in(own, 4), (count // 2,), 0, 1 << 20) % (slack + 1)
    lengths = lengths.at[donor].add(-shifted).at[sink].add(shifted)
    members = jnp.searchsorted(jnp.cumsum(lengths), jnp.arange(rows * top), side="right").astype(jnp.int32)
    table = members.reshape(top, rows).T
    table = table[jax.random.permutation(jax.random.fold_in(own, 1), rows)]
    turn = jax.random.randint(jax.random.fold_in(own, 2), (rows, 1), 0, top)
    return jnp.take_along_axis(table, (jnp.arange(top)[None, :] + turn) % top, axis=1)


def portions_of(count, total, limit, lean, full):
    portions = [(1 << 20) // math.isqrt(rank ** lean) + 1 for rank in range(1, count + 1)]
    largest = limit if full else min(limit, max(-(-total // count), total * portions[0] // sum(portions)))
    least = 1 if total - largest >= count - 1 else 0
    counts, spare = [largest] + [least] * (count - 1), total - largest - least * (count - 1)
    while spare > 0:
        movable = [i for i in range(1, count) if counts[i] < largest] or [i for i in range(1, count) if counts[i] < limit]
        whole, budget = sum([portions[i] for i in movable]), spare
        for i in movable:
            extra = min(limit - counts[i], max(1, budget * portions[i] // whole), spare)
            counts[i] = counts[i] + extra
            spare = spare - extra
    return np.array(counts)


def gaussian(own_key, shape, scale, reach, split=(), kind=jnp.bfloat16):
    array = scale * jax.random.normal(own_key, shape, jnp.float32)
    if split:
        array = array * block_levels(own_key, shape, split, -0.22, 0.18)
    return jnp.clip(array, -reach, reach).astype(kind)


def setup_inputs(seed: int = 0) -> dict:
    key_of = jax.random.split(jax.random.key(seed), 14)
    layer_input = gaussian(key_of[0], (TOKENS, D), 1.0, 6.0, ((0, 128),))
    positions = draw_positions(jax.random.fold_in(key_of[13], 71), 0)
    expert_ids_keys = jax.random.split(jax.random.fold_in(key_of[2], 1), TOKENS // TOK_DEV)
    expert_ids_turns = jax.random.permutation(jax.random.fold_in(key_of[2], 3), TOKENS // TOK_DEV)
    expert_ids = jax.vmap(lambda own, number: routed_block(jax.random.fold_in(key_of[2], 2), own, number, TOK_DEV, EXPERTS, TOP, CAP, 1))(expert_ids_keys, expert_ids_turns).reshape((TOKENS, TOP))
    attn_gain = jnp.clip(1.0 + 0.1 * jax.random.normal(key_of[3], (D,), jnp.float32), 0.5, 1.5).astype(jnp.bfloat16)
    w_query = gaussian(key_of[4], (D, HEADS * HEAD_DIM), (D // 16) ** -0.5, 0.75, ((0, 16), (1, 8)))
    w_key = gaussian(key_of[5], (D, KV_HEADS * HEAD_DIM), (D // 16) ** -0.5, 0.75, ((0, 16), (1, 8)))
    w_value = gaussian(key_of[6], (D, KV_HEADS * HEAD_DIM), D ** -0.5, 0.1875, ((0, 16), (1, 8)))
    w_attn_out = gaussian(key_of[7], (HEADS * HEAD_DIM, D), 2 ** -0.5, 4.0, ((0, 8), (1, 16)))
    ffn_gain = jnp.clip(1.0 + 0.1 * jax.random.normal(key_of[8], (D,), jnp.float32), 0.5, 1.5).astype(jnp.bfloat16)
    router = gaussian(key_of[9], (D, EXPERTS), (4 * D) ** -0.5, 0.09375, ((0, 16),))
    w_in = gaussian(key_of[10], (EXPERTS, D, 2 * FF), D ** -0.5, 0.1875, ((0, 8), (1, 16)))
    w_out = gaussian(key_of[11], (EXPERTS, FF, D), (max(FF // 256, 1)) ** -0.5, 4.0, ((0, 8), (2, 16)))
    cotangent = gaussian(key_of[12], (TOKENS, D), 1.0, 6.0, ((0, 128),))
    return {"layer_input": layer_input, "positions": positions, "expert_ids": expert_ids, "attn_gain": attn_gain, "w_query": w_query, "w_key": w_key, "w_value": w_value, "w_attn_out": w_attn_out, "ffn_gain": ffn_gain, "router": router, "w_in": w_in, "w_out": w_out, "cotangent": cotangent}


@jax.custom_vjp
def low(v):
    return lax.optimization_barrier(v.astype(jnp.bfloat16)).astype(jnp.float32)

@jax.custom_vjp
def low_back(v):
    return v

def low_keep(v):
    return (low(v), None)

def low_pass(kept, grad):
    return (grad,)

def back_keep(v):
    return (v, None)

def back_low(kept, grad):
    return (low(grad),)
low.defvjp(low_keep, low_pass)
low_back.defvjp(back_keep, back_low)
epsilon = 1e-06
branch_scale = 0.22
score_scale = 0.015625
rope_base = 10000.0
highest = lax.Precision.HIGHEST

def matmul(left, right):
    return jnp.dot(left, right, precision=highest, preferred_element_type=jnp.float32)

def phases(positions, head_width):
    steps_up = jnp.arange(head_width // 2).astype(jnp.float32)
    frequency = rope_base ** (-2.0 * steps_up / head_width)
    angles = positions.astype(jnp.float32)[:, None] * frequency[None, :]
    angles = jnp.concatenate([angles, angles], axis=1)
    return (jnp.cos(angles), jnp.sin(angles))

def rotate(values, cosine, sine):
    half_width = values.shape[-1] // 2
    turned = jnp.concatenate([-values[..., half_width:], values[..., :half_width]], axis=-1)
    return values * cosine + turned * sine

def rms_norm(values, gain):
    return values * lax.rsqrt(lax.optimization_barrier(jnp.mean(values * values, axis=-1, keepdims=True)) + epsilon) * gain

def layer(inputs, attn_gain, w_query, w_key, w_value, w_attn_out, ffn_gain, router, w_in, w_out, positions, expert_ids):
    normed = low(rms_norm(inputs, attn_gain))
    cosine, sine = phases(positions, HEAD_DIM)
    cosine = cosine[:, None, :]
    sine = sine[:, None, :]
    queries = low(rotate(low_back(matmul(normed, w_query)).reshape(TOKENS, HEADS, HEAD_DIM), cosine, sine))
    keys_all = low(rotate(low_back(matmul(normed, w_key)).reshape(TOKENS, KV_HEADS, HEAD_DIM), cosine, sine))
    values_all = low(low_back(matmul(normed, w_value))).reshape(TOKENS, KV_HEADS, HEAD_DIM)
    block_rows = min(TOKENS, 1024)
    blocks = TOKENS // block_rows
    columns = jnp.arange(TOKENS, dtype=jnp.int32)

    def attend_block(item_index):
        block_no = item_index // HEADS
        head_no = item_index % HEADS
        first = (block_no * block_rows).astype(jnp.int32)
        query_rows = lax.dynamic_index_in_dim(lax.dynamic_slice_in_dim(queries, first, block_rows, 0), head_no, 1, False)
        key_rows = lax.dynamic_index_in_dim(keys_all, head_no // GROUP, 1, False)
        value_rows = lax.dynamic_index_in_dim(values_all, head_no // GROUP, 1, False)
        scores = low_back(score_scale * matmul(query_rows, key_rows.T))
        visible = columns[None, :] <= (first + jnp.arange(block_rows, dtype=jnp.int32))[:, None]
        scores = jnp.where(visible, scores, -1e+30)
        weights = low(jax.nn.softmax(scores, axis=-1))
        return matmul(weights, value_rows)
    attended = lax.map(jax.checkpoint(attend_block), jnp.arange(blocks * HEADS, dtype=jnp.int32))
    attended = attended.reshape(blocks, HEADS, block_rows, HEAD_DIM).transpose(0, 2, 1, 3).reshape(TOKENS, HEADS * HEAD_DIM)
    outputs = low(low_back(attended))
    hidden = inputs + branch_scale * low_back(matmul(outputs, w_attn_out))
    routed = low(rms_norm(hidden, ffn_gain))
    logits = matmul(routed, router)
    chosen = jnp.take_along_axis(logits, expert_ids, axis=1)
    gates = jax.nn.softmax(chosen, axis=-1)
    slot_range = jnp.arange(EXPERTS * CAP, dtype=jnp.int32)
    expert_range = jnp.arange(EXPERTS, dtype=jnp.int32)

    def expert_block(block_no):
        first = (block_no * TOK_DEV).astype(jnp.int32)
        token_rows = lax.dynamic_slice_in_dim(routed, first, TOK_DEV, 0)
        picked = lax.dynamic_slice_in_dim(expert_ids, first, TOK_DEV, 0).reshape(-1)
        shares = lax.dynamic_slice_in_dim(gates, first, TOK_DEV, 0)
        member = (picked[:, None] == expert_range[None, :]).astype(jnp.int32)
        running = (jnp.cumsum(member, axis=0) - 1).astype(jnp.int32)
        slots = lax.optimization_barrier(jnp.sum(member * running, axis=1)).astype(jnp.int32)
        target = (picked * CAP + slots).astype(jnp.int32)
        placing = (target[:, None] == slot_range[None, :]).astype(jnp.float32)
        sources = jnp.repeat(token_rows, TOP, axis=0)
        dispatched = matmul(placing.T, sources).reshape(EXPERTS, CAP, D)
        gate_up = low_back(jnp.einsum('ecd,edf->ecf', dispatched, w_in, precision=highest))
        active = low(jax.nn.silu(gate_up[..., :FF]) * gate_up[..., FF:])
        produced = low(low_back(jnp.einsum('ecf,efd->ecd', active, w_out, precision=highest)))
        returned = matmul(placing, produced.reshape(EXPERTS * CAP, D)).reshape(TOK_DEV, TOP, D)
        return lax.optimization_barrier(jnp.sum(returned * shares[:, :, None], axis=1))
    mixed = lax.map(jax.checkpoint(expert_block), jnp.arange(TOKENS // TOK_DEV, dtype=jnp.int32)).reshape(TOKENS, D)
    return hidden + branch_scale * mixed

def reference(layer_input, positions, expert_ids, attn_gain, w_query, w_key, w_value, w_attn_out, ffn_gain, router, w_in, w_out, cotangent):

    def forward(inputs, gain_one, query_w, key_w, value_w, out_w, gain_two, router_w, in_w, out_expert):
        return layer(inputs, gain_one, query_w, key_w, value_w, out_w, gain_two, router_w, in_w, out_expert, positions, expert_ids)
    result, pullback = jax.vjp(forward, layer_input.astype(jnp.float32), attn_gain.astype(jnp.float32), w_query.astype(jnp.float32), w_key.astype(jnp.float32), w_value.astype(jnp.float32), w_attn_out.astype(jnp.float32), ffn_gain.astype(jnp.float32), router.astype(jnp.float32), w_in.astype(jnp.float32), w_out.astype(jnp.float32))
    grads = pullback(cotangent.astype(jnp.float32))
    return (result.astype(jnp.bfloat16), grads[0].astype(jnp.bfloat16), grads[1], grads[2], grads[3], grads[4], grads[5], grads[6], grads[7], grads[8], grads[9])
```

```python
import functools

import jax
import jax.numpy as jnp
from jax import lax
from jax.experimental import pallas as pl
from jax.experimental.pallas import tpu as pltpu
from jax.sharding import PartitionSpec as P

MESH = pl.DeviceIdType.MESH
epsilon = 1e-06
branch_scale = 0.22
score_scale = 0.015625
rope_base = 10000.0
highest = lax.Precision.HIGHEST
log2_e = 1.4426950408889634
bf16 = jnp.bfloat16
f32 = jnp.float32
CTX, MP = 16, 8
HEAD = 64
TOK = 128
BLOCK = 1024
HALF = 512
ANY = pl.BlockSpec(memory_space=pl.ANY)
VM = pl.BlockSpec(memory_space=pltpu.VMEM)
VMEM_LIMIT = 56 * 1024 * 1024


def contract(left, right, left_dim, right_dim):
    return lax.dot_general(
        left, right, (((left_dim,), (right_dim,)), ((), ())), preferred_element_type=f32
    )


def place():
    return lax.axis_index("ctx"), lax.axis_index("mp")


def greet(signal_to, expected):
    barrier = pltpu.get_barrier_semaphore()
    for target in signal_to:
        pl.semaphore_signal(barrier, inc=1, device_id=target, device_id_type=MESH)
    pl.semaphore_wait(barrier, expected)


def remote(src, dst, send, recv, target):
    return pltpu.make_async_remote_copy(
        src_ref=src, dst_ref=dst, send_sem=send, recv_sem=recv,
        device_id=target, device_id_type=MESH,
    )


def comm_call(kernel, number, arrays, outs, sems, cost):
    return pl.pallas_call(
        kernel,
        out_shape=outs,
        in_specs=[ANY] * len(arrays),
        out_specs=[ANY] * len(outs),
        scratch_shapes=[pltpu.SemaphoreType.DMA((n,)) for n in sems],
        compiler_params=pltpu.CompilerParams(collective_id=number, has_side_effects=True),
        cost_estimate=pl.CostEstimate(flops=0, bytes_accessed=cost, transcendentals=0),
    )(*arrays)


def shape(dims, kind=bf16):
    return jax.ShapeDtypeStruct(dims, kind)


def start_kernel(x_ref, id_ref, w_ref, xo, ido, wo, xs, xr, ids, idr, ws, wr, loc):
    c, m = place()
    upper = m >= MP // 2
    t = jnp.where(upper, CTX - 1 - c, c)
    signals = []
    for k in range(1, MP):
        sender = lax.rem(m + k, MP)
        signals.append((jnp.where(sender >= MP // 2, CTX - 1 - c, c), sender))
    for k in range(1, CTX):
        signals.append((lax.rem(c + k, CTX), m))
    barrier = pltpu.get_barrier_semaphore()
    for target in signals:
        pl.semaphore_signal(barrier, inc=1, device_id=target, device_id_type=MESH)

    @pl.when(upper)
    def _():
        pl.semaphore_signal(barrier, inc=1, device_id=(CTX - 1 - c, m), device_id_type=MESH)
        pl.semaphore_wait(barrier, MP + CTX - 1)

    @pl.when(jnp.logical_not(upper))
    def _():
        pl.semaphore_wait(barrier, MP + CTX - 2)

    own_w = pltpu.make_async_copy(w_ref, wo.at[c], loc.at[0])
    own_w.start()
    x_copies, id_copies, w_copies = [], [], []
    for k in range(MP):
        target = (t, lax.rem(m + k, MP))
        x_copies.append(remote(x_ref, xo.at[m], xs.at[k], xr.at[k], target))
        id_copies.append(remote(id_ref, ido.at[m], ids.at[k], idr.at[k], target))
    for k in range(1, CTX):
        w_copies.append(remote(w_ref, wo.at[c], ws.at[k], wr.at[k], (lax.rem(c + k, CTX), m)))
    own_x = pltpu.make_async_copy(x_ref, xo.at[m], loc.at[1])
    own_id = pltpu.make_async_copy(id_ref, ido.at[m], loc.at[2])

    @pl.when(upper)
    def _():
        x_copies[0].start()
        id_copies[0].start()

    @pl.when(jnp.logical_not(upper))
    def _():
        own_x.start()
        own_id.start()

    for k in range(1, MP):
        x_copies[k].start()
        id_copies[k].start()
    for copy in w_copies:
        copy.start()
    for k in range(1, MP):
        x_copies[k].wait()
        id_copies[k].wait()
    for copy in w_copies:
        copy.wait()
    own_w.wait()

    @pl.when(upper)
    def _():
        x_copies[0].wait()
        id_copies[0].wait()

    @pl.when(jnp.logical_not(upper))
    def _():
        own_x.wait()
        own_id.wait()


def keys_kernel(kv_ref, w_ref, kvo, wo, send, recv, send2, recv2, ws, wr, loc):
    c, m = place()
    chip, core = c // 2, lax.rem(c, 2)
    sibling = (chip * 2 + 1 - core, m)
    others = [(lax.rem(chip + k, 8) * 2 + core, m) for k in range(1, 8)]
    mates = [(c, lax.rem(m + k, MP)) for k in range(1, MP)]
    greet(others + [sibling] + mates, 7 + 1 + 7)
    own = pltpu.make_async_copy(kv_ref, kvo.at[c], loc.at[0])
    own.start()
    own_w = pltpu.make_async_copy(w_ref, wo.at[m], loc.at[1])
    own_w.start()
    far, near, rows = [], [], []
    for k in range(1, 8):
        copy = remote(kv_ref, kvo.at[c], send.at[k], recv.at[k], others[k - 1])
        copy.start()
        far.append(copy)
    first = remote(kv_ref, kvo.at[c], send.at[0], recv.at[0], sibling)
    first.start()
    for k in range(1, MP):
        copy = remote(w_ref, wo.at[m], ws.at[k], wr.at[k], mates[k - 1])
        copy.start()
        rows.append(copy)
    for k in range(1, 8):
        far[k - 1].wait_recv()
        slot = lax.rem(chip + 8 - k, 8) * 2 + core
        copy = remote(kvo.at[slot], kvo.at[slot], send2.at[k], recv2.at[k], sibling)
        copy.start()
        near.append(copy)
    first.wait()
    for k in range(1, 8):
        far[k - 1].wait_send()
        near[k - 1].wait()
        rows[k - 1].wait()
    own.wait()
    own_w.wait()


def gather_kernel(a_ref, out, send, recv, loc):
    c, m = place()
    mates = [(c, lax.rem(m + k, MP)) for k in range(1, MP)]
    greet(mates, MP - 1)
    own = pltpu.make_async_copy(a_ref, out.at[m], loc.at[0])
    own.start()
    copies = []
    for k in range(1, MP):
        copy = remote(a_ref, out.at[m], send.at[k], recv.at[k], mates[k - 1])
        copy.start()
        copies.append(copy)
    for copy in copies:
        copy.wait()
    own.wait()


def scatter_kernel(a_ref, b_ref, ao, bo, s1, r1, s2, r2, loc):
    c, m = place()
    mates = [(c, lax.rem(m + k, MP)) for k in range(1, MP)]
    greet(mates, MP - 1)
    own_a = pltpu.make_async_copy(a_ref.at[m], ao.at[m], loc.at[0])
    own_a.start()
    own_b = pltpu.make_async_copy(b_ref.at[m], bo.at[m], loc.at[1])
    own_b.start()
    copies = []
    for k in range(1, MP):
        to = lax.rem(m + k, MP)
        copies.append(remote(a_ref.at[to], ao.at[m], s1.at[k], r1.at[k], mates[k - 1]))
        copies.append(remote(b_ref.at[to], bo.at[m], s2.at[k], r2.at[k], mates[k - 1]))
    for copy in copies:
        copy.start()
    for copy in copies:
        copy.wait()
    own_a.wait()
    own_b.wait()


def sibling_kernel(a_ref, out, send, recv):
    c, m = place()
    chip, core = c // 2, lax.rem(c, 2)
    sibling = (chip * 2 + 1 - core, m)
    greet([sibling], 1)
    copy = remote(a_ref.at[:, 1 - core], out, send.at[0], recv.at[0], sibling)
    copy.start()
    copy.wait()


def chips_kernel(a_ref, out, send, recv, loc):
    c, m = place()
    chip, core = c // 2, lax.rem(c, 2)
    others = [(lax.rem(chip + k, 8) * 2 + core, m) for k in range(1, 8)]
    greet(others, 7)
    own = pltpu.make_async_copy(a_ref.at[chip], out.at[chip], loc.at[0])
    own.start()
    copies = []
    for k in range(1, 8):
        to = lax.rem(chip + k, 8)
        copy = remote(a_ref.at[to], out.at[chip], send.at[k], recv.at[k], others[k - 1])
        copy.start()
        copies.append(copy)
    for copy in copies:
        copy.wait()
    own.wait()


def finish_kernel(a_ref, g_ref, ao, go, s1, r1, s2, r2, loc):
    c, m = place()
    upper = m >= MP // 2
    t = jnp.where(upper, CTX - 1 - c, c)
    barrier = pltpu.get_barrier_semaphore()
    for k in range(1, MP):
        pl.semaphore_signal(
            barrier, inc=1, device_id=(t, lax.rem(m + k, MP)), device_id_type=MESH
        )
    for k in range(1, CTX):
        pl.semaphore_signal(
            barrier, inc=1, device_id=(lax.rem(c + k, CTX), m), device_id_type=MESH
        )

    @pl.when(upper)
    def _():
        pl.semaphore_signal(barrier, inc=1, device_id=(t, m), device_id_type=MESH)
        pl.semaphore_wait(barrier, MP + CTX - 1)

    @pl.when(jnp.logical_not(upper))
    def _():
        pl.semaphore_wait(barrier, MP + CTX - 2)

    own_g = pltpu.make_async_copy(g_ref.at[c], go.at[c], loc.at[0])
    own_g.start()
    own_a = pltpu.make_async_copy(a_ref.at[m], ao.at[m], loc.at[1])
    a_copies, g_copies = [], []
    for k in range(MP):
        to = lax.rem(m + k, MP)
        target = (jnp.where(to >= MP // 2, CTX - 1 - c, c), to)
        a_copies.append(remote(a_ref.at[to], ao.at[m], s1.at[k], r1.at[k], target))
    for k in range(1, CTX):
        to = lax.rem(c + k, CTX)
        g_copies.append(remote(g_ref.at[to], go.at[c], s2.at[k], r2.at[k], (to, m)))

    @pl.when(upper)
    def _():
        a_copies[0].start()

    @pl.when(jnp.logical_not(upper))
    def _():
        own_a.start()

    for k in range(1, MP):
        a_copies[k].start()
    for copy in g_copies:
        copy.start()
    for k in range(1, MP):
        a_copies[k].wait()
    for copy in g_copies:
        copy.wait()
    own_g.wait()

    @pl.when(upper)
    def _():
        a_copies[0].wait()

    @pl.when(jnp.logical_not(upper))
    def _():
        own_a.wait()


def sums_kernel(a_ref, out, got, part, got2, s1, r1, s2, r2):
    c, m = place()
    peers = [(lax.rem(c + k, CTX), m) for k in range(1, CTX)]
    mates = [(c, lax.rem(m + k, MP)) for k in range(1, MP)]
    greet(peers + mates, CTX - 1 + MP - 1)
    copies = []
    for k in range(1, CTX):
        to = lax.rem(c + k, CTX)
        copy = remote(a_ref.at[to], got.at[k], s1.at[k], r1.at[k], peers[k - 1])
        copy.start()
        copies.append(copy)
    total = a_ref[c]
    for copy in copies:
        copy.wait()
    for k in range(1, CTX):
        total = total + got[k]
    part[...] = total
    copies = []
    for k in range(1, MP):
        to = lax.rem(m + k, MP)
        copy = remote(part.at[to], got2.at[k], s2.at[k], r2.at[k], mates[k - 1])
        copy.start()
        copies.append(copy)
    last = part[m]
    for copy in copies:
        copy.wait()
    for k in range(1, MP):
        last = last + got2[k]
    out[...] = last


def small_sums(terms):
    dims = terms.shape[2:]
    return pl.pallas_call(
        sums_kernel,
        out_shape=shape(dims, f32),
        in_specs=[VM],
        out_specs=VM,
        scratch_shapes=[
            pltpu.VMEM((CTX, MP) + dims, f32),
            pltpu.VMEM((MP,) + dims, f32),
            pltpu.VMEM((MP,) + dims, f32),
            pltpu.SemaphoreType.DMA((CTX,)),
            pltpu.SemaphoreType.DMA((CTX,)),
            pltpu.SemaphoreType.DMA((MP,)),
            pltpu.SemaphoreType.DMA((MP,)),
        ],
        compiler_params=pltpu.CompilerParams(collective_id=9, has_side_effects=True),
    )(terms)


def unit(index, first_half):
    second = index > first_half
    part = second.astype(jnp.int32)
    key_half = jnp.where(second, index - first_half - 1, index)
    odd = lax.rem(key_half, 2) == 1
    slot = jnp.where(odd, 2 * CTX - key_half, key_half)
    diagonal = jnp.logical_or(index == first_half, index == 2 * CTX)
    return part, slot, diagonal


def visible_mask(rows):
    key_at = lax.broadcasted_iota(jnp.int32, (HALF, rows), 0)
    query_at = lax.rem(lax.broadcasted_iota(jnp.int32, (HALF, rows), 1), HALF)
    return key_at <= query_at


def forward_kernel(q_ref, kv_ref, out_ref, lse_ref, best, total, summed):
    first_half = 2 * lax.axis_index("ctx")
    best[...] = jnp.full(best.shape, -1e30, f32)
    total[...] = jnp.zeros(total.shape, f32)
    summed[...] = jnp.zeros(summed.shape, f32)

    def work(part, slot, masked):
        kv = kv_ref[slot]
        scores = contract(kv, q_ref[part], 1, 1)
        if masked:
            scores = jnp.where(visible_mask(scores.shape[1]), scores, -jnp.inf)
        old = best[part]
        new = jnp.maximum(old, jnp.max(scores, axis=0, keepdims=True))
        weights = jnp.exp2(scores * log2_e - new * log2_e)
        fading = jnp.exp2((old - new) * log2_e)
        total[part] = total[part] * fading + jnp.sum(weights, axis=0, keepdims=True)
        summed[part] = summed[part] * fading + contract(kv, weights.astype(bf16), 0, 0)
        best[part] = new

    def step(index, carry):
        part, slot, diagonal = unit(index, first_half)

        @pl.when(diagonal)
        def _():
            work(part, slot, True)

        @pl.when(jnp.logical_not(diagonal))
        def _():
            work(part, slot, False)

        return carry

    lax.fori_loop(0, 2 * CTX + 1, step, 0)
    for part in range(2):
        out_ref[part] = summed[part][HEAD:, :] / total[part]
        lse_ref[part] = best[part] + jnp.log(total[part])


def attention(q_rows, kv_all):
    rows = q_rows.shape[1]
    return pl.pallas_call(
        forward_kernel,
        out_shape=[shape((2, HEAD, rows), f32), shape((2, 1, rows), f32)],
        in_specs=[VM, VM],
        out_specs=[VM, VM],
        scratch_shapes=[
            pltpu.VMEM((2, 1, rows), f32),
            pltpu.VMEM((2, 1, rows), f32),
            pltpu.VMEM((2, 2 * HEAD, rows), f32),
        ],
        compiler_params=pltpu.CompilerParams(vmem_limit_bytes=VMEM_LIMIT),
        cost_estimate=pl.CostEstimate(
            flops=33 * 4 * HALF * rows * 256, bytes_accessed=1 << 23, transcendentals=33 * HALF * rows
        ),
    )(q_rows, kv_all)


def backward_kernel(q_ref, do_ref, lse_ref, delta_ref, kv_ref, dkv_ref, dq_ref, total):
    first_half = 2 * lax.axis_index("ctx")
    dq_ref[...] = jnp.zeros(dq_ref.shape, f32)

    def clear(index, carry):
        total[index] = jnp.zeros(total.shape[1:], f32)
        return carry

    lax.fori_loop(0, 2 * CTX, clear, 0)

    def work(part, slot, masked):
        kv = kv_ref[slot]
        queries = q_ref[part]
        grads = do_ref[part]
        scores = contract(kv, queries, 1, 1)
        probs = jnp.exp2((scores - lse_ref[part]) * log2_e)
        if masked:
            probs = jnp.where(visible_mask(scores.shape[1]), probs, 0.0)
        prob_grad = contract(kv, grads, 1, 1)
        score_grad = (probs * (prob_grad - delta_ref[part])).astype(bf16)
        total[slot] += contract(probs.astype(bf16), grads, 1, 0) + contract(
            score_grad, queries, 1, 0
        )
        dq_ref[part] += contract(kv, score_grad, 0, 0)

    def step(index, carry):
        part, slot, diagonal = unit(index, first_half)

        @pl.when(diagonal)
        def _():
            work(part, slot, True)

        @pl.when(jnp.logical_not(diagonal))
        def _():
            work(part, slot, False)

        return carry

    lax.fori_loop(0, 2 * CTX + 1, step, 0)

    def write(index, carry):
        dkv_ref[index] = total[index].astype(bf16)
        return carry

    lax.fori_loop(0, 2 * CTX, write, 0)


def attention_back(q_rows, do_rows, lse, delta, kv_all):
    rows = q_rows.shape[1]
    return pl.pallas_call(
        backward_kernel,
        out_shape=[shape(kv_all.shape, bf16), shape((2, 2 * HEAD, rows), f32)],
        in_specs=[VM] * 5,
        out_specs=[VM] * 2,
        scratch_shapes=[pltpu.VMEM(kv_all.shape, f32)],
        compiler_params=pltpu.CompilerParams(vmem_limit_bytes=VMEM_LIMIT),
        cost_estimate=pl.CostEstimate(
            flops=33 * 10 * HALF * rows * 256, bytes_accessed=1 << 24, transcendentals=33 * HALF * rows
        ),
    )(q_rows, do_rows, lse, delta, kv_all)


def phases(positions, head_width):
    steps_up = jnp.arange(head_width // 2).astype(f32)
    frequency = rope_base ** (-2.0 * steps_up / head_width)
    angles = positions.astype(f32)[:, None] * frequency[None, :]
    angles = jnp.concatenate([angles, angles], axis=1)
    return (jnp.cos(angles), jnp.sin(angles))


def rotate(values, cosine, sine):
    half_width = values.shape[-1] // 2
    turned = jnp.concatenate([-values[..., half_width:], values[..., :half_width]], axis=-1)
    return values * cosine + turned * sine


def rotate_back(grads, cosine, sine):
    half_width = grads.shape[-1] // 2
    turned = grads * sine
    turned = jnp.concatenate([turned[..., half_width:], -turned[..., :half_width]], axis=-1)
    return grads * cosine + turned


def normalize(values):
    inverse = lax.rsqrt(jnp.mean(values * values, axis=-1, keepdims=True) + epsilon)
    return (values * inverse, inverse)


def norm_back(grads, scaled, inverse, gain):
    inner = grads * gain
    return (
        inverse * (inner - scaled * jnp.mean(inner * scaled, axis=-1, keepdims=True)),
        jnp.sum(grads * scaled, axis=0),
    )


def swap_home(array):
    pairs = []
    for c in range(CTX):
        for m in range(MP):
            t = CTX - 1 - c if m >= MP // 2 else c
            pairs.append((c * MP + m, t * MP + m))
    return lax.ppermute(array, ("ctx", "mp"), pairs)


def sum_over_ctx(terms):
    c = lax.axis_index("ctx")
    chip, core = c // 2, lax.rem(c, 2)
    mine = lax.dynamic_index_in_dim(terms, core, 1, False)
    theirs = lax.dynamic_index_in_dim(terms, 1 - core, 1, False)
    got = lax.ppermute(theirs, "ctx", [(i, i ^ 1) for i in range(CTX)])
    pair = (mine.astype(f32) + got.astype(f32)).astype(bf16)
    total = lax.dynamic_index_in_dim(pair, chip, 0, False).astype(f32)
    for k in range(1, 8):
        piece = lax.dynamic_index_in_dim(pair, jnp.bitwise_xor(chip, k), 0, False)
        total = total + lax.ppermute(
            piece, "ctx", [(i, i ^ (2 * k)) for i in range(CTX)]
        ).astype(f32)
    return total


def heads_to_rows(values):
    return values.reshape(2, HALF, 2, HEAD).transpose(0, 2, 1, 3).reshape(2, 2 * HALF, HEAD)


def body(
    layer_input,
    positions,
    expert_ids,
    attn_gain,
    w_query,
    w_key,
    w_value,
    w_attn_out,
    ffn_gain,
    router,
    w_in,
    w_out,
    cotangent,
):
    c, m = place()
    in_w = lax.all_gather(w_in, "ctx", axis=1, tiled=True)
    out_expert = lax.all_gather(w_out, "ctx", axis=2, tiled=True)
    dy_all = lax.all_gather(swap_home(cotangent), "mp", axis=0, tiled=True)

    own_positions = lax.dynamic_slice_in_dim(positions, m * TOK, TOK, 0)
    id_pack = jnp.concatenate(
        [expert_ids.T, own_positions[None, :], jnp.zeros((7, TOK), jnp.int32)], axis=0
    )
    w_pack = jnp.concatenate(
        [
            w_query,
            w_key,
            w_value,
            router,
            attn_gain[:, None],
            ffn_gain[:, None],
            jnp.zeros((64, 94), bf16),
            w_attn_out.T,
        ],
        axis=1,
    )
    x_all, id_all, w_all = comm_call(
        start_kernel,
        1,
        [layer_input, id_pack, w_pack],
        [
            shape((MP, TOK, 1024)),
            shape((MP, 16, TOK), jnp.int32),
            shape((CTX, 64, 512)),
        ],
        [MP, MP, MP, MP, CTX, CTX, 3],
        4 << 20,
    )
    inputs = x_all.reshape(BLOCK, 1024).astype(f32)
    ids = id_all[:, :8, :].transpose(1, 0, 2).reshape(8, BLOCK)
    places = id_all[:, 8, :].reshape(BLOCK)
    w_all = w_all.reshape(1024, 512)
    qkv_w = w_all[:, :256]
    router_w = w_all[:, 256:288]
    gain_one = w_all[:, 288].astype(f32)
    gain_two = w_all[:, 289].astype(f32)
    out_w = w_all[:, 384:].T

    scaled_all, _ = normalize(inputs)
    normed = (scaled_all * gain_one).astype(bf16)
    qkv = jnp.dot(normed, qkv_w, preferred_element_type=f32)
    cosine, sine = phases(places, HEAD)
    cos2, sin2 = cosine[:, None, :], sine[:, None, :]
    queries = rotate(qkv[:, :128].reshape(BLOCK, 2, HEAD), cos2, sin2).astype(bf16)
    queries = queries * jnp.asarray(score_scale, bf16)
    q_rows = heads_to_rows(queries.reshape(BLOCK, 128))
    q_rows = jnp.concatenate([q_rows, jnp.zeros_like(q_rows)], axis=-1)
    keys = rotate(qkv[:, 128:192], cosine, sine).astype(bf16)
    kv_new = jnp.concatenate([keys, qkv[:, 192:].astype(bf16)], axis=-1)
    kv_all, out_w_all = comm_call(
        keys_kernel,
        2,
        [kv_new, out_w],
        [shape((CTX, BLOCK, 128)), shape((MP, 128, 1024))],
        [8, 8, 8, 8, MP, MP, 2],
        8 << 20,
    )
    kv_all = kv_all.reshape(2 * CTX, HALF, 128)
    out_cols, lse = attention(q_rows, kv_all)
    attended = (
        out_cols.reshape(2, HEAD, 2, HALF).transpose(0, 3, 2, 1).reshape(BLOCK, 128)
    )
    out_rows = attended.astype(bf16)
    (rows_all,) = comm_call(
        gather_kernel, 3, [out_rows], [shape((MP, BLOCK, 128))], [MP, MP, 1], 4 << 20
    )
    branch = lax.dot_general(
        rows_all, out_w_all, (((0, 2), (0, 1)), ((), ())), preferred_element_type=f32
    )
    hidden = inputs + branch_scale * branch
    scaled_two, inverse_two = normalize(hidden)
    routed = (scaled_two * gain_two).astype(bf16)

    logits = contract(router_w, routed, 0, 1)
    experts = lax.broadcasted_iota(jnp.int32, (32, BLOCK), 0)
    member = jnp.any(ids[:, None, :] == experts[None], axis=0)
    chosen = jnp.where(member, logits, -jnp.inf)
    top_logit = jnp.max(chosen, axis=0, keepdims=True)
    powers = jnp.exp(chosen - top_logit)
    gates = powers / jnp.sum(powers, axis=0, keepdims=True)

    here = 4 * m + lax.broadcasted_iota(jnp.int32, (4, BLOCK), 0)
    selected = jnp.any(ids[:, None, :] == here[None], axis=0)
    earlier = (
        lax.broadcasted_iota(jnp.int32, (BLOCK, BLOCK), 0)
        <= lax.broadcasted_iota(jnp.int32, (BLOCK, BLOCK), 1)
    ).astype(bf16)
    counts = jnp.dot(selected.astype(bf16), earlier, preferred_element_type=f32)
    rank = jnp.where(selected, counts.astype(jnp.int32) - 1, -1)
    capacity = 288
    place_bool = rank[:, None, :] == lax.broadcasted_iota(jnp.int32, (4, capacity, BLOCK), 1)
    placing = place_bool.astype(bf16).reshape(4 * capacity, BLOCK)
    gates_here = lax.dynamic_slice_in_dim(gates, 4 * m, 4, 0)
    slot_gate = jnp.sum(jnp.where(place_bool, gates_here[:, None, :], 0.0), axis=2)

    incoming = jnp.dot(placing, routed, preferred_element_type=f32).astype(bf16)
    incoming = incoming.reshape(4, capacity, 1024)
    dy_rows = jnp.dot(placing, dy_all, preferred_element_type=f32).reshape(4, capacity, 1024)
    gate_up = jnp.einsum("esd,edf->esf", incoming, in_w, preferred_element_type=f32)
    gate_part, up_part = gate_up[..., :512], gate_up[..., 512:]
    squashed = jax.nn.sigmoid(gate_part)
    silu_part = gate_part * squashed
    active = (silu_part * up_part).astype(bf16)
    produced = jnp.einsum(
        "esf,efd->esd", active, out_expert, preferred_element_type=f32
    ).astype(bf16)
    produced_f = produced.astype(f32)
    d_produced = (branch_scale * slot_gate[..., None] * dy_rows).astype(bf16)
    slot_share = branch_scale * jnp.sum(dy_rows * produced_f, axis=2)
    weighted = (slot_gate[..., None] * produced_f).astype(bf16).reshape(4 * capacity, 1024)
    mixed = branch_scale * contract(placing, weighted, 0, 0)
    mixed = mixed.astype(bf16).reshape(MP, TOK, 1024)

    d_active = jnp.einsum("esd,efd->esf", d_produced, out_expert, preferred_element_type=f32)
    slope = squashed * (1.0 + gate_part * (1.0 - squashed))
    d_gate_up = jnp.concatenate(
        [d_active * up_part * slope, d_active * silu_part], axis=-1
    ).astype(bf16)
    row_grads = jnp.einsum(
        "esf,edf->esd", d_gate_up, in_w, preferred_element_type=f32
    ).astype(bf16)
    routed_terms = contract(placing, row_grads.reshape(4 * capacity, 1024), 0, 0)
    routed_terms = routed_terms.astype(bf16).reshape(MP, TOK, 1024)
    share = jnp.sum(jnp.where(place_bool, slot_share[:, :, None], 0.0), axis=1)
    share = jnp.pad(share.reshape(4, MP, TOK).transpose(1, 0, 2), ((0, 0), (0, 4), (0, 0)))
    routed_got, share_got = comm_call(
        scatter_kernel,
        4,
        [routed_terms, share],
        [shape((MP, TOK, 1024)), shape((MP, 8, TOK), f32)],
        [MP, MP, MP, MP, 2],
        4 << 20,
    )

    def own_rows(array):
        return lax.dynamic_slice_in_dim(array, m * TOK, TOK, 0)

    hidden_own = own_rows(hidden)
    scaled_own, inverse_own = normalize(hidden_own)
    routed_own = (scaled_own * gain_two).astype(bf16).astype(f32)
    dy_own = own_rows(dy_all).astype(f32)
    gates_own = lax.dynamic_slice_in_dim(gates, m * TOK, TOK, 1)
    share_own = share_got[:, :4, :].reshape(32, TOK)
    logit_grad = gates_own * (
        share_own - jnp.sum(gates_own * share_own, axis=0, keepdims=True)
    )
    routed_grad = jnp.sum(routed_got.astype(f32), axis=0) + lax.dot_general(
        logit_grad,
        router_w.astype(f32),
        (((0,), (1,)), ((), ())),
        precision=highest,
        preferred_element_type=f32,
    )
    router_grad = lax.dot_general(
        routed_own,
        logit_grad,
        (((0,), (1,)), ((), ())),
        precision=highest,
        preferred_element_type=f32,
    )
    hidden_grad, gain_two_grad = norm_back(routed_grad, scaled_own, inverse_own, gain_two)
    hidden_grad = hidden_grad + dy_own
    branch_grad = (branch_scale * hidden_grad).astype(bf16)
    (branch_rows,) = comm_call(
        gather_kernel, 5, [branch_grad], [shape((MP, TOK, 1024))], [MP, MP, 1], 4 << 20
    )
    branch_rows = branch_rows.reshape(BLOCK, 1024)
    hidden_grad_home = swap_home(hidden_grad)

    out_expert_grad = jnp.einsum(
        "esf,esd->efd", active, d_produced, preferred_element_type=f32
    ).astype(bf16)
    in_expert_grad = jnp.einsum(
        "esd,esf->edf", incoming, d_gate_up, preferred_element_type=f32
    ).astype(bf16)
    in_terms = in_expert_grad.reshape(4, 8, 2, 64, 1024).transpose(1, 2, 0, 3, 4)
    out_terms = out_expert_grad.reshape(4, 512, 8, 2, 64).transpose(2, 3, 0, 1, 4)
    expert_in = sum_over_ctx(in_terms.reshape(8, 2, 4 * 64, 1024)).reshape(4, 64, 1024)
    expert_out = sum_over_ctx(out_terms.reshape(8, 2, 4 * 512, 64)).reshape(4, 512, 64)

    mixed_got = lax.all_to_all(mixed, "mp", split_axis=0, concat_axis=0, tiled=True)
    outputs = (hidden_own + jnp.sum(mixed_got.astype(f32), axis=0)).astype(bf16)
    outputs = swap_home(outputs)

    out_grad = contract(branch_rows, out_w, 1, 1).astype(bf16)
    do_rows = heads_to_rows(out_grad)
    delta = jnp.sum(do_rows.astype(f32) * heads_to_rows(attended), axis=-1)[:, None, :]
    do_rows = jnp.concatenate([jnp.zeros_like(do_rows), do_rows], axis=-1)
    dkv_terms, dq_cols = attention_back(q_rows, do_rows, lse, delta, kv_all)
    dkv_terms = dkv_terms.reshape(8, 2, BLOCK, 128)
    (theirs,) = comm_call(
        sibling_kernel, 6, [dkv_terms], [shape((8, BLOCK, 128))], [1, 1], 4 << 20
    )
    mine = lax.dynamic_index_in_dim(dkv_terms, lax.rem(c, 2), 1, False)
    pair = (mine.astype(f32) + theirs.astype(f32)).astype(bf16)
    (dkv_got,) = comm_call(
        chips_kernel, 7, [pair], [shape((8, BLOCK, 128))], [8, 8, 1], 4 << 20
    )
    dkv = jnp.sum(dkv_got.astype(f32), axis=0)
    d_key = rotate_back(dkv[:, :HEAD], cosine, sine).astype(bf16)
    d_value = dkv[:, HEAD:].astype(bf16)
    dq = score_scale * dq_cols[:, :HEAD, :]
    dq = dq.reshape(2, HEAD, 2, HALF).transpose(0, 3, 2, 1).reshape(BLOCK, 2, HEAD)
    d_query = rotate_back(dq, cos2, sin2).reshape(BLOCK, 128).astype(bf16)
    d_qkv = jnp.concatenate([d_query, d_key, d_value], axis=1)
    qkv_w_grad = contract(normed, d_qkv, 0, 0)
    out_w_grad = contract(branch_rows, out_rows, 0, 0)
    w_terms = jnp.concatenate([qkv_w_grad, out_w_grad], axis=1).astype(bf16)
    normed_terms = contract(d_qkv, qkv_w, 1, 1).astype(bf16).reshape(MP, TOK, 1024)
    normed_got, w_got = comm_call(
        finish_kernel,
        8,
        [normed_terms, w_terms.reshape(CTX, 64, 384)],
        [shape((MP, TOK, 1024)), shape((CTX, 64, 384))],
        [MP, MP, CTX, CTX, 2],
        5 << 20,
    )
    w_grad = jnp.sum(w_got.astype(f32), axis=0)
    normed_grad = jnp.sum(normed_got.astype(f32), axis=0)
    scaled_one, inverse_one = normalize(layer_input.astype(f32))
    input_grad, gain_one_grad = norm_back(normed_grad, scaled_one, inverse_one, gain_one)
    input_grad = (input_grad + hidden_grad_home).astype(bf16)

    small = jnp.concatenate(
        [
            router_grad,
            gain_one_grad[:, None],
            gain_two_grad[:, None],
            jnp.zeros((1024, 94), f32),
        ],
        axis=1,
    )
    sums = small_sums(small.reshape(CTX, MP, 8, 128))
    return (
        outputs,
        input_grad,
        sums[:, 32],
        w_grad[:, :128],
        w_grad[:, 128:192],
        w_grad[:, 192:256],
        w_grad[:, 256:].T,
        sums[:, 33],
        sums[:, :32],
        expert_in,
        expert_out,
    )


def solution(mesh):
    placed = (
        P(("ctx", "mp"), None),
        P("ctx"),
        P(("ctx", "mp"), None),
        P("ctx"),
        P("ctx", "mp"),
        P("ctx", "mp"),
        P("ctx", "mp"),
        P("mp", "ctx"),
        P("ctx"),
        P("ctx", None),
        P("mp", "ctx", None),
        P("mp", None, "ctx"),
        P(("ctx", "mp"), None),
    )
    return jax.shard_map(
        body,
        mesh=mesh,
        in_specs=placed,
        out_specs=(
            P(("ctx", "mp"), None),
            P(("ctx", "mp"), None),
            P(("ctx", "mp")),
            P("ctx", "mp"),
            P("ctx", "mp"),
            P("ctx", "mp"),
            P("mp", "ctx"),
            P(("ctx", "mp")),
            P(("ctx", "mp"), None),
            P("mp", "ctx", None),
            P("mp", None, "ctx"),
        ),
        check_vma=False,
    )
```

```python
import functools

import jax
import jax.numpy as jnp
from jax import lax
from jax.experimental import pallas as pl
from jax.experimental.pallas import tpu as pltpu
from jax.sharding import PartitionSpec as P

MESH = pl.DeviceIdType.MESH
epsilon = 1e-06
branch_scale = 0.22
score_scale = 0.015625
rope_base = 10000.0
highest = lax.Precision.HIGHEST
log2_e = 1.4426950408889634
bf16 = jnp.bfloat16
f32 = jnp.float32
CTX, MP = 16, 8
HEAD = 64
TOK = 128
BLOCK = 1024
HALF = 512
ANY = pl.BlockSpec(memory_space=pl.ANY)
VM = pl.BlockSpec(memory_space=pltpu.VMEM)
VMEM_LIMIT = 56 * 1024 * 1024


def contract(left, right, left_dim, right_dim):
    return lax.dot_general(
        left, right, (((left_dim,), (right_dim,)), ((), ())), preferred_element_type=f32
    )


def place():
    return lax.axis_index("ctx"), lax.axis_index("mp")


def greet(signal_to, expected):
    barrier = pltpu.get_barrier_semaphore()
    for target in signal_to:
        pl.semaphore_signal(barrier, inc=1, device_id=target, device_id_type=MESH)
    pl.semaphore_wait(barrier, expected)


def remote(src, dst, send, recv, target):
    return pltpu.make_async_remote_copy(
        src_ref=src, dst_ref=dst, send_sem=send, recv_sem=recv,
        device_id=target, device_id_type=MESH,
    )


def comm_call(kernel, number, arrays, outs, sems, cost):
    return pl.pallas_call(
        kernel,
        out_shape=outs,
        in_specs=[ANY] * len(arrays),
        out_specs=[ANY] * len(outs),
        scratch_shapes=[
            pltpu.SemaphoreType.DMA((n,)) if isinstance(n, int) else n for n in sems
        ],
        compiler_params=pltpu.CompilerParams(collective_id=number, has_side_effects=True),
        cost_estimate=pl.CostEstimate(flops=0, bytes_accessed=cost, transcendentals=0),
    )(*arrays)


def shape(dims, kind=bf16):
    return jax.ShapeDtypeStruct(dims, kind)


def flip(index, stride):
    return index + stride - 2 * stride * lax.rem(index // stride, 2)


class Ring:
    def __init__(self, own, dst, index, spread, near, stride, target, sems, sibling=None):
        send, recv, loc = sems[:3]
        count = spread
        plus, minus = lax.rem(index + stride, count), lax.rem(index + count - stride, count)
        far = lax.rem(index + 2 * stride, count)
        near_of = lambda slot: flip(slot, near)
        me_near = near_of(index)

        def copy(src, place_of, at, to):
            return lambda: remote(src, place_of, send.at[at], recv.at[at], target(to))

        def relay(slot, part, at, to):
            return copy(dst(slot, part), dst(slot, part), at, to)

        self.own = lambda: pltpu.make_async_copy(own, dst(index, None), loc)
        self.to_near = copy(own, dst(index, None), 0, me_near)
        self.plus_own = copy(own, dst(index, None), 1, plus)
        self.minus_own = copy(own, dst(index, None), 2, minus)
        self.plus_near = relay(me_near, None, 3, plus)
        self.minus_near = relay(me_near, None, 4, minus)
        self.plus_far = relay(minus, 0, 5, plus)
        self.minus_far = relay(plus, 1, 6, minus)
        self.plus_far_near = relay(near_of(minus), 0, 7, plus)
        self.minus_far_near = relay(near_of(plus), 1, 8, minus)
        self.over = None
        if sibling is not None:
            send2, recv2 = sems[3:]
            parts = [
                (index, None),
                (me_near, None),
                (minus, None),
                (plus, None),
                (near_of(minus), None),
                (near_of(plus), None),
                (far, 0),
                (far, 1),
                (near_of(far), 0),
                (near_of(far), 1),
            ]

            def over(at):
                slot, part = parts[at]
                src = own if at == 0 else dst(slot, part)
                return remote(src, dst(slot, part), send2.at[at], recv2.at[at], sibling)

            self.over = over

    def cross(self, *numbers):
        if self.over is not None:
            for at in numbers:
                self.over(at).start()

    def start(self):
        self.own().start()
        for copy in (self.to_near, self.plus_own, self.minus_own):
            copy().start()
        self.cross(0)

    def relay_near(self):
        self.to_near().wait_recv()
        self.plus_near().start()
        self.minus_near().start()
        self.cross(1)

    def relay_own(self):
        self.plus_own().wait_recv()
        self.plus_far().start()
        self.minus_own().wait_recv()
        self.minus_far().start()
        self.cross(2, 3)

    def relay_far(self):
        self.plus_near().wait_recv()
        self.plus_far_near().start()
        self.minus_near().wait_recv()
        self.minus_far_near().start()
        self.cross(4, 5)

    def finish(self):
        last = (self.plus_far, self.minus_far, self.plus_far_near, self.minus_far_near)
        for number, copy in enumerate(last):
            copy().wait_recv()
            self.cross(6 + number)
        for copy in (
            self.to_near,
            self.plus_own,
            self.minus_own,
            self.plus_near,
            self.minus_near,
        ) + last:
            copy().wait_send()
        if self.over is not None:
            for at in range(10):
                self.over(at).wait()
        self.own().wait()


def mp_ring(own, dst, sems):
    c, m = place()
    return Ring(own, dst, m, MP, 1, 2, lambda slot: (c, slot), sems)


def ctx_ring(own, dst, sems):
    c, m = place()
    return Ring(own, dst, c, CTX, 2, 4, lambda slot: (slot, m), sems, (flip(c, 1), m))


def mp_neighbours():
    c, m = place()
    return [(c, flip(m, 1)), (c, lax.rem(m + 2, MP)), (c, lax.rem(m + 6, MP))]


def ctx_neighbours():
    c, m = place()
    return [
        (flip(c, 2), m),
        (lax.rem(c + 4, CTX), m),
        (lax.rem(c + 12, CTX), m),
        (flip(c, 1), m),
    ]


def slots(ref):
    half = ref.shape[1] // 2

    def dst(slot, part):
        return ref.at[slot] if part is None else ref.at[slot, pl.ds(part * half, half)]

    return dst


def row_slots(ref):
    half = ref.shape[0] // 2

    def dst(slot, part):
        rows = pl.ds(pl.multiple_of(slot * 64, 64), 64)
        return ref.at[:, rows] if part is None else ref.at[pl.ds(part * half, half), rows]

    return dst


MP_SEMS = [pltpu.SemaphoreType.DMA((9,)), pltpu.SemaphoreType.DMA((9,)), pltpu.SemaphoreType.DMA]
CTX_SEMS = MP_SEMS + [pltpu.SemaphoreType.DMA((10,)), pltpu.SemaphoreType.DMA((10,))]


def start_kernel(x_ref, id_ref, w_ref, xo, ido, wo, xs, xr, ids, idr, ws, wr, loc):
    c, m = place()
    upper = m >= MP // 2
    t = jnp.where(upper, CTX - 1 - c, c)
    signals = []
    for k in range(1, MP):
        sender = lax.rem(m + k, MP)
        signals.append((jnp.where(sender >= MP // 2, CTX - 1 - c, c), sender))
    for k in range(1, CTX):
        signals.append((lax.rem(c + k, CTX), m))
    barrier = pltpu.get_barrier_semaphore()
    for target in signals:
        pl.semaphore_signal(barrier, inc=1, device_id=target, device_id_type=MESH)

    @pl.when(upper)
    def _():
        pl.semaphore_signal(barrier, inc=1, device_id=(CTX - 1 - c, m), device_id_type=MESH)
        pl.semaphore_wait(barrier, MP + CTX - 1)

    @pl.when(jnp.logical_not(upper))
    def _():
        pl.semaphore_wait(barrier, MP + CTX - 2)

    own_w = pltpu.make_async_copy(w_ref, wo.at[c], loc.at[0])
    own_w.start()
    x_copies, id_copies, w_copies = [], [], []
    for k in range(MP):
        target = (t, lax.rem(m + k, MP))
        x_copies.append(remote(x_ref, xo.at[m], xs.at[k], xr.at[k], target))
        id_copies.append(remote(id_ref, ido.at[m], ids.at[k], idr.at[k], target))
    for k in range(1, CTX):
        w_copies.append(remote(w_ref, wo.at[c], ws.at[k], wr.at[k], (lax.rem(c + k, CTX), m)))
    own_x = pltpu.make_async_copy(x_ref, xo.at[m], loc.at[1])
    own_id = pltpu.make_async_copy(id_ref, ido.at[m], loc.at[2])

    @pl.when(upper)
    def _():
        x_copies[0].start()
        id_copies[0].start()

    @pl.when(jnp.logical_not(upper))
    def _():
        own_x.start()
        own_id.start()

    for k in range(1, MP):
        x_copies[k].start()
        id_copies[k].start()
    for copy in w_copies:
        copy.start()
    for k in range(1, MP):
        x_copies[k].wait()
        id_copies[k].wait()
    for copy in w_copies:
        copy.wait()
    own_w.wait()

    @pl.when(upper)
    def _():
        x_copies[0].wait()
        id_copies[0].wait()

    @pl.when(jnp.logical_not(upper))
    def _():
        own_x.wait()
        own_id.wait()


def keys_kernel(kv_ref, out, *sems):
    greet(ctx_neighbours(), 4)
    ring = ctx_ring(kv_ref, slots(out), sems)
    ring.start()
    ring.relay_near()
    ring.relay_own()
    ring.relay_far()
    ring.finish()


def gather_kernel(a_ref, out, *sems):
    greet(mp_neighbours(), 3)
    ring = mp_ring(a_ref, slots(out), sems)
    ring.start()
    ring.relay_near()
    ring.relay_own()
    ring.relay_far()
    ring.finish()


def outputs_kernel(a_ref, g_ref, h_ref, ao, go, ho, s1, r1, s2, r2, loc):
    c, m = place()
    core = lax.rem(c, 2)
    sibling = (flip(c, 1), m)
    mates = [(c, lax.rem(m + k, MP)) for k in range(1, MP)]
    greet(mates + [sibling], MP)
    own_a = pltpu.make_async_copy(a_ref.at[m], ao.at[m], loc.at[0])
    own_a.start()
    copies = []
    for k in range(1, MP):
        to = lax.rem(m + k, MP)
        copies.append(remote(a_ref.at[to], ao.at[m], s1.at[k], r1.at[k], mates[k - 1]))
    copies.append(remote(g_ref.at[:, :, 1 - core], go, s2.at[0], r2.at[0], sibling))
    copies.append(remote(h_ref.at[:, :, 1 - core], ho, s2.at[1], r2.at[1], sibling))
    for copy in copies:
        copy.start()
    for copy in copies:
        copy.wait()
    own_a.wait()


def scatter_kernel(a_ref, b_ref, ao, bo, s1, r1, s2, r2, loc):
    c, m = place()
    mates = [(c, lax.rem(m + k, MP)) for k in range(1, MP)]
    greet(mates, MP - 1)
    own_a = pltpu.make_async_copy(a_ref.at[m], ao.at[m], loc.at[0])
    own_a.start()
    own_b = pltpu.make_async_copy(b_ref.at[m], bo.at[m], loc.at[1])
    own_b.start()
    copies = []
    for k in range(1, MP):
        to = lax.rem(m + k, MP)
        copies.append(remote(a_ref.at[to], ao.at[m], s1.at[k], r1.at[k], mates[k - 1]))
        copies.append(remote(b_ref.at[to], bo.at[m], s2.at[k], r2.at[k], mates[k - 1]))
    for copy in copies:
        copy.start()
    for copy in copies:
        copy.wait()
    own_a.wait()
    own_b.wait()


def sibling_kernel(a_ref, out, send, recv):
    c, m = place()
    chip, core = c // 2, lax.rem(c, 2)
    sibling = (chip * 2 + 1 - core, m)
    greet([sibling], 1)
    copy = remote(a_ref.at[:, 1 - core], out, send.at[0], recv.at[0], sibling)
    copy.start()
    copy.wait()


def chips_kernel(a_ref, out, send, recv, loc):
    c, m = place()
    chip, core = c // 2, lax.rem(c, 2)
    others = [(lax.rem(chip + k, 8) * 2 + core, m) for k in range(1, 8)]
    greet(others, 7)
    own = pltpu.make_async_copy(a_ref.at[chip], out.at[chip], loc.at[0])
    own.start()
    copies = []
    for k in range(1, 8):
        to = lax.rem(chip + k, 8)
        copy = remote(a_ref.at[to], out.at[chip], send.at[k], recv.at[k], others[k - 1])
        copy.start()
        copies.append(copy)
    for copy in copies:
        copy.wait()
    own.wait()


def finish_kernel(a_ref, g_ref, ao, go, s1, r1, s2, r2, loc):
    c, m = place()
    upper = m >= MP // 2
    t = jnp.where(upper, CTX - 1 - c, c)
    barrier = pltpu.get_barrier_semaphore()
    for k in range(1, MP):
        pl.semaphore_signal(
            barrier, inc=1, device_id=(t, lax.rem(m + k, MP)), device_id_type=MESH
        )
    for k in range(1, CTX):
        pl.semaphore_signal(
            barrier, inc=1, device_id=(lax.rem(c + k, CTX), m), device_id_type=MESH
        )

    @pl.when(upper)
    def _():
        pl.semaphore_signal(barrier, inc=1, device_id=(t, m), device_id_type=MESH)
        pl.semaphore_wait(barrier, MP + CTX - 1)

    @pl.when(jnp.logical_not(upper))
    def _():
        pl.semaphore_wait(barrier, MP + CTX - 2)

    own_g = pltpu.make_async_copy(g_ref.at[c], go.at[c], loc.at[0])
    own_g.start()
    own_a = pltpu.make_async_copy(a_ref.at[m], ao.at[m], loc.at[1])
    a_copies, g_copies = [], []
    for k in range(MP):
        to = lax.rem(m + k, MP)
        target = (jnp.where(to >= MP // 2, CTX - 1 - c, c), to)
        a_copies.append(remote(a_ref.at[to], ao.at[m], s1.at[k], r1.at[k], target))
    for k in range(1, CTX):
        to = lax.rem(c + k, CTX)
        g_copies.append(remote(g_ref.at[to], go.at[c], s2.at[k], r2.at[k], (to, m)))

    @pl.when(upper)
    def _():
        a_copies[0].start()

    @pl.when(jnp.logical_not(upper))
    def _():
        own_a.start()

    for k in range(1, MP):
        a_copies[k].start()
    for copy in g_copies:
        copy.start()
    for k in range(1, MP):
        a_copies[k].wait()
    for copy in g_copies:
        copy.wait()
    own_g.wait()

    @pl.when(upper)
    def _():
        a_copies[0].wait()

    @pl.when(jnp.logical_not(upper))
    def _():
        own_a.wait()


def sums_kernel(a_ref, out, got, part, got2, s1, r1, s2, r2):
    c, m = place()
    peers = [(lax.rem(c + k, CTX), m) for k in range(1, CTX)]
    mates = [(c, lax.rem(m + k, MP)) for k in range(1, MP)]
    greet(peers + mates, CTX - 1 + MP - 1)
    copies = []
    for k in range(1, CTX):
        to = lax.rem(c + k, CTX)
        copy = remote(a_ref.at[to], got.at[k], s1.at[k], r1.at[k], peers[k - 1])
        copy.start()
        copies.append(copy)
    total = a_ref[c]
    for copy in copies:
        copy.wait()
    for k in range(1, CTX):
        total = total + got[k]
    part[...] = total
    copies = []
    for k in range(1, MP):
        to = lax.rem(m + k, MP)
        copy = remote(part.at[to], got2.at[k], s2.at[k], r2.at[k], mates[k - 1])
        copy.start()
        copies.append(copy)
    last = part[m]
    for copy in copies:
        copy.wait()
    for k in range(1, MP):
        last = last + got2[k]
    out[...] = last


def small_sums(terms):
    dims = terms.shape[2:]
    return pl.pallas_call(
        sums_kernel,
        out_shape=shape(dims, f32),
        in_specs=[VM],
        out_specs=VM,
        scratch_shapes=[
            pltpu.VMEM((CTX, MP) + dims, f32),
            pltpu.VMEM((MP,) + dims, f32),
            pltpu.VMEM((MP,) + dims, f32),
            pltpu.SemaphoreType.DMA((CTX,)),
            pltpu.SemaphoreType.DMA((CTX,)),
            pltpu.SemaphoreType.DMA((MP,)),
            pltpu.SemaphoreType.DMA((MP,)),
        ],
        compiler_params=pltpu.CompilerParams(collective_id=9, has_side_effects=True),
    )(terms)


def unit(index, first_half):
    second = index > first_half
    part = second.astype(jnp.int32)
    key_half = jnp.where(second, index - first_half - 1, index)
    odd = lax.rem(key_half, 2) == 1
    slot = jnp.where(odd, 2 * CTX - key_half, key_half)
    diagonal = jnp.logical_or(index == first_half, index == 2 * CTX)
    return part, slot, diagonal


def visible_mask(rows):
    key_at = lax.broadcasted_iota(jnp.int32, (HALF, rows), 0)
    query_at = lax.rem(lax.broadcasted_iota(jnp.int32, (HALF, rows), 1), HALF)
    return key_at <= query_at


def forward_kernel(
    q_ref, kv_ref, in_ref, outw_ref, dy_ref, rows_ref,
    out_ref, lse_ref, in_all, outw_all, dy_all, rows_all,
    best, total, summed, *sems,
):
    first_half = 2 * lax.axis_index("ctx")
    greet(ctx_neighbours() + mp_neighbours(), 7)
    weights_rings = [
        ctx_ring(in_ref, row_slots(in_all), sems[0:5]),
        ctx_ring(outw_ref, row_slots(outw_all), sems[5:10]),
    ]
    rows_rings = [
        mp_ring(rows_ref, slots(rows_all), sems[10:13]),
        mp_ring(dy_ref, slots(dy_all), sems[13:16]),
    ]
    for ring in weights_rings + rows_rings:
        ring.start()
    best[...] = jnp.full(best.shape, -1e30, f32)
    total[...] = jnp.zeros(total.shape, f32)
    summed[...] = jnp.zeros(summed.shape, f32)

    def work(part, slot, masked):
        kv = kv_ref[slot]
        scores = contract(kv, q_ref[part], 1, 1)
        if masked:
            scores = jnp.where(visible_mask(scores.shape[1]), scores, -jnp.inf)
        old = best[part]
        new = jnp.maximum(old, jnp.max(scores, axis=0, keepdims=True))
        weights = jnp.exp2(scores * log2_e - new * log2_e)
        fading = jnp.exp2((old - new) * log2_e)
        total[part] = total[part] * fading + jnp.sum(weights, axis=0, keepdims=True)
        summed[part] = summed[part] * fading + contract(kv, weights.astype(bf16), 0, 0)
        best[part] = new

    def step(index, carry):
        part, slot, diagonal = unit(index, first_half)

        @pl.when(index == 11)
        def _():
            for ring in rows_rings:
                ring.relay_near()
                ring.relay_own()

        @pl.when(index == 16)
        def _():
            for ring in weights_rings:
                ring.relay_near()
                ring.relay_own()

        @pl.when(index == 20)
        def _():
            for ring in rows_rings:
                ring.relay_far()

        @pl.when(index == 30)
        def _():
            for ring in weights_rings:
                ring.relay_far()

        @pl.when(diagonal)
        def _():
            work(part, slot, True)

        @pl.when(jnp.logical_not(diagonal))
        def _():
            work(part, slot, False)

        return carry

    lax.fori_loop(0, 2 * CTX + 1, step, 0)
    for part in range(2):
        out_ref[part] = summed[part][HEAD:, :] / total[part]
        lse_ref[part] = best[part] + jnp.log(total[part])
    for ring in rows_rings + weights_rings:
        ring.finish()


def attention(q_rows, kv_all, w_in, w_out_t, dy, out_rows_w):
    rows = q_rows.shape[1]
    return pl.pallas_call(
        forward_kernel,
        out_shape=[
            shape((2, HEAD, rows), f32),
            shape((2, 1, rows), f32),
            shape((4, 1024, 1024)),
            shape((4, 1024, 512)),
            shape((MP, TOK, 1024)),
            shape((MP, TOK, 1024)),
        ],
        in_specs=[VM, VM, ANY, ANY, ANY, ANY],
        out_specs=[VM, VM, ANY, ANY, ANY, ANY],
        scratch_shapes=[
            pltpu.VMEM((2, 1, rows), f32),
            pltpu.VMEM((2, 1, rows), f32),
            pltpu.VMEM((2, 2 * HEAD, rows), f32),
        ]
        + CTX_SEMS * 2
        + MP_SEMS * 2,
        compiler_params=pltpu.CompilerParams(
            vmem_limit_bytes=VMEM_LIMIT, collective_id=10, has_side_effects=True
        ),
        cost_estimate=pl.CostEstimate(
            flops=33 * 4 * HALF * rows * 256, bytes_accessed=1 << 23, transcendentals=33 * HALF * rows
        ),
    )(q_rows, kv_all, w_in, w_out_t, dy, out_rows_w)


def backward_kernel(
    q_ref, do_ref, lse_ref, delta_ref, kv_ref, pair_ref, br_ref, qw_ref,
    dkv_ref, dq_ref, grad_ref, br_all, qw_all,
    total, got_a, got_b, sum_a, sum_b, last_a, last_b, *sems,
):
    c, m = place()
    first_half = 2 * c
    x, y = c // 4, lax.rem(c // 2, 2)
    peers = [(lax.rem(c + 4 * k, CTX), m) for k in range(1, 4)]
    across = (flip(c, 2), m)
    greet(peers + [across] + mp_neighbours(), 7)
    sa, ra, sb, rb = sems[:4]
    rings = [
        mp_ring(br_ref, slots(br_all), sems[4:7]),
        mp_ring(qw_ref, slots(qw_all), sems[7:10]),
    ]

    def first_copies():
        copies = [
            remote(
                pair_ref.at[pl.ds(0, 2), lax.rem(x + k, 4)],
                got_a.at[k - 1], sa.at[k], ra.at[k], peers[k - 1],
            )
            for k in range(1, 4)
        ]
        copies.append(
            remote(pair_ref.at[pl.ds(2, 2), :, 1 - y], got_b, sa.at[0], ra.at[0], across)
        )
        return copies

    def second_copies():
        copies = [
            remote(
                sum_b.at[:, lax.rem(x + k, 4)], last_b.at[k - 1], sb.at[k], rb.at[k], peers[k - 1]
            )
            for k in range(1, 4)
        ]
        copies.append(remote(sum_a.at[:, 1 - y], last_a, sb.at[0], rb.at[0], across))
        return copies

    for copy in first_copies():
        copy.start()
    for ring in rings:
        ring.start()
    dq_ref[...] = jnp.zeros(dq_ref.shape, f32)

    def clear(index, carry):
        total[index] = jnp.zeros(total.shape[1:], f32)
        return carry

    lax.fori_loop(0, 2 * CTX, clear, 0)

    def work(part, slot, masked):
        kv = kv_ref[slot]
        queries = q_ref[part]
        grads = do_ref[part]
        scores = contract(kv, queries, 1, 1)
        probs = jnp.exp2((scores - lse_ref[part]) * log2_e)
        if masked:
            probs = jnp.where(visible_mask(scores.shape[1]), probs, 0.0)
        prob_grad = contract(kv, grads, 1, 1)
        score_grad = (probs * (prob_grad - delta_ref[part])).astype(bf16)
        total[slot] += contract(probs.astype(bf16), grads, 1, 0) + contract(
            score_grad, queries, 1, 0
        )
        dq_ref[part] += contract(kv, score_grad, 0, 0)

    def middle():
        for copy in first_copies():
            copy.wait()
        for e in range(2):
            for j in range(2):
                term = pair_ref[e, x, j].astype(f32)
                for k in range(3):
                    term = term + got_a[k, e, j].astype(f32)
                sum_a[e, j] = term.astype(bf16)
            for j in range(4):
                term = pair_ref[2 + e, j, y].astype(f32) + got_b[e, j].astype(f32)
                sum_b[e, j] = term.astype(bf16)
        for copy in second_copies():
            copy.start()

    def step(index, carry):
        part, slot, diagonal = unit(index, first_half)

        @pl.when(index == 11)
        def _():
            for ring in rings:
                ring.relay_near()
                ring.relay_own()

        @pl.when(index == 21)
        def _():
            for ring in rings:
                ring.relay_far()

        @pl.when(index == 23)
        def _():
            middle()

        @pl.when(diagonal)
        def _():
            work(part, slot, True)

        @pl.when(jnp.logical_not(diagonal))
        def _():
            work(part, slot, False)

        return carry

    lax.fori_loop(0, 2 * CTX + 1, step, 0)

    def write(index, carry):
        dkv_ref[index] = total[index].astype(bf16)
        return carry

    lax.fori_loop(0, 2 * CTX, write, 0)
    for ring in rings:
        ring.finish()
    for copy in second_copies():
        copy.wait()
    for e in range(2):
        grad_ref[e] = sum_a[e, y].astype(f32) + last_a[e].astype(f32)
        term = sum_b[e, x].astype(f32)
        for k in range(3):
            term = term + last_b[k, e].astype(f32)
        grad_ref[2 + e] = term


def attention_back(q_rows, do_rows, lse, delta, kv_all, pair, branch_grad, qkv_w):
    rows = q_rows.shape[1]
    wide = pair.shape[-1]
    return pl.pallas_call(
        backward_kernel,
        out_shape=[
            shape(kv_all.shape, bf16),
            shape((2, 2 * HEAD, rows), f32),
            shape((4, 64, wide), f32),
            shape((MP, TOK, 1024)),
            shape((MP,) + qkv_w.shape),
        ],
        in_specs=[VM] * 6 + [ANY] * 2,
        out_specs=[VM] * 3 + [ANY] * 2,
        scratch_shapes=[
            pltpu.VMEM(kv_all.shape, f32),
            pltpu.VMEM((3, 2, 2, 64, wide), bf16),
            pltpu.VMEM((2, 4, 64, wide), bf16),
            pltpu.VMEM((2, 2, 64, wide), bf16),
            pltpu.VMEM((2, 4, 64, wide), bf16),
            pltpu.VMEM((2, 64, wide), bf16),
            pltpu.VMEM((3, 2, 64, wide), bf16),
        ]
        + [pltpu.SemaphoreType.DMA((4,))] * 4
        + MP_SEMS * 2,
        compiler_params=pltpu.CompilerParams(
            vmem_limit_bytes=VMEM_LIMIT, collective_id=11, has_side_effects=True
        ),
        cost_estimate=pl.CostEstimate(
            flops=33 * 10 * HALF * rows * 256, bytes_accessed=1 << 24, transcendentals=33 * HALF * rows
        ),
    )(q_rows, do_rows, lse, delta, kv_all, pair, branch_grad, qkv_w)


def phases(positions, head_width):
    steps_up = jnp.arange(head_width // 2).astype(f32)
    frequency = rope_base ** (-2.0 * steps_up / head_width)
    angles = positions.astype(f32)[:, None] * frequency[None, :]
    angles = jnp.concatenate([angles, angles], axis=1)
    return (jnp.cos(angles), jnp.sin(angles))


def rotate(values, cosine, sine):
    half_width = values.shape[-1] // 2
    turned = jnp.concatenate([-values[..., half_width:], values[..., :half_width]], axis=-1)
    return values * cosine + turned * sine


def rotate_back(grads, cosine, sine):
    half_width = grads.shape[-1] // 2
    turned = grads * sine
    turned = jnp.concatenate([turned[..., half_width:], -turned[..., :half_width]], axis=-1)
    return grads * cosine + turned


def normalize(values):
    inverse = lax.rsqrt(jnp.mean(values * values, axis=-1, keepdims=True) + epsilon)
    return (values * inverse, inverse)


def norm_back(grads, scaled, inverse, gain):
    inner = grads * gain
    return (
        inverse * (inner - scaled * jnp.mean(inner * scaled, axis=-1, keepdims=True)),
        jnp.sum(grads * scaled, axis=0),
    )


def swap_home(array):
    pairs = []
    for c in range(CTX):
        for m in range(MP):
            t = CTX - 1 - c if m >= MP // 2 else c
            pairs.append((c * MP + m, t * MP + m))
    return lax.ppermute(array, ("ctx", "mp"), pairs)


def heads_to_rows(values):
    return values.reshape(2, HALF, 2, HEAD).transpose(0, 2, 1, 3).reshape(2, 2 * HALF, HEAD)


def body(
    layer_input,
    positions,
    expert_ids,
    attn_gain,
    w_query,
    w_key,
    w_value,
    w_attn_out,
    ffn_gain,
    router,
    w_in,
    w_out,
    cotangent,
):
    c, m = place()
    dy_swapped = swap_home(cotangent)
    own_positions = lax.dynamic_slice_in_dim(positions, m * TOK, TOK, 0)
    id_pack = jnp.concatenate(
        [expert_ids.T, own_positions[None, :], jnp.zeros((7, TOK), jnp.int32)], axis=0
    )
    w_pack = jnp.concatenate(
        [
            w_query,
            w_key,
            w_value,
            router,
            attn_gain[:, None],
            ffn_gain[:, None],
            jnp.zeros((64, 94), bf16),
            w_attn_out.T,
        ],
        axis=1,
    )
    x_all, id_all, w_all = comm_call(
        start_kernel,
        1,
        [layer_input, id_pack, w_pack],
        [
            shape((MP, TOK, 1024)),
            shape((MP, 16, TOK), jnp.int32),
            shape((CTX, 64, 512)),
        ],
        [MP, MP, MP, MP, CTX, CTX, 3],
        4 << 20,
    )
    inputs = x_all.reshape(BLOCK, 1024).astype(f32)
    ids = id_all[:, :8, :].transpose(1, 0, 2).reshape(8, BLOCK)
    places = id_all[:, 8, :].reshape(BLOCK)
    w_all = w_all.reshape(1024, 512)
    qkv_w = w_all[:, :256]
    router_w = w_all[:, 256:288]
    gain_one = w_all[:, 288].astype(f32)
    gain_two = w_all[:, 289].astype(f32)
    out_w = w_all[:, 384:].T

    scaled_all, _ = normalize(inputs)
    normed = (scaled_all * gain_one).astype(bf16)
    qkv = jnp.dot(normed, qkv_w, preferred_element_type=f32)
    cosine, sine = phases(places, HEAD)
    cosine, sine = lax.optimization_barrier((cosine, sine))
    cos2, sin2 = cosine[:, None, :], sine[:, None, :]
    queries = rotate(qkv[:, :128].reshape(BLOCK, 2, HEAD), cos2, sin2).astype(bf16)
    queries = queries * jnp.asarray(score_scale, bf16)
    q_rows = heads_to_rows(queries.reshape(BLOCK, 128))
    q_rows = jnp.concatenate([q_rows, jnp.zeros_like(q_rows)], axis=-1)
    keys = rotate(qkv[:, 128:192], cosine, sine).astype(bf16)
    kv_new = jnp.concatenate([keys, qkv[:, 192:].astype(bf16)], axis=-1)
    (kv_all,) = comm_call(
        keys_kernel, 2, [kv_new], [shape((CTX, BLOCK, 128))], CTX_SEMS, 4 << 20
    )
    kv_all = kv_all.reshape(2 * CTX, HALF, 128)
    out_cols, lse, in_w, out_w_t, dy_all, out_w_all = attention(
        q_rows, kv_all, w_in, w_out.transpose(0, 2, 1), dy_swapped, out_w
    )
    dy_all = dy_all.reshape(BLOCK, 1024)
    attended = (
        out_cols.reshape(2, HEAD, 2, HALF).transpose(0, 3, 2, 1).reshape(BLOCK, 128)
    )
    out_rows = attended.astype(bf16)
    (rows_all,) = comm_call(
        gather_kernel, 3, [out_rows], [shape((MP, BLOCK, 128))], MP_SEMS, 4 << 20
    )
    branch = lax.dot_general(
        rows_all, out_w_all, (((0, 2), (0, 1)), ((), ())), preferred_element_type=f32
    )
    hidden = inputs + branch_scale * branch
    scaled_two, inverse_two = normalize(hidden)
    routed = (scaled_two * gain_two).astype(bf16)

    logits = contract(router_w, routed, 0, 1)
    experts = lax.broadcasted_iota(jnp.int32, (32, BLOCK), 0)
    member = jnp.any(ids[:, None, :] == experts[None], axis=0)
    chosen = jnp.where(member, logits, -jnp.inf)
    top_logit = jnp.max(chosen, axis=0, keepdims=True)
    powers = jnp.exp(chosen - top_logit)
    gates = powers / jnp.sum(powers, axis=0, keepdims=True)

    here = 4 * m + lax.broadcasted_iota(jnp.int32, (4, BLOCK), 0)
    selected = jnp.any(ids[:, None, :] == here[None], axis=0)
    earlier = (
        lax.broadcasted_iota(jnp.int32, (BLOCK, BLOCK), 0)
        <= lax.broadcasted_iota(jnp.int32, (BLOCK, BLOCK), 1)
    ).astype(bf16)
    counts = jnp.dot(selected.astype(bf16), earlier, preferred_element_type=f32)
    rank = jnp.where(selected, counts.astype(jnp.int32) - 1, -1)
    capacity = 288
    place_bool = rank[:, None, :] == lax.broadcasted_iota(jnp.int32, (4, capacity, BLOCK), 1)
    placing = place_bool.astype(bf16).reshape(4 * capacity, BLOCK)
    gates_here = lax.dynamic_slice_in_dim(gates, 4 * m, 4, 0)
    slot_gate = jnp.sum(jnp.where(place_bool, gates_here[:, None, :], 0.0), axis=2)

    incoming = jnp.dot(placing, routed, preferred_element_type=f32).astype(bf16)
    incoming = incoming.reshape(4, capacity, 1024)
    dy_rows = jnp.dot(placing, dy_all, preferred_element_type=f32).reshape(4, capacity, 1024)
    gate_up = jnp.einsum("esd,edf->esf", incoming, in_w, preferred_element_type=f32)
    gate_part, up_part = gate_up[..., :512], gate_up[..., 512:]
    squashed = jax.nn.sigmoid(gate_part)
    silu_part = gate_part * squashed
    active = (silu_part * up_part).astype(bf16)
    produced = jnp.einsum(
        "esf,edf->esd", active, out_w_t, preferred_element_type=f32
    ).astype(bf16)
    produced_f = produced.astype(f32)
    d_produced = (branch_scale * slot_gate[..., None] * dy_rows).astype(bf16)
    slot_share = branch_scale * jnp.sum(dy_rows * produced_f, axis=2)
    weighted = (slot_gate[..., None] * produced_f).astype(bf16).reshape(4 * capacity, 1024)
    mixed = branch_scale * contract(placing, weighted, 0, 0)
    mixed = mixed.astype(bf16).reshape(MP, TOK, 1024)

    d_active = jnp.einsum("esd,edf->esf", d_produced, out_w_t, preferred_element_type=f32)
    slope = squashed * (1.0 + gate_part * (1.0 - squashed))
    d_gate_up = jnp.concatenate(
        [d_active * up_part * slope, d_active * silu_part], axis=-1
    ).astype(bf16)
    row_grads = jnp.einsum(
        "esf,edf->esd", d_gate_up, in_w, preferred_element_type=f32
    ).astype(bf16)
    routed_terms = contract(placing, row_grads.reshape(4 * capacity, 1024), 0, 0)
    routed_terms = routed_terms.astype(bf16).reshape(MP, TOK, 1024)
    share = jnp.sum(jnp.where(place_bool, slot_share[:, :, None], 0.0), axis=1)
    share = jnp.pad(share.reshape(4, MP, TOK).transpose(1, 0, 2), ((0, 0), (0, 4), (0, 0)))
    routed_got, share_got = comm_call(
        scatter_kernel,
        4,
        [routed_terms, share],
        [shape((MP, TOK, 1024)), shape((MP, 8, TOK), f32)],
        [MP, MP, MP, MP, 2],
        4 << 20,
    )

    def own_rows(array):
        return lax.dynamic_slice_in_dim(array, m * TOK, TOK, 0)

    hidden_own = own_rows(hidden)
    scaled_own, inverse_own = normalize(hidden_own)
    routed_own = (scaled_own * gain_two).astype(bf16).astype(f32)
    dy_own = own_rows(dy_all).astype(f32)
    gates_own = lax.dynamic_slice_in_dim(gates, m * TOK, TOK, 1)
    share_own = share_got[:, :4, :].reshape(32, TOK)
    logit_grad = gates_own * (
        share_own - jnp.sum(gates_own * share_own, axis=0, keepdims=True)
    )
    routed_grad = jnp.sum(routed_got.astype(f32), axis=0) + lax.dot_general(
        logit_grad,
        router_w.astype(f32),
        (((0,), (1,)), ((), ())),
        precision=highest,
        preferred_element_type=f32,
    )
    router_grad = lax.dot_general(
        routed_own,
        logit_grad,
        (((0,), (1,)), ((), ())),
        precision=highest,
        preferred_element_type=f32,
    )
    hidden_grad, gain_two_grad = norm_back(routed_grad, scaled_own, inverse_own, gain_two)
    hidden_grad = hidden_grad + dy_own
    branch_grad = (branch_scale * hidden_grad).astype(bf16)
    hidden_grad_home = swap_home(hidden_grad)

    out_expert_grad = jnp.einsum(
        "esd,esf->edf", d_produced, active, preferred_element_type=f32
    ).astype(bf16)
    in_expert_grad = jnp.einsum(
        "esd,esf->edf", incoming, d_gate_up, preferred_element_type=f32
    ).astype(bf16)
    in_terms = in_expert_grad.reshape(4, 8, 2, 64, 1024)
    out_terms = out_expert_grad.reshape(4, 8, 2, 64, 512)
    out_grad_terms = jnp.einsum(
        "td,hfd->htf", branch_grad, out_w_all, preferred_element_type=f32
    ).astype(bf16)
    out_grad, in_theirs, out_theirs = comm_call(
        outputs_kernel,
        5,
        [out_grad_terms, in_terms, out_terms],
        [shape((MP, TOK, 128)), shape((4, 8, 64, 1024)), shape((4, 8, 64, 512))],
        [MP, MP, 2, 2, 1],
        8 << 20,
    )
    out_grad = out_grad.reshape(BLOCK, 128)
    core = lax.rem(c, 2)

    def with_sibling(own, theirs):
        mine = lax.dynamic_index_in_dim(own, core, 2, False)
        return (mine.astype(f32) + theirs.astype(f32)).astype(bf16)

    pair = jnp.concatenate(
        [with_sibling(in_terms, in_theirs), with_sibling(out_terms, out_theirs)], axis=-1
    ).reshape(4, 4, 2, 64, 1536)

    mixed_got = lax.all_to_all(mixed, "mp", split_axis=0, concat_axis=0, tiled=True)
    outputs = (hidden_own + jnp.sum(mixed_got.astype(f32), axis=0)).astype(bf16)
    outputs = swap_home(outputs)

    do_rows = heads_to_rows(out_grad)
    delta = jnp.sum(do_rows.astype(f32) * heads_to_rows(attended), axis=-1)[:, None, :]
    do_rows = jnp.concatenate([jnp.zeros_like(do_rows), do_rows], axis=-1)
    dkv_terms, dq_cols, expert_grad, branch_rows, qkv_w_all = attention_back(
        q_rows, do_rows, lse, delta, kv_all, pair, branch_grad, qkv_w
    )
    branch_rows = branch_rows.reshape(BLOCK, 1024)
    dkv_terms = dkv_terms.reshape(8, 2, BLOCK, 128)
    (theirs,) = comm_call(
        sibling_kernel, 6, [dkv_terms], [shape((8, BLOCK, 128))], [1, 1], 4 << 20
    )
    mine = lax.dynamic_index_in_dim(dkv_terms, lax.rem(c, 2), 1, False)
    pair = (mine.astype(f32) + theirs.astype(f32)).astype(bf16)
    (dkv_got,) = comm_call(
        chips_kernel, 7, [pair], [shape((8, BLOCK, 128))], [8, 8, 1], 4 << 20
    )
    dkv = jnp.sum(dkv_got.astype(f32), axis=0)
    d_key = rotate_back(dkv[:, :HEAD], cosine, sine).astype(bf16)
    d_value = dkv[:, HEAD:].astype(bf16)
    dq = score_scale * dq_cols[:, :HEAD, :]
    dq = dq.reshape(2, HEAD, 2, HALF).transpose(0, 3, 2, 1).reshape(BLOCK, 2, HEAD)
    d_query = rotate_back(dq, cos2, sin2).reshape(BLOCK, 128).astype(bf16)
    d_qkv = jnp.concatenate([d_query, d_key, d_value], axis=1)
    qkv_w_grad = contract(normed, d_qkv, 0, 0)
    out_w_grad = contract(branch_rows, out_rows, 0, 0)
    w_terms = jnp.concatenate([qkv_w_grad, out_w_grad], axis=1).astype(bf16)
    qkv_got, w_got = comm_call(
        finish_kernel,
        8,
        [d_qkv.reshape(MP, TOK, 256), w_terms.reshape(CTX, 64, 384)],
        [shape((MP, TOK, 256)), shape((CTX, 64, 384))],
        [MP, MP, CTX, CTX, 2],
        5 << 20,
    )
    w_grad = jnp.sum(w_got.astype(f32), axis=0)
    normed_grad = jnp.einsum(
        "htf,hdf->td", qkv_got, qkv_w_all, preferred_element_type=f32
    )
    scaled_one, inverse_one = normalize(layer_input.astype(f32))
    input_grad, gain_one_grad = norm_back(normed_grad, scaled_one, inverse_one, gain_one)
    input_grad = (input_grad + hidden_grad_home).astype(bf16)

    small = jnp.concatenate(
        [
            router_grad,
            gain_one_grad[:, None],
            gain_two_grad[:, None],
            jnp.zeros((1024, 94), f32),
        ],
        axis=1,
    )
    sums = small_sums(small.reshape(CTX, MP, 8, 128))
    return (
        outputs,
        input_grad,
        sums[:, 32],
        w_grad[:, :128],
        w_grad[:, 128:192],
        w_grad[:, 192:256],
        w_grad[:, 256:].T,
        sums[:, 33],
        sums[:, :32],
        expert_grad[..., :1024],
        expert_grad[..., 1024:].transpose(0, 2, 1),
    )


def solution(mesh):
    placed = (
        P(("ctx", "mp"), None),
        P("ctx"),
        P(("ctx", "mp"), None),
        P("ctx"),
        P("ctx", "mp"),
        P("ctx", "mp"),
        P("ctx", "mp"),
        P("mp", "ctx"),
        P("ctx"),
        P("ctx", None),
        P("mp", "ctx", None),
        P("mp", None, "ctx"),
        P(("ctx", "mp"), None),
    )
    return jax.shard_map(
        body,
        mesh=mesh,
        in_specs=placed,
        out_specs=(
            P(("ctx", "mp"), None),
            P(("ctx", "mp"), None),
            P(("ctx", "mp")),
            P("ctx", "mp"),
            P("ctx", "mp"),
            P("ctx", "mp"),
            P("mp", "ctx"),
            P(("ctx", "mp")),
            P(("ctx", "mp"), None),
            P("mp", "ctx", None),
            P("mp", None, "ctx"),
        ),
        check_vma=False,
    )
```

```python
import functools

import jax
import jax.numpy as jnp
from jax import lax
from jax.experimental import pallas as pl
from jax.experimental.pallas import tpu as pltpu
from jax.sharding import PartitionSpec as P

MESH = pl.DeviceIdType.MESH
epsilon = 1e-06
branch_scale = 0.22
score_scale = 0.015625
rope_base = 10000.0
highest = lax.Precision.HIGHEST
log2_e = 1.4426950408889634
bf16 = jnp.bfloat16
f32 = jnp.float32
CTX, MP = 16, 8
HEAD = 64
TOK = 128
BLOCK = 1024
HALF = 512
ANY = pl.BlockSpec(memory_space=pl.ANY)
VM = pl.BlockSpec(memory_space=pltpu.VMEM)
VMEM_LIMIT = 56 * 1024 * 1024


def contract(left, right, left_dim, right_dim):
    return lax.dot_general(
        left, right, (((left_dim,), (right_dim,)), ((), ())), preferred_element_type=f32
    )


def place():
    return lax.axis_index("ctx"), lax.axis_index("mp")


def greet(signal_to, expected):
    barrier = pltpu.get_barrier_semaphore()
    for target in signal_to:
        pl.semaphore_signal(barrier, inc=1, device_id=target, device_id_type=MESH)
    pl.semaphore_wait(barrier, expected)


def remote(src, dst, send, recv, target):
    return pltpu.make_async_remote_copy(
        src_ref=src, dst_ref=dst, send_sem=send, recv_sem=recv,
        device_id=target, device_id_type=MESH,
    )


def comm_call(kernel, number, arrays, outs, sems, cost):
    return pl.pallas_call(
        kernel,
        out_shape=outs,
        in_specs=[ANY] * len(arrays),
        out_specs=[ANY] * len(outs),
        scratch_shapes=[
            pltpu.SemaphoreType.DMA((n,)) if isinstance(n, int) else n for n in sems
        ],
        compiler_params=pltpu.CompilerParams(collective_id=number, has_side_effects=True),
        cost_estimate=pl.CostEstimate(flops=0, bytes_accessed=cost, transcendentals=0),
    )(*arrays)


def shape(dims, kind=bf16):
    return jax.ShapeDtypeStruct(dims, kind)


def flip(index, stride):
    return index + stride - 2 * stride * lax.rem(index // stride, 2)


class Ring:
    def __init__(self, own, dst, index, spread, near, stride, target, sems, sibling=None):
        send, recv, loc = sems[:3]
        count = spread
        plus, minus = lax.rem(index + stride, count), lax.rem(index + count - stride, count)
        far = lax.rem(index + 2 * stride, count)
        near_of = lambda slot: flip(slot, near)
        me_near = near_of(index)

        def copy(src, place_of, at, to):
            return lambda: remote(src, place_of, send.at[at], recv.at[at], target(to))

        def relay(slot, part, at, to):
            return copy(dst(slot, part), dst(slot, part), at, to)

        self.own = lambda: pltpu.make_async_copy(own, dst(index, None), loc)
        self.to_near = copy(own, dst(index, None), 0, me_near)
        self.plus_own = copy(own, dst(index, None), 1, plus)
        self.minus_own = copy(own, dst(index, None), 2, minus)
        self.plus_near = relay(me_near, None, 3, plus)
        self.minus_near = relay(me_near, None, 4, minus)
        self.plus_far = relay(minus, 0, 5, plus)
        self.minus_far = relay(plus, 1, 6, minus)
        self.plus_far_near = relay(near_of(minus), 0, 7, plus)
        self.minus_far_near = relay(near_of(plus), 1, 8, minus)
        self.over = None
        if sibling is not None:
            send2, recv2 = sems[3:]
            parts = [
                (index, None),
                (me_near, None),
                (minus, None),
                (plus, None),
                (near_of(minus), None),
                (near_of(plus), None),
                (far, 0),
                (far, 1),
                (near_of(far), 0),
                (near_of(far), 1),
            ]

            def over(at):
                slot, part = parts[at]
                src = own if at == 0 else dst(slot, part)
                return remote(src, dst(slot, part), send2.at[at], recv2.at[at], sibling)

            self.over = over

    def cross(self, *numbers):
        if self.over is not None:
            for at in numbers:
                self.over(at).start()

    def start(self):
        self.own().start()
        for copy in (self.to_near, self.plus_own, self.minus_own):
            copy().start()
        self.cross(0)

    def relay_near(self):
        self.to_near().wait_recv()
        self.plus_near().start()
        self.minus_near().start()
        self.cross(1)

    def relay_own(self):
        self.plus_own().wait_recv()
        self.plus_far().start()
        self.minus_own().wait_recv()
        self.minus_far().start()
        self.cross(2, 3)

    def relay_far(self):
        self.plus_near().wait_recv()
        self.plus_far_near().start()
        self.minus_near().wait_recv()
        self.minus_far_near().start()
        self.cross(4, 5)

    def finish(self):
        last = (self.plus_far, self.minus_far, self.plus_far_near, self.minus_far_near)
        for number, copy in enumerate(last):
            copy().wait_recv()
            self.cross(6 + number)
        for copy in (
            self.to_near,
            self.plus_own,
            self.minus_own,
            self.plus_near,
            self.minus_near,
        ) + last:
            copy().wait_send()
        if self.over is not None:
            for at in range(10):
                self.over(at).wait()
        self.own().wait()


def mp_ring(own, dst, sems):
    c, m = place()
    return Ring(own, dst, m, MP, 1, 2, lambda slot: (c, slot), sems)


def ctx_ring(own, dst, sems):
    c, m = place()
    return Ring(own, dst, c, CTX, 2, 4, lambda slot: (slot, m), sems, (flip(c, 1), m))


def mp_neighbours():
    c, m = place()
    return [(c, flip(m, 1)), (c, lax.rem(m + 2, MP)), (c, lax.rem(m + 6, MP))]


def ctx_neighbours():
    c, m = place()
    return [
        (flip(c, 2), m),
        (lax.rem(c + 4, CTX), m),
        (lax.rem(c + 12, CTX), m),
        (flip(c, 1), m),
    ]


def slots(ref):
    half = ref.shape[1] // 2

    def dst(slot, part):
        return ref.at[slot] if part is None else ref.at[slot, pl.ds(part * half, half)]

    return dst


def row_slots(ref):
    half = ref.shape[0] // 2

    def dst(slot, part):
        rows = pl.ds(pl.multiple_of(slot * 64, 64), 64)
        return ref.at[:, rows] if part is None else ref.at[pl.ds(part * half, half), rows]

    return dst


MP_SEMS = [pltpu.SemaphoreType.DMA((9,)), pltpu.SemaphoreType.DMA((9,)), pltpu.SemaphoreType.DMA]
CTX_SEMS = MP_SEMS + [pltpu.SemaphoreType.DMA((10,)), pltpu.SemaphoreType.DMA((10,))]


def start_kernel(x_ref, id_ref, w_ref, xo, ido, wo, xs, xr, ids, idr, loc, *sems):
    c, m = place()
    upper = m >= MP // 2
    t = jnp.where(upper, CTX - 1 - c, c)
    signals = []
    for k in range(1, MP):
        sender = lax.rem(m + k, MP)
        signals.append((jnp.where(sender >= MP // 2, CTX - 1 - c, c), sender))
    signals += ctx_neighbours()
    barrier = pltpu.get_barrier_semaphore()
    for target in signals:
        pl.semaphore_signal(barrier, inc=1, device_id=target, device_id_type=MESH)

    @pl.when(upper)
    def _():
        pl.semaphore_signal(barrier, inc=1, device_id=(CTX - 1 - c, m), device_id_type=MESH)
        pl.semaphore_wait(barrier, MP + 4)

    @pl.when(jnp.logical_not(upper))
    def _():
        pl.semaphore_wait(barrier, MP + 3)

    ring = ctx_ring(w_ref, slots(wo), sems)
    ring.start()
    x_copies, id_copies = [], []
    for k in range(MP):
        target = (t, lax.rem(m + k, MP))
        x_copies.append(remote(x_ref, xo.at[m], xs.at[k], xr.at[k], target))
        id_copies.append(remote(id_ref, ido.at[m], ids.at[k], idr.at[k], target))
    own_x = pltpu.make_async_copy(x_ref, xo.at[m], loc.at[0])
    own_id = pltpu.make_async_copy(id_ref, ido.at[m], loc.at[1])

    @pl.when(upper)
    def _():
        x_copies[0].start()
        id_copies[0].start()

    @pl.when(jnp.logical_not(upper))
    def _():
        own_x.start()
        own_id.start()

    for k in range(1, MP):
        x_copies[k].start()
        id_copies[k].start()
    ring.relay_near()
    ring.relay_own()
    ring.relay_far()
    ring.finish()
    for k in range(1, MP):
        x_copies[k].wait()
        id_copies[k].wait()

    @pl.when(upper)
    def _():
        x_copies[0].wait()
        id_copies[0].wait()

    @pl.when(jnp.logical_not(upper))
    def _():
        own_x.wait()
        own_id.wait()


def keys_kernel(kv_ref, dy_ref, out, dy_out, *sems):
    greet(ctx_neighbours() + mp_neighbours(), 7)
    ring = ctx_ring(kv_ref, slots(out), sems[:5])
    rows = mp_ring(dy_ref, slots(dy_out), sems[5:])
    ring.start()
    rows.start()
    ring.relay_near()
    ring.relay_own()
    rows.relay_near()
    rows.relay_own()
    ring.relay_far()
    rows.relay_far()
    ring.finish()
    rows.finish()


def gather_kernel(a_ref, out, *sems):
    greet(mp_neighbours(), 3)
    ring = mp_ring(a_ref, slots(out), sems)
    ring.start()
    ring.relay_near()
    ring.relay_own()
    ring.relay_far()
    ring.finish()


def outputs_kernel(a_ref, g_ref, h_ref, ao, go, ho, s1, r1, s2, r2, loc):
    c, m = place()
    core = lax.rem(c, 2)
    sibling = (flip(c, 1), m)
    mates = [(c, lax.rem(m + k, MP)) for k in range(1, MP)]
    greet(mates + [sibling], MP)
    own_a = pltpu.make_async_copy(a_ref.at[m], ao.at[m], loc.at[0])
    own_a.start()
    copies = []
    for k in range(1, MP):
        to = lax.rem(m + k, MP)
        copies.append(remote(a_ref.at[to], ao.at[m], s1.at[k], r1.at[k], mates[k - 1]))
    copies.append(remote(g_ref.at[:, :, 1 - core], go, s2.at[0], r2.at[0], sibling))
    copies.append(remote(h_ref.at[:, :, 1 - core], ho, s2.at[1], r2.at[1], sibling))
    for copy in copies:
        copy.start()
    for copy in copies:
        copy.wait()
    own_a.wait()


def scatter_kernel(
    a_ref, b_ref, dp_ref, act_ref, in_ref, dgu_ref,
    ao, bo, pair_ref,
    terms, theirs, s1, r1, s2, r2, s3, r3, loc,
):
    c, m = place()
    core = lax.rem(c, 2)
    sibling = (flip(c, 1), m)
    mates = [(c, lax.rem(m + k, MP)) for k in range(1, MP)]
    greet(mates + [sibling], MP)
    own_a = pltpu.make_async_copy(a_ref.at[m], ao.at[m], loc.at[0])
    own_a.start()
    own_b = pltpu.make_async_copy(b_ref.at[m], bo.at[m], loc.at[1])
    own_b.start()
    copies = []
    for k in range(1, MP):
        to = lax.rem(m + k, MP)
        copies.append(remote(a_ref.at[to], ao.at[m], s1.at[k], r1.at[k], mates[k - 1]))
        copies.append(remote(b_ref.at[to], bo.at[m], s2.at[k], r2.at[k], mates[k - 1]))
    for copy in copies:
        copy.start()
    crossing = [
        remote(terms.at[1 - core, e], theirs.at[e], s3.at[e], r3.at[e], sibling)
        for e in range(4)
    ]
    for e in range(4):
        gate_up_grads = dgu_ref[e]
        active = act_ref[e]

        def chunk(at, carry):
            columns = pl.ds(pl.multiple_of(at * 256, 256), 256)
            in_part = contract(in_ref[e, :, columns], gate_up_grads, 0, 0).astype(bf16)
            out_part = contract(dp_ref[e, :, columns], active, 0, 0).astype(bf16)
            for j in range(4):
                rows = slice(64 * j, 64 * j + 64)
                terms[j % 2, e, 2 * at + j // 2, :, 0:1024] = in_part[rows]
                terms[j % 2, e, 2 * at + j // 2, :, 1024:1536] = out_part[rows]
            return carry

        lax.fori_loop(0, 4, chunk, 0)
        crossing[e].start()
    for e in range(4):
        crossing[e].wait()

        def add(chip, carry):
            pair_ref[e, chip] = (
                terms[core, e, chip].astype(f32) + theirs[e, chip].astype(f32)
            ).astype(bf16)
            return carry

        lax.fori_loop(0, 8, add, 0)
    for copy in copies:
        copy.wait()
    own_a.wait()
    own_b.wait()


def scatter_rows(routed_terms, share, d_produced, active, incoming, d_gate_up):
    return pl.pallas_call(
        scatter_kernel,
        out_shape=[
            shape((MP, TOK, 1024)),
            shape((MP, 8, TOK), f32),
            shape((4, 8, 64, 1536)),
        ],
        in_specs=[ANY, ANY, VM, VM, VM, VM],
        out_specs=[ANY, ANY, VM],
        scratch_shapes=[
            pltpu.VMEM((2, 4, 8, 64, 1536), bf16),
            pltpu.VMEM((4, 8, 64, 1536), bf16),
        ]
        + [pltpu.SemaphoreType.DMA((MP,))] * 4
        + [pltpu.SemaphoreType.DMA((4,))] * 2
        + [pltpu.SemaphoreType.DMA((2,))],
        compiler_params=pltpu.CompilerParams(
            vmem_limit_bytes=VMEM_LIMIT, collective_id=4, has_side_effects=True
        ),
    )(routed_terms, share, d_produced, active, incoming, d_gate_up)


def outputs_kernel(a_ref, ao, s1, r1, loc):
    c, m = place()
    mates = [(c, lax.rem(m + k, MP)) for k in range(1, MP)]
    greet(mates, MP - 1)
    own_a = pltpu.make_async_copy(a_ref.at[m], ao.at[m], loc.at[0])
    own_a.start()
    copies = []
    for k in range(1, MP):
        to = lax.rem(m + k, MP)
        copies.append(remote(a_ref.at[to], ao.at[m], s1.at[k], r1.at[k], mates[k - 1]))
    for copy in copies:
        copy.start()
    for copy in copies:
        copy.wait()
    own_a.wait()


def keys_grad_kernel(
    a_ref, out, theirs, pair_a, pair_b, got_a, got_b, sum_a, sum_b, last_a, last_b,
    s0, r0, s1, r1, s2, r2,
):
    c, m = place()
    core = lax.rem(c, 2)
    x, y = c // 4, lax.rem(c // 2, 2)
    sibling = (flip(c, 1), m)
    across = (flip(c, 2), m)
    peers = [(lax.rem(c + 4 * k, CTX), m) for k in range(1, 4)]
    greet(peers + [across, sibling], 5)
    low, high = pl.ds(0, HALF), pl.ds(HALF, HALF)
    crossing = [
        remote(
            a_ref.at[:, :, 1 - core, rows], theirs.at[:, :, rows], s0.at[at], r0.at[at], sibling
        )
        for at, rows in enumerate((high, low))
    ]
    for copy in crossing:
        copy.start()

    def add(a, b):
        return a.astype(f32) + b.astype(f32)

    crossing[0].wait()
    for i in range(4):
        for j in range(2):
            pair_b[i, j] = add(a_ref[i, j, core, high], theirs[i, j, high]).astype(bf16)
    first = [remote(pair_b.at[:, 1 - y], got_b, s1.at[0], r1.at[0], across)]
    first[0].start()
    crossing[1].wait()
    for i in range(4):
        for j in range(2):
            pair_a[i, j] = add(a_ref[i, j, core, low], theirs[i, j, low]).astype(bf16)
    for k in range(1, 4):
        copy = remote(
            pair_a.at[lax.rem(x + k, 4)], got_a.at[k - 1], s1.at[k], r1.at[k], peers[k - 1]
        )
        copy.start()
        first.append(copy)
    first[0].wait()
    for i in range(4):
        sum_b[i] = add(pair_b[i, y], got_b[i]).astype(bf16)
    second = []
    for k in range(1, 4):
        copy = remote(
            sum_b.at[lax.rem(x + k, 4)], last_b.at[k - 1], s2.at[k], r2.at[k], peers[k - 1]
        )
        copy.start()
        second.append(copy)
    for copy in first[1:]:
        copy.wait()
    for j in range(2):
        sum_a[j] = (add(pair_a[x, j], got_a[0, j]) + add(got_a[1, j], got_a[2, j])).astype(bf16)
    copy = remote(sum_a.at[1 - y], last_a, s2.at[0], r2.at[0], across)
    copy.start()
    second.append(copy)
    for copy in second:
        copy.wait()
    out[low] = add(sum_a[y], last_a[...])
    out[high] = add(sum_b[x], last_b[0]) + add(last_b[1], last_b[2])


def keys_grad(terms):
    piece = (HALF, 128)
    return pl.pallas_call(
        keys_grad_kernel,
        out_shape=shape((BLOCK, 128), f32),
        in_specs=[VM],
        out_specs=VM,
        scratch_shapes=[
            pltpu.VMEM((4, 2, BLOCK, 128), bf16),
            pltpu.VMEM((4, 2) + piece, bf16),
            pltpu.VMEM((4, 2) + piece, bf16),
            pltpu.VMEM((3, 2) + piece, bf16),
            pltpu.VMEM((4,) + piece, bf16),
            pltpu.VMEM((2,) + piece, bf16),
            pltpu.VMEM((4,) + piece, bf16),
            pltpu.VMEM(piece, bf16),
            pltpu.VMEM((3,) + piece, bf16),
        ]
        + [pltpu.SemaphoreType.DMA((2,))] * 2
        + [pltpu.SemaphoreType.DMA((4,))] * 4,
        compiler_params=pltpu.CompilerParams(
            vmem_limit_bytes=VMEM_LIMIT, collective_id=6, has_side_effects=True
        ),
    )(terms)


def finish_kernel(a_ref, g_ref, ao, go, s1, r1, s2, r2, loc):
    c, m = place()
    upper = m >= MP // 2
    t = jnp.where(upper, CTX - 1 - c, c)
    barrier = pltpu.get_barrier_semaphore()
    for k in range(1, MP):
        pl.semaphore_signal(
            barrier, inc=1, device_id=(t, lax.rem(m + k, MP)), device_id_type=MESH
        )
    for k in range(1, CTX):
        pl.semaphore_signal(
            barrier, inc=1, device_id=(lax.rem(c + k, CTX), m), device_id_type=MESH
        )

    @pl.when(upper)
    def _():
        pl.semaphore_signal(barrier, inc=1, device_id=(t, m), device_id_type=MESH)
        pl.semaphore_wait(barrier, MP + CTX - 1)

    @pl.when(jnp.logical_not(upper))
    def _():
        pl.semaphore_wait(barrier, MP + CTX - 2)

    own_g = pltpu.make_async_copy(g_ref.at[c], go.at[c], loc.at[0])
    own_g.start()
    own_a = pltpu.make_async_copy(a_ref.at[m], ao.at[m], loc.at[1])
    a_copies, g_copies = [], []
    for k in range(MP):
        to = lax.rem(m + k, MP)
        target = (jnp.where(to >= MP // 2, CTX - 1 - c, c), to)
        a_copies.append(remote(a_ref.at[to], ao.at[m], s1.at[k], r1.at[k], target))
    for k in range(1, CTX):
        to = lax.rem(c + k, CTX)
        g_copies.append(remote(g_ref.at[to], go.at[c], s2.at[k], r2.at[k], (to, m)))

    @pl.when(upper)
    def _():
        a_copies[0].start()

    @pl.when(jnp.logical_not(upper))
    def _():
        own_a.start()

    for k in range(1, MP):
        a_copies[k].start()
    for copy in g_copies:
        copy.start()
    for k in range(1, MP):
        a_copies[k].wait()
    for copy in g_copies:
        copy.wait()
    own_g.wait()

    @pl.when(upper)
    def _():
        a_copies[0].wait()

    @pl.when(jnp.logical_not(upper))
    def _():
        own_a.wait()


def sums_kernel(a_ref, out, got, part, got2, s1, r1, s2, r2):
    c, m = place()
    peers = [(lax.rem(c + k, CTX), m) for k in range(1, CTX)]
    mates = [(c, lax.rem(m + k, MP)) for k in range(1, MP)]
    greet(peers + mates, CTX - 1 + MP - 1)
    copies = []
    for k in range(1, CTX):
        to = lax.rem(c + k, CTX)
        copy = remote(a_ref.at[to], got.at[k], s1.at[k], r1.at[k], peers[k - 1])
        copy.start()
        copies.append(copy)
    total = a_ref[c]
    for copy in copies:
        copy.wait()
    for k in range(1, CTX):
        total = total + got[k]
    part[...] = total
    copies = []
    for k in range(1, MP):
        to = lax.rem(m + k, MP)
        copy = remote(part.at[to], got2.at[k], s2.at[k], r2.at[k], mates[k - 1])
        copy.start()
        copies.append(copy)
    last = part[m]
    for copy in copies:
        copy.wait()
    for k in range(1, MP):
        last = last + got2[k]
    out[...] = last


def small_sums(terms):
    dims = terms.shape[2:]
    return pl.pallas_call(
        sums_kernel,
        out_shape=shape(dims, f32),
        in_specs=[VM],
        out_specs=VM,
        scratch_shapes=[
            pltpu.VMEM((CTX, MP) + dims, f32),
            pltpu.VMEM((MP,) + dims, f32),
            pltpu.VMEM((MP,) + dims, f32),
            pltpu.SemaphoreType.DMA((CTX,)),
            pltpu.SemaphoreType.DMA((CTX,)),
            pltpu.SemaphoreType.DMA((MP,)),
            pltpu.SemaphoreType.DMA((MP,)),
        ],
        compiler_params=pltpu.CompilerParams(collective_id=9, has_side_effects=True),
    )(terms)


def unit(index, first_half):
    second = index > first_half
    part = second.astype(jnp.int32)
    key_half = jnp.where(second, index - first_half - 1, index)
    odd = lax.rem(key_half, 2) == 1
    slot = jnp.where(odd, 2 * CTX - key_half, key_half)
    diagonal = jnp.logical_or(index == first_half, index == 2 * CTX)
    return part, slot, diagonal


def visible_mask(rows):
    key_at = lax.broadcasted_iota(jnp.int32, (HALF, rows), 0)
    query_at = lax.rem(lax.broadcasted_iota(jnp.int32, (HALF, rows), 1), HALF)
    return key_at <= query_at


def forward_kernel(
    q_ref, kv_ref, in_ref, outw_ref, qw_ref, rows_ref,
    out_ref, lse_ref, in_all, outw_all, qw_all, rows_all,
    best, total, summed, *sems,
):
    first_half = 2 * lax.axis_index("ctx")
    greet(ctx_neighbours() + mp_neighbours(), 7)
    weights_rings = [
        ctx_ring(in_ref, row_slots(in_all), sems[0:5]),
        ctx_ring(outw_ref, row_slots(outw_all), sems[5:10]),
    ]
    rows_rings = [
        mp_ring(rows_ref, slots(rows_all), sems[10:13]),
        mp_ring(qw_ref, slots(qw_all), sems[13:16]),
    ]
    for ring in weights_rings + rows_rings:
        ring.start()
    best[...] = jnp.full(best.shape, -1e30, f32)
    total[...] = jnp.zeros(total.shape, f32)
    summed[...] = jnp.zeros(summed.shape, f32)

    def work(part, slot, masked):
        kv = kv_ref[slot]
        scores = contract(kv, q_ref[part], 1, 1)
        if masked:
            scores = jnp.where(visible_mask(scores.shape[1]), scores, -jnp.inf)
        old = best[part]
        new = jnp.maximum(old, jnp.max(scores, axis=0, keepdims=True))
        weights = jnp.exp2(scores * log2_e - new * log2_e)
        fading = jnp.exp2((old - new) * log2_e)
        total[part] = total[part] * fading + jnp.sum(weights, axis=0, keepdims=True)
        summed[part] = summed[part] * fading + contract(kv, weights.astype(bf16), 0, 0)
        best[part] = new

    def step(index, carry):
        part, slot, diagonal = unit(index, first_half)

        @pl.when(index == 12)
        def _():
            for ring in weights_rings:
                ring.relay_own()

        @pl.when(index == 15)
        def _():
            for ring in weights_rings:
                ring.relay_near()
            for ring in rows_rings:
                ring.relay_near()
                ring.relay_own()

        @pl.when(index == 25)
        def _():
            for ring in rows_rings + weights_rings:
                ring.relay_far()

        @pl.when(diagonal)
        def _():
            work(part, slot, True)

        @pl.when(jnp.logical_not(diagonal))
        def _():
            work(part, slot, False)

        return carry

    lax.fori_loop(0, 2 * CTX + 1, step, 0)
    for part in range(2):
        out_ref[part] = summed[part][HEAD:, :] / total[part]
        lse_ref[part] = best[part] + jnp.log(total[part])
    for ring in rows_rings + weights_rings:
        ring.finish()


def attention(q_rows, kv_all, w_in, w_out_t, qkv_w, out_rows_w):
    rows = q_rows.shape[1]
    return pl.pallas_call(
        forward_kernel,
        out_shape=[
            shape((2, HEAD, rows), f32),
            shape((2, 1, rows), f32),
            shape((4, 1024, 1024)),
            shape((4, 1024, 512)),
            shape((MP,) + qkv_w.shape),
            shape((MP, TOK, 1024)),
        ],
        in_specs=[VM, VM, ANY, ANY, ANY, ANY],
        out_specs=[VM, VM, ANY, ANY, ANY, ANY],
        scratch_shapes=[
            pltpu.VMEM((2, 1, rows), f32),
            pltpu.VMEM((2, 1, rows), f32),
            pltpu.VMEM((2, 2 * HEAD, rows), f32),
        ]
        + CTX_SEMS * 2
        + MP_SEMS * 2,
        compiler_params=pltpu.CompilerParams(
            vmem_limit_bytes=VMEM_LIMIT, collective_id=10, has_side_effects=True
        ),
        cost_estimate=pl.CostEstimate(
            flops=33 * 4 * HALF * rows * 256, bytes_accessed=1 << 23, transcendentals=33 * HALF * rows
        ),
    )(q_rows, kv_all, w_in, w_out_t, qkv_w, out_rows_w)


def backward_kernel(
    q_ref, do_ref, lse_ref, delta_ref, kv_ref, pair_ref, br_ref,
    dkv_ref, dq_ref, in_grad, out_grad, br_all,
    total, got_a, got_b, sum_a, sum_b, last_a, last_b, *sems,
):
    c, m = place()
    first_half = 2 * c
    x, y = c // 4, lax.rem(c // 2, 2)
    peers = [(lax.rem(c + 4 * k, CTX), m) for k in range(1, 4)]
    across = (flip(c, 2), m)
    greet(peers + [across] + mp_neighbours(), 7)
    sa, ra, sb, rb = sems[:4]
    ring = mp_ring(br_ref, slots(br_all), sems[4:7])

    def first_copies():
        copies = [
            remote(
                pair_ref.at[pl.ds(0, 2), lax.rem(x + k, 4)],
                got_a.at[k - 1], sa.at[k], ra.at[k], peers[k - 1],
            )
            for k in range(1, 4)
        ]
        copies.append(
            remote(pair_ref.at[pl.ds(2, 2), :, 1 - y], got_b, sa.at[0], ra.at[0], across)
        )
        return copies

    def second_copies():
        copies = [
            remote(
                sum_b.at[:, lax.rem(x + k, 4)], last_b.at[k - 1], sb.at[k], rb.at[k], peers[k - 1]
            )
            for k in range(1, 4)
        ]
        copies.append(remote(sum_a.at[:, 1 - y], last_a, sb.at[0], rb.at[0], across))
        return copies

    for copy in first_copies():
        copy.start()
    ring.start()
    dq_ref[...] = jnp.zeros(dq_ref.shape, f32)

    def clear(index, carry):
        total[index] = jnp.zeros(total.shape[1:], f32)
        return carry

    lax.fori_loop(0, 2 * CTX, clear, 0)

    def work(part, slot, masked):
        kv = kv_ref[slot]
        queries = q_ref[part]
        grads = do_ref[part]
        scores = contract(kv, queries, 1, 1)
        probs = jnp.exp2((scores - lse_ref[part]) * log2_e)
        if masked:
            probs = jnp.where(visible_mask(scores.shape[1]), probs, 0.0)
        prob_grad = contract(kv, grads, 1, 1)
        score_grad = (probs * (prob_grad - delta_ref[part])).astype(bf16)
        total[slot] += contract(probs.astype(bf16), grads, 1, 0) + contract(
            score_grad, queries, 1, 0
        )
        dq_ref[part] += contract(kv, score_grad, 0, 0)

    def middle():
        for copy in first_copies():
            copy.wait()
        for e in range(2):
            for j in range(2):
                term = pair_ref[e, x, j].astype(f32)
                for k in range(3):
                    term = term + got_a[k, e, j].astype(f32)
                sum_a[e, j] = term.astype(bf16)
            for j in range(4):
                term = pair_ref[2 + e, j, y].astype(f32) + got_b[e, j].astype(f32)
                sum_b[e, j] = term.astype(bf16)
        for copy in second_copies():
            copy.start()

    def step(index, carry):
        part, slot, diagonal = unit(index, first_half)

        @pl.when(index == 7)
        def _():
            ring.relay_near()
            ring.relay_own()

        @pl.when(index == 14)
        def _():
            ring.relay_far()

        @pl.when(index == 21)
        def _():
            middle()

        @pl.when(diagonal)
        def _():
            work(part, slot, True)

        @pl.when(jnp.logical_not(diagonal))
        def _():
            work(part, slot, False)

        return carry

    lax.fori_loop(0, 2 * CTX + 1, step, 0)

    def write(index, carry):
        dkv_ref[index] = total[index].astype(bf16)
        return carry

    lax.fori_loop(0, 2 * CTX, write, 0)
    ring.finish()
    for copy in second_copies():
        copy.wait()
    for e in range(2):
        for at, term in (
            (e, sum_a[e, y].astype(f32) + last_a[e].astype(f32)),
            (
                2 + e,
                sum_b[e, x].astype(f32)
                + last_b[0, e].astype(f32)
                + last_b[1, e].astype(f32)
                + last_b[2, e].astype(f32),
            ),
        ):
            in_grad[at] = term[:, :1024]
            out_grad[at] = term[:, 1024:]


def attention_back(q_rows, do_rows, lse, delta, kv_all, pair, branch_grad):
    rows = q_rows.shape[1]
    wide = pair.shape[-1]
    return pl.pallas_call(
        backward_kernel,
        out_shape=[
            shape(kv_all.shape, bf16),
            shape((2, 2 * HEAD, rows), f32),
            shape((4, 64, 1024), f32),
            shape((4, 64, 512), f32),
            shape((MP, TOK, 1024)),
        ],
        in_specs=[VM] * 6 + [ANY],
        out_specs=[VM] * 4 + [ANY],
        scratch_shapes=[
            pltpu.VMEM(kv_all.shape, f32),
            pltpu.VMEM((3, 2, 2, 64, wide), bf16),
            pltpu.VMEM((2, 4, 64, wide), bf16),
            pltpu.VMEM((2, 2, 64, wide), bf16),
            pltpu.VMEM((2, 4, 64, wide), bf16),
            pltpu.VMEM((2, 64, wide), bf16),
            pltpu.VMEM((3, 2, 64, wide), bf16),
        ]
        + [pltpu.SemaphoreType.DMA((4,))] * 4
        + MP_SEMS,
        compiler_params=pltpu.CompilerParams(
            vmem_limit_bytes=VMEM_LIMIT, collective_id=11, has_side_effects=True
        ),
        cost_estimate=pl.CostEstimate(
            flops=33 * 10 * HALF * rows * 256, bytes_accessed=1 << 24, transcendentals=33 * HALF * rows
        ),
    )(q_rows, do_rows, lse, delta, kv_all, pair, branch_grad)


def phases(positions, head_width):
    steps_up = jnp.arange(head_width // 2).astype(f32)
    frequency = rope_base ** (-2.0 * steps_up / head_width)
    angles = positions.astype(f32)[:, None] * frequency[None, :]
    angles = jnp.concatenate([angles, angles], axis=1)
    return (jnp.cos(angles), jnp.sin(angles))


def rotate(values, cosine, sine):
    half_width = values.shape[-1] // 2
    turned = jnp.concatenate([-values[..., half_width:], values[..., :half_width]], axis=-1)
    return values * cosine + turned * sine


def rotate_back(grads, cosine, sine):
    half_width = grads.shape[-1] // 2
    turned = grads * sine
    turned = jnp.concatenate([turned[..., half_width:], -turned[..., :half_width]], axis=-1)
    return grads * cosine + turned


def normalize(values):
    inverse = lax.rsqrt(jnp.mean(values * values, axis=-1, keepdims=True) + epsilon)
    return (values * inverse, inverse)


def norm_back(grads, scaled, inverse, gain):
    inner = grads * gain
    return (
        inverse * (inner - scaled * jnp.mean(inner * scaled, axis=-1, keepdims=True)),
        jnp.sum(grads * scaled, axis=0),
    )


def swap_home(array):
    pairs = []
    for c in range(CTX):
        for m in range(MP):
            t = CTX - 1 - c if m >= MP // 2 else c
            pairs.append((c * MP + m, t * MP + m))
    return lax.ppermute(array, ("ctx", "mp"), pairs)


def heads_to_rows(values):
    return values.reshape(2, HALF, 2, HEAD).transpose(0, 2, 1, 3).reshape(2, 2 * HALF, HEAD)


def body(
    layer_input,
    positions,
    expert_ids,
    attn_gain,
    w_query,
    w_key,
    w_value,
    w_attn_out,
    ffn_gain,
    router,
    w_in,
    w_out,
    cotangent,
):
    c, m = place()
    dy_swapped = swap_home(cotangent)
    own_positions = lax.dynamic_slice_in_dim(positions, m * TOK, TOK, 0)
    id_pack = jnp.concatenate(
        [expert_ids.T, own_positions[None, :], jnp.zeros((7, TOK), jnp.int32)], axis=0
    )
    w_pack = jnp.concatenate(
        [
            w_query,
            w_key,
            w_value,
            router,
            attn_gain[:, None],
            ffn_gain[:, None],
            jnp.zeros((64, 94), bf16),
            w_attn_out.T,
        ],
        axis=1,
    )
    x_all, id_all, w_all = comm_call(
        start_kernel,
        1,
        [layer_input, id_pack, w_pack],
        [
            shape((MP, TOK, 1024)),
            shape((MP, 16, TOK), jnp.int32),
            shape((CTX, 64, 512)),
        ],
        [MP, MP, MP, MP, 2] + CTX_SEMS,
        4 << 20,
    )
    inputs = x_all.reshape(BLOCK, 1024).astype(f32)
    ids = id_all[:, :8, :].transpose(1, 0, 2).reshape(8, BLOCK)
    places = id_all[:, 8, :].reshape(BLOCK)
    w_all = w_all.reshape(1024, 512)
    qkv_w = w_all[:, :256]
    router_w = w_all[:, 256:288]
    gain_one = w_all[:, 288].astype(f32)
    gain_two = w_all[:, 289].astype(f32)
    out_w = w_all[:, 384:].T

    scaled_all, _ = normalize(inputs)
    normed = (scaled_all * gain_one).astype(bf16)
    qkv = jnp.dot(normed, qkv_w, preferred_element_type=f32)
    cosine, sine = phases(places, HEAD)
    cosine, sine = lax.optimization_barrier((cosine, sine))
    cos2, sin2 = cosine[:, None, :], sine[:, None, :]
    queries = rotate(qkv[:, :128].reshape(BLOCK, 2, HEAD), cos2, sin2).astype(bf16)
    queries = queries * jnp.asarray(score_scale, bf16)
    q_rows = heads_to_rows(queries.reshape(BLOCK, 128))
    q_rows = jnp.concatenate([q_rows, jnp.zeros_like(q_rows)], axis=-1)
    keys = rotate(qkv[:, 128:192], cosine, sine).astype(bf16)
    kv_new = jnp.concatenate([keys, qkv[:, 192:].astype(bf16)], axis=-1)
    kv_all, dy_all = comm_call(
        keys_kernel,
        2,
        [kv_new, dy_swapped],
        [shape((CTX, BLOCK, 128)), shape((MP, TOK, 1024))],
        CTX_SEMS + MP_SEMS,
        6 << 20,
    )
    kv_all = kv_all.reshape(2 * CTX, HALF, 128)
    out_cols, lse, in_w, out_w_t, qkv_w_all, out_w_all = attention(
        q_rows, kv_all, w_in, w_out.transpose(0, 2, 1), qkv_w, out_w
    )
    dy_all = dy_all.reshape(BLOCK, 1024)
    attended = (
        out_cols.reshape(2, HEAD, 2, HALF).transpose(0, 3, 2, 1).reshape(BLOCK, 128)
    )
    out_rows = attended.astype(bf16)
    (rows_all,) = comm_call(
        gather_kernel, 3, [out_rows], [shape((MP, BLOCK, 128))], MP_SEMS, 4 << 20
    )
    branch = lax.dot_general(
        rows_all, out_w_all, (((0, 2), (0, 1)), ((), ())), preferred_element_type=f32
    )
    hidden = inputs + branch_scale * branch
    scaled_two, inverse_two = normalize(hidden)
    routed = (scaled_two * gain_two).astype(bf16)

    logits = contract(router_w, routed, 0, 1)
    experts = lax.broadcasted_iota(jnp.int32, (32, BLOCK), 0)
    member = jnp.any(ids[:, None, :] == experts[None], axis=0)
    chosen = jnp.where(member, logits, -jnp.inf)
    top_logit = jnp.max(chosen, axis=0, keepdims=True)
    powers = jnp.exp(chosen - top_logit)
    gates = powers / jnp.sum(powers, axis=0, keepdims=True)

    here = 4 * m + lax.broadcasted_iota(jnp.int32, (4, BLOCK), 0)
    selected = jnp.any(ids[:, None, :] == here[None], axis=0)
    earlier = (
        lax.broadcasted_iota(jnp.int32, (BLOCK, BLOCK), 0)
        <= lax.broadcasted_iota(jnp.int32, (BLOCK, BLOCK), 1)
    ).astype(bf16)
    counts = jnp.dot(selected.astype(bf16), earlier, preferred_element_type=f32)
    rank = jnp.where(selected, counts.astype(jnp.int32) - 1, -1)
    capacity = 288
    place_bool = rank[:, None, :] == lax.broadcasted_iota(jnp.int32, (4, capacity, BLOCK), 1)
    placing = place_bool.astype(bf16).reshape(4 * capacity, BLOCK)
    gates_here = lax.dynamic_slice_in_dim(gates, 4 * m, 4, 0)
    slot_gate = jnp.sum(jnp.where(place_bool, gates_here[:, None, :], 0.0), axis=2)

    incoming = jnp.dot(placing, routed, preferred_element_type=f32).astype(bf16)
    incoming = incoming.reshape(4, capacity, 1024)
    dy_rows = jnp.dot(placing, dy_all, preferred_element_type=f32).reshape(4, capacity, 1024)
    gate_up = jnp.einsum("esd,edf->esf", incoming, in_w, preferred_element_type=f32)
    gate_part, up_part = gate_up[..., :512], gate_up[..., 512:]
    squashed = jax.nn.sigmoid(gate_part)
    silu_part = gate_part * squashed
    active = (silu_part * up_part).astype(bf16)
    produced = jnp.einsum(
        "esf,edf->esd", active, out_w_t, preferred_element_type=f32
    ).astype(bf16)
    produced_f = produced.astype(f32)
    d_produced = (branch_scale * slot_gate[..., None] * dy_rows).astype(bf16)
    slot_share = branch_scale * jnp.sum(dy_rows * produced_f, axis=2)
    weighted = (slot_gate[..., None] * produced_f).astype(bf16).reshape(4 * capacity, 1024)
    mixed = branch_scale * contract(placing, weighted, 0, 0)
    mixed = mixed.astype(bf16).reshape(MP, TOK, 1024)

    d_active = jnp.einsum("esd,edf->esf", d_produced, out_w_t, preferred_element_type=f32)
    slope = squashed * (1.0 + gate_part * (1.0 - squashed))
    d_gate_up = jnp.concatenate(
        [d_active * up_part * slope, d_active * silu_part], axis=-1
    ).astype(bf16)
    row_grads = jnp.einsum(
        "esf,edf->esd", d_gate_up, in_w, preferred_element_type=f32
    ).astype(bf16)
    routed_terms = contract(placing, row_grads.reshape(4 * capacity, 1024), 0, 0)
    routed_terms = routed_terms.astype(bf16).reshape(MP, TOK, 1024)
    share = jnp.sum(jnp.where(place_bool, slot_share[:, :, None], 0.0), axis=1)
    share = jnp.pad(share.reshape(4, MP, TOK).transpose(1, 0, 2), ((0, 0), (0, 4), (0, 0)))
    routed_got, share_got, pair = scatter_rows(
        routed_terms, share, d_produced, active, incoming, d_gate_up
    )

    def own_rows(array):
        return lax.dynamic_slice_in_dim(array, m * TOK, TOK, 0)

    hidden_own = own_rows(hidden)
    scaled_own, inverse_own = normalize(hidden_own)
    routed_own = (scaled_own * gain_two).astype(bf16).astype(f32)
    dy_own = own_rows(dy_all).astype(f32)
    gates_own = lax.dynamic_slice_in_dim(gates, m * TOK, TOK, 1)
    share_own = share_got[:, :4, :].reshape(32, TOK)
    logit_grad = gates_own * (
        share_own - jnp.sum(gates_own * share_own, axis=0, keepdims=True)
    )
    routed_grad = jnp.sum(routed_got.astype(f32), axis=0) + lax.dot_general(
        logit_grad,
        router_w.astype(f32),
        (((0,), (1,)), ((), ())),
        precision=highest,
        preferred_element_type=f32,
    )
    router_grad = lax.dot_general(
        routed_own,
        logit_grad,
        (((0,), (1,)), ((), ())),
        precision=highest,
        preferred_element_type=f32,
    )
    hidden_grad, gain_two_grad = norm_back(routed_grad, scaled_own, inverse_own, gain_two)
    hidden_grad = hidden_grad + dy_own
    branch_grad = (branch_scale * hidden_grad).astype(bf16)
    hidden_grad_home = swap_home(hidden_grad)

    out_grad_terms = jnp.einsum(
        "td,hfd->htf", branch_grad, out_w_all, preferred_element_type=f32
    ).astype(bf16)
    (out_grad,) = comm_call(
        outputs_kernel, 5, [out_grad_terms], [shape((MP, TOK, 128))], [MP, MP, 1], 1 << 20
    )
    out_grad = out_grad.reshape(BLOCK, 128)
    pair = pair.reshape(4, 4, 2, 64, 1536)

    mixed_got = lax.all_to_all(mixed, "mp", split_axis=0, concat_axis=0, tiled=True)
    outputs = (hidden_own + jnp.sum(mixed_got.astype(f32), axis=0)).astype(bf16)
    outputs = swap_home(outputs)

    do_rows = heads_to_rows(out_grad)
    delta = jnp.sum(do_rows.astype(f32) * heads_to_rows(attended), axis=-1)[:, None, :]
    do_rows = jnp.concatenate([jnp.zeros_like(do_rows), do_rows], axis=-1)
    dkv_terms, dq_cols, in_w_grad, out_w_grad_t, branch_rows = attention_back(
        q_rows, do_rows, lse, delta, kv_all, pair, branch_grad
    )
    branch_rows = branch_rows.reshape(BLOCK, 1024)
    dkv = keys_grad(dkv_terms.reshape(4, 2, 2, BLOCK, 128))
    d_key = rotate_back(dkv[:, :HEAD], cosine, sine).astype(bf16)
    d_value = dkv[:, HEAD:].astype(bf16)
    dq = score_scale * dq_cols[:, :HEAD, :]
    dq = dq.reshape(2, HEAD, 2, HALF).transpose(0, 3, 2, 1).reshape(BLOCK, 2, HEAD)
    d_query = rotate_back(dq, cos2, sin2).reshape(BLOCK, 128).astype(bf16)
    d_qkv = jnp.concatenate([d_query, d_key, d_value], axis=1)
    qkv_w_grad = contract(normed, d_qkv, 0, 0)
    out_w_grad = contract(branch_rows, out_rows, 0, 0)
    w_terms = jnp.concatenate([qkv_w_grad, out_w_grad], axis=1).astype(bf16)
    qkv_got, w_got = comm_call(
        finish_kernel,
        8,
        [d_qkv.reshape(MP, TOK, 256), w_terms.reshape(CTX, 64, 384)],
        [shape((MP, TOK, 256)), shape((CTX, 64, 384))],
        [MP, MP, CTX, CTX, 2],
        5 << 20,
    )
    w_grad = jnp.sum(w_got.astype(f32), axis=0)
    normed_grad = jnp.einsum(
        "htf,hdf->td", qkv_got, qkv_w_all, preferred_element_type=f32
    )
    scaled_one, inverse_one = normalize(layer_input.astype(f32))
    input_grad, gain_one_grad = norm_back(normed_grad, scaled_one, inverse_one, gain_one)
    input_grad = (input_grad + hidden_grad_home).astype(bf16)

    small = jnp.concatenate(
        [
            router_grad,
            gain_one_grad[:, None],
            gain_two_grad[:, None],
            jnp.zeros((1024, 94), f32),
        ],
        axis=1,
    )
    sums = small_sums(small.reshape(CTX, MP, 8, 128))
    return (
        outputs,
        input_grad,
        sums[:, 32],
        w_grad[:, :128],
        w_grad[:, 128:192],
        w_grad[:, 192:256],
        w_grad[:, 256:].T,
        sums[:, 33],
        sums[:, :32],
        in_w_grad,
        out_w_grad_t.transpose(0, 2, 1),
    )


def solution(mesh):
    placed = (
        P(("ctx", "mp"), None),
        P("ctx"),
        P(("ctx", "mp"), None),
        P("ctx"),
        P("ctx", "mp"),
        P("ctx", "mp"),
        P("ctx", "mp"),
        P("mp", "ctx"),
        P("ctx"),
        P("ctx", None),
        P("mp", "ctx", None),
        P("mp", None, "ctx"),
        P(("ctx", "mp"), None),
    )
    return jax.shard_map(
        body,
        mesh=mesh,
        in_specs=placed,
        out_specs=(
            P(("ctx", "mp"), None),
            P(("ctx", "mp"), None),
            P(("ctx", "mp")),
            P("ctx", "mp"),
            P("ctx", "mp"),
            P("ctx", "mp"),
            P("mp", "ctx"),
            P(("ctx", "mp")),
            P(("ctx", "mp"), None),
            P("mp", "ctx", None),
            P("mp", None, "ctx"),
        ),
        check_vma=False,
    )
```

```python
import functools

import jax
import jax.numpy as jnp
from jax import lax
from jax.experimental import pallas as pl
from jax.experimental.pallas import tpu as pltpu
from jax.sharding import PartitionSpec as P

MESH = pl.DeviceIdType.MESH
epsilon = 1e-06
branch_scale = 0.22
score_scale = 0.015625
rope_base = 10000.0
highest = lax.Precision.HIGHEST
log2_e = 1.4426950408889634
bf16 = jnp.bfloat16
f32 = jnp.float32
CTX, MP = 16, 8
HEAD = 64
TOK = 128
BLOCK = 1024
HALF = 512
ANY = pl.BlockSpec(memory_space=pl.ANY)
VM = pl.BlockSpec(memory_space=pltpu.VMEM)
VMEM_LIMIT = 56 * 1024 * 1024


def contract(left, right, left_dim, right_dim):
    return lax.dot_general(
        left, right, (((left_dim,), (right_dim,)), ((), ())), preferred_element_type=f32
    )


def place():
    return lax.axis_index("ctx"), lax.axis_index("mp")


def greet(signal_to, expected):
    barrier = pltpu.get_barrier_semaphore()
    for target in signal_to:
        pl.semaphore_signal(barrier, inc=1, device_id=target, device_id_type=MESH)
    pl.semaphore_wait(barrier, expected)


def remote(src, dst, send, recv, target):
    return pltpu.make_async_remote_copy(
        src_ref=src, dst_ref=dst, send_sem=send, recv_sem=recv,
        device_id=target, device_id_type=MESH,
    )


def comm_call(kernel, number, arrays, outs, sems, cost):
    return pl.pallas_call(
        kernel,
        out_shape=outs,
        in_specs=[ANY] * len(arrays),
        out_specs=[ANY] * len(outs),
        scratch_shapes=[
            pltpu.SemaphoreType.DMA((n,)) if isinstance(n, int) else n for n in sems
        ],
        compiler_params=pltpu.CompilerParams(collective_id=number, has_side_effects=True),
        cost_estimate=pl.CostEstimate(flops=0, bytes_accessed=cost, transcendentals=0),
    )(*arrays)


def shape(dims, kind=bf16):
    return jax.ShapeDtypeStruct(dims, kind)


def flip(index, stride):
    return index + stride - 2 * stride * lax.rem(index // stride, 2)


class Ring:
    def __init__(self, own, dst, index, spread, near, stride, target, sems, sibling=None):
        send, recv, loc = sems[:3]
        count = spread
        plus, minus = lax.rem(index + stride, count), lax.rem(index + count - stride, count)
        far = lax.rem(index + 2 * stride, count)
        near_of = lambda slot: flip(slot, near)
        me_near = near_of(index)

        def copy(src, place_of, at, to):
            return lambda: remote(src, place_of, send.at[at], recv.at[at], target(to))

        def relay(slot, part, at, to):
            return copy(dst(slot, part), dst(slot, part), at, to)

        self.own = lambda: pltpu.make_async_copy(own, dst(index, None), loc)
        self.to_near = copy(own, dst(index, None), 0, me_near)
        self.plus_own = copy(own, dst(index, None), 1, plus)
        self.minus_own = copy(own, dst(index, None), 2, minus)
        self.plus_near = relay(me_near, None, 3, plus)
        self.minus_near = relay(me_near, None, 4, minus)
        self.plus_far = relay(minus, 0, 5, plus)
        self.minus_far = relay(plus, 1, 6, minus)
        self.plus_far_near = relay(near_of(minus), 0, 7, plus)
        self.minus_far_near = relay(near_of(plus), 1, 8, minus)
        self.over = None
        if sibling is not None:
            send2, recv2 = sems[3:]
            parts = [
                (index, None),
                (me_near, None),
                (minus, None),
                (plus, None),
                (near_of(minus), None),
                (near_of(plus), None),
                (far, 0),
                (far, 1),
                (near_of(far), 0),
                (near_of(far), 1),
            ]

            def over(at):
                slot, part = parts[at]
                src = own if at == 0 else dst(slot, part)
                return remote(src, dst(slot, part), send2.at[at], recv2.at[at], sibling)

            self.over = over

    def cross(self, *numbers):
        if self.over is not None:
            for at in numbers:
                self.over(at).start()

    def start(self):
        self.own().start()
        for copy in (self.to_near, self.plus_own, self.minus_own):
            copy().start()
        self.cross(0)

    def relay_near(self):
        self.to_near().wait_recv()
        self.plus_near().start()
        self.minus_near().start()
        self.cross(1)

    def relay_own(self):
        self.plus_own().wait_recv()
        self.plus_far().start()
        self.minus_own().wait_recv()
        self.minus_far().start()
        self.cross(2, 3)

    def relay_far(self):
        self.plus_near().wait_recv()
        self.plus_far_near().start()
        self.minus_near().wait_recv()
        self.minus_far_near().start()
        self.cross(4, 5)

    def finish(self):
        last = (self.plus_far, self.minus_far, self.plus_far_near, self.minus_far_near)
        for number, copy in enumerate(last):
            copy().wait_recv()
            self.cross(6 + number)
        for copy in (
            self.to_near,
            self.plus_own,
            self.minus_own,
            self.plus_near,
            self.minus_near,
        ) + last:
            copy().wait_send()
        if self.over is not None:
            for at in range(10):
                self.over(at).wait()
        self.own().wait()


def mp_ring(own, dst, sems):
    c, m = place()
    return Ring(own, dst, m, MP, 1, 2, lambda slot: (c, slot), sems)


def ctx_ring(own, dst, sems):
    c, m = place()
    return Ring(own, dst, c, CTX, 2, 4, lambda slot: (slot, m), sems, (flip(c, 1), m))


def mp_neighbours():
    c, m = place()
    return [(c, flip(m, 1)), (c, lax.rem(m + 2, MP)), (c, lax.rem(m + 6, MP))]


def ctx_neighbours():
    c, m = place()
    return [
        (flip(c, 2), m),
        (lax.rem(c + 4, CTX), m),
        (lax.rem(c + 12, CTX), m),
        (flip(c, 1), m),
    ]


def slots(ref):
    half = ref.shape[1] // 2

    def dst(slot, part):
        return ref.at[slot] if part is None else ref.at[slot, pl.ds(part * half, half)]

    return dst


def row_slots(ref):
    half = ref.shape[0] // 2

    def dst(slot, part):
        rows = pl.ds(pl.multiple_of(slot * 64, 64), 64)
        return ref.at[:, rows] if part is None else ref.at[pl.ds(part * half, half), rows]

    return dst


MP_SEMS = [pltpu.SemaphoreType.DMA((9,)), pltpu.SemaphoreType.DMA((9,)), pltpu.SemaphoreType.DMA]
CTX_SEMS = MP_SEMS + [pltpu.SemaphoreType.DMA((10,)), pltpu.SemaphoreType.DMA((10,))]


def start_kernel(x_ref, id_ref, w_ref, xo, ido, wo, xs, xr, ids, idr, loc, *sems):
    c, m = place()
    upper = m >= MP // 2
    t = jnp.where(upper, CTX - 1 - c, c)
    signals = []
    for k in range(1, MP):
        sender = lax.rem(m + k, MP)
        signals.append((jnp.where(sender >= MP // 2, CTX - 1 - c, c), sender))
    signals += ctx_neighbours()
    barrier = pltpu.get_barrier_semaphore()
    for target in signals:
        pl.semaphore_signal(barrier, inc=1, device_id=target, device_id_type=MESH)

    @pl.when(upper)
    def _():
        pl.semaphore_signal(barrier, inc=1, device_id=(CTX - 1 - c, m), device_id_type=MESH)
        pl.semaphore_wait(barrier, MP + 4)

    @pl.when(jnp.logical_not(upper))
    def _():
        pl.semaphore_wait(barrier, MP + 3)

    ring = ctx_ring(w_ref, slots(wo), sems)
    ring.start()
    x_copies, id_copies = [], []
    for k in range(MP):
        target = (t, lax.rem(m + k, MP))
        x_copies.append(remote(x_ref, xo.at[m], xs.at[k], xr.at[k], target))
        id_copies.append(remote(id_ref, ido.at[m], ids.at[k], idr.at[k], target))
    own_x = pltpu.make_async_copy(x_ref, xo.at[m], loc.at[0])
    own_id = pltpu.make_async_copy(id_ref, ido.at[m], loc.at[1])

    @pl.when(upper)
    def _():
        x_copies[0].start()
        id_copies[0].start()

    @pl.when(jnp.logical_not(upper))
    def _():
        own_x.start()
        own_id.start()

    for k in range(1, MP):
        x_copies[k].start()
        id_copies[k].start()
    ring.relay_near()
    ring.relay_own()
    ring.relay_far()
    ring.finish()
    for k in range(1, MP):
        x_copies[k].wait()
        id_copies[k].wait()

    @pl.when(upper)
    def _():
        x_copies[0].wait()
        id_copies[0].wait()

    @pl.when(jnp.logical_not(upper))
    def _():
        own_x.wait()
        own_id.wait()


def lanes(rows):
    return lax.broadcasted_iota(jnp.int32, (rows, 128), 1)


def phase_rows(ref, at, rows):
    part = ref[:, at : at + rows]
    return jnp.concatenate([part] * 4, axis=0).T


def turn(values, cosine, sine):
    first = lax.rem(lanes(values.shape[0]), HEAD) < HEAD // 2
    turned = jnp.where(first, -pltpu.roll(values, 96, 1), pltpu.roll(values, 32, 1))
    return values * cosine + turned * sine


def turn_back(grads, cosine, sine):
    first = lax.rem(lanes(grads.shape[0]), HEAD) < HEAD // 2
    scaled = grads * sine
    turned = jnp.where(first, pltpu.roll(scaled, 96, 1), -pltpu.roll(scaled, 32, 1))
    return grads * cosine + turned


def keys_kernel(
    x_ref, gain_ref, w_ref, cos_ref, sin_ref, dy_ref,
    normed_ref, q_ref, kv_out, dy_out,
    kv_own, *sems,
):
    greet(ctx_neighbours() + mp_neighbours(), 7)
    ring = ctx_ring(kv_own, slots(kv_out), sems[:5])
    rows = mp_ring(dy_ref, slots(dy_out), sems[5:])
    rows.start()
    size = 256
    low = lanes(size) < HEAD
    for part in range(4):
        at = part * size
        block = slice(at, at + size)
        x = x_ref[block].astype(f32)
        inverse = lax.rsqrt(jnp.mean(x * x, axis=1, keepdims=True) + epsilon)
        normed = (x * inverse * gain_ref[...]).astype(bf16)
        normed_ref[block] = normed
        qkv = jnp.dot(normed, w_ref[...], preferred_element_type=f32)
        cosine, sine = phase_rows(cos_ref, at, size), phase_rows(sin_ref, at, size)
        queries = turn(qkv[:, :128], cosine, sine).astype(bf16).astype(f32) * score_scale
        half, place_in = part // 2, at % HALF
        q_ref[half, place_in : place_in + size] = jnp.where(low, queries, 0.0).astype(bf16)
        q_ref[half, HALF + place_in : HALF + place_in + size] = jnp.where(
            low, pltpu.roll(queries, HEAD, 1), 0.0
        ).astype(bf16)
        kv = qkv[:, 128:]
        kv_own[block] = jnp.where(low, turn(kv, cosine, sine), kv).astype(bf16)
    ring.start()
    rows.relay_near()
    rows.relay_own()
    ring.relay_near()
    ring.relay_own()
    rows.relay_far()
    ring.relay_far()
    rows.finish()
    ring.finish()


def keys_and_values(x_all, gain, qkv_w, cosine, sine, dy):
    return pl.pallas_call(
        keys_kernel,
        out_shape=[
            shape((BLOCK, 1024)),
            shape((2, 2 * HALF, 128)),
            shape((CTX, BLOCK, 128)),
            shape((MP, TOK, 1024)),
        ],
        in_specs=[VM] * 5 + [ANY],
        out_specs=[VM] * 2 + [ANY] * 2,
        scratch_shapes=[pltpu.VMEM((BLOCK, 128), bf16)] + CTX_SEMS + MP_SEMS,
        compiler_params=pltpu.CompilerParams(
            vmem_limit_bytes=VMEM_LIMIT, collective_id=2, has_side_effects=True
        ),
    )(x_all, gain, qkv_w, cosine, sine, dy)


def gather_kernel(a_ref, w_ref, out, w_out, *sems):
    greet(ctx_neighbours() + mp_neighbours(), 7)
    ring = mp_ring(a_ref, slots(out), sems[:3])
    weights = ctx_ring(w_ref, row_slots(w_out), sems[3:])
    ring.start()
    weights.start()
    ring.relay_near()
    ring.relay_own()
    weights.relay_near()
    weights.relay_own()
    ring.relay_far()
    weights.relay_far()
    ring.finish()
    weights.finish()


def scatter_kernel(
    a_ref, b_ref, dp_ref, act_ref, in_ref, dgu_ref,
    ao, bo, pair_ref,
    terms, theirs, s1, r1, s2, r2, s3, r3, loc,
):
    c, m = place()
    core = lax.rem(c, 2)
    sibling = (flip(c, 1), m)
    mates = [(c, lax.rem(m + k, MP)) for k in range(1, MP)]
    greet(mates + [sibling], MP)
    own_a = pltpu.make_async_copy(a_ref.at[m], ao.at[m], loc.at[0])
    own_a.start()
    own_b = pltpu.make_async_copy(b_ref.at[m], bo.at[m], loc.at[1])
    own_b.start()
    copies = []
    for k in range(1, MP):
        to = lax.rem(m + k, MP)
        copies.append(remote(a_ref.at[to], ao.at[m], s1.at[k], r1.at[k], mates[k - 1]))
        copies.append(remote(b_ref.at[to], bo.at[m], s2.at[k], r2.at[k], mates[k - 1]))
    for copy in copies:
        copy.start()
    crossing = [
        remote(terms.at[1 - core, e], theirs.at[e], s3.at[e], r3.at[e], sibling)
        for e in range(4)
    ]
    for e in range(4):
        gate_up_grads = dgu_ref[e]
        active = act_ref[e]

        def chunk(at, carry):
            columns = pl.ds(pl.multiple_of(at * 256, 256), 256)
            in_part = contract(in_ref[e, :, columns], gate_up_grads, 0, 0).astype(bf16)
            out_part = contract(dp_ref[e, :, columns], active, 0, 0).astype(bf16)
            for j in range(4):
                rows = slice(64 * j, 64 * j + 64)
                terms[j % 2, e, 2 * at + j // 2, :, 0:1024] = in_part[rows]
                terms[j % 2, e, 2 * at + j // 2, :, 1024:1536] = out_part[rows]
            return carry

        lax.fori_loop(0, 4, chunk, 0)
        crossing[e].start()
    for e in range(4):
        crossing[e].wait()

        def add(chip, carry):
            pair_ref[e, chip] = (
                terms[core, e, chip].astype(f32) + theirs[e, chip].astype(f32)
            ).astype(bf16)
            return carry

        lax.fori_loop(0, 8, add, 0)
    for copy in copies:
        copy.wait()
    own_a.wait()
    own_b.wait()


def scatter_rows(routed_terms, share, d_produced, active, incoming, d_gate_up):
    return pl.pallas_call(
        scatter_kernel,
        out_shape=[
            shape((MP, TOK, 1024)),
            shape((MP, 8, TOK), f32),
            shape((4, 8, 64, 1536)),
        ],
        in_specs=[ANY, ANY, VM, VM, VM, VM],
        out_specs=[ANY, ANY, VM],
        scratch_shapes=[
            pltpu.VMEM((2, 4, 8, 64, 1536), bf16),
            pltpu.VMEM((4, 8, 64, 1536), bf16),
        ]
        + [pltpu.SemaphoreType.DMA((MP,))] * 4
        + [pltpu.SemaphoreType.DMA((4,))] * 2
        + [pltpu.SemaphoreType.DMA((2,))],
        compiler_params=pltpu.CompilerParams(
            vmem_limit_bytes=VMEM_LIMIT, collective_id=4, has_side_effects=True
        ),
    )(routed_terms, share, d_produced, active, incoming, d_gate_up)


def outputs_kernel(a_ref, ao, s1, r1, loc):
    c, m = place()
    mates = [(c, lax.rem(m + k, MP)) for k in range(1, MP)]
    greet(mates, MP - 1)
    own_a = pltpu.make_async_copy(a_ref.at[m], ao.at[m], loc.at[0])
    own_a.start()
    copies = []
    for k in range(1, MP):
        to = lax.rem(m + k, MP)
        copies.append(remote(a_ref.at[to], ao.at[m], s1.at[k], r1.at[k], mates[k - 1]))
    for copy in copies:
        copy.start()
    for copy in copies:
        copy.wait()
    own_a.wait()


def keys_grad_kernel(
    a_ref, out, theirs, pair_a, pair_b, got_a, got_b, sum_a, sum_b, last_a, last_b,
    s0, r0, s1, r1, s2, r2,
):
    c, m = place()
    core = lax.rem(c, 2)
    x, y = c // 4, lax.rem(c // 2, 2)
    sibling = (flip(c, 1), m)
    across = (flip(c, 2), m)
    peers = [(lax.rem(c + 4 * k, CTX), m) for k in range(1, 4)]
    greet(peers + [across, sibling], 5)
    low, high = pl.ds(0, HALF), pl.ds(HALF, HALF)
    crossing = [
        remote(
            a_ref.at[:, :, 1 - core, rows], theirs.at[:, :, rows], s0.at[at], r0.at[at], sibling
        )
        for at, rows in enumerate((high, low))
    ]
    for copy in crossing:
        copy.start()

    def add(a, b):
        return a.astype(f32) + b.astype(f32)

    crossing[0].wait()
    for i in range(4):
        for j in range(2):
            pair_b[i, j] = add(a_ref[i, j, core, high], theirs[i, j, high]).astype(bf16)
    first = [remote(pair_b.at[:, 1 - y], got_b, s1.at[0], r1.at[0], across)]
    first[0].start()
    crossing[1].wait()
    for i in range(4):
        for j in range(2):
            pair_a[i, j] = add(a_ref[i, j, core, low], theirs[i, j, low]).astype(bf16)
    for k in range(1, 4):
        copy = remote(
            pair_a.at[lax.rem(x + k, 4)], got_a.at[k - 1], s1.at[k], r1.at[k], peers[k - 1]
        )
        copy.start()
        first.append(copy)
    first[0].wait()
    for i in range(4):
        sum_b[i] = add(pair_b[i, y], got_b[i]).astype(bf16)
    second = []
    for k in range(1, 4):
        copy = remote(
            sum_b.at[lax.rem(x + k, 4)], last_b.at[k - 1], s2.at[k], r2.at[k], peers[k - 1]
        )
        copy.start()
        second.append(copy)
    for copy in first[1:]:
        copy.wait()
    for j in range(2):
        sum_a[j] = (add(pair_a[x, j], got_a[0, j]) + add(got_a[1, j], got_a[2, j])).astype(bf16)
    copy = remote(sum_a.at[1 - y], last_a, s2.at[0], r2.at[0], across)
    copy.start()
    second.append(copy)
    for copy in second:
        copy.wait()
    out[low] = add(sum_a[y], last_a[...])
    out[high] = add(sum_b[x], last_b[0]) + add(last_b[1], last_b[2])


def keys_grad(terms):
    piece = (HALF, 128)
    return pl.pallas_call(
        keys_grad_kernel,
        out_shape=shape((BLOCK, 128), f32),
        in_specs=[VM],
        out_specs=VM,
        scratch_shapes=[
            pltpu.VMEM((4, 2, BLOCK, 128), bf16),
            pltpu.VMEM((4, 2) + piece, bf16),
            pltpu.VMEM((4, 2) + piece, bf16),
            pltpu.VMEM((3, 2) + piece, bf16),
            pltpu.VMEM((4,) + piece, bf16),
            pltpu.VMEM((2,) + piece, bf16),
            pltpu.VMEM((4,) + piece, bf16),
            pltpu.VMEM(piece, bf16),
            pltpu.VMEM((3,) + piece, bf16),
        ]
        + [pltpu.SemaphoreType.DMA((2,))] * 2
        + [pltpu.SemaphoreType.DMA((4,))] * 4,
        compiler_params=pltpu.CompilerParams(
            vmem_limit_bytes=VMEM_LIMIT, collective_id=6, has_side_effects=True
        ),
    )(terms)


def finish_kernel(
    dq_ref, dkv_ref, cos_ref, sin_ref, normed_ref, br_ref, rows_ref, hid_ref, y_ref,
    ao, go, hid_out, y_out,
    d_qkv, terms, s1, r1, s2, r2, s3, r3, loc,
):
    c, m = place()
    upper = m >= MP // 2
    t = jnp.where(upper, CTX - 1 - c, c)
    barrier = pltpu.get_barrier_semaphore()
    for k in range(1, MP):
        pl.semaphore_signal(
            barrier, inc=1, device_id=(t, lax.rem(m + k, MP)), device_id_type=MESH
        )
    for k in range(1, CTX):
        pl.semaphore_signal(
            barrier, inc=1, device_id=(lax.rem(c + k, CTX), m), device_id_type=MESH
        )

    @pl.when(upper)
    def _():
        pl.semaphore_signal(barrier, inc=1, device_id=(t, m), device_id_type=MESH)
        pl.semaphore_wait(barrier, MP + CTX - 1)

    @pl.when(jnp.logical_not(upper))
    def _():
        pl.semaphore_wait(barrier, MP + CTX - 2)

    home = [
        remote(hid_ref, hid_out, s3.at[0], r3.at[0], (t, m)),
        remote(y_ref, y_out, s3.at[1], r3.at[1], (t, m)),
    ]
    stay = [
        pltpu.make_async_copy(hid_ref, hid_out, loc.at[2]),
        pltpu.make_async_copy(y_ref, y_out, loc.at[3]),
    ]

    @pl.when(upper)
    def _():
        for copy in home:
            copy.start()

    @pl.when(jnp.logical_not(upper))
    def _():
        for copy in stay:
            copy.start()

    low = lanes(TOK) < HEAD
    for i in range(MP):
        at = i * TOK
        part, inside = at // HALF, at % HALF
        columns = dq_ref[part]
        heads = jnp.concatenate(
            [
                columns[:HEAD, inside : inside + TOK],
                columns[:HEAD, HALF + inside : HALF + inside + TOK],
            ],
            axis=0,
        ).T
        cosine, sine = phase_rows(cos_ref, at, TOK), phase_rows(sin_ref, at, TOK)
        d_qkv[i, :, 0:128] = turn_back(heads * score_scale, cosine, sine).astype(bf16)
        dkv = dkv_ref[at : at + TOK]
        d_qkv[i, :, 128:256] = jnp.where(low, turn_back(dkv, cosine, sine), dkv).astype(bf16)

    own_a = pltpu.make_async_copy(d_qkv.at[m], ao.at[m], loc.at[1])
    a_copies, g_copies = [], []
    for k in range(MP):
        to = lax.rem(m + k, MP)
        target = (jnp.where(to >= MP // 2, CTX - 1 - c, c), to)
        a_copies.append(remote(d_qkv.at[to], ao.at[m], s1.at[k], r1.at[k], target))

    @pl.when(upper)
    def _():
        a_copies[0].start()

    @pl.when(jnp.logical_not(upper))
    def _():
        own_a.start()

    for k in range(1, MP):
        a_copies[k].start()
    grads = d_qkv[...].reshape(BLOCK, 256)
    columns = jnp.concatenate(
        [
            contract(grads, normed_ref[...], 0, 0),
            contract(rows_ref[...], br_ref[...], 0, 0),
        ],
        axis=0,
    )
    terms[...] = columns.T.astype(bf16).reshape(terms.shape)
    own_g = pltpu.make_async_copy(terms.at[c], go.at[c], loc.at[0])
    own_g.start()
    for k in range(1, CTX):
        to = lax.rem(c + k, CTX)
        copy = remote(terms.at[to], go.at[c], s2.at[k], r2.at[k], (to, m))
        copy.start()
        g_copies.append(copy)
    for k in range(1, MP):
        a_copies[k].wait()
    for copy in g_copies:
        copy.wait()
    own_g.wait()

    @pl.when(upper)
    def _():
        a_copies[0].wait()
        for copy in home:
            copy.wait()

    @pl.when(jnp.logical_not(upper))
    def _():
        own_a.wait()
        for copy in stay:
            copy.wait()


def finish(dq, dkv, cosine, sine, normed, branch_rows, out_rows, hidden_grad, outputs):
    return pl.pallas_call(
        finish_kernel,
        out_shape=[
            shape((MP, TOK, 256)),
            shape((CTX, 64, 384)),
            shape((TOK, 1024)),
            shape((TOK, 1024)),
        ],
        in_specs=[VM] * 7 + [ANY] * 2,
        out_specs=[ANY] * 4,
        scratch_shapes=[
            pltpu.VMEM((MP, TOK, 256), bf16),
            pltpu.VMEM((CTX, 64, 384), bf16),
        ]
        + [pltpu.SemaphoreType.DMA((n,)) for n in (MP, MP, CTX, CTX, 2, 2, 4)],
        compiler_params=pltpu.CompilerParams(
            vmem_limit_bytes=VMEM_LIMIT, collective_id=8, has_side_effects=True
        ),
    )(dq, dkv, cosine, sine, normed, branch_rows, out_rows, hidden_grad, outputs)


def sums_kernel(
    a_ref, sum_a, sum_b, out, in_grad, out_grad,
    got, part, got2, last_a, last_b, s1, r1, s2, r2, s3, r3,
):
    c, m = place()
    x, y = c // 4, lax.rem(c // 2, 2)
    peers = [(lax.rem(c + k, CTX), m) for k in range(1, CTX)]
    mates = [(c, lax.rem(m + k, MP)) for k in range(1, MP)]
    greet(peers + mates, CTX - 1 + MP - 1)
    copies = []
    for k in range(1, CTX):
        to = lax.rem(c + k, CTX)
        copy = remote(a_ref.at[to], got.at[k], s1.at[k], r1.at[k], peers[k - 1])
        copy.start()
        copies.append(copy)
    experts = [
        remote(
            sum_b.at[:, lax.rem(x + k, 4)],
            last_b.at[k - 1], s3.at[k], r3.at[k], (lax.rem(c + 4 * k, CTX), m),
        )
        for k in range(1, 4)
    ]
    experts.append(remote(sum_a.at[:, 1 - y], last_a, s3.at[0], r3.at[0], (flip(c, 2), m)))
    for copy in experts:
        copy.start()
    total = a_ref[c]
    for copy in copies:
        copy.wait()
    for k in range(1, CTX):
        total = total + got[k]
    part[...] = total
    copies = []
    for k in range(1, MP):
        to = lax.rem(m + k, MP)
        copy = remote(part.at[to], got2.at[k], s2.at[k], r2.at[k], mates[k - 1])
        copy.start()
        copies.append(copy)
    for copy in experts:
        copy.wait()

    def put(at, term):
        in_grad[at] = term[:, :1024]
        out_grad[at] = term[:, 1024:].T

    for e in range(FIRST):
        put(e, sum_a[e, y].astype(f32) + last_a[e].astype(f32))
    for e in range(4 - FIRST):
        term = sum_b[e, x].astype(f32)
        for k in range(3):
            term = term + last_b[k, e].astype(f32)
        put(FIRST + e, term)
    last = part[m]
    for copy in copies:
        copy.wait()
    for k in range(1, MP):
        last = last + got2[k]
    out[...] = last


def small_sums(terms, sum_a, sum_b):
    dims = terms.shape[2:]
    wide = sum_a.shape[-1]
    return pl.pallas_call(
        sums_kernel,
        out_shape=[shape(dims, f32), shape((4, 64, 1024), f32), shape((4, 512, 64), f32)],
        in_specs=[VM] * 3,
        out_specs=[VM] * 3,
        scratch_shapes=[
            pltpu.VMEM((CTX, MP) + dims, f32),
            pltpu.VMEM((MP,) + dims, f32),
            pltpu.VMEM((MP,) + dims, f32),
            pltpu.VMEM((FIRST, 64, wide), bf16),
            pltpu.VMEM((3, 4 - FIRST, 64, wide), bf16),
            pltpu.SemaphoreType.DMA((CTX,)),
            pltpu.SemaphoreType.DMA((CTX,)),
            pltpu.SemaphoreType.DMA((MP,)),
            pltpu.SemaphoreType.DMA((MP,)),
            pltpu.SemaphoreType.DMA((4,)),
            pltpu.SemaphoreType.DMA((4,)),
        ],
        compiler_params=pltpu.CompilerParams(
            vmem_limit_bytes=VMEM_LIMIT, collective_id=9, has_side_effects=True
        ),
    )(terms, sum_a, sum_b)


def unit(index, first_half):
    second = index > first_half
    part = second.astype(jnp.int32)
    key_half = jnp.where(second, index - first_half - 1, index)
    odd = lax.rem(key_half, 2) == 1
    slot = jnp.where(odd, 2 * CTX - key_half, key_half)
    diagonal = jnp.logical_or(index == first_half, index == 2 * CTX)
    return part, slot, diagonal


def visible_mask(rows):
    key_at = lax.broadcasted_iota(jnp.int32, (HALF, rows), 0)
    query_at = lax.rem(lax.broadcasted_iota(jnp.int32, (HALF, rows), 1), HALF)
    return key_at <= query_at


def forward_kernel(
    q_ref, kv_ref, in_ref, qw_ref, rows_ref,
    out_ref, rows_out, lse_ref, in_all, qw_all, rows_all,
    best, total, summed, *sems,
):
    first_half = 2 * lax.axis_index("ctx")
    greet(ctx_neighbours() + mp_neighbours(), 7)
    weights_rings = [ctx_ring(in_ref, row_slots(in_all), sems[0:5])]
    rows_rings = [
        mp_ring(rows_ref, slots(rows_all), sems[5:8]),
        mp_ring(qw_ref, slots(qw_all), sems[8:11]),
    ]
    for ring in weights_rings + rows_rings:
        ring.start()
    best[...] = jnp.full(best.shape, -1e30, f32)
    total[...] = jnp.zeros(total.shape, f32)
    summed[...] = jnp.zeros(summed.shape, f32)

    def work(part, slot, masked):
        kv = kv_ref[slot]
        scores = contract(kv, q_ref[part], 1, 1)
        if masked:
            scores = jnp.where(visible_mask(scores.shape[1]), scores, -jnp.inf)
        old = best[part]
        new = jnp.maximum(old, jnp.max(scores, axis=0, keepdims=True))
        weights = jnp.exp2(scores * log2_e - new * log2_e)
        fading = jnp.exp2((old - new) * log2_e)
        total[part] = total[part] * fading + jnp.sum(weights, axis=0, keepdims=True)
        summed[part] = summed[part] * fading + contract(kv, weights.astype(bf16), 0, 0)
        best[part] = new

    def step(index, carry):
        part, slot, diagonal = unit(index, first_half)

        @pl.when(index == 10)
        def _():
            for ring in weights_rings:
                ring.relay_own()
                ring.relay_near()

        @pl.when(index == 14)
        def _():
            for ring in rows_rings:
                ring.relay_near()
                ring.relay_own()

        @pl.when(index == 21)
        def _():
            for ring in weights_rings:
                ring.relay_far()

        @pl.when(index == 26)
        def _():
            for ring in rows_rings:
                ring.relay_far()

        @pl.when(diagonal)
        def _():
            work(part, slot, True)

        @pl.when(jnp.logical_not(diagonal))
        def _():
            work(part, slot, False)

        return carry

    lax.fori_loop(0, 2 * CTX + 1, step, 0)
    for part in range(2):
        columns = summed[part][HEAD:, :] / total[part]
        heads = jnp.concatenate([columns[:, :HALF], columns[:, HALF:]], axis=0).T
        out_ref[part * HALF : part * HALF + HALF] = heads
        rows_out[part * HALF : part * HALF + HALF] = heads.astype(bf16)
        lse_ref[part] = best[part] + jnp.log(total[part])
    for ring in weights_rings + rows_rings:
        ring.finish()


def attention(q_rows, kv_all, w_in, qkv_w, out_rows_w):
    rows = q_rows.shape[1]
    return pl.pallas_call(
        forward_kernel,
        out_shape=[
            shape((BLOCK, 128), f32),
            shape((BLOCK, 128)),
            shape((2, 1, rows), f32),
            shape((4, 1024, 1024)),
            shape((MP,) + qkv_w.shape),
            shape((MP, TOK, 1024)),
        ],
        in_specs=[VM, VM, ANY, ANY, ANY],
        out_specs=[VM, VM, VM, ANY, ANY, ANY],
        scratch_shapes=[
            pltpu.VMEM((2, 1, rows), f32),
            pltpu.VMEM((2, 1, rows), f32),
            pltpu.VMEM((2, 2 * HEAD, rows), f32),
        ]
        + CTX_SEMS
        + MP_SEMS * 2,
        compiler_params=pltpu.CompilerParams(
            vmem_limit_bytes=VMEM_LIMIT, collective_id=10, has_side_effects=True
        ),
        cost_estimate=pl.CostEstimate(
            flops=33 * 4 * HALF * rows * 256, bytes_accessed=1 << 23, transcendentals=33 * HALF * rows
        ),
    )(q_rows, kv_all, w_in, qkv_w, out_rows_w)


FIRST = 3


def backward_kernel(
    q_ref, og_ref, att_ref, lse_ref, kv_ref, pair_ref, br_ref, mixed_ref,
    dkv_ref, dq_ref, sum_a, sum_b, br_all, mixed_out,
    total, do_ref, delta_ref, got_a, got_b, *sems,
):
    c, m = place()
    first_half = 2 * c
    x, y = c // 4, lax.rem(c // 2, 2)
    peers = [(lax.rem(c + 4 * k, CTX), m) for k in range(1, 4)]
    across = (flip(c, 2), m)
    mates = [(c, lax.rem(m + k, MP)) for k in range(1, MP)]
    greet(peers + [across] + mates, 4 + MP - 1)
    sa, ra, sm, rm, loc = sems[:5]
    ring = mp_ring(br_ref, slots(br_all), sems[5:8])

    def first_copies():
        copies = [
            remote(
                pair_ref.at[pl.ds(0, FIRST), lax.rem(x + k, 4)],
                got_a.at[k - 1], sa.at[k], ra.at[k], peers[k - 1],
            )
            for k in range(1, 4)
        ]
        copies.append(
            remote(
                pair_ref.at[pl.ds(FIRST, 4 - FIRST), :, 1 - y], got_b, sa.at[0], ra.at[0], across
            )
        )
        return copies

    def mixed_copies():
        copies = []
        for k in range(1, MP):
            to = lax.rem(m + k, MP)
            copies.append(
                remote(mixed_ref.at[to], mixed_out.at[m], sm.at[k], rm.at[k], mates[k - 1])
            )
        return copies

    def own_mixed():
        return pltpu.make_async_copy(mixed_ref.at[m], mixed_out.at[m], loc)

    for copy in first_copies():
        copy.start()
    ring.start()
    low = lanes(HALF) < HEAD
    for part in range(2):
        rows = slice(part * HALF, part * HALF + HALF)
        grads = og_ref[rows].astype(f32)
        product = (grads * att_ref[rows]).T
        delta_ref[part, :, 0:HALF] = jnp.sum(product[:HEAD], axis=0, keepdims=True)
        delta_ref[part, :, HALF:] = jnp.sum(product[HEAD:], axis=0, keepdims=True)
        do_ref[part, 0:HALF] = jnp.where(low, 0.0, pltpu.roll(grads, HEAD, 1)).astype(bf16)
        do_ref[part, HALF:] = jnp.where(low, 0.0, grads).astype(bf16)
    dq_ref[...] = jnp.zeros(dq_ref.shape, f32)

    def clear(index, carry):
        total[index] = jnp.zeros(total.shape[1:], f32)
        return carry

    lax.fori_loop(0, 2 * CTX, clear, 0)

    def work(part, slot, masked):
        kv = kv_ref[slot]
        queries = q_ref[part]
        grads = do_ref[part]
        scores = contract(kv, queries, 1, 1)
        probs = jnp.exp2((scores - lse_ref[part]) * log2_e)
        if masked:
            probs = jnp.where(visible_mask(scores.shape[1]), probs, 0.0)
        prob_grad = contract(kv, grads, 1, 1)
        score_grad = (probs * (prob_grad - delta_ref[part])).astype(bf16)
        total[slot] += contract(probs.astype(bf16), grads, 1, 0) + contract(
            score_grad, queries, 1, 0
        )
        dq_ref[part] += contract(kv, score_grad, 0, 0)

    def step(index, carry):
        part, slot, diagonal = unit(index, first_half)

        @pl.when(index == 5)
        def _():
            ring.relay_near()
            ring.relay_own()

        @pl.when(index == 10)
        def _():
            ring.relay_far()
            own_mixed().start()
            for copy in mixed_copies():
                copy.start()

        @pl.when(diagonal)
        def _():
            work(part, slot, True)

        @pl.when(jnp.logical_not(diagonal))
        def _():
            work(part, slot, False)

        return carry

    lax.fori_loop(0, 2 * CTX + 1, step, 0)

    def write(index, carry):
        dkv_ref[index] = total[index].astype(bf16)
        return carry

    lax.fori_loop(0, 2 * CTX, write, 0)
    ring.finish()
    for copy in first_copies():
        copy.wait()
    for e in range(FIRST):
        for j in range(2):
            term = pair_ref[e, x, j].astype(f32)
            for k in range(3):
                term = term + got_a[k, e, j].astype(f32)
            sum_a[e, j] = term.astype(bf16)
    for e in range(4 - FIRST):
        for j in range(4):
            term = pair_ref[FIRST + e, j, y].astype(f32) + got_b[e, j].astype(f32)
            sum_b[e, j] = term.astype(bf16)
    for copy in mixed_copies():
        copy.wait()
    own_mixed().wait()


def attention_back(q_rows, out_grad, attended, lse, kv_all, pair, branch_grad, mixed):
    rows = q_rows.shape[1]
    wide = pair.shape[-1]
    return pl.pallas_call(
        backward_kernel,
        out_shape=[
            shape(kv_all.shape, bf16),
            shape((2, 2 * HEAD, rows), f32),
            shape((FIRST, 2, 64, wide)),
            shape((4 - FIRST, 4, 64, wide)),
            shape((MP, TOK, 1024)),
            shape((MP, TOK, 1024)),
        ],
        in_specs=[VM] * 6 + [ANY] * 2,
        out_specs=[VM] * 4 + [ANY] * 2,
        scratch_shapes=[
            pltpu.VMEM(kv_all.shape, f32),
            pltpu.VMEM(q_rows.shape, bf16),
            pltpu.VMEM((2, 1, rows), f32),
            pltpu.VMEM((3, FIRST, 2, 64, wide), bf16),
            pltpu.VMEM((4 - FIRST, 4, 64, wide), bf16),
        ]
        + [pltpu.SemaphoreType.DMA((4,))] * 2
        + [pltpu.SemaphoreType.DMA((MP,))] * 2
        + [pltpu.SemaphoreType.DMA]
        + MP_SEMS,
        compiler_params=pltpu.CompilerParams(
            vmem_limit_bytes=VMEM_LIMIT, collective_id=11, has_side_effects=True
        ),
        cost_estimate=pl.CostEstimate(
            flops=33 * 10 * HALF * rows * 256, bytes_accessed=1 << 24, transcendentals=33 * HALF * rows
        ),
    )(q_rows, out_grad, attended, lse, kv_all, pair, branch_grad, mixed)


def phases(positions, head_width):
    steps_up = jnp.arange(head_width // 2).astype(f32)
    frequency = rope_base ** (-2.0 * steps_up / head_width)
    angles = frequency[:, None] * positions.astype(f32)[None, :]
    return (jnp.cos(angles), jnp.sin(angles))


def normalize(values):
    inverse = lax.rsqrt(jnp.mean(values * values, axis=-1, keepdims=True) + epsilon)
    return (values * inverse, inverse)


def norm_back(grads, scaled, inverse, gain):
    inner = grads * gain
    return (
        inverse * (inner - scaled * jnp.mean(inner * scaled, axis=-1, keepdims=True)),
        jnp.sum(grads * scaled, axis=0),
    )


def swap_home(array):
    pairs = []
    for c in range(CTX):
        for m in range(MP):
            t = CTX - 1 - c if m >= MP // 2 else c
            pairs.append((c * MP + m, t * MP + m))
    return lax.ppermute(array, ("ctx", "mp"), pairs)


def body(
    layer_input,
    positions,
    expert_ids,
    attn_gain,
    w_query,
    w_key,
    w_value,
    w_attn_out,
    ffn_gain,
    router,
    w_in,
    w_out,
    cotangent,
):
    c, m = place()
    dy_swapped = swap_home(cotangent)
    own_positions = lax.dynamic_slice_in_dim(positions, m * TOK, TOK, 0)
    id_pack = jnp.concatenate(
        [expert_ids.T, own_positions[None, :], jnp.zeros((7, TOK), jnp.int32)], axis=0
    )
    w_pack = jnp.concatenate(
        [
            w_query,
            w_key,
            w_value,
            router,
            attn_gain[:, None],
            ffn_gain[:, None],
            jnp.zeros((64, 94), bf16),
            w_attn_out.T,
        ],
        axis=1,
    )
    x_all, id_all, w_all = comm_call(
        start_kernel,
        1,
        [layer_input, id_pack, w_pack],
        [
            shape((MP, TOK, 1024)),
            shape((MP, 16, TOK), jnp.int32),
            shape((CTX, 64, 512)),
        ],
        [MP, MP, MP, MP, 2] + CTX_SEMS,
        4 << 20,
    )
    inputs = x_all.reshape(BLOCK, 1024).astype(f32)
    ids = id_all[:, :8, :].transpose(1, 0, 2).reshape(8, BLOCK)
    places = id_all[:, 8, :].reshape(BLOCK)
    w_all = w_all.reshape(1024, 512)
    qkv_w = w_all[:, :256]
    router_w = w_all[:, 256:288]
    gain_one = w_all[:, 288].astype(f32)
    gain_two = w_all[:, 289].astype(f32)
    out_w = w_all[:, 384:].T

    cosine, sine = lax.optimization_barrier(phases(places, HEAD))
    normed, q_rows, kv_all, dy_all = keys_and_values(
        x_all.reshape(BLOCK, 1024), gain_one[None, :], qkv_w, cosine, sine, dy_swapped
    )
    kv_all = kv_all.reshape(2 * CTX, HALF, 128)
    attended, out_rows, lse, in_w, qkv_w_all, out_w_all = attention(
        q_rows, kv_all, w_in, qkv_w, out_w
    )
    dy_all = dy_all.reshape(BLOCK, 1024)
    rows_all, out_w_t = comm_call(
        gather_kernel,
        3,
        [out_rows, w_out.transpose(0, 2, 1)],
        [shape((MP, BLOCK, 128)), shape((4, 1024, 512))],
        MP_SEMS + CTX_SEMS,
        8 << 20,
    )
    branch = lax.dot_general(
        rows_all, out_w_all, (((0, 2), (0, 1)), ((), ())), preferred_element_type=f32
    )
    hidden = inputs + branch_scale * branch
    scaled_two, inverse_two = normalize(hidden)
    routed = (scaled_two * gain_two).astype(bf16)

    logits = contract(router_w, routed, 0, 1)
    experts = lax.broadcasted_iota(jnp.int32, (32, BLOCK), 0)
    member = jnp.any(ids[:, None, :] == experts[None], axis=0)
    chosen = jnp.where(member, logits, -jnp.inf)
    top_logit = jnp.max(chosen, axis=0, keepdims=True)
    powers = jnp.exp(chosen - top_logit)
    gates = powers / jnp.sum(powers, axis=0, keepdims=True)

    here = 4 * m + lax.broadcasted_iota(jnp.int32, (4, BLOCK), 0)
    selected = jnp.any(ids[:, None, :] == here[None], axis=0)
    earlier = (
        lax.broadcasted_iota(jnp.int32, (BLOCK, BLOCK), 0)
        <= lax.broadcasted_iota(jnp.int32, (BLOCK, BLOCK), 1)
    ).astype(bf16)
    counts = jnp.dot(selected.astype(bf16), earlier, preferred_element_type=f32)
    rank = jnp.where(selected, counts.astype(jnp.int32) - 1, -1)
    capacity = 288
    place_bool = rank[:, None, :] == lax.broadcasted_iota(jnp.int32, (4, capacity, BLOCK), 1)
    placing = place_bool.astype(bf16).reshape(4 * capacity, BLOCK)
    gates_here = lax.dynamic_slice_in_dim(gates, 4 * m, 4, 0)
    slot_gate = jnp.sum(jnp.where(place_bool, gates_here[:, None, :], 0.0), axis=2)

    incoming = jnp.dot(placing, routed, preferred_element_type=f32).astype(bf16)
    incoming = incoming.reshape(4, capacity, 1024)
    dy_rows = jnp.dot(placing, dy_all, preferred_element_type=f32).reshape(4, capacity, 1024)
    gate_up = jnp.einsum("esd,edf->esf", incoming, in_w, preferred_element_type=f32)
    gate_part, up_part = gate_up[..., :512], gate_up[..., 512:]
    squashed = jax.nn.sigmoid(gate_part)
    silu_part = gate_part * squashed
    active = (silu_part * up_part).astype(bf16)
    produced = jnp.einsum(
        "esf,edf->esd", active, out_w_t, preferred_element_type=f32
    ).astype(bf16)
    produced_f = produced.astype(f32)
    d_produced = (branch_scale * slot_gate[..., None] * dy_rows).astype(bf16)
    slot_share = branch_scale * jnp.sum(dy_rows * produced_f, axis=2)
    weighted = (slot_gate[..., None] * produced_f).astype(bf16).reshape(4 * capacity, 1024)
    mixed = branch_scale * contract(placing, weighted, 0, 0)
    mixed = mixed.astype(bf16).reshape(MP, TOK, 1024)

    d_active = jnp.einsum("esd,edf->esf", d_produced, out_w_t, preferred_element_type=f32)
    slope = squashed * (1.0 + gate_part * (1.0 - squashed))
    d_gate_up = jnp.concatenate(
        [d_active * up_part * slope, d_active * silu_part], axis=-1
    ).astype(bf16)
    row_grads = jnp.einsum(
        "esf,edf->esd", d_gate_up, in_w, preferred_element_type=f32
    ).astype(bf16)
    routed_terms = contract(placing, row_grads.reshape(4 * capacity, 1024), 0, 0)
    routed_terms = routed_terms.astype(bf16).reshape(MP, TOK, 1024)
    share = jnp.sum(jnp.where(place_bool, slot_share[:, :, None], 0.0), axis=1)
    share = jnp.pad(share.reshape(4, MP, TOK).transpose(1, 0, 2), ((0, 0), (0, 4), (0, 0)))
    routed_got, share_got, pair = scatter_rows(
        routed_terms, share, d_produced, active, incoming, d_gate_up
    )

    def own_rows(array):
        return lax.dynamic_slice_in_dim(array, m * TOK, TOK, 0)

    hidden_own = own_rows(hidden)
    scaled_own, inverse_own = normalize(hidden_own)
    routed_own = (scaled_own * gain_two).astype(bf16).astype(f32)
    dy_own = own_rows(dy_all).astype(f32)
    gates_own = lax.dynamic_slice_in_dim(gates, m * TOK, TOK, 1)
    share_own = share_got[:, :4, :].reshape(32, TOK)
    logit_grad = gates_own * (
        share_own - jnp.sum(gates_own * share_own, axis=0, keepdims=True)
    )
    routed_grad = jnp.sum(routed_got.astype(f32), axis=0) + lax.dot_general(
        logit_grad,
        router_w.astype(f32),
        (((0,), (1,)), ((), ())),
        precision=highest,
        preferred_element_type=f32,
    )
    router_grad = lax.dot_general(
        routed_own,
        logit_grad,
        (((0,), (1,)), ((), ())),
        precision=highest,
        preferred_element_type=f32,
    )
    hidden_grad, gain_two_grad = norm_back(routed_grad, scaled_own, inverse_own, gain_two)
    hidden_grad = hidden_grad + dy_own
    branch_grad = (branch_scale * hidden_grad).astype(bf16)

    out_grad_terms = jnp.einsum(
        "td,hfd->htf", branch_grad, out_w_all, preferred_element_type=f32
    ).astype(bf16)
    (out_grad,) = comm_call(
        outputs_kernel, 5, [out_grad_terms], [shape((MP, TOK, 128))], [MP, MP, 1], 1 << 20
    )
    out_grad = out_grad.reshape(BLOCK, 128)
    pair = pair.reshape(4, 4, 2, 64, 1536)

    dkv_terms, dq_cols, sum_a, sum_b, branch_rows, mixed_got = attention_back(
        q_rows, out_grad, attended, lse, kv_all, pair, branch_grad, mixed
    )
    outputs = (hidden_own + jnp.sum(mixed_got.astype(f32), axis=0)).astype(bf16)
    dkv = keys_grad(dkv_terms.reshape(4, 2, 2, BLOCK, 128))
    qkv_got, w_got, hidden_grad_home, outputs = finish(
        dq_cols,
        dkv,
        cosine,
        sine,
        normed,
        branch_rows.reshape(BLOCK, 1024),
        out_rows,
        hidden_grad.astype(bf16),
        outputs,
    )
    w_grad = jnp.sum(w_got.astype(f32), axis=0)
    normed_grad = jnp.einsum(
        "htf,hdf->td", qkv_got, qkv_w_all, preferred_element_type=f32
    )
    scaled_one, inverse_one = normalize(layer_input.astype(f32))
    input_grad, gain_one_grad = norm_back(normed_grad, scaled_one, inverse_one, gain_one)
    input_grad = (input_grad + hidden_grad_home.astype(f32)).astype(bf16)

    small = jnp.concatenate(
        [
            router_grad,
            gain_one_grad[:, None],
            gain_two_grad[:, None],
            jnp.zeros((1024, 94), f32),
        ],
        axis=1,
    )
    sums, expert_in, expert_out = small_sums(small.reshape(CTX, MP, 8, 128), sum_a, sum_b)
    return (
        outputs,
        input_grad,
        sums[:, 32],
        w_grad[:, :128],
        w_grad[:, 128:192],
        w_grad[:, 192:256],
        w_grad[:, 256:].T,
        sums[:, 33],
        sums[:, :32],
        expert_in,
        expert_out,
    )


def solution(mesh):
    placed = (
        P(("ctx", "mp"), None),
        P("ctx"),
        P(("ctx", "mp"), None),
        P("ctx"),
        P("ctx", "mp"),
        P("ctx", "mp"),
        P("ctx", "mp"),
        P("mp", "ctx"),
        P("ctx"),
        P("ctx", None),
        P("mp", "ctx", None),
        P("mp", None, "ctx"),
        P(("ctx", "mp"), None),
    )
    return jax.shard_map(
        body,
        mesh=mesh,
        in_specs=placed,
        out_specs=(
            P(("ctx", "mp"), None),
            P(("ctx", "mp"), None),
            P(("ctx", "mp")),
            P("ctx", "mp"),
            P("ctx", "mp"),
            P("ctx", "mp"),
            P("mp", "ctx"),
            P(("ctx", "mp")),
            P(("ctx", "mp"), None),
            P("mp", "ctx", None),
            P("mp", None, "ctx"),
        ),
        check_vma=False,
    )
```

```python
import functools

import jax
import jax.numpy as jnp
from jax import lax
from jax.experimental import pallas as pl
from jax.experimental.pallas import tpu as pltpu
from jax.sharding import PartitionSpec as P

MESH = pl.DeviceIdType.MESH
epsilon = 1e-06
branch_scale = 0.22
score_scale = 0.015625
rope_base = 10000.0
highest = lax.Precision.HIGHEST
log2_e = 1.4426950408889634
bf16 = jnp.bfloat16
f32 = jnp.float32
CTX, MP = 16, 8
HEAD = 64
TOK = 128
BLOCK = 1024
HALF = 512
ANY = pl.BlockSpec(memory_space=pl.ANY)
VM = pl.BlockSpec(memory_space=pltpu.VMEM)
VMEM_LIMIT = 56 * 1024 * 1024


def contract(left, right, left_dim, right_dim):
    return lax.dot_general(
        left, right, (((left_dim,), (right_dim,)), ((), ())), preferred_element_type=f32
    )


def place():
    return lax.axis_index("ctx"), lax.axis_index("mp")


def greet(signal_to, expected):
    barrier = pltpu.get_barrier_semaphore()
    for target in signal_to:
        pl.semaphore_signal(barrier, inc=1, device_id=target, device_id_type=MESH)
    pl.semaphore_wait(barrier, expected)


def remote(src, dst, send, recv, target):
    return pltpu.make_async_remote_copy(
        src_ref=src, dst_ref=dst, send_sem=send, recv_sem=recv,
        device_id=target, device_id_type=MESH,
    )


def comm_call(kernel, number, arrays, outs, sems, cost):
    return pl.pallas_call(
        kernel,
        out_shape=outs,
        in_specs=[ANY] * len(arrays),
        out_specs=[ANY] * len(outs),
        scratch_shapes=[
            pltpu.SemaphoreType.DMA((n,)) if isinstance(n, int) else n for n in sems
        ],
        compiler_params=pltpu.CompilerParams(collective_id=number, has_side_effects=True),
        cost_estimate=pl.CostEstimate(flops=0, bytes_accessed=cost, transcendentals=0),
    )(*arrays)


def shape(dims, kind=bf16):
    return jax.ShapeDtypeStruct(dims, kind)


def flip(index, stride):
    return index + stride - 2 * stride * lax.rem(index // stride, 2)


class Ring:
    def __init__(self, own, dst, index, spread, near, stride, target, sems, sibling=None):
        send, recv, loc = sems[:3]
        count = spread
        plus, minus = lax.rem(index + stride, count), lax.rem(index + count - stride, count)
        far = lax.rem(index + 2 * stride, count)
        near_of = lambda slot: flip(slot, near)
        me_near = near_of(index)

        def copy(src, place_of, at, to):
            return lambda: remote(src, place_of, send.at[at], recv.at[at], target(to))

        def relay(slot, part, at, to):
            return copy(dst(slot, part), dst(slot, part), at, to)

        self.own = lambda: pltpu.make_async_copy(own, dst(index, None), loc)
        self.to_near = copy(own, dst(index, None), 0, me_near)
        self.plus_own = copy(own, dst(index, None), 1, plus)
        self.minus_own = copy(own, dst(index, None), 2, minus)
        self.plus_near = relay(me_near, None, 3, plus)
        self.minus_near = relay(me_near, None, 4, minus)
        self.plus_far = relay(minus, 0, 5, plus)
        self.minus_far = relay(plus, 1, 6, minus)
        self.plus_far_near = relay(near_of(minus), 0, 7, plus)
        self.minus_far_near = relay(near_of(plus), 1, 8, minus)
        self.over = None
        if sibling is not None:
            send2, recv2 = sems[3:]
            parts = [
                (index, None),
                (me_near, None),
                (minus, None),
                (plus, None),
                (near_of(minus), None),
                (near_of(plus), None),
                (far, 0),
                (far, 1),
                (near_of(far), 0),
                (near_of(far), 1),
            ]

            def over(at):
                slot, part = parts[at]
                src = own if at == 0 else dst(slot, part)
                return remote(src, dst(slot, part), send2.at[at], recv2.at[at], sibling)

            self.over = over

    def cross(self, *numbers):
        if self.over is not None:
            for at in numbers:
                self.over(at).start()

    def start(self):
        self.own().start()
        for copy in (self.to_near, self.plus_own, self.minus_own):
            copy().start()
        self.cross(0)

    def relay_near(self):
        self.to_near().wait_recv()
        self.plus_near().start()
        self.minus_near().start()
        self.cross(1)

    def relay_own(self):
        self.plus_own().wait_recv()
        self.plus_far().start()
        self.minus_own().wait_recv()
        self.minus_far().start()
        self.cross(2, 3)

    def relay_far(self):
        self.plus_near().wait_recv()
        self.plus_far_near().start()
        self.minus_near().wait_recv()
        self.minus_far_near().start()
        self.cross(4, 5)

    def finish(self):
        last = (self.plus_far, self.minus_far, self.plus_far_near, self.minus_far_near)
        for number, copy in enumerate(last):
            copy().wait_recv()
            self.cross(6 + number)
        for copy in (
            self.to_near,
            self.plus_own,
            self.minus_own,
            self.plus_near,
            self.minus_near,
        ) + last:
            copy().wait_send()
        if self.over is not None:
            for at in range(10):
                self.over(at).wait()
        self.own().wait()


def mp_ring(own, dst, sems):
    c, m = place()
    return Ring(own, dst, m, MP, 1, 2, lambda slot: (c, slot), sems)


def shared_ring(own, out, sems):
    c, m = place()
    half = own.shape[0] // 2
    first = pl.multiple_of(lax.rem(c, 2) * half, half)

    def dst(slot, part):
        if part is None:
            return out.at[slot, pl.ds(first, half)]
        return out.at[slot, pl.ds(first + part * (half // 2), half // 2)]

    mine = own.at[pl.ds(first, half)]
    return Ring(mine, dst, m, MP, 1, 2, lambda slot: (c, slot), sems, (flip(c, 1), m))


def ctx_ring(own, dst, sems):
    c, m = place()
    return Ring(own, dst, c, CTX, 2, 4, lambda slot: (slot, m), sems, (flip(c, 1), m))


def mp_neighbours():
    c, m = place()
    return [(c, flip(m, 1)), (c, lax.rem(m + 2, MP)), (c, lax.rem(m + 6, MP))]


def ctx_neighbours():
    c, m = place()
    return [
        (flip(c, 2), m),
        (lax.rem(c + 4, CTX), m),
        (lax.rem(c + 12, CTX), m),
        (flip(c, 1), m),
    ]


def slots(ref):
    half = ref.shape[1] // 2

    def dst(slot, part):
        return ref.at[slot] if part is None else ref.at[slot, pl.ds(part * half, half)]

    return dst


def row_slots(ref):
    half = ref.shape[0] // 2

    def dst(slot, part):
        rows = pl.ds(pl.multiple_of(slot * 64, 64), 64)
        return ref.at[:, rows] if part is None else ref.at[pl.ds(part * half, half), rows]

    return dst


MP_SEMS = [pltpu.SemaphoreType.DMA((9,)), pltpu.SemaphoreType.DMA((9,)), pltpu.SemaphoreType.DMA]
CTX_SEMS = MP_SEMS + [pltpu.SemaphoreType.DMA((10,)), pltpu.SemaphoreType.DMA((10,))]


def start_kernel(x_ref, id_ref, w_ref, xo, ido, wo, xs, xr, ids, idr, loc, *sems):
    c, m = place()
    upper = m >= MP // 2
    t = jnp.where(upper, CTX - 1 - c, c)
    signals = []
    for k in range(1, MP):
        sender = lax.rem(m + k, MP)
        signals.append((jnp.where(sender >= MP // 2, CTX - 1 - c, c), sender))
    signals += ctx_neighbours()
    barrier = pltpu.get_barrier_semaphore()
    for target in signals:
        pl.semaphore_signal(barrier, inc=1, device_id=target, device_id_type=MESH)

    @pl.when(upper)
    def _():
        pl.semaphore_signal(barrier, inc=1, device_id=(CTX - 1 - c, m), device_id_type=MESH)
        pl.semaphore_wait(barrier, MP + 4)

    @pl.when(jnp.logical_not(upper))
    def _():
        pl.semaphore_wait(barrier, MP + 3)

    ring = ctx_ring(w_ref, slots(wo), sems)
    ring.start()
    x_copies, id_copies = [], []
    for k in range(MP):
        target = (t, lax.rem(m + k, MP))
        x_copies.append(remote(x_ref, xo.at[m], xs.at[k], xr.at[k], target))
        id_copies.append(remote(id_ref, ido.at[m], ids.at[k], idr.at[k], target))
    own_x = pltpu.make_async_copy(x_ref, xo.at[m], loc.at[0])
    own_id = pltpu.make_async_copy(id_ref, ido.at[m], loc.at[1])

    @pl.when(upper)
    def _():
        x_copies[0].start()
        id_copies[0].start()

    @pl.when(jnp.logical_not(upper))
    def _():
        own_x.start()
        own_id.start()

    for k in range(1, MP):
        x_copies[k].start()
        id_copies[k].start()
    ring.relay_near()
    ring.relay_own()
    ring.relay_far()
    ring.finish()
    for k in range(1, MP):
        x_copies[k].wait()
        id_copies[k].wait()

    @pl.when(upper)
    def _():
        x_copies[0].wait()
        id_copies[0].wait()

    @pl.when(jnp.logical_not(upper))
    def _():
        own_x.wait()
        own_id.wait()


def lanes(rows):
    return lax.broadcasted_iota(jnp.int32, (rows, 128), 1)


def phase_rows(ref, at, rows):
    part = ref[:, at : at + rows]
    return jnp.concatenate([part] * 4, axis=0).T


def turn(values, cosine, sine):
    first = lax.rem(lanes(values.shape[0]), HEAD) < HEAD // 2
    turned = jnp.where(first, -pltpu.roll(values, 96, 1), pltpu.roll(values, 32, 1))
    return values * cosine + turned * sine


def turn_back(grads, cosine, sine):
    first = lax.rem(lanes(grads.shape[0]), HEAD) < HEAD // 2
    scaled = grads * sine
    turned = jnp.where(first, pltpu.roll(scaled, 96, 1), -pltpu.roll(scaled, 32, 1))
    return grads * cosine + turned


def keys_kernel(
    x_ref, gain_ref, w_ref, cos_ref, sin_ref, dy_ref,
    normed_ref, q_ref, kv_out, dy_out,
    kv_own, *sems,
):
    greet(ctx_neighbours() + mp_neighbours(), 7)
    ring = ctx_ring(kv_own, slots(kv_out), sems[:5])
    rows = mp_ring(dy_ref, slots(dy_out), sems[5:])
    rows.start()
    size = 256
    low = lanes(size) < HEAD
    for part in range(4):
        at = part * size
        block = slice(at, at + size)
        x = x_ref[block].astype(f32)
        inverse = lax.rsqrt(jnp.mean(x * x, axis=1, keepdims=True) + epsilon)
        normed = (x * inverse * gain_ref[...]).astype(bf16)
        normed_ref[block] = normed
        qkv = jnp.dot(normed, w_ref[...], preferred_element_type=f32)
        cosine, sine = phase_rows(cos_ref, at, size), phase_rows(sin_ref, at, size)
        queries = turn(qkv[:, :128], cosine, sine).astype(bf16).astype(f32) * score_scale
        half, place_in = part // 2, at % HALF
        q_ref[half, place_in : place_in + size] = jnp.where(low, queries, 0.0).astype(bf16)
        q_ref[half, HALF + place_in : HALF + place_in + size] = jnp.where(
            low, pltpu.roll(queries, HEAD, 1), 0.0
        ).astype(bf16)
        kv = qkv[:, 128:]
        kv_own[block] = jnp.where(low, turn(kv, cosine, sine), kv).astype(bf16)
    ring.start()
    rows.relay_near()
    rows.relay_own()
    ring.relay_near()
    ring.relay_own()
    rows.relay_far()
    ring.relay_far()
    rows.finish()
    ring.finish()


def keys_and_values(x_all, gain, qkv_w, cosine, sine, dy):
    return pl.pallas_call(
        keys_kernel,
        out_shape=[
            shape((BLOCK, 1024)),
            shape((2, 2 * HALF, 128)),
            shape((CTX, BLOCK, 128)),
            shape((MP, TOK, 1024)),
        ],
        in_specs=[VM] * 5 + [ANY],
        out_specs=[VM] * 2 + [ANY] * 2,
        scratch_shapes=[pltpu.VMEM((BLOCK, 128), bf16)] + CTX_SEMS + MP_SEMS,
        compiler_params=pltpu.CompilerParams(
            vmem_limit_bytes=VMEM_LIMIT, collective_id=2, has_side_effects=True
        ),
    )(x_all, gain, qkv_w, cosine, sine, dy)


def gather_kernel(a_ref, w_ref, out, w_out, *sems):
    greet(ctx_neighbours() + mp_neighbours(), 7)
    ring = mp_ring(a_ref, slots(out), sems[:3])
    weights = ctx_ring(w_ref, row_slots(w_out), sems[3:])
    ring.start()
    weights.start()
    ring.relay_near()
    ring.relay_own()
    weights.relay_near()
    weights.relay_own()
    ring.relay_far()
    weights.relay_far()
    ring.finish()
    weights.finish()


def scatter_kernel(
    a_ref, b_ref, dp_ref, act_ref, in_ref, dgu_ref,
    ao, bo, pair_ref, sum_ref,
    terms, theirs, got, own, s1, r1, s2, r2, s3, r3, s4, r4, loc,
):
    c, m = place()
    core = lax.rem(c, 2)
    x = c // 4
    sibling = (flip(c, 1), m)
    mates = [(c, lax.rem(m + k, MP)) for k in range(1, MP)]
    peers = [(lax.rem(c + 4 * k, CTX), m) for k in range(1, 4)]
    greet(mates + [sibling] + peers, MP + 3)
    own_a = pltpu.make_async_copy(a_ref.at[m], ao.at[m], loc.at[0])
    own_a.start()
    own_b = pltpu.make_async_copy(b_ref.at[m], bo.at[m], loc.at[1])
    own_b.start()
    copies = []
    for k in range(1, MP):
        to = lax.rem(m + k, MP)
        copies.append(remote(a_ref.at[to], ao.at[m], s1.at[k], r1.at[k], mates[k - 1]))
        copies.append(remote(b_ref.at[to], bo.at[m], s2.at[k], r2.at[k], mates[k - 1]))
    for copy in copies:
        copy.start()
    crossing = [
        remote(terms.at[1 - core, e], theirs.at[e], s3.at[e], r3.at[e], sibling)
        for e in range(4)
    ]
    first = [
        remote(own.at[lax.rem(x + k, 4)], got.at[k - 1], s4.at[k], r4.at[k], peers[k - 1])
        for k in range(1, 4)
    ]

    def join(e, put):
        crossing[e].wait()

        def add(chip, carry):
            put(
                chip,
                (terms[core, e, chip].astype(f32) + theirs[e, chip].astype(f32)).astype(bf16),
            )
            return carry

        lax.fori_loop(0, 8, add, 0)

    def put_own(chip, value):
        own[chip // 2, lax.rem(chip, 2)] = value

    def put_pair(e):
        def put(chip, value):
            pair_ref[e, chip // 2, lax.rem(chip, 2)] = value

        return put

    for e in range(4):
        gate_up_grads = dgu_ref[e]
        active = act_ref[e]

        def chunk(at, carry):
            columns = pl.ds(pl.multiple_of(at * 256, 256), 256)
            in_part = contract(in_ref[e, :, columns], gate_up_grads, 0, 0).astype(bf16)
            out_part = contract(dp_ref[e, :, columns], active, 0, 0).astype(bf16)
            for j in range(4):
                rows = slice(64 * j, 64 * j + 64)
                terms[j % 2, e, 2 * at + j // 2, :, 0:1024] = in_part[rows]
                terms[j % 2, e, 2 * at + j // 2, :, 1024:1536] = out_part[rows]
            return carry

        lax.fori_loop(0, 4, chunk, 0)
        crossing[e].start()
        if e == 1:
            join(0, put_own)
            for copy in first:
                copy.start()
    for e in range(1, 4):
        join(e, put_pair(e - 1))
    for copy in first:
        copy.wait()
    for j in range(2):
        term = own[x, j].astype(f32)
        for k in range(3):
            term = term + got[k, j].astype(f32)
        sum_ref[j] = term.astype(bf16)
    for copy in copies:
        copy.wait()
    own_a.wait()
    own_b.wait()


def scatter_rows(routed_terms, share, d_produced, active, incoming, d_gate_up):
    return pl.pallas_call(
        scatter_kernel,
        out_shape=[
            shape((MP, TOK, 1024)),
            shape((MP, 8, TOK), f32),
            shape((3, 4, 2, 64, 1536)),
            shape((2, 64, 1536)),
        ],
        in_specs=[ANY, ANY, VM, VM, VM, VM],
        out_specs=[ANY, ANY, VM, VM],
        scratch_shapes=[
            pltpu.VMEM((2, 4, 8, 64, 1536), bf16),
            pltpu.VMEM((4, 8, 64, 1536), bf16),
            pltpu.VMEM((3, 2, 64, 1536), bf16),
            pltpu.VMEM((4, 2, 64, 1536), bf16),
        ]
        + [pltpu.SemaphoreType.DMA((MP,))] * 4
        + [pltpu.SemaphoreType.DMA((4,))] * 4
        + [pltpu.SemaphoreType.DMA((2,))],
        compiler_params=pltpu.CompilerParams(
            vmem_limit_bytes=VMEM_LIMIT, collective_id=4, has_side_effects=True
        ),
    )(routed_terms, share, d_produced, active, incoming, d_gate_up)


def outputs_kernel(a_ref, ao, s1, r1, loc):
    c, m = place()
    mates = [(c, lax.rem(m + k, MP)) for k in range(1, MP)]
    greet(mates, MP - 1)
    own_a = pltpu.make_async_copy(a_ref.at[m], ao.at[m], loc.at[0])
    own_a.start()
    copies = []
    for k in range(1, MP):
        to = lax.rem(m + k, MP)
        copies.append(remote(a_ref.at[to], ao.at[m], s1.at[k], r1.at[k], mates[k - 1]))
    for copy in copies:
        copy.start()
    for copy in copies:
        copy.wait()
    own_a.wait()


def keys_grad_kernel(
    a_ref, out, theirs, pair_a, pair_b, got_a, got_b, sum_a, sum_b, last_a, last_b,
    s0, r0, s1, r1, s2, r2,
):
    c, m = place()
    core = lax.rem(c, 2)
    x, y = c // 4, lax.rem(c // 2, 2)
    sibling = (flip(c, 1), m)
    across = (flip(c, 2), m)
    peers = [(lax.rem(c + 4 * k, CTX), m) for k in range(1, 4)]
    greet(peers + [across, sibling], 5)
    low, high = pl.ds(0, HALF), pl.ds(HALF, HALF)
    crossing = [
        remote(
            a_ref.at[:, :, 1 - core, rows], theirs.at[:, :, rows], s0.at[at], r0.at[at], sibling
        )
        for at, rows in enumerate((high, low))
    ]
    for copy in crossing:
        copy.start()

    def add(a, b):
        return a.astype(f32) + b.astype(f32)

    crossing[0].wait()
    for i in range(4):
        for j in range(2):
            pair_b[i, j] = add(a_ref[i, j, core, high], theirs[i, j, high]).astype(bf16)
    first = [remote(pair_b.at[:, 1 - y], got_b, s1.at[0], r1.at[0], across)]
    first[0].start()
    crossing[1].wait()
    for i in range(4):
        for j in range(2):
            pair_a[i, j] = add(a_ref[i, j, core, low], theirs[i, j, low]).astype(bf16)
    for k in range(1, 4):
        copy = remote(
            pair_a.at[lax.rem(x + k, 4)], got_a.at[k - 1], s1.at[k], r1.at[k], peers[k - 1]
        )
        copy.start()
        first.append(copy)
    first[0].wait()
    for i in range(4):
        sum_b[i] = add(pair_b[i, y], got_b[i]).astype(bf16)
    second = []
    for k in range(1, 4):
        copy = remote(
            sum_b.at[lax.rem(x + k, 4)], last_b.at[k - 1], s2.at[k], r2.at[k], peers[k - 1]
        )
        copy.start()
        second.append(copy)
    for copy in first[1:]:
        copy.wait()
    for j in range(2):
        sum_a[j] = (add(pair_a[x, j], got_a[0, j]) + add(got_a[1, j], got_a[2, j])).astype(bf16)
    copy = remote(sum_a.at[1 - y], last_a, s2.at[0], r2.at[0], across)
    copy.start()
    second.append(copy)
    for copy in second:
        copy.wait()
    out[low] = add(sum_a[y], last_a[...])
    out[high] = add(sum_b[x], last_b[0]) + add(last_b[1], last_b[2])


def keys_grad(terms):
    piece = (HALF, 128)
    return pl.pallas_call(
        keys_grad_kernel,
        out_shape=shape((BLOCK, 128), f32),
        in_specs=[VM],
        out_specs=VM,
        scratch_shapes=[
            pltpu.VMEM((4, 2, BLOCK, 128), bf16),
            pltpu.VMEM((4, 2) + piece, bf16),
            pltpu.VMEM((4, 2) + piece, bf16),
            pltpu.VMEM((3, 2) + piece, bf16),
            pltpu.VMEM((4,) + piece, bf16),
            pltpu.VMEM((2,) + piece, bf16),
            pltpu.VMEM((4,) + piece, bf16),
            pltpu.VMEM(piece, bf16),
            pltpu.VMEM((3,) + piece, bf16),
        ]
        + [pltpu.SemaphoreType.DMA((2,))] * 2
        + [pltpu.SemaphoreType.DMA((4,))] * 4,
        compiler_params=pltpu.CompilerParams(
            vmem_limit_bytes=VMEM_LIMIT, collective_id=6, has_side_effects=True
        ),
    )(terms)


def finish_kernel(
    dq_ref, dkv_ref, cos_ref, sin_ref, normed_ref, br_ref, rows_ref, hid_ref, y_ref,
    ao, go, hid_out, y_out,
    d_qkv, terms, s1, r1, s2, r2, s3, r3, loc,
):
    c, m = place()
    upper = m >= MP // 2
    t = jnp.where(upper, CTX - 1 - c, c)
    barrier = pltpu.get_barrier_semaphore()
    for k in range(1, MP):
        pl.semaphore_signal(
            barrier, inc=1, device_id=(t, lax.rem(m + k, MP)), device_id_type=MESH
        )
    for k in range(1, CTX):
        pl.semaphore_signal(
            barrier, inc=1, device_id=(lax.rem(c + k, CTX), m), device_id_type=MESH
        )

    @pl.when(upper)
    def _():
        pl.semaphore_signal(barrier, inc=1, device_id=(t, m), device_id_type=MESH)
        pl.semaphore_wait(barrier, MP + CTX - 1)

    @pl.when(jnp.logical_not(upper))
    def _():
        pl.semaphore_wait(barrier, MP + CTX - 2)

    home = [
        remote(hid_ref, hid_out, s3.at[0], r3.at[0], (t, m)),
        remote(y_ref, y_out, s3.at[1], r3.at[1], (t, m)),
    ]
    stay = [
        pltpu.make_async_copy(hid_ref, hid_out, loc.at[2]),
        pltpu.make_async_copy(y_ref, y_out, loc.at[3]),
    ]

    @pl.when(upper)
    def _():
        for copy in home:
            copy.start()

    @pl.when(jnp.logical_not(upper))
    def _():
        for copy in stay:
            copy.start()

    low = lanes(TOK) < HEAD
    for i in range(MP):
        at = i * TOK
        part, inside = at // HALF, at % HALF
        columns = dq_ref[part]
        heads = jnp.concatenate(
            [
                columns[:HEAD, inside : inside + TOK],
                columns[:HEAD, HALF + inside : HALF + inside + TOK],
            ],
            axis=0,
        ).T
        cosine, sine = phase_rows(cos_ref, at, TOK), phase_rows(sin_ref, at, TOK)
        d_qkv[i, :, 0:128] = turn_back(heads * score_scale, cosine, sine).astype(bf16)
        dkv = dkv_ref[at : at + TOK]
        d_qkv[i, :, 128:256] = jnp.where(low, turn_back(dkv, cosine, sine), dkv).astype(bf16)

    own_a = pltpu.make_async_copy(d_qkv.at[m], ao.at[m], loc.at[1])
    a_copies, g_copies = [], []
    for k in range(MP):
        to = lax.rem(m + k, MP)
        target = (jnp.where(to >= MP // 2, CTX - 1 - c, c), to)
        a_copies.append(remote(d_qkv.at[to], ao.at[m], s1.at[k], r1.at[k], target))

    @pl.when(upper)
    def _():
        a_copies[0].start()

    @pl.when(jnp.logical_not(upper))
    def _():
        own_a.start()

    for k in range(1, MP):
        a_copies[k].start()
    grads = d_qkv[...].reshape(BLOCK, 256)
    columns = jnp.concatenate(
        [
            contract(grads, normed_ref[...], 0, 0),
            contract(rows_ref[...], br_ref[...], 0, 0),
        ],
        axis=0,
    )
    terms[...] = columns.T.astype(bf16).reshape(terms.shape)
    own_g = pltpu.make_async_copy(terms.at[c], go.at[c], loc.at[0])
    own_g.start()
    for k in range(1, CTX):
        to = lax.rem(c + k, CTX)
        copy = remote(terms.at[to], go.at[c], s2.at[k], r2.at[k], (to, m))
        copy.start()
        g_copies.append(copy)
    for k in range(1, MP):
        a_copies[k].wait()
    for copy in g_copies:
        copy.wait()
    own_g.wait()

    @pl.when(upper)
    def _():
        a_copies[0].wait()
        for copy in home:
            copy.wait()

    @pl.when(jnp.logical_not(upper))
    def _():
        own_a.wait()
        for copy in stay:
            copy.wait()


def finish(dq, dkv, cosine, sine, normed, branch_rows, out_rows, hidden_grad, outputs):
    return pl.pallas_call(
        finish_kernel,
        out_shape=[
            shape((MP, TOK, 256)),
            shape((CTX, 64, 384)),
            shape((TOK, 1024)),
            shape((TOK, 1024)),
        ],
        in_specs=[VM] * 7 + [ANY] * 2,
        out_specs=[ANY] * 4,
        scratch_shapes=[
            pltpu.VMEM((MP, TOK, 256), bf16),
            pltpu.VMEM((CTX, 64, 384), bf16),
        ]
        + [pltpu.SemaphoreType.DMA((n,)) for n in (MP, MP, CTX, CTX, 2, 2, 4)],
        compiler_params=pltpu.CompilerParams(
            vmem_limit_bytes=VMEM_LIMIT, collective_id=8, has_side_effects=True
        ),
    )(dq, dkv, cosine, sine, normed, branch_rows, out_rows, hidden_grad, outputs)


def sums_kernel(a_ref, out, got, part, got2, s1, r1, s2, r2):
    c, m = place()
    peers = [(lax.rem(c + k, CTX), m) for k in range(1, CTX)]
    mates = [(c, lax.rem(m + k, MP)) for k in range(1, MP)]
    greet(peers + mates, CTX - 1 + MP - 1)
    copies = []
    for k in range(1, CTX):
        to = lax.rem(c + k, CTX)
        copy = remote(a_ref.at[to], got.at[k], s1.at[k], r1.at[k], peers[k - 1])
        copy.start()
        copies.append(copy)
    total = a_ref[c]
    for copy in copies:
        copy.wait()
    for k in range(1, CTX):
        total = total + got[k]
    part[...] = total
    copies = []
    for k in range(1, MP):
        to = lax.rem(m + k, MP)
        copy = remote(part.at[to], got2.at[k], s2.at[k], r2.at[k], mates[k - 1])
        copy.start()
        copies.append(copy)
    last = part[m]
    for copy in copies:
        copy.wait()
    for k in range(1, MP):
        last = last + got2[k]
    out[...] = last


def small_sums(terms):
    dims = terms.shape[2:]
    return pl.pallas_call(
        sums_kernel,
        out_shape=shape(dims, f32),
        in_specs=[VM],
        out_specs=VM,
        scratch_shapes=[
            pltpu.VMEM((CTX, MP) + dims, f32),
            pltpu.VMEM((MP,) + dims, f32),
            pltpu.VMEM((MP,) + dims, f32),
            pltpu.SemaphoreType.DMA((CTX,)),
            pltpu.SemaphoreType.DMA((CTX,)),
            pltpu.SemaphoreType.DMA((MP,)),
            pltpu.SemaphoreType.DMA((MP,)),
        ],
        compiler_params=pltpu.CompilerParams(collective_id=9, has_side_effects=True),
    )(terms)


def unit(index, first_half):
    second = index > first_half
    part = second.astype(jnp.int32)
    key_half = jnp.where(second, index - first_half - 1, index)
    odd = lax.rem(key_half, 2) == 1
    slot = jnp.where(odd, 2 * CTX - key_half, key_half)
    diagonal = jnp.logical_or(index == first_half, index == 2 * CTX)
    return part, slot, diagonal


def visible_mask(rows):
    key_at = lax.broadcasted_iota(jnp.int32, (HALF, rows), 0)
    query_at = lax.rem(lax.broadcasted_iota(jnp.int32, (HALF, rows), 1), HALF)
    return key_at <= query_at


def forward_kernel(
    q_ref, kv_ref, in_ref, qw_ref, rows_ref,
    out_ref, rows_out, lse_ref, in_all, qw_all, rows_all,
    best, total, summed, *sems,
):
    first_half = 2 * lax.axis_index("ctx")
    greet(ctx_neighbours() + mp_neighbours(), 7)
    weights_rings = [ctx_ring(in_ref, row_slots(in_all), sems[0:5])]
    rows_rings = [
        shared_ring(rows_ref, rows_all, sems[5:10]),
        shared_ring(qw_ref, qw_all, sems[10:15]),
    ]
    for ring in weights_rings + rows_rings:
        ring.start()
    best[...] = jnp.full(best.shape, -1e30, f32)
    total[...] = jnp.zeros(total.shape, f32)
    summed[...] = jnp.zeros(summed.shape, f32)

    def work(part, slot, masked):
        kv = kv_ref[slot]
        scores = contract(kv, q_ref[part], 1, 1)
        if masked:
            scores = jnp.where(visible_mask(scores.shape[1]), scores, -jnp.inf)
        old = best[part]
        new = jnp.maximum(old, jnp.max(scores, axis=0, keepdims=True))
        weights = jnp.exp2(scores * log2_e - new * log2_e)
        fading = jnp.exp2((old - new) * log2_e)
        total[part] = total[part] * fading + jnp.sum(weights, axis=0, keepdims=True)
        summed[part] = summed[part] * fading + contract(kv, weights.astype(bf16), 0, 0)
        best[part] = new

    def step(index, carry):
        part, slot, diagonal = unit(index, first_half)

        @pl.when(index == 7)
        def _():
            for ring in rows_rings:
                ring.relay_near()
                ring.relay_own()

        @pl.when(index == 9)
        def _():
            for ring in weights_rings:
                ring.relay_own()
                ring.relay_near()

        @pl.when(index == 14)
        def _():
            for ring in rows_rings:
                ring.relay_far()

        @pl.when(index == 21)
        def _():
            for ring in weights_rings:
                ring.relay_far()

        @pl.when(diagonal)
        def _():
            work(part, slot, True)

        @pl.when(jnp.logical_not(diagonal))
        def _():
            work(part, slot, False)

        return carry

    lax.fori_loop(0, 2 * CTX + 1, step, 0)
    for part in range(2):
        columns = summed[part][HEAD:, :] / total[part]
        heads = jnp.concatenate([columns[:, :HALF], columns[:, HALF:]], axis=0).T
        out_ref[part * HALF : part * HALF + HALF] = heads
        rows_out[part * HALF : part * HALF + HALF] = heads.astype(bf16)
        lse_ref[part] = best[part] + jnp.log(total[part])
    for ring in weights_rings + rows_rings:
        ring.finish()


def attention(q_rows, kv_all, w_in, qkv_w, out_rows_w):
    rows = q_rows.shape[1]
    return pl.pallas_call(
        forward_kernel,
        out_shape=[
            shape((BLOCK, 128), f32),
            shape((BLOCK, 128)),
            shape((2, 1, rows), f32),
            shape((4, 1024, 1024)),
            shape((MP,) + qkv_w.shape),
            shape((MP, TOK, 1024)),
        ],
        in_specs=[VM, VM, ANY, ANY, ANY],
        out_specs=[VM, VM, VM, ANY, ANY, ANY],
        scratch_shapes=[
            pltpu.VMEM((2, 1, rows), f32),
            pltpu.VMEM((2, 1, rows), f32),
            pltpu.VMEM((2, 2 * HEAD, rows), f32),
        ]
        + CTX_SEMS * 3,
        compiler_params=pltpu.CompilerParams(
            vmem_limit_bytes=VMEM_LIMIT, collective_id=10, has_side_effects=True
        ),
        cost_estimate=pl.CostEstimate(
            flops=33 * 4 * HALF * rows * 256, bytes_accessed=1 << 23, transcendentals=33 * HALF * rows
        ),
    )(q_rows, kv_all, w_in, qkv_w, out_rows_w)


def backward_kernel(
    q_ref, og_ref, att_ref, lse_ref, kv_ref, sum_0, pair_ref, br_ref, mixed_ref,
    dkv_ref, dq_ref, in_grad, out_grad, br_all, mixed_out,
    total, do_ref, delta_ref, own_a, own_b, got_a, got_b, sum_a, sum_b, last_0, last_a, last_b,
    *sems,
):
    c, m = place()
    first_half = 2 * c
    x, y = c // 4, lax.rem(c // 2, 2)
    peers = [(lax.rem(c + 4 * k, CTX), m) for k in range(1, 4)]
    across = (flip(c, 2), m)
    mates = [(c, lax.rem(m + k, MP)) for k in range(1, MP)]
    greet(peers + [across] + mates, 4 + MP - 1)
    sa, ra, sb, rb, sm, rm, loc = sems[:7]
    ring = mp_ring(br_ref, slots(br_all), sems[7:10])

    def first_copies():
        copies = [
            remote(
                pair_ref.at[pl.ds(0, 2), lax.rem(x + k, 4)],
                got_a.at[k - 1], sa.at[k], ra.at[k], peers[k - 1],
            )
            for k in range(1, 4)
        ]
        copies.append(remote(pair_ref.at[2, :, 1 - y], got_b, sa.at[0], ra.at[0], across))
        return copies

    def own_copies():
        return [
            pltpu.make_async_copy(pair_ref.at[pl.ds(0, 2), x], own_a, loc.at[1]),
            pltpu.make_async_copy(pair_ref.at[2, :, y], own_b, loc.at[2]),
        ]

    def sum_0_copy():
        return remote(sum_0.at[1 - y], last_0, sb.at[0], rb.at[0], across)

    def second_copies():
        copies = [
            remote(
                sum_b.at[lax.rem(x + k, 4)], last_b.at[k - 1], sb.at[k], rb.at[k], peers[k - 1]
            )
            for k in range(1, 4)
        ]
        copies.append(remote(sum_a.at[:, 1 - y], last_a, sb.at[4], rb.at[4], across))
        return copies

    def middle():
        for copy in first_copies() + own_copies():
            copy.wait()
        for e in range(2):
            for j in range(2):
                term = own_a[e, j].astype(f32)
                for k in range(3):
                    term = term + got_a[k, e, j].astype(f32)
                sum_a[e, j] = term.astype(bf16)
        for j in range(4):
            sum_b[j] = (own_b[j].astype(f32) + got_b[j].astype(f32)).astype(bf16)
        for copy in second_copies():
            copy.start()

    def mixed_copies():
        copies = []
        for k in range(1, MP):
            to = lax.rem(m + k, MP)
            copies.append(
                remote(mixed_ref.at[to], mixed_out.at[m], sm.at[k], rm.at[k], mates[k - 1])
            )
        return copies

    def own_mixed():
        return pltpu.make_async_copy(mixed_ref.at[m], mixed_out.at[m], loc.at[0])

    for copy in first_copies() + own_copies() + [sum_0_copy()]:
        copy.start()
    ring.start()
    low = lanes(HALF) < HEAD
    for part in range(2):
        rows = slice(part * HALF, part * HALF + HALF)
        grads = og_ref[rows].astype(f32)
        product = (grads * att_ref[rows]).T
        delta_ref[part, :, 0:HALF] = jnp.sum(product[:HEAD], axis=0, keepdims=True)
        delta_ref[part, :, HALF:] = jnp.sum(product[HEAD:], axis=0, keepdims=True)
        do_ref[part, 0:HALF] = jnp.where(low, 0.0, pltpu.roll(grads, HEAD, 1)).astype(bf16)
        do_ref[part, HALF:] = jnp.where(low, 0.0, grads).astype(bf16)
    dq_ref[...] = jnp.zeros(dq_ref.shape, f32)

    def clear(index, carry):
        total[index] = jnp.zeros(total.shape[1:], f32)
        return carry

    lax.fori_loop(0, 2 * CTX, clear, 0)

    def work(part, slot, masked):
        kv = kv_ref[slot]
        queries = q_ref[part]
        grads = do_ref[part]
        scores = contract(kv, queries, 1, 1)
        probs = jnp.exp2((scores - lse_ref[part]) * log2_e)
        if masked:
            probs = jnp.where(visible_mask(scores.shape[1]), probs, 0.0)
        prob_grad = contract(kv, grads, 1, 1)
        score_grad = (probs * (prob_grad - delta_ref[part])).astype(bf16)
        total[slot] += contract(probs.astype(bf16), grads, 1, 0) + contract(
            score_grad, queries, 1, 0
        )
        dq_ref[part] += contract(kv, score_grad, 0, 0)

    def step(index, carry):
        part, slot, diagonal = unit(index, first_half)

        @pl.when(index == 5)
        def _():
            ring.relay_near()
            ring.relay_own()

        @pl.when(index == 10)
        def _():
            ring.relay_far()
            own_mixed().start()
            for copy in mixed_copies():
                copy.start()

        @pl.when(index == 22)
        def _():
            middle()

        @pl.when(diagonal)
        def _():
            work(part, slot, True)

        @pl.when(jnp.logical_not(diagonal))
        def _():
            work(part, slot, False)

        return carry

    lax.fori_loop(0, 2 * CTX + 1, step, 0)

    def write(index, carry):
        dkv_ref[index] = total[index].astype(bf16)
        return carry

    lax.fori_loop(0, 2 * CTX, write, 0)
    ring.finish()
    sum_0_copy().wait()
    for copy in second_copies():
        copy.wait()

    def put(at, term):
        in_grad[at] = term[:, :1024]
        out_grad[at] = term[:, 1024:].T

    put(0, sum_0[y].astype(f32) + last_0[...].astype(f32))
    for e in range(2):
        put(1 + e, sum_a[e, y].astype(f32) + last_a[e].astype(f32))
    term = sum_b[x].astype(f32)
    for k in range(3):
        term = term + last_b[k].astype(f32)
    put(3, term)
    for copy in mixed_copies():
        copy.wait()
    own_mixed().wait()


def attention_back(
    q_rows, out_grad, attended, lse, kv_all, sum_first, pair, branch_grad, mixed
):
    rows = q_rows.shape[1]
    wide = pair.shape[-1]
    return pl.pallas_call(
        backward_kernel,
        out_shape=[
            shape(kv_all.shape, bf16),
            shape((2, 2 * HEAD, rows), f32),
            shape((4, 64, 1024), f32),
            shape((4, 512, 64), f32),
            shape((MP, TOK, 1024)),
            shape((MP, TOK, 1024)),
        ],
        in_specs=[VM] * 6 + [ANY] * 3,
        out_specs=[VM] * 4 + [ANY] * 2,
        scratch_shapes=[
            pltpu.VMEM(kv_all.shape, f32),
            pltpu.VMEM(q_rows.shape, bf16),
            pltpu.VMEM((2, 1, rows), f32),
            pltpu.VMEM((2, 2, 64, wide), bf16),
            pltpu.VMEM((4, 64, wide), bf16),
            pltpu.VMEM((3, 2, 2, 64, wide), bf16),
            pltpu.VMEM((4, 64, wide), bf16),
            pltpu.VMEM((2, 2, 64, wide), bf16),
            pltpu.VMEM((4, 64, wide), bf16),
            pltpu.VMEM((64, wide), bf16),
            pltpu.VMEM((2, 64, wide), bf16),
            pltpu.VMEM((3, 64, wide), bf16),
        ]
        + [pltpu.SemaphoreType.DMA((4,))] * 2
        + [pltpu.SemaphoreType.DMA((5,))] * 2
        + [pltpu.SemaphoreType.DMA((MP,))] * 2
        + [pltpu.SemaphoreType.DMA((3,))]
        + MP_SEMS,
        compiler_params=pltpu.CompilerParams(
            vmem_limit_bytes=VMEM_LIMIT, collective_id=11, has_side_effects=True
        ),
        cost_estimate=pl.CostEstimate(
            flops=33 * 10 * HALF * rows * 256, bytes_accessed=1 << 24, transcendentals=33 * HALF * rows
        ),
    )(q_rows, out_grad, attended, lse, kv_all, sum_first, pair, branch_grad, mixed)


def phases(positions, head_width):
    steps_up = jnp.arange(head_width // 2).astype(f32)
    frequency = rope_base ** (-2.0 * steps_up / head_width)
    angles = frequency[:, None] * positions.astype(f32)[None, :]
    return (jnp.cos(angles), jnp.sin(angles))


def normalize(values):
    inverse = lax.rsqrt(jnp.mean(values * values, axis=-1, keepdims=True) + epsilon)
    return (values * inverse, inverse)


def norm_back(grads, scaled, inverse, gain):
    inner = grads * gain
    return (
        inverse * (inner - scaled * jnp.mean(inner * scaled, axis=-1, keepdims=True)),
        jnp.sum(grads * scaled, axis=0),
    )


def swap_home(array):
    pairs = []
    for c in range(CTX):
        for m in range(MP):
            t = CTX - 1 - c if m >= MP // 2 else c
            pairs.append((c * MP + m, t * MP + m))
    return lax.ppermute(array, ("ctx", "mp"), pairs)


def body(
    layer_input,
    positions,
    expert_ids,
    attn_gain,
    w_query,
    w_key,
    w_value,
    w_attn_out,
    ffn_gain,
    router,
    w_in,
    w_out,
    cotangent,
):
    c, m = place()
    dy_swapped = swap_home(cotangent)
    own_positions = lax.dynamic_slice_in_dim(positions, m * TOK, TOK, 0)
    id_pack = jnp.concatenate(
        [expert_ids.T, own_positions[None, :], jnp.zeros((7, TOK), jnp.int32)], axis=0
    )
    w_pack = jnp.concatenate(
        [
            w_query,
            w_key,
            w_value,
            router,
            attn_gain[:, None],
            ffn_gain[:, None],
            jnp.zeros((64, 94), bf16),
            w_attn_out.T,
        ],
        axis=1,
    )
    x_all, id_all, w_all = comm_call(
        start_kernel,
        1,
        [layer_input, id_pack, w_pack],
        [
            shape((MP, TOK, 1024)),
            shape((MP, 16, TOK), jnp.int32),
            shape((CTX, 64, 512)),
        ],
        [MP, MP, MP, MP, 2] + CTX_SEMS,
        4 << 20,
    )
    inputs = x_all.reshape(BLOCK, 1024).astype(f32)
    ids = id_all[:, :8, :].transpose(1, 0, 2).reshape(8, BLOCK)
    places = id_all[:, 8, :].reshape(BLOCK)
    w_all = w_all.reshape(1024, 512)
    qkv_w = w_all[:, :256]
    router_w = w_all[:, 256:288]
    gain_one = w_all[:, 288].astype(f32)
    gain_two = w_all[:, 289].astype(f32)
    out_w = w_all[:, 384:].T

    cosine, sine = lax.optimization_barrier(phases(places, HEAD))
    normed, q_rows, kv_all, dy_all = keys_and_values(
        x_all.reshape(BLOCK, 1024), gain_one[None, :], qkv_w, cosine, sine, dy_swapped
    )
    kv_all = kv_all.reshape(2 * CTX, HALF, 128)
    attended, out_rows, lse, in_w, qkv_w_all, out_w_all = attention(
        q_rows, kv_all, w_in, qkv_w, out_w
    )
    dy_all = dy_all.reshape(BLOCK, 1024)
    rows_all, out_w_t = comm_call(
        gather_kernel,
        3,
        [out_rows, w_out.transpose(0, 2, 1)],
        [shape((MP, BLOCK, 128)), shape((4, 1024, 512))],
        MP_SEMS + CTX_SEMS,
        8 << 20,
    )
    branch = lax.dot_general(
        rows_all, out_w_all, (((0, 2), (0, 1)), ((), ())), preferred_element_type=f32
    )
    hidden = inputs + branch_scale * branch
    scaled_two, inverse_two = normalize(hidden)
    routed = (scaled_two * gain_two).astype(bf16)

    logits = contract(router_w, routed, 0, 1)
    experts = lax.broadcasted_iota(jnp.int32, (32, BLOCK), 0)
    member = jnp.any(ids[:, None, :] == experts[None], axis=0)
    chosen = jnp.where(member, logits, -jnp.inf)
    top_logit = jnp.max(chosen, axis=0, keepdims=True)
    powers = jnp.exp(chosen - top_logit)
    gates = powers / jnp.sum(powers, axis=0, keepdims=True)

    here = 4 * m + lax.broadcasted_iota(jnp.int32, (4, BLOCK), 0)
    selected = jnp.any(ids[:, None, :] == here[None], axis=0)
    earlier = (
        lax.broadcasted_iota(jnp.int32, (BLOCK, BLOCK), 0)
        <= lax.broadcasted_iota(jnp.int32, (BLOCK, BLOCK), 1)
    ).astype(bf16)
    counts = jnp.dot(selected.astype(bf16), earlier, preferred_element_type=f32)
    rank = jnp.where(selected, counts.astype(jnp.int32) - 1, -1)
    capacity = 288
    place_bool = rank[:, None, :] == lax.broadcasted_iota(jnp.int32, (4, capacity, BLOCK), 1)
    placing = place_bool.astype(bf16).reshape(4 * capacity, BLOCK)
    gates_here = lax.dynamic_slice_in_dim(gates, 4 * m, 4, 0)
    slot_gate = jnp.sum(jnp.where(place_bool, gates_here[:, None, :], 0.0), axis=2)

    incoming = jnp.dot(placing, routed, preferred_element_type=f32).astype(bf16)
    incoming = incoming.reshape(4, capacity, 1024)
    dy_rows = jnp.dot(placing, dy_all, preferred_element_type=f32).reshape(4, capacity, 1024)
    gate_up = jnp.einsum("esd,edf->esf", incoming, in_w, preferred_element_type=f32)
    gate_part, up_part = gate_up[..., :512], gate_up[..., 512:]
    squashed = jax.nn.sigmoid(gate_part)
    silu_part = gate_part * squashed
    active = (silu_part * up_part).astype(bf16)
    produced = jnp.einsum(
        "esf,edf->esd", active, out_w_t, preferred_element_type=f32
    ).astype(bf16)
    produced_f = produced.astype(f32)
    d_produced = (branch_scale * slot_gate[..., None] * dy_rows).astype(bf16)
    slot_share = branch_scale * jnp.sum(dy_rows * produced_f, axis=2)
    weighted = (slot_gate[..., None] * produced_f).astype(bf16).reshape(4 * capacity, 1024)
    mixed = branch_scale * contract(placing, weighted, 0, 0)
    mixed = mixed.astype(bf16).reshape(MP, TOK, 1024)

    d_active = jnp.einsum("esd,edf->esf", d_produced, out_w_t, preferred_element_type=f32)
    slope = squashed * (1.0 + gate_part * (1.0 - squashed))
    d_gate_up = jnp.concatenate(
        [d_active * up_part * slope, d_active * silu_part], axis=-1
    ).astype(bf16)
    row_grads = jnp.einsum(
        "esf,edf->esd", d_gate_up, in_w, preferred_element_type=f32
    ).astype(bf16)
    row_grads = lax.optimization_barrier(row_grads)
    routed_terms = contract(placing, row_grads.reshape(4 * capacity, 1024), 0, 0)
    routed_terms = routed_terms.astype(bf16).reshape(MP, TOK, 1024)
    share = jnp.sum(jnp.where(place_bool, slot_share[:, :, None], 0.0), axis=1)
    share = jnp.pad(share.reshape(4, MP, TOK).transpose(1, 0, 2), ((0, 0), (0, 4), (0, 0)))
    routed_got, share_got, pair, sum_first = scatter_rows(
        routed_terms, share, d_produced, active, incoming, d_gate_up
    )

    def own_rows(array):
        return lax.dynamic_slice_in_dim(array, m * TOK, TOK, 0)

    hidden_own = own_rows(hidden)
    scaled_own, inverse_own = normalize(hidden_own)
    routed_own = (scaled_own * gain_two).astype(bf16).astype(f32)
    dy_own = own_rows(dy_all).astype(f32)
    gates_own = lax.dynamic_slice_in_dim(gates, m * TOK, TOK, 1)
    share_own = share_got[:, :4, :].reshape(32, TOK)
    logit_grad = gates_own * (
        share_own - jnp.sum(gates_own * share_own, axis=0, keepdims=True)
    )
    routed_grad = jnp.sum(routed_got.astype(f32), axis=0) + lax.dot_general(
        logit_grad,
        router_w.astype(f32),
        (((0,), (1,)), ((), ())),
        precision=highest,
        preferred_element_type=f32,
    )
    router_grad = lax.dot_general(
        routed_own,
        logit_grad,
        (((0,), (1,)), ((), ())),
        precision=highest,
        preferred_element_type=f32,
    )
    hidden_grad, gain_two_grad = norm_back(routed_grad, scaled_own, inverse_own, gain_two)
    hidden_grad = hidden_grad + dy_own
    branch_grad = (branch_scale * hidden_grad).astype(bf16)

    out_grad_terms = jnp.einsum(
        "td,hfd->htf", branch_grad, out_w_all, preferred_element_type=f32
    ).astype(bf16)
    (out_grad,) = comm_call(
        outputs_kernel, 5, [out_grad_terms], [shape((MP, TOK, 128))], [MP, MP, 1], 1 << 20
    )
    out_grad = out_grad.reshape(BLOCK, 128)

    dkv_terms, dq_cols, expert_in, expert_out, branch_rows, mixed_got = attention_back(
        q_rows, out_grad, attended, lse, kv_all, sum_first, pair, branch_grad, mixed
    )
    outputs = (hidden_own + jnp.sum(mixed_got.astype(f32), axis=0)).astype(bf16)
    dkv = keys_grad(dkv_terms.reshape(4, 2, 2, BLOCK, 128))
    qkv_got, w_got, hidden_grad_home, outputs = finish(
        dq_cols,
        dkv,
        cosine,
        sine,
        normed,
        branch_rows.reshape(BLOCK, 1024),
        out_rows,
        hidden_grad.astype(bf16),
        outputs,
    )
    w_grad = jnp.sum(w_got.astype(f32), axis=0)
    normed_grad = jnp.einsum(
        "htf,hdf->td", qkv_got, qkv_w_all, preferred_element_type=f32
    )
    scaled_one, inverse_one = normalize(layer_input.astype(f32))
    input_grad, gain_one_grad = norm_back(normed_grad, scaled_one, inverse_one, gain_one)
    input_grad = (input_grad + hidden_grad_home.astype(f32)).astype(bf16)

    small = jnp.concatenate(
        [
            router_grad,
            gain_one_grad[:, None],
            gain_two_grad[:, None],
            jnp.zeros((1024, 94), f32),
        ],
        axis=1,
    )
    sums = small_sums(small.reshape(CTX, MP, 8, 128))
    return (
        outputs,
        input_grad,
        sums[:, 32],
        w_grad[:, :128],
        w_grad[:, 128:192],
        w_grad[:, 192:256],
        w_grad[:, 256:].T,
        sums[:, 33],
        sums[:, :32],
        expert_in,
        expert_out,
    )


def solution(mesh):
    placed = (
        P(("ctx", "mp"), None),
        P("ctx"),
        P(("ctx", "mp"), None),
        P("ctx"),
        P("ctx", "mp"),
        P("ctx", "mp"),
        P("ctx", "mp"),
        P("mp", "ctx"),
        P("ctx"),
        P("ctx", None),
        P("mp", "ctx", None),
        P("mp", None, "ctx"),
        P(("ctx", "mp"), None),
    )
    return jax.shard_map(
        body,
        mesh=mesh,
        in_specs=placed,
        out_specs=(
            P(("ctx", "mp"), None),
            P(("ctx", "mp"), None),
            P(("ctx", "mp")),
            P("ctx", "mp"),
            P("ctx", "mp"),
            P("ctx", "mp"),
            P("mp", "ctx"),
            P(("ctx", "mp")),
            P(("ctx", "mp"), None),
            P("mp", "ctx", None),
            P("mp", None, "ctx"),
        ),
        check_vma=False,
    )
```

```python
import functools

import jax
import jax.numpy as jnp
from jax import lax
from jax.experimental import pallas as pl
from jax.experimental.pallas import tpu as pltpu
from jax.sharding import PartitionSpec as P

MESH = pl.DeviceIdType.MESH
epsilon = 1e-06
branch_scale = 0.22
score_scale = 0.015625
rope_base = 10000.0
highest = lax.Precision.HIGHEST
log2_e = 1.4426950408889634
bf16 = jnp.bfloat16
f32 = jnp.float32
CTX, MP = 16, 8
HEAD = 64
TOK = 128
BLOCK = 1024
HALF = 512
ANY = pl.BlockSpec(memory_space=pl.ANY)
VM = pl.BlockSpec(memory_space=pltpu.VMEM)
VMEM_LIMIT = 56 * 1024 * 1024


def contract(left, right, left_dim, right_dim):
    return lax.dot_general(
        left, right, (((left_dim,), (right_dim,)), ((), ())), preferred_element_type=f32
    )


def place():
    return lax.axis_index("ctx"), lax.axis_index("mp")


def greet(signal_to, expected):
    barrier = pltpu.get_barrier_semaphore()
    for target in signal_to:
        pl.semaphore_signal(barrier, inc=1, device_id=target, device_id_type=MESH)
    pl.semaphore_wait(barrier, expected)


def remote(src, dst, send, recv, target):
    return pltpu.make_async_remote_copy(
        src_ref=src, dst_ref=dst, send_sem=send, recv_sem=recv,
        device_id=target, device_id_type=MESH,
    )


def comm_call(kernel, number, arrays, outs, sems, cost):
    return pl.pallas_call(
        kernel,
        out_shape=outs,
        in_specs=[ANY] * len(arrays),
        out_specs=[ANY] * len(outs),
        scratch_shapes=[
            pltpu.SemaphoreType.DMA((n,)) if isinstance(n, int) else n for n in sems
        ],
        compiler_params=pltpu.CompilerParams(collective_id=number, has_side_effects=True),
        cost_estimate=pl.CostEstimate(flops=0, bytes_accessed=cost, transcendentals=0),
    )(*arrays)


def shape(dims, kind=bf16):
    return jax.ShapeDtypeStruct(dims, kind)


def flip(index, stride):
    return index + stride - 2 * stride * lax.rem(index // stride, 2)


class Ring:
    def __init__(self, own, dst, index, spread, near, stride, target, sems, sibling=None):
        send, recv, loc = sems[:3]
        count = spread
        plus, minus = lax.rem(index + stride, count), lax.rem(index + count - stride, count)
        far = lax.rem(index + 2 * stride, count)
        near_of = lambda slot: flip(slot, near)
        me_near = near_of(index)

        def copy(src, place_of, at, to):
            return lambda: remote(src, place_of, send.at[at], recv.at[at], target(to))

        def relay(slot, part, at, to):
            return copy(dst(slot, part), dst(slot, part), at, to)

        self.own = lambda: pltpu.make_async_copy(own, dst(index, None), loc)
        self.to_near = copy(own, dst(index, None), 0, me_near)
        self.plus_own = copy(own, dst(index, None), 1, plus)
        self.minus_own = copy(own, dst(index, None), 2, minus)
        self.plus_near = relay(me_near, None, 3, plus)
        self.minus_near = relay(me_near, None, 4, minus)
        self.plus_far = relay(minus, 0, 5, plus)
        self.minus_far = relay(plus, 1, 6, minus)
        self.plus_far_near = relay(near_of(minus), 0, 7, plus)
        self.minus_far_near = relay(near_of(plus), 1, 8, minus)
        self.over = None
        if sibling is not None:
            send2, recv2 = sems[3:]
            parts = [
                (index, None),
                (me_near, None),
                (minus, None),
                (plus, None),
                (near_of(minus), None),
                (near_of(plus), None),
                (far, 0),
                (far, 1),
                (near_of(far), 0),
                (near_of(far), 1),
            ]

            def over(at):
                slot, part = parts[at]
                src = own if at == 0 else dst(slot, part)
                return remote(src, dst(slot, part), send2.at[at], recv2.at[at], sibling)

            self.over = over

    def cross(self, *numbers):
        if self.over is not None:
            for at in numbers:
                self.over(at).start()

    def start(self):
        self.own().start()
        for copy in (self.to_near, self.plus_own, self.minus_own):
            copy().start()
        self.cross(0)

    def relay_near(self):
        self.to_near().wait_recv()
        self.plus_near().start()
        self.minus_near().start()
        self.cross(1)

    def relay_own(self):
        self.plus_own().wait_recv()
        self.plus_far().start()
        self.minus_own().wait_recv()
        self.minus_far().start()
        self.cross(2, 3)

    def relay_far(self):
        self.plus_near().wait_recv()
        self.plus_far_near().start()
        self.minus_near().wait_recv()
        self.minus_far_near().start()
        self.cross(4, 5)

    def finish(self):
        last = (self.plus_far, self.minus_far, self.plus_far_near, self.minus_far_near)
        for number, copy in enumerate(last):
            copy().wait_recv()
            self.cross(6 + number)
        for copy in (
            self.to_near,
            self.plus_own,
            self.minus_own,
            self.plus_near,
            self.minus_near,
        ) + last:
            copy().wait_send()
        if self.over is not None:
            for at in range(10):
                self.over(at).wait()
        self.own().wait()


def mp_ring(own, dst, sems):
    c, m = place()
    return Ring(own, dst, m, MP, 1, 2, lambda slot: (c, slot), sems)


def shared_ring(own, out, sems):
    c, m = place()
    half = own.shape[0] // 2
    first = pl.multiple_of(lax.rem(c, 2) * half, half)

    def dst(slot, part):
        if part is None:
            return out.at[slot, pl.ds(first, half)]
        return out.at[slot, pl.ds(first + part * (half // 2), half // 2)]

    mine = own.at[pl.ds(first, half)]
    return Ring(mine, dst, m, MP, 1, 2, lambda slot: (c, slot), sems, (flip(c, 1), m))


def ctx_ring(own, dst, sems):
    c, m = place()
    return Ring(own, dst, c, CTX, 2, 4, lambda slot: (slot, m), sems, (flip(c, 1), m))


def mp_neighbours():
    c, m = place()
    return [(c, flip(m, 1)), (c, lax.rem(m + 2, MP)), (c, lax.rem(m + 6, MP))]


def ctx_neighbours():
    c, m = place()
    return [
        (flip(c, 2), m),
        (lax.rem(c + 4, CTX), m),
        (lax.rem(c + 12, CTX), m),
        (flip(c, 1), m),
    ]


def slots(ref):
    half = ref.shape[1] // 2

    def dst(slot, part):
        return ref.at[slot] if part is None else ref.at[slot, pl.ds(part * half, half)]

    return dst


def row_slots(ref):
    half = ref.shape[0] // 2

    def dst(slot, part):
        rows = pl.ds(pl.multiple_of(slot * 64, 64), 64)
        return ref.at[:, rows] if part is None else ref.at[pl.ds(part * half, half), rows]

    return dst


MP_SEMS = [pltpu.SemaphoreType.DMA((9,)), pltpu.SemaphoreType.DMA((9,)), pltpu.SemaphoreType.DMA]
CTX_SEMS = MP_SEMS + [pltpu.SemaphoreType.DMA((10,)), pltpu.SemaphoreType.DMA((10,))]


def start_kernel(x_ref, id_ref, w_ref, xo, ido, wo, xs, xr, ids, idr, loc, *sems):
    c, m = place()
    upper = m >= MP // 2
    t = jnp.where(upper, CTX - 1 - c, c)
    signals = []
    for k in range(1, MP):
        sender = lax.rem(m + k, MP)
        signals.append((jnp.where(sender >= MP // 2, CTX - 1 - c, c), sender))
    signals += ctx_neighbours()
    barrier = pltpu.get_barrier_semaphore()
    for target in signals:
        pl.semaphore_signal(barrier, inc=1, device_id=target, device_id_type=MESH)

    @pl.when(upper)
    def _():
        pl.semaphore_signal(barrier, inc=1, device_id=(CTX - 1 - c, m), device_id_type=MESH)
        pl.semaphore_wait(barrier, MP + 4)

    @pl.when(jnp.logical_not(upper))
    def _():
        pl.semaphore_wait(barrier, MP + 3)

    ring = ctx_ring(w_ref, slots(wo), sems)
    ring.start()
    x_copies, id_copies = [], []
    for k in range(MP):
        target = (t, lax.rem(m + k, MP))
        x_copies.append(remote(x_ref, xo.at[m], xs.at[k], xr.at[k], target))
        id_copies.append(remote(id_ref, ido.at[m], ids.at[k], idr.at[k], target))
    own_x = pltpu.make_async_copy(x_ref, xo.at[m], loc.at[0])
    own_id = pltpu.make_async_copy(id_ref, ido.at[m], loc.at[1])

    @pl.when(upper)
    def _():
        x_copies[0].start()
        id_copies[0].start()

    @pl.when(jnp.logical_not(upper))
    def _():
        own_x.start()
        own_id.start()

    for k in range(1, MP):
        if k == 3:
            ring.relay_near()
            ring.relay_own()
        if k == 5:
            ring.relay_far()
        x_copies[k].start()
        id_copies[k].start()
    ring.finish()
    for k in range(1, MP):
        x_copies[k].wait()
        id_copies[k].wait()

    @pl.when(upper)
    def _():
        x_copies[0].wait()
        id_copies[0].wait()

    @pl.when(jnp.logical_not(upper))
    def _():
        own_x.wait()
        own_id.wait()


def lanes(rows):
    return lax.broadcasted_iota(jnp.int32, (rows, 128), 1)


def phase_rows(ref, at, rows):
    part = ref[:, at : at + rows]
    return jnp.concatenate([part] * 4, axis=0).T


def turn(values, cosine, sine):
    first = lax.rem(lanes(values.shape[0]), HEAD) < HEAD // 2
    turned = jnp.where(first, -pltpu.roll(values, 96, 1), pltpu.roll(values, 32, 1))
    return values * cosine + turned * sine


def turn_back(grads, cosine, sine):
    first = lax.rem(lanes(grads.shape[0]), HEAD) < HEAD // 2
    scaled = grads * sine
    turned = jnp.where(first, pltpu.roll(scaled, 96, 1), -pltpu.roll(scaled, 32, 1))
    return grads * cosine + turned


def keys_kernel(
    x_ref, gain_ref, w_ref, cos_ref, sin_ref, dy_ref,
    normed_ref, q_ref, kv_out, dy_out,
    kv_own, *sems,
):
    greet(ctx_neighbours() + mp_neighbours(), 7)
    ring = ctx_ring(kv_own, slots(kv_out), sems[:5])
    rows = mp_ring(dy_ref, slots(dy_out), sems[5:])
    rows.start()
    size = 256
    low = lanes(size) < HEAD
    for part in range(4):
        at = part * size
        block = slice(at, at + size)
        x = x_ref[block].astype(f32)
        inverse = lax.rsqrt(jnp.mean(x * x, axis=1, keepdims=True) + epsilon)
        normed = (x * inverse * gain_ref[...]).astype(bf16)
        normed_ref[block] = normed
        qkv = jnp.dot(normed, w_ref[...], preferred_element_type=f32)
        cosine, sine = phase_rows(cos_ref, at, size), phase_rows(sin_ref, at, size)
        queries = turn(qkv[:, :128], cosine, sine).astype(bf16).astype(f32) * score_scale
        half, place_in = part // 2, at % HALF
        q_ref[half, place_in : place_in + size] = jnp.where(low, queries, 0.0).astype(bf16)
        q_ref[half, HALF + place_in : HALF + place_in + size] = jnp.where(
            low, pltpu.roll(queries, HEAD, 1), 0.0
        ).astype(bf16)
        kv = qkv[:, 128:]
        kv_own[block] = jnp.where(low, turn(kv, cosine, sine), kv).astype(bf16)
    ring.start()
    rows.relay_near()
    rows.relay_own()
    ring.relay_near()
    ring.relay_own()
    rows.relay_far()
    ring.relay_far()
    rows.finish()
    ring.finish()


def keys_and_values(x_all, gain, qkv_w, cosine, sine, dy):
    return pl.pallas_call(
        keys_kernel,
        out_shape=[
            shape((BLOCK, 1024)),
            shape((2, 2 * HALF, 128)),
            shape((CTX, BLOCK, 128)),
            shape((MP, TOK, 1024)),
        ],
        in_specs=[VM] * 5 + [ANY],
        out_specs=[VM] * 2 + [ANY] * 2,
        scratch_shapes=[pltpu.VMEM((BLOCK, 128), bf16)] + CTX_SEMS + MP_SEMS,
        compiler_params=pltpu.CompilerParams(
            vmem_limit_bytes=VMEM_LIMIT, collective_id=2, has_side_effects=True
        ),
    )(x_all, gain, qkv_w, cosine, sine, dy)


def gather_kernel(a_ref, w_ref, out, w_out, *sems):
    greet(ctx_neighbours() + mp_neighbours(), 7)
    ring = mp_ring(a_ref, slots(out), sems[:3])
    weights = ctx_ring(w_ref, row_slots(w_out), sems[3:])
    ring.start()
    weights.start()
    ring.relay_near()
    ring.relay_own()
    weights.relay_near()
    weights.relay_own()
    ring.relay_far()
    weights.relay_far()
    ring.finish()
    weights.finish()


def scatter_kernel(
    a_ref, b_ref, dp_ref, act_ref, in_ref, dgu_ref,
    ao, bo, pair_ref, sum_ref,
    terms, theirs, got, own, s1, r1, s2, r2, s3, r3, s4, r4, loc,
):
    c, m = place()
    core = lax.rem(c, 2)
    x = c // 4
    sibling = (flip(c, 1), m)
    mates = [(c, lax.rem(m + k, MP)) for k in range(1, MP)]
    peers = [(lax.rem(c + 4 * k, CTX), m) for k in range(1, 4)]
    greet(mates + [sibling] + peers, MP + 3)
    own_a = pltpu.make_async_copy(a_ref.at[m], ao.at[m], loc.at[0])
    own_a.start()
    own_b = pltpu.make_async_copy(b_ref.at[m], bo.at[m], loc.at[1])
    own_b.start()
    copies = []
    for k in range(1, MP):
        to = lax.rem(m + k, MP)
        copies.append(remote(a_ref.at[to], ao.at[m], s1.at[k], r1.at[k], mates[k - 1]))
        copies.append(remote(b_ref.at[to], bo.at[m], s2.at[k], r2.at[k], mates[k - 1]))
    for copy in copies:
        copy.start()
    crossing = [
        remote(terms.at[1 - core, e], theirs.at[e], s3.at[e], r3.at[e], sibling)
        for e in range(4)
    ]
    first = [
        remote(own.at[lax.rem(x + k, 4)], got.at[k - 1], s4.at[k], r4.at[k], peers[k - 1])
        for k in range(1, 4)
    ]

    def join(e, put):
        crossing[e].wait()

        def add(chip, carry):
            put(
                chip,
                (terms[core, e, chip].astype(f32) + theirs[e, chip].astype(f32)).astype(bf16),
            )
            return carry

        lax.fori_loop(0, 8, add, 0)

    def put_own(chip, value):
        own[chip // 2, lax.rem(chip, 2)] = value

    def put_pair(e):
        def put(chip, value):
            pair_ref[e, chip // 2, lax.rem(chip, 2)] = value

        return put

    for e in range(4):
        gate_up_grads = dgu_ref[e]
        active = act_ref[e]

        def chunk(at, carry):
            columns = pl.ds(pl.multiple_of(at * 256, 256), 256)
            in_part = contract(in_ref[e, :, columns], gate_up_grads, 0, 0).astype(bf16)
            out_part = contract(dp_ref[e, :, columns], active, 0, 0).astype(bf16)
            for j in range(4):
                rows = slice(64 * j, 64 * j + 64)
                terms[j % 2, e, 2 * at + j // 2, :, 0:1024] = in_part[rows]
                terms[j % 2, e, 2 * at + j // 2, :, 1024:1536] = out_part[rows]
            return carry

        lax.fori_loop(0, 4, chunk, 0)
        crossing[e].start()
        if e == 1:
            join(0, put_own)
            for copy in first:
                copy.start()
    for e in range(1, 4):
        join(e, put_pair(e - 1))
    for copy in first:
        copy.wait()
    for j in range(2):
        term = own[x, j].astype(f32)
        for k in range(3):
            term = term + got[k, j].astype(f32)
        sum_ref[j] = term.astype(bf16)
    for copy in copies:
        copy.wait()
    own_a.wait()
    own_b.wait()


def scatter_rows(routed_terms, share, d_produced, active, incoming, d_gate_up):
    return pl.pallas_call(
        scatter_kernel,
        out_shape=[
            shape((MP, TOK, 1024)),
            shape((MP, 8, TOK), f32),
            shape((3, 4, 2, 64, 1536)),
            shape((2, 64, 1536)),
        ],
        in_specs=[ANY, ANY, VM, VM, VM, VM],
        out_specs=[ANY, ANY, VM, VM],
        scratch_shapes=[
            pltpu.VMEM((2, 4, 8, 64, 1536), bf16),
            pltpu.VMEM((4, 8, 64, 1536), bf16),
            pltpu.VMEM((3, 2, 64, 1536), bf16),
            pltpu.VMEM((4, 2, 64, 1536), bf16),
        ]
        + [pltpu.SemaphoreType.DMA((MP,))] * 4
        + [pltpu.SemaphoreType.DMA((4,))] * 4
        + [pltpu.SemaphoreType.DMA((2,))],
        compiler_params=pltpu.CompilerParams(
            vmem_limit_bytes=VMEM_LIMIT, collective_id=4, has_side_effects=True
        ),
    )(routed_terms, share, d_produced, active, incoming, d_gate_up)


def outputs_kernel(a_ref, ao, s1, r1, loc):
    c, m = place()
    mates = [(c, lax.rem(m + k, MP)) for k in range(1, MP)]
    greet(mates, MP - 1)
    own_a = pltpu.make_async_copy(a_ref.at[m], ao.at[m], loc.at[0])
    own_a.start()
    copies = []
    for k in range(1, MP):
        to = lax.rem(m + k, MP)
        copies.append(remote(a_ref.at[to], ao.at[m], s1.at[k], r1.at[k], mates[k - 1]))
    for copy in copies:
        copy.start()
    for copy in copies:
        copy.wait()
    own_a.wait()


def keys_grad_kernel(
    a_ref, out, theirs, pair_a, pair_b, got_a, got_b, sum_a, sum_b, last_a, last_b,
    s0, r0, s1, r1, s2, r2,
):
    c, m = place()
    core = lax.rem(c, 2)
    x, y = c // 4, lax.rem(c // 2, 2)
    sibling = (flip(c, 1), m)
    across = (flip(c, 2), m)
    peers = [(lax.rem(c + 4 * k, CTX), m) for k in range(1, 4)]
    greet(peers + [across, sibling], 5)
    low, high = pl.ds(0, HALF), pl.ds(HALF, HALF)
    crossing = [
        remote(
            a_ref.at[:, :, 1 - core, rows], theirs.at[:, :, rows], s0.at[at], r0.at[at], sibling
        )
        for at, rows in enumerate((high, low))
    ]
    for copy in crossing:
        copy.start()

    def add(a, b):
        return a.astype(f32) + b.astype(f32)

    crossing[0].wait()
    for i in range(4):
        for j in range(2):
            pair_b[i, j] = add(a_ref[i, j, core, high], theirs[i, j, high]).astype(bf16)
    first = [remote(pair_b.at[:, 1 - y], got_b, s1.at[0], r1.at[0], across)]
    first[0].start()
    crossing[1].wait()
    for i in range(4):
        for j in range(2):
            pair_a[i, j] = add(a_ref[i, j, core, low], theirs[i, j, low]).astype(bf16)
    for k in range(1, 4):
        copy = remote(
            pair_a.at[lax.rem(x + k, 4)], got_a.at[k - 1], s1.at[k], r1.at[k], peers[k - 1]
        )
        copy.start()
        first.append(copy)
    first[0].wait()
    for i in range(4):
        sum_b[i] = add(pair_b[i, y], got_b[i]).astype(bf16)
    second = []
    for k in range(1, 4):
        copy = remote(
            sum_b.at[lax.rem(x + k, 4)], last_b.at[k - 1], s2.at[k], r2.at[k], peers[k - 1]
        )
        copy.start()
        second.append(copy)
    for copy in first[1:]:
        copy.wait()
    for j in range(2):
        sum_a[j] = (add(pair_a[x, j], got_a[0, j]) + add(got_a[1, j], got_a[2, j])).astype(bf16)
    copy = remote(sum_a.at[1 - y], last_a, s2.at[0], r2.at[0], across)
    copy.start()
    second.append(copy)
    for copy in second:
        copy.wait()
    out[low] = add(sum_a[y], last_a[...])
    out[high] = add(sum_b[x], last_b[0]) + add(last_b[1], last_b[2])


def keys_grad(terms):
    piece = (HALF, 128)
    return pl.pallas_call(
        keys_grad_kernel,
        out_shape=shape((BLOCK, 128), f32),
        in_specs=[VM],
        out_specs=VM,
        scratch_shapes=[
            pltpu.VMEM((4, 2, BLOCK, 128), bf16),
            pltpu.VMEM((4, 2) + piece, bf16),
            pltpu.VMEM((4, 2) + piece, bf16),
            pltpu.VMEM((3, 2) + piece, bf16),
            pltpu.VMEM((4,) + piece, bf16),
            pltpu.VMEM((2,) + piece, bf16),
            pltpu.VMEM((4,) + piece, bf16),
            pltpu.VMEM(piece, bf16),
            pltpu.VMEM((3,) + piece, bf16),
        ]
        + [pltpu.SemaphoreType.DMA((2,))] * 2
        + [pltpu.SemaphoreType.DMA((4,))] * 4,
        compiler_params=pltpu.CompilerParams(
            vmem_limit_bytes=VMEM_LIMIT, collective_id=6, has_side_effects=True
        ),
    )(terms)


def finish_kernel(
    dq_ref, dkv_ref, cos_ref, sin_ref, normed_ref, br_ref, rows_ref, hid_ref, y_ref,
    ao, go, hid_out, y_out,
    d_qkv, terms, s1, r1, s2, r2, s3, r3, loc,
):
    c, m = place()
    upper = m >= MP // 2
    t = jnp.where(upper, CTX - 1 - c, c)
    barrier = pltpu.get_barrier_semaphore()
    for k in range(1, MP):
        pl.semaphore_signal(
            barrier, inc=1, device_id=(t, lax.rem(m + k, MP)), device_id_type=MESH
        )
    for k in range(1, CTX):
        pl.semaphore_signal(
            barrier, inc=1, device_id=(lax.rem(c + k, CTX), m), device_id_type=MESH
        )

    @pl.when(upper)
    def _():
        pl.semaphore_signal(barrier, inc=1, device_id=(t, m), device_id_type=MESH)
        pl.semaphore_wait(barrier, MP + CTX - 1)

    @pl.when(jnp.logical_not(upper))
    def _():
        pl.semaphore_wait(barrier, MP + CTX - 2)

    home = [
        remote(hid_ref, hid_out, s3.at[0], r3.at[0], (t, m)),
        remote(y_ref, y_out, s3.at[1], r3.at[1], (t, m)),
    ]
    stay = [
        pltpu.make_async_copy(hid_ref, hid_out, loc.at[2]),
        pltpu.make_async_copy(y_ref, y_out, loc.at[3]),
    ]

    @pl.when(upper)
    def _():
        for copy in home:
            copy.start()

    @pl.when(jnp.logical_not(upper))
    def _():
        for copy in stay:
            copy.start()

    low = lanes(TOK) < HEAD
    for i in range(MP):
        at = i * TOK
        part, inside = at // HALF, at % HALF
        columns = dq_ref[part]
        heads = jnp.concatenate(
            [
                columns[:HEAD, inside : inside + TOK],
                columns[:HEAD, HALF + inside : HALF + inside + TOK],
            ],
            axis=0,
        ).T
        cosine, sine = phase_rows(cos_ref, at, TOK), phase_rows(sin_ref, at, TOK)
        d_qkv[i, :, 0:128] = turn_back(heads * score_scale, cosine, sine).astype(bf16)
        dkv = dkv_ref[at : at + TOK]
        d_qkv[i, :, 128:256] = jnp.where(low, turn_back(dkv, cosine, sine), dkv).astype(bf16)

    own_a = pltpu.make_async_copy(d_qkv.at[m], ao.at[m], loc.at[1])
    a_copies, g_copies = [], []
    for k in range(MP):
        to = lax.rem(m + k, MP)
        target = (jnp.where(to >= MP // 2, CTX - 1 - c, c), to)
        a_copies.append(remote(d_qkv.at[to], ao.at[m], s1.at[k], r1.at[k], target))

    @pl.when(upper)
    def _():
        a_copies[0].start()

    @pl.when(jnp.logical_not(upper))
    def _():
        own_a.start()

    for k in range(1, MP):
        a_copies[k].start()
    grads = d_qkv[...].reshape(BLOCK, 256)
    columns = jnp.concatenate(
        [
            contract(grads, normed_ref[...], 0, 0),
            contract(rows_ref[...], br_ref[...], 0, 0),
        ],
        axis=0,
    )
    terms[...] = columns.T.astype(bf16).reshape(terms.shape)
    own_g = pltpu.make_async_copy(terms.at[c], go.at[c], loc.at[0])
    own_g.start()
    for k in range(1, CTX):
        to = lax.rem(c + k, CTX)
        copy = remote(terms.at[to], go.at[c], s2.at[k], r2.at[k], (to, m))
        copy.start()
        g_copies.append(copy)
    for k in range(1, MP):
        a_copies[k].wait()
    for copy in g_copies:
        copy.wait()
    own_g.wait()

    @pl.when(upper)
    def _():
        a_copies[0].wait()
        for copy in home:
            copy.wait()

    @pl.when(jnp.logical_not(upper))
    def _():
        own_a.wait()
        for copy in stay:
            copy.wait()


def finish(dq, dkv, cosine, sine, normed, branch_rows, out_rows, hidden_grad, outputs):
    return pl.pallas_call(
        finish_kernel,
        out_shape=[
            shape((MP, TOK, 256)),
            shape((CTX, 64, 384)),
            shape((TOK, 1024)),
            shape((TOK, 1024)),
        ],
        in_specs=[VM] * 7 + [ANY] * 2,
        out_specs=[ANY] * 4,
        scratch_shapes=[
            pltpu.VMEM((MP, TOK, 256), bf16),
            pltpu.VMEM((CTX, 64, 384), bf16),
        ]
        + [pltpu.SemaphoreType.DMA((n,)) for n in (MP, MP, CTX, CTX, 2, 2, 4)],
        compiler_params=pltpu.CompilerParams(
            vmem_limit_bytes=VMEM_LIMIT, collective_id=8, has_side_effects=True
        ),
    )(dq, dkv, cosine, sine, normed, branch_rows, out_rows, hidden_grad, outputs)


def sums_kernel(
    small_ref, qg_ref, qw_ref, x_ref, gain_ref, hid_ref, w_ref,
    out, ig_ref, wq_ref, wk_ref, wv_ref, wo_ref,
    terms, got, part, got2, s1, r1, s2, r2,
):
    c, m = place()
    peers = [(lax.rem(c + k, CTX), m) for k in range(1, CTX)]
    mates = [(c, lax.rem(m + k, MP)) for k in range(1, MP)]
    barrier = pltpu.get_barrier_semaphore()
    for target in peers + mates:
        pl.semaphore_signal(barrier, inc=1, device_id=target, device_id_type=MESH)
    grads = contract(qg_ref[0], qw_ref[0], 1, 1)
    for h in range(1, MP):
        grads = grads + contract(qg_ref[h], qw_ref[h], 1, 1)
    x = x_ref[...].astype(f32)
    inverse = lax.rsqrt(jnp.mean(x * x, axis=1, keepdims=True) + epsilon)
    scaled = x * inverse
    inner = grads * gain_ref[...]
    gain_grad = jnp.sum(grads * scaled, axis=0, keepdims=True)
    columns = jnp.broadcast_to(gain_grad, (128, 1024)).T
    terms[...] = jnp.where(lanes(1024) == 32, columns, small_ref[...]).reshape(terms.shape)
    pl.semaphore_wait(barrier, CTX - 1 + MP - 1)
    copies = []
    for k in range(1, CTX):
        to = lax.rem(c + k, CTX)
        copy = remote(terms.at[to], got.at[k], s1.at[k], r1.at[k], peers[k - 1])
        copy.start()
        copies.append(copy)
    ig = inverse * (inner - scaled * jnp.mean(inner * scaled, axis=1, keepdims=True))
    ig_ref[...] = (ig + hid_ref[...].astype(f32)).astype(bf16)
    weights = w_ref[0].astype(f32)
    for k in range(1, CTX):
        weights = weights + w_ref[k].astype(f32)
    wq_ref[...] = weights[:, :128]
    wk_ref[...] = weights[:, 128:192]
    wv_ref[...] = weights[:, 192:256]
    wo_ref[...] = weights[:, 256:].T
    total = terms[c]
    for copy in copies:
        copy.wait()
    for k in range(1, CTX):
        total = total + got[k]
    part[...] = total
    copies = []
    for k in range(1, MP):
        to = lax.rem(m + k, MP)
        copy = remote(part.at[to], got2.at[k], s2.at[k], r2.at[k], mates[k - 1])
        copy.start()
        copies.append(copy)
    last = part[m]
    for copy in copies:
        copy.wait()
    for k in range(1, MP):
        last = last + got2[k]
    out[...] = last


def last_sums(small, qkv_got, qkv_w_all, x, gain, hidden_grad, w_got):
    dims = (8, 128)
    return pl.pallas_call(
        sums_kernel,
        out_shape=[
            shape(dims, f32),
            shape((TOK, 1024)),
            shape((64, 128), f32),
            shape((64, 64), f32),
            shape((64, 64), f32),
            shape((128, 64), f32),
        ],
        in_specs=[VM] * 7,
        out_specs=[VM] * 6,
        scratch_shapes=[
            pltpu.VMEM((CTX, MP) + dims, f32),
            pltpu.VMEM((CTX, MP) + dims, f32),
            pltpu.VMEM((MP,) + dims, f32),
            pltpu.VMEM((MP,) + dims, f32),
            pltpu.SemaphoreType.DMA((CTX,)),
            pltpu.SemaphoreType.DMA((CTX,)),
            pltpu.SemaphoreType.DMA((MP,)),
            pltpu.SemaphoreType.DMA((MP,)),
        ],
        compiler_params=pltpu.CompilerParams(
            vmem_limit_bytes=VMEM_LIMIT, collective_id=9, has_side_effects=True
        ),
    )(small, qkv_got, qkv_w_all, x, gain, hidden_grad, w_got)


def unit(index, first_half):
    second = index > first_half
    part = second.astype(jnp.int32)
    key_half = jnp.where(second, index - first_half - 1, index)
    odd = lax.rem(key_half, 2) == 1
    slot = jnp.where(odd, 2 * CTX - key_half, key_half)
    diagonal = jnp.logical_or(index == first_half, index == 2 * CTX)
    return part, slot, diagonal


def visible_mask(rows):
    key_at = lax.broadcasted_iota(jnp.int32, (HALF, rows), 0)
    query_at = lax.rem(lax.broadcasted_iota(jnp.int32, (HALF, rows), 1), HALF)
    return key_at <= query_at


def forward_kernel(
    q_ref, kv_ref, in_ref, qw_ref, rows_ref,
    out_ref, rows_out, lse_ref, in_all, qw_all, rows_all,
    best, total, summed, *sems,
):
    first_half = 2 * lax.axis_index("ctx")
    greet(ctx_neighbours() + mp_neighbours(), 7)
    weights_rings = [ctx_ring(in_ref, row_slots(in_all), sems[0:5])]
    rows_rings = [
        shared_ring(rows_ref, rows_all, sems[5:10]),
        shared_ring(qw_ref, qw_all, sems[10:15]),
    ]
    for ring in weights_rings + rows_rings:
        ring.start()
    best[...] = jnp.full(best.shape, -1e30, f32)
    total[...] = jnp.zeros(total.shape, f32)
    summed[...] = jnp.zeros(summed.shape, f32)

    def work(part, slot, masked):
        kv = kv_ref[slot]
        scores = contract(kv, q_ref[part], 1, 1)
        if masked:
            scores = jnp.where(visible_mask(scores.shape[1]), scores, -jnp.inf)
        old = best[part]
        new = jnp.maximum(old, jnp.max(scores, axis=0, keepdims=True))
        weights = jnp.exp2(scores * log2_e - new * log2_e)
        fading = jnp.exp2((old - new) * log2_e)
        total[part] = total[part] * fading + jnp.sum(weights, axis=0, keepdims=True)
        summed[part] = summed[part] * fading + contract(kv, weights.astype(bf16), 0, 0)
        best[part] = new

    def step(index, carry):
        part, slot, diagonal = unit(index, first_half)

        @pl.when(index == 11)
        def _():
            for ring in weights_rings:
                ring.relay_near()
                ring.relay_own()

        @pl.when(index == 16)
        def _():
            for ring in rows_rings:
                ring.relay_near()
                ring.relay_own()

        @pl.when(index == 24)
        def _():
            for ring in rows_rings:
                ring.relay_far()

        @pl.when(index == 25)
        def _():
            for ring in weights_rings:
                ring.relay_far()

        @pl.when(diagonal)
        def _():
            work(part, slot, True)

        @pl.when(jnp.logical_not(diagonal))
        def _():
            work(part, slot, False)

        return carry

    lax.fori_loop(0, 2 * CTX + 1, step, 0)
    for part in range(2):
        columns = summed[part][HEAD:, :] / total[part]
        heads = jnp.concatenate([columns[:, :HALF], columns[:, HALF:]], axis=0).T
        out_ref[part * HALF : part * HALF + HALF] = heads
        rows_out[part * HALF : part * HALF + HALF] = heads.astype(bf16)
        lse_ref[part] = best[part] + jnp.log(total[part])
    for ring in weights_rings + rows_rings:
        ring.finish()


def attention(q_rows, kv_all, w_in, qkv_w, out_rows_w):
    rows = q_rows.shape[1]
    return pl.pallas_call(
        forward_kernel,
        out_shape=[
            shape((BLOCK, 128), f32),
            shape((BLOCK, 128)),
            shape((2, 1, rows), f32),
            shape((4, 1024, 1024)),
            shape((MP,) + qkv_w.shape),
            shape((MP, TOK, 1024)),
        ],
        in_specs=[VM, VM, ANY, ANY, ANY],
        out_specs=[VM, VM, VM, ANY, ANY, ANY],
        scratch_shapes=[
            pltpu.VMEM((2, 1, rows), f32),
            pltpu.VMEM((2, 1, rows), f32),
            pltpu.VMEM((2, 2 * HEAD, rows), f32),
        ]
        + CTX_SEMS * 3,
        compiler_params=pltpu.CompilerParams(
            vmem_limit_bytes=VMEM_LIMIT, collective_id=10, has_side_effects=True
        ),
        cost_estimate=pl.CostEstimate(
            flops=33 * 4 * HALF * rows * 256, bytes_accessed=1 << 23, transcendentals=33 * HALF * rows
        ),
    )(q_rows, kv_all, w_in, qkv_w, out_rows_w)


def backward_kernel(
    q_ref, og_ref, att_ref, lse_ref, kv_ref, sum_0, pair_ref, br_ref, mixed_ref,
    dkv_ref, dq_ref, in_grad, out_grad, br_all, mixed_out,
    total, do_ref, delta_ref, own_a, own_b, got_a, got_b, sum_a, sum_b, last_0, last_a, last_b,
    *sems,
):
    c, m = place()
    first_half = 2 * c
    x, y = c // 4, lax.rem(c // 2, 2)
    peers = [(lax.rem(c + 4 * k, CTX), m) for k in range(1, 4)]
    across = (flip(c, 2), m)
    mates = [(c, lax.rem(m + k, MP)) for k in range(1, MP)]
    greet(peers + [across] + mates, 4 + MP - 1)
    sa, ra, sb, rb, sm, rm, loc = sems[:7]
    ring = mp_ring(br_ref, slots(br_all), sems[7:10])

    def first_copies():
        copies = [
            remote(
                pair_ref.at[pl.ds(0, 2), lax.rem(x + k, 4)],
                got_a.at[k - 1], sa.at[k], ra.at[k], peers[k - 1],
            )
            for k in range(1, 4)
        ]
        copies.append(remote(pair_ref.at[2, :, 1 - y], got_b, sa.at[0], ra.at[0], across))
        return copies

    def own_copies():
        return [
            pltpu.make_async_copy(pair_ref.at[pl.ds(0, 2), x], own_a, loc.at[1]),
            pltpu.make_async_copy(pair_ref.at[2, :, y], own_b, loc.at[2]),
        ]

    def sum_0_copy():
        return remote(sum_0.at[1 - y], last_0, sb.at[0], rb.at[0], across)

    def second_copies():
        copies = [
            remote(
                sum_b.at[lax.rem(x + k, 4)], last_b.at[k - 1], sb.at[k], rb.at[k], peers[k - 1]
            )
            for k in range(1, 4)
        ]
        copies.append(remote(sum_a.at[:, 1 - y], last_a, sb.at[4], rb.at[4], across))
        return copies

    def middle():
        for copy in first_copies() + own_copies():
            copy.wait()
        for e in range(2):
            for j in range(2):
                term = own_a[e, j].astype(f32)
                for k in range(3):
                    term = term + got_a[k, e, j].astype(f32)
                sum_a[e, j] = term.astype(bf16)
        for j in range(4):
            sum_b[j] = (own_b[j].astype(f32) + got_b[j].astype(f32)).astype(bf16)
        for copy in second_copies():
            copy.start()

    def mixed_copies():
        copies = []
        for k in range(1, MP):
            to = lax.rem(m + k, MP)
            copies.append(
                remote(mixed_ref.at[to], mixed_out.at[m], sm.at[k], rm.at[k], mates[k - 1])
            )
        return copies

    def own_mixed():
        return pltpu.make_async_copy(mixed_ref.at[m], mixed_out.at[m], loc.at[0])

    ring.start()
    for copy in first_copies() + own_copies() + [sum_0_copy()]:
        copy.start()
    low = lanes(HALF) < HEAD
    for part in range(2):
        rows = slice(part * HALF, part * HALF + HALF)
        grads = og_ref[rows].astype(f32)
        product = (grads * att_ref[rows]).T
        delta_ref[part, :, 0:HALF] = jnp.sum(product[:HEAD], axis=0, keepdims=True)
        delta_ref[part, :, HALF:] = jnp.sum(product[HEAD:], axis=0, keepdims=True)
        do_ref[part, 0:HALF] = jnp.where(low, 0.0, pltpu.roll(grads, HEAD, 1)).astype(bf16)
        do_ref[part, HALF:] = jnp.where(low, 0.0, grads).astype(bf16)
    dq_ref[...] = jnp.zeros(dq_ref.shape, f32)

    def clear(index, carry):
        total[index] = jnp.zeros(total.shape[1:], f32)
        return carry

    lax.fori_loop(0, 2 * CTX, clear, 0)

    def work(part, slot, masked):
        kv = kv_ref[slot]
        queries = q_ref[part]
        grads = do_ref[part]
        scores = contract(kv, queries, 1, 1)
        probs = jnp.exp2((scores - lse_ref[part]) * log2_e)
        if masked:
            probs = jnp.where(visible_mask(scores.shape[1]), probs, 0.0)
        prob_grad = contract(kv, grads, 1, 1)
        score_grad = (probs * (prob_grad - delta_ref[part])).astype(bf16)
        total[slot] += contract(probs.astype(bf16), grads, 1, 0) + contract(
            score_grad, queries, 1, 0
        )
        dq_ref[part] += contract(kv, score_grad, 0, 0)

    def step(index, carry):
        part, slot, diagonal = unit(index, first_half)

        @pl.when(index == 1)
        def _():
            own_mixed().start()
            for copy in mixed_copies():
                copy.start()

        @pl.when(index == 18)
        def _():
            ring.relay_near()
            ring.relay_own()

        @pl.when(index == 25)
        def _():
            middle()

        @pl.when(index == 27)
        def _():
            ring.relay_far()

        @pl.when(diagonal)
        def _():
            work(part, slot, True)

        @pl.when(jnp.logical_not(diagonal))
        def _():
            work(part, slot, False)

        return carry

    lax.fori_loop(0, 2 * CTX + 1, step, 0)

    def write(index, carry):
        dkv_ref[index] = total[index].astype(bf16)
        return carry

    lax.fori_loop(0, 2 * CTX, write, 0)
    ring.finish()
    sum_0_copy().wait()
    for copy in second_copies():
        copy.wait()

    def put(at, term):
        in_grad[at] = term[:, :1024]
        out_grad[at] = term[:, 1024:].T

    put(0, sum_0[y].astype(f32) + last_0[...].astype(f32))
    for e in range(2):
        put(1 + e, sum_a[e, y].astype(f32) + last_a[e].astype(f32))
    term = sum_b[x].astype(f32)
    for k in range(3):
        term = term + last_b[k].astype(f32)
    put(3, term)
    for copy in mixed_copies():
        copy.wait()
    own_mixed().wait()


def attention_back(
    q_rows, out_grad, attended, lse, kv_all, sum_first, pair, branch_grad, mixed
):
    rows = q_rows.shape[1]
    wide = pair.shape[-1]
    return pl.pallas_call(
        backward_kernel,
        out_shape=[
            shape(kv_all.shape, bf16),
            shape((2, 2 * HEAD, rows), f32),
            shape((4, 64, 1024), f32),
            shape((4, 512, 64), f32),
            shape((MP, TOK, 1024)),
            shape((MP, TOK, 1024)),
        ],
        in_specs=[VM] * 6 + [ANY] * 3,
        out_specs=[VM] * 4 + [ANY] * 2,
        scratch_shapes=[
            pltpu.VMEM(kv_all.shape, f32),
            pltpu.VMEM(q_rows.shape, bf16),
            pltpu.VMEM((2, 1, rows), f32),
            pltpu.VMEM((2, 2, 64, wide), bf16),
            pltpu.VMEM((4, 64, wide), bf16),
            pltpu.VMEM((3, 2, 2, 64, wide), bf16),
            pltpu.VMEM((4, 64, wide), bf16),
            pltpu.VMEM((2, 2, 64, wide), bf16),
            pltpu.VMEM((4, 64, wide), bf16),
            pltpu.VMEM((64, wide), bf16),
            pltpu.VMEM((2, 64, wide), bf16),
            pltpu.VMEM((3, 64, wide), bf16),
        ]
        + [pltpu.SemaphoreType.DMA((4,))] * 2
        + [pltpu.SemaphoreType.DMA((5,))] * 2
        + [pltpu.SemaphoreType.DMA((MP,))] * 2
        + [pltpu.SemaphoreType.DMA((3,))]
        + MP_SEMS,
        compiler_params=pltpu.CompilerParams(
            vmem_limit_bytes=VMEM_LIMIT, collective_id=11, has_side_effects=True
        ),
        cost_estimate=pl.CostEstimate(
            flops=33 * 10 * HALF * rows * 256, bytes_accessed=1 << 24, transcendentals=33 * HALF * rows
        ),
    )(q_rows, out_grad, attended, lse, kv_all, sum_first, pair, branch_grad, mixed)


def phases(positions, head_width):
    steps_up = jnp.arange(head_width // 2).astype(f32)
    frequency = rope_base ** (-2.0 * steps_up / head_width)
    angles = frequency[:, None] * positions.astype(f32)[None, :]
    return (jnp.cos(angles), jnp.sin(angles))


def normalize(values):
    inverse = lax.rsqrt(jnp.mean(values * values, axis=-1, keepdims=True) + epsilon)
    return (values * inverse, inverse)


def norm_back(grads, scaled, inverse, gain):
    inner = grads * gain
    return (
        inverse * (inner - scaled * jnp.mean(inner * scaled, axis=-1, keepdims=True)),
        jnp.sum(grads * scaled, axis=0),
    )


def swap_home(array):
    pairs = []
    for c in range(CTX):
        for m in range(MP):
            t = CTX - 1 - c if m >= MP // 2 else c
            pairs.append((c * MP + m, t * MP + m))
    return lax.ppermute(array, ("ctx", "mp"), pairs)


def body(
    layer_input,
    positions,
    expert_ids,
    attn_gain,
    w_query,
    w_key,
    w_value,
    w_attn_out,
    ffn_gain,
    router,
    w_in,
    w_out,
    cotangent,
):
    c, m = place()
    dy_swapped = swap_home(cotangent)
    own_positions = lax.dynamic_slice_in_dim(positions, m * TOK, TOK, 0)
    id_pack = jnp.concatenate(
        [expert_ids.T, own_positions[None, :], jnp.zeros((7, TOK), jnp.int32)], axis=0
    )
    w_pack = jnp.concatenate(
        [
            w_query,
            w_key,
            w_value,
            router,
            attn_gain[:, None],
            ffn_gain[:, None],
            jnp.zeros((64, 94), bf16),
            w_attn_out.T,
        ],
        axis=1,
    )
    x_all, id_all, w_all = comm_call(
        start_kernel,
        1,
        [layer_input, id_pack, w_pack],
        [
            shape((MP, TOK, 1024)),
            shape((MP, 16, TOK), jnp.int32),
            shape((CTX, 64, 512)),
        ],
        [MP, MP, MP, MP, 2] + CTX_SEMS,
        4 << 20,
    )
    inputs = x_all.reshape(BLOCK, 1024).astype(f32)
    ids = id_all[:, :8, :].transpose(1, 0, 2).reshape(8, BLOCK)
    places = id_all[:, 8, :].reshape(BLOCK)
    w_all = w_all.reshape(1024, 512)
    qkv_w = w_all[:, :256]
    router_w = w_all[:, 256:288]
    gain_one = w_all[:, 288].astype(f32)
    gain_two = w_all[:, 289].astype(f32)
    out_w = w_all[:, 384:].T

    cosine, sine = lax.optimization_barrier(phases(places, HEAD))
    normed, q_rows, kv_all, dy_all = keys_and_values(
        x_all.reshape(BLOCK, 1024), gain_one[None, :], qkv_w, cosine, sine, dy_swapped
    )
    kv_all = kv_all.reshape(2 * CTX, HALF, 128)
    attended, out_rows, lse, in_w, qkv_w_all, out_w_all = attention(
        q_rows, kv_all, w_in, qkv_w, out_w
    )
    dy_all = dy_all.reshape(BLOCK, 1024)
    rows_all, out_w_t = comm_call(
        gather_kernel,
        3,
        [out_rows, w_out.transpose(0, 2, 1)],
        [shape((MP, BLOCK, 128)), shape((4, 1024, 512))],
        MP_SEMS + CTX_SEMS,
        8 << 20,
    )
    branch = lax.dot_general(
        rows_all, out_w_all, (((0, 2), (0, 1)), ((), ())), preferred_element_type=f32
    )
    hidden = inputs + branch_scale * branch
    scaled_two, inverse_two = normalize(hidden)
    routed = (scaled_two * gain_two).astype(bf16)

    logits = contract(router_w, routed, 0, 1)
    experts = lax.broadcasted_iota(jnp.int32, (32, BLOCK), 0)
    member = jnp.any(ids[:, None, :] == experts[None], axis=0)
    chosen = jnp.where(member, logits, -jnp.inf)
    top_logit = jnp.max(chosen, axis=0, keepdims=True)
    powers = jnp.exp(chosen - top_logit)
    gates = powers / jnp.sum(powers, axis=0, keepdims=True)

    here = 4 * m + lax.broadcasted_iota(jnp.int32, (4, BLOCK), 0)
    selected = jnp.any(ids[:, None, :] == here[None], axis=0)
    earlier = (
        lax.broadcasted_iota(jnp.int32, (BLOCK, BLOCK), 0)
        <= lax.broadcasted_iota(jnp.int32, (BLOCK, BLOCK), 1)
    ).astype(bf16)
    counts = jnp.dot(selected.astype(bf16), earlier, preferred_element_type=f32)
    rank = jnp.where(selected, counts.astype(jnp.int32) - 1, -1)
    capacity = 288
    place_bool = rank[:, None, :] == lax.broadcasted_iota(jnp.int32, (4, capacity, BLOCK), 1)
    placing = place_bool.astype(bf16).reshape(4 * capacity, BLOCK)
    gates_here = lax.dynamic_slice_in_dim(gates, 4 * m, 4, 0)
    slot_gate = jnp.sum(jnp.where(place_bool, gates_here[:, None, :], 0.0), axis=2)

    incoming = jnp.dot(placing, routed, preferred_element_type=f32).astype(bf16)
    incoming = incoming.reshape(4, capacity, 1024)
    dy_rows = jnp.dot(placing, dy_all, preferred_element_type=f32).reshape(4, capacity, 1024)
    gate_up = jnp.einsum("esd,edf->esf", incoming, in_w, preferred_element_type=f32)
    gate_part, up_part = gate_up[..., :512], gate_up[..., 512:]
    squashed = jax.nn.sigmoid(gate_part)
    silu_part = gate_part * squashed
    active = (silu_part * up_part).astype(bf16)
    produced = jnp.einsum(
        "esf,edf->esd", active, out_w_t, preferred_element_type=f32
    ).astype(bf16)
    produced_f = produced.astype(f32)
    d_produced = (branch_scale * slot_gate[..., None] * dy_rows).astype(bf16)
    slot_share = branch_scale * jnp.sum(dy_rows * produced_f, axis=2)
    weighted = (slot_gate[..., None] * produced_f).astype(bf16).reshape(4 * capacity, 1024)
    mixed = branch_scale * contract(placing, weighted, 0, 0)
    mixed = mixed.astype(bf16).reshape(MP, TOK, 1024)

    d_active = jnp.einsum("esd,edf->esf", d_produced, out_w_t, preferred_element_type=f32)
    slope = squashed * (1.0 + gate_part * (1.0 - squashed))
    d_gate_up = jnp.concatenate(
        [d_active * up_part * slope, d_active * silu_part], axis=-1
    ).astype(bf16)
    d_gate_up = lax.optimization_barrier(d_gate_up)
    row_grads = jnp.einsum(
        "esf,edf->esd", d_gate_up, in_w, preferred_element_type=f32
    ).astype(bf16)
    row_grads = lax.optimization_barrier(row_grads)
    routed_terms = contract(placing, row_grads.reshape(4 * capacity, 1024), 0, 0)
    routed_terms = routed_terms.astype(bf16).reshape(MP, TOK, 1024)
    share = jnp.sum(jnp.where(place_bool, slot_share[:, :, None], 0.0), axis=1)
    share = jnp.pad(share.reshape(4, MP, TOK).transpose(1, 0, 2), ((0, 0), (0, 4), (0, 0)))
    routed_got, share_got, pair, sum_first = scatter_rows(
        routed_terms, share, d_produced, active, incoming, d_gate_up
    )

    def own_rows(array):
        return lax.dynamic_slice_in_dim(array, m * TOK, TOK, 0)

    hidden_own = own_rows(hidden)
    scaled_own, inverse_own = normalize(hidden_own)
    routed_own = (scaled_own * gain_two).astype(bf16).astype(f32)
    dy_own = own_rows(dy_all).astype(f32)
    gates_own = lax.dynamic_slice_in_dim(gates, m * TOK, TOK, 1)
    share_own = share_got[:, :4, :].reshape(32, TOK)
    logit_grad = gates_own * (
        share_own - jnp.sum(gates_own * share_own, axis=0, keepdims=True)
    )
    routed_grad = jnp.sum(routed_got.astype(f32), axis=0) + lax.dot_general(
        logit_grad,
        router_w.astype(f32),
        (((0,), (1,)), ((), ())),
        precision=highest,
        preferred_element_type=f32,
    )
    router_grad = lax.dot_general(
        routed_own,
        logit_grad,
        (((0,), (1,)), ((), ())),
        precision=highest,
        preferred_element_type=f32,
    )
    hidden_grad, gain_two_grad = norm_back(routed_grad, scaled_own, inverse_own, gain_two)
    hidden_grad = hidden_grad + dy_own
    branch_grad = (branch_scale * hidden_grad).astype(bf16)

    out_grad_terms = jnp.einsum(
        "td,hfd->htf", branch_grad, out_w_all, preferred_element_type=f32
    ).astype(bf16)
    (out_grad,) = comm_call(
        outputs_kernel, 5, [out_grad_terms], [shape((MP, TOK, 128))], [MP, MP, 1], 1 << 20
    )
    out_grad = out_grad.reshape(BLOCK, 128)

    dkv_terms, dq_cols, expert_in, expert_out, branch_rows, mixed_got = attention_back(
        q_rows, out_grad, attended, lse, kv_all, sum_first, pair, branch_grad, mixed
    )
    outputs = (hidden_own + jnp.sum(mixed_got.astype(f32), axis=0)).astype(bf16)
    dkv = keys_grad(dkv_terms.reshape(4, 2, 2, BLOCK, 128))
    qkv_got, w_got, hidden_grad_home, outputs = finish(
        dq_cols,
        dkv,
        cosine,
        sine,
        normed,
        branch_rows.reshape(BLOCK, 1024),
        out_rows,
        hidden_grad.astype(bf16),
        outputs,
    )
    small = jnp.concatenate(
        [
            router_grad,
            jnp.zeros((1024, 1), f32),
            gain_two_grad[:, None],
            jnp.zeros((1024, 94), f32),
        ],
        axis=1,
    )
    sums, input_grad, query_grad, key_grad, value_grad, attn_out_grad = last_sums(
        small, qkv_got, qkv_w_all, layer_input, gain_one[None, :], hidden_grad_home, w_got
    )
    return (
        outputs,
        input_grad,
        sums[:, 32],
        query_grad,
        key_grad,
        value_grad,
        attn_out_grad,
        sums[:, 33],
        sums[:, :32],
        expert_in,
        expert_out,
    )


def solution(mesh):
    placed = (
        P(("ctx", "mp"), None),
        P("ctx"),
        P(("ctx", "mp"), None),
        P("ctx"),
        P("ctx", "mp"),
        P("ctx", "mp"),
        P("ctx", "mp"),
        P("mp", "ctx"),
        P("ctx"),
        P("ctx", None),
        P("mp", "ctx", None),
        P("mp", None, "ctx"),
        P(("ctx", "mp"), None),
    )
    return jax.shard_map(
        body,
        mesh=mesh,
        in_specs=placed,
        out_specs=(
            P(("ctx", "mp"), None),
            P(("ctx", "mp"), None),
            P(("ctx", "mp")),
            P("ctx", "mp"),
            P("ctx", "mp"),
            P("ctx", "mp"),
            P("mp", "ctx"),
            P(("ctx", "mp")),
            P(("ctx", "mp"), None),
            P("mp", "ctx", None),
            P("mp", None, "ctx"),
        ),
        check_vma=False,
    )
```

```python
import functools

import jax
import jax.numpy as jnp
from jax import lax
from jax.experimental import pallas as pl
from jax.experimental.pallas import tpu as pltpu
from jax.sharding import PartitionSpec as P

MESH = pl.DeviceIdType.MESH
epsilon = 1e-06
branch_scale = 0.22
score_scale = 0.015625
rope_base = 10000.0
highest = lax.Precision.HIGHEST
log2_e = 1.4426950408889634
bf16 = jnp.bfloat16
f32 = jnp.float32
CTX, MP = 16, 8
HEAD = 64
TOK = 128
BLOCK = 1024
HALF = 512
ANY = pl.BlockSpec(memory_space=pl.ANY)
VM = pl.BlockSpec(memory_space=pltpu.VMEM)
VMEM_LIMIT = 56 * 1024 * 1024


def contract(left, right, left_dim, right_dim):
    return lax.dot_general(
        left, right, (((left_dim,), (right_dim,)), ((), ())), preferred_element_type=f32
    )


def place():
    return lax.axis_index("ctx"), lax.axis_index("mp")


def greet(signal_to, expected):
    barrier = pltpu.get_barrier_semaphore()
    for target in signal_to:
        pl.semaphore_signal(barrier, inc=1, device_id=target, device_id_type=MESH)
    pl.semaphore_wait(barrier, expected)


def remote(src, dst, send, recv, target):
    return pltpu.make_async_remote_copy(
        src_ref=src, dst_ref=dst, send_sem=send, recv_sem=recv,
        device_id=target, device_id_type=MESH,
    )


def comm_call(kernel, number, arrays, outs, sems, cost):
    return pl.pallas_call(
        kernel,
        out_shape=outs,
        in_specs=[ANY] * len(arrays),
        out_specs=[ANY] * len(outs),
        scratch_shapes=[
            pltpu.SemaphoreType.DMA((n,)) if isinstance(n, int) else n for n in sems
        ],
        compiler_params=pltpu.CompilerParams(collective_id=number, has_side_effects=True),
        cost_estimate=pl.CostEstimate(flops=0, bytes_accessed=cost, transcendentals=0),
    )(*arrays)


def shape(dims, kind=bf16):
    return jax.ShapeDtypeStruct(dims, kind)


def flip(index, stride):
    return index + stride - 2 * stride * lax.rem(index // stride, 2)


class Ring:
    def __init__(self, own, dst, index, spread, near, stride, target, sems, sibling=None):
        send, recv, loc = sems[:3]
        count = spread
        plus, minus = lax.rem(index + stride, count), lax.rem(index + count - stride, count)
        far = lax.rem(index + 2 * stride, count)
        near_of = lambda slot: flip(slot, near)
        me_near = near_of(index)

        def copy(src, place_of, at, to):
            return lambda: remote(src, place_of, send.at[at], recv.at[at], target(to))

        def relay(slot, part, at, to):
            return copy(dst(slot, part), dst(slot, part), at, to)

        self.own = None
        if own is not None:
            self.own = lambda: pltpu.make_async_copy(own, dst(index, None), loc)
        own = dst(index, None) if own is None else own
        self.to_near = copy(own, dst(index, None), 0, me_near)
        self.plus_own = copy(own, dst(index, None), 1, plus)
        self.minus_own = copy(own, dst(index, None), 2, minus)
        self.plus_near = relay(me_near, None, 3, plus)
        self.minus_near = relay(me_near, None, 4, minus)
        self.plus_far = relay(minus, 0, 5, plus)
        self.minus_far = relay(plus, 1, 6, minus)
        self.plus_far_near = relay(near_of(minus), 0, 7, plus)
        self.minus_far_near = relay(near_of(plus), 1, 8, minus)
        self.over = None
        if sibling is not None:
            send2, recv2 = sems[3:]
            parts = [
                (index, None),
                (me_near, None),
                (minus, None),
                (plus, None),
                (near_of(minus), None),
                (near_of(plus), None),
                (far, 0),
                (far, 1),
                (near_of(far), 0),
                (near_of(far), 1),
            ]

            def over(at):
                slot, part = parts[at]
                src = own if at == 0 else dst(slot, part)
                return remote(src, dst(slot, part), send2.at[at], recv2.at[at], sibling)

            self.over = over

    def cross(self, *numbers):
        if self.over is not None:
            for at in numbers:
                self.over(at).start()

    def start(self):
        if self.own is not None:
            self.own().start()
        for copy in (self.to_near, self.plus_own, self.minus_own):
            copy().start()
        self.cross(0)

    def relay_near(self):
        self.to_near().wait_recv()
        self.plus_near().start()
        self.minus_near().start()
        self.cross(1)

    def relay_own(self):
        self.plus_own().wait_recv()
        self.plus_far().start()
        self.minus_own().wait_recv()
        self.minus_far().start()
        self.cross(2, 3)

    def relay_far(self):
        self.plus_near().wait_recv()
        self.plus_far_near().start()
        self.minus_near().wait_recv()
        self.minus_far_near().start()
        self.cross(4, 5)

    def finish(self):
        last = (self.plus_far, self.minus_far, self.plus_far_near, self.minus_far_near)
        for number, copy in enumerate(last):
            copy().wait_recv()
            self.cross(6 + number)
        for copy in (
            self.to_near,
            self.plus_own,
            self.minus_own,
            self.plus_near,
            self.minus_near,
        ) + last:
            copy().wait_send()
        if self.over is not None:
            for at in range(10):
                self.over(at).wait()
        if self.own is not None:
            self.own().wait()


def mp_ring(own, dst, sems):
    c, m = place()
    return Ring(own, dst, m, MP, 1, 2, lambda slot: (c, slot), sems)


def shared_ring(own, out, sems):
    c, m = place()
    half = own.shape[0] // 2
    first = pl.multiple_of(lax.rem(c, 2) * half, half)

    def dst(slot, part):
        if part is None:
            return out.at[slot, pl.ds(first, half)]
        return out.at[slot, pl.ds(first + part * (half // 2), half // 2)]

    mine = own.at[pl.ds(first, half)]
    return Ring(mine, dst, m, MP, 1, 2, lambda slot: (c, slot), sems, (flip(c, 1), m))


def ctx_ring(own, dst, sems):
    c, m = place()
    return Ring(own, dst, c, CTX, 2, 4, lambda slot: (slot, m), sems, (flip(c, 1), m))


def mp_neighbours():
    c, m = place()
    return [(c, flip(m, 1)), (c, lax.rem(m + 2, MP)), (c, lax.rem(m + 6, MP))]


def ctx_neighbours():
    c, m = place()
    return [
        (flip(c, 2), m),
        (lax.rem(c + 4, CTX), m),
        (lax.rem(c + 12, CTX), m),
        (flip(c, 1), m),
    ]


def slots(ref):
    half = ref.shape[1] // 2

    def dst(slot, part):
        return ref.at[slot] if part is None else ref.at[slot, pl.ds(part * half, half)]

    return dst


def row_slots(ref):
    half = ref.shape[0] // 2

    def dst(slot, part):
        rows = pl.ds(pl.multiple_of(slot * 64, 64), 64)
        return ref.at[:, rows] if part is None else ref.at[pl.ds(part * half, half), rows]

    return dst


MP_SEMS = [pltpu.SemaphoreType.DMA((9,)), pltpu.SemaphoreType.DMA((9,)), pltpu.SemaphoreType.DMA]
CTX_SEMS = MP_SEMS + [pltpu.SemaphoreType.DMA((10,)), pltpu.SemaphoreType.DMA((10,))]


def start_kernel(x_ref, id_ref, w_ref, xo, ido, wo, s1, r1, loc, *sems):
    c, m = place()
    upper = m >= MP // 2
    opposite = (CTX - 1 - c, m)
    greet([opposite] + ctx_neighbours() + mp_neighbours(), 8)
    ring = ctx_ring(w_ref, slots(wo), sems[0:5])
    rings = [
        mp_ring(None, slots(xo), sems[5:8]),
        mp_ring(None, slots(ido), sems[8:11]),
    ]
    moves = [
        remote(x_ref, xo.at[m], s1.at[0], r1.at[0], opposite),
        remote(id_ref, ido.at[m], s1.at[1], r1.at[1], opposite),
    ]
    stays = [
        pltpu.make_async_copy(x_ref, xo.at[m], loc.at[0]),
        pltpu.make_async_copy(id_ref, ido.at[m], loc.at[1]),
    ]

    @pl.when(upper)
    def _():
        for copy in moves:
            copy.start()

    @pl.when(jnp.logical_not(upper))
    def _():
        for copy in stays:
            copy.start()

    ring.start()

    @pl.when(upper)
    def _():
        for copy in moves:
            copy.wait()

    @pl.when(jnp.logical_not(upper))
    def _():
        for copy in stays:
            copy.wait()

    for one in rings:
        one.start()
    ring.relay_near()
    ring.relay_own()
    for one in rings:
        one.relay_near()
        one.relay_own()
    ring.relay_far()
    for one in rings:
        one.relay_far()
    for one in rings:
        one.finish()
    ring.finish()


def lanes(rows):
    return lax.broadcasted_iota(jnp.int32, (rows, 128), 1)


def phase_rows(ref, at, rows):
    part = ref[:, at : at + rows]
    return jnp.concatenate([part] * 4, axis=0).T


def turn(values, cosine, sine):
    first = lax.rem(lanes(values.shape[0]), HEAD) < HEAD // 2
    turned = jnp.where(first, -pltpu.roll(values, 96, 1), pltpu.roll(values, 32, 1))
    return values * cosine + turned * sine


def turn_back(grads, cosine, sine):
    first = lax.rem(lanes(grads.shape[0]), HEAD) < HEAD // 2
    scaled = grads * sine
    turned = jnp.where(first, pltpu.roll(scaled, 96, 1), -pltpu.roll(scaled, 32, 1))
    return grads * cosine + turned


def keys_kernel(
    x_ref, gain_ref, w_ref, cos_ref, sin_ref, dy_ref,
    normed_ref, q_ref, kv_out, dy_out,
    kv_own, *sems,
):
    greet(ctx_neighbours() + mp_neighbours(), 7)
    ring = ctx_ring(kv_own, slots(kv_out), sems[:5])
    rows = mp_ring(dy_ref, slots(dy_out), sems[5:])
    rows.start()
    size = 256
    low = lanes(size) < HEAD
    for part in range(4):
        at = part * size
        block = slice(at, at + size)
        x = x_ref[block].astype(f32)
        inverse = lax.rsqrt(jnp.mean(x * x, axis=1, keepdims=True) + epsilon)
        normed = (x * inverse * gain_ref[...]).astype(bf16)
        normed_ref[block] = normed
        qkv = jnp.dot(normed, w_ref[...], preferred_element_type=f32)
        cosine, sine = phase_rows(cos_ref, at, size), phase_rows(sin_ref, at, size)
        queries = turn(qkv[:, :128], cosine, sine).astype(bf16).astype(f32) * score_scale
        half, place_in = part // 2, at % HALF
        q_ref[half, place_in : place_in + size] = jnp.where(low, queries, 0.0).astype(bf16)
        q_ref[half, HALF + place_in : HALF + place_in + size] = jnp.where(
            low, pltpu.roll(queries, HEAD, 1), 0.0
        ).astype(bf16)
        kv = qkv[:, 128:]
        kv_own[block] = jnp.where(low, turn(kv, cosine, sine), kv).astype(bf16)
    ring.start()
    rows.relay_near()
    rows.relay_own()
    ring.relay_near()
    ring.relay_own()
    rows.relay_far()
    ring.relay_far()
    rows.finish()
    ring.finish()


def keys_and_values(x_all, gain, qkv_w, cosine, sine, dy):
    return pl.pallas_call(
        keys_kernel,
        out_shape=[
            shape((BLOCK, 1024)),
            shape((2, 2 * HALF, 128)),
            shape((CTX, BLOCK, 128)),
            shape((MP, TOK, 1024)),
        ],
        in_specs=[VM] * 5 + [ANY],
        out_specs=[VM] * 2 + [ANY] * 2,
        scratch_shapes=[pltpu.VMEM((BLOCK, 128), bf16)] + CTX_SEMS + MP_SEMS,
        compiler_params=pltpu.CompilerParams(
            vmem_limit_bytes=VMEM_LIMIT, collective_id=2, has_side_effects=True
        ),
    )(x_all, gain, qkv_w, cosine, sine, dy)


def gather_kernel(a_ref, w_ref, out, w_out, *sems):
    greet(ctx_neighbours() + mp_neighbours(), 7)
    ring = mp_ring(a_ref, slots(out), sems[:3])
    weights = ctx_ring(w_ref, row_slots(w_out), sems[3:])
    ring.start()
    weights.start()
    ring.relay_near()
    ring.relay_own()
    weights.relay_near()
    weights.relay_own()
    ring.relay_far()
    weights.relay_far()
    ring.finish()
    weights.finish()


def scatter_kernel(
    a_ref, b_ref, dp_ref, act_ref, in_ref, dgu_ref,
    ao, bo, pair_ref, sum_ref,
    terms, theirs, got, own, s1, r1, s2, r2, s3, r3, s4, r4, loc,
):
    c, m = place()
    core = lax.rem(c, 2)
    x = c // 4
    sibling = (flip(c, 1), m)
    mates = [(c, lax.rem(m + k, MP)) for k in range(1, MP)]
    peers = [(lax.rem(c + 4 * k, CTX), m) for k in range(1, 4)]
    greet(mates + [sibling] + peers, MP + 3)
    own_a = pltpu.make_async_copy(a_ref.at[m], ao.at[m], loc.at[0])
    own_a.start()
    own_b = pltpu.make_async_copy(b_ref.at[m], bo.at[m], loc.at[1])
    own_b.start()
    copies = []
    for k in range(1, MP):
        to = lax.rem(m + k, MP)
        copies.append(remote(a_ref.at[to], ao.at[m], s1.at[k], r1.at[k], mates[k - 1]))
        copies.append(remote(b_ref.at[to], bo.at[m], s2.at[k], r2.at[k], mates[k - 1]))
    for copy in copies:
        copy.start()
    crossing = [
        remote(terms.at[1 - core, e], theirs.at[e], s3.at[e], r3.at[e], sibling)
        for e in range(4)
    ]
    first = [
        remote(own.at[lax.rem(x + k, 4)], got.at[k - 1], s4.at[k], r4.at[k], peers[k - 1])
        for k in range(1, 4)
    ]

    def join(e, put):
        crossing[e].wait()

        def add(chip, carry):
            put(
                chip,
                (terms[core, e, chip].astype(f32) + theirs[e, chip].astype(f32)).astype(bf16),
            )
            return carry

        lax.fori_loop(0, 8, add, 0)

    def put_own(chip, value):
        own[chip // 2, lax.rem(chip, 2)] = value

    def put_pair(e):
        def put(chip, value):
            pair_ref[e, chip // 2, lax.rem(chip, 2)] = value

        return put

    for e in range(4):
        gate_up_grads = dgu_ref[e]
        active = act_ref[e]

        def chunk(at, carry):
            columns = pl.ds(pl.multiple_of(at * 256, 256), 256)
            in_part = contract(in_ref[e, :, columns], gate_up_grads, 0, 0).astype(bf16)
            out_part = contract(dp_ref[e, :, columns], active, 0, 0).astype(bf16)
            for j in range(4):
                rows = slice(64 * j, 64 * j + 64)
                terms[j % 2, e, 2 * at + j // 2, :, 0:1024] = in_part[rows]
                terms[j % 2, e, 2 * at + j // 2, :, 1024:1536] = out_part[rows]
            return carry

        lax.fori_loop(0, 4, chunk, 0)
        crossing[e].start()
        if e == 1:
            join(0, put_own)
            for copy in first:
                copy.start()
    for e in range(1, 4):
        join(e, put_pair(e - 1))
    for copy in first:
        copy.wait()
    for j in range(2):
        term = own[x, j].astype(f32)
        for k in range(3):
            term = term + got[k, j].astype(f32)
        sum_ref[j] = term.astype(bf16)
    for copy in copies:
        copy.wait()
    own_a.wait()
    own_b.wait()


def scatter_rows(routed_terms, share, d_produced, active, incoming, d_gate_up):
    return pl.pallas_call(
        scatter_kernel,
        out_shape=[
            shape((MP, TOK, 1024)),
            shape((MP, 8, TOK), f32),
            shape((3, 4, 2, 64, 1536)),
            shape((2, 64, 1536)),
        ],
        in_specs=[ANY, ANY, VM, VM, VM, VM],
        out_specs=[ANY, ANY, VM, VM],
        scratch_shapes=[
            pltpu.VMEM((2, 4, 8, 64, 1536), bf16),
            pltpu.VMEM((4, 8, 64, 1536), bf16),
            pltpu.VMEM((3, 2, 64, 1536), bf16),
            pltpu.VMEM((4, 2, 64, 1536), bf16),
        ]
        + [pltpu.SemaphoreType.DMA((MP,))] * 4
        + [pltpu.SemaphoreType.DMA((4,))] * 4
        + [pltpu.SemaphoreType.DMA((2,))],
        compiler_params=pltpu.CompilerParams(
            vmem_limit_bytes=VMEM_LIMIT, collective_id=4, has_side_effects=True
        ),
    )(routed_terms, share, d_produced, active, incoming, d_gate_up)


def outputs_kernel(a_ref, hid_ref, ao, hid_out, s1, r1, loc):
    c, m = place()
    upper = m >= MP // 2
    opposite = (CTX - 1 - c, m)
    mates = [(c, lax.rem(m + k, MP)) for k in range(1, MP)]
    greet(mates + [opposite], MP)
    own_a = pltpu.make_async_copy(a_ref.at[m], ao.at[m], loc.at[0])
    own_a.start()
    copies = []
    for k in range(1, MP):
        to = lax.rem(m + k, MP)
        copies.append(remote(a_ref.at[to], ao.at[m], s1.at[k], r1.at[k], mates[k - 1]))
    for copy in copies:
        copy.start()
    move = remote(hid_ref, hid_out, s1.at[0], r1.at[0], opposite)
    stay = pltpu.make_async_copy(hid_ref, hid_out, loc.at[1])

    @pl.when(upper)
    def _():
        move.start()

    @pl.when(jnp.logical_not(upper))
    def _():
        stay.start()

    for copy in copies:
        copy.wait()
    own_a.wait()

    @pl.when(upper)
    def _():
        move.wait()

    @pl.when(jnp.logical_not(upper))
    def _():
        stay.wait()


def keys_grad_kernel(
    a_ref, out, theirs, pair_a, pair_b, got_a, got_b, sum_a, sum_b, last_a, last_b,
    s0, r0, s1, r1, s2, r2,
):
    c, m = place()
    core = lax.rem(c, 2)
    x, y = c // 4, lax.rem(c // 2, 2)
    sibling = (flip(c, 1), m)
    across = (flip(c, 2), m)
    peers = [(lax.rem(c + 4 * k, CTX), m) for k in range(1, 4)]
    greet(peers + [across, sibling], 5)
    low, high = pl.ds(0, HALF), pl.ds(HALF, HALF)
    crossing = [
        remote(
            a_ref.at[:, :, 1 - core, rows], theirs.at[:, :, rows], s0.at[at], r0.at[at], sibling
        )
        for at, rows in enumerate((high, low))
    ]
    for copy in crossing:
        copy.start()

    def add(a, b):
        return a.astype(f32) + b.astype(f32)

    crossing[0].wait()
    for i in range(4):
        for j in range(2):
            pair_b[i, j] = add(a_ref[i, j, core, high], theirs[i, j, high]).astype(bf16)
    first = [remote(pair_b.at[:, 1 - y], got_b, s1.at[0], r1.at[0], across)]
    first[0].start()
    crossing[1].wait()
    for i in range(4):
        for j in range(2):
            pair_a[i, j] = add(a_ref[i, j, core, low], theirs[i, j, low]).astype(bf16)
    for k in range(1, 4):
        copy = remote(
            pair_a.at[lax.rem(x + k, 4)], got_a.at[k - 1], s1.at[k], r1.at[k], peers[k - 1]
        )
        copy.start()
        first.append(copy)
    first[0].wait()
    for i in range(4):
        sum_b[i] = add(pair_b[i, y], got_b[i]).astype(bf16)
    second = []
    for k in range(1, 4):
        copy = remote(
            sum_b.at[lax.rem(x + k, 4)], last_b.at[k - 1], s2.at[k], r2.at[k], peers[k - 1]
        )
        copy.start()
        second.append(copy)
    for copy in first[1:]:
        copy.wait()
    for j in range(2):
        sum_a[j] = (add(pair_a[x, j], got_a[0, j]) + add(got_a[1, j], got_a[2, j])).astype(bf16)
    copy = remote(sum_a.at[1 - y], last_a, s2.at[0], r2.at[0], across)
    copy.start()
    second.append(copy)
    for copy in second:
        copy.wait()
    out[low] = add(sum_a[y], last_a[...])
    out[high] = add(sum_b[x], last_b[0]) + add(last_b[1], last_b[2])


def keys_grad(terms):
    piece = (HALF, 128)
    return pl.pallas_call(
        keys_grad_kernel,
        out_shape=shape((BLOCK, 128), f32),
        in_specs=[VM],
        out_specs=VM,
        scratch_shapes=[
            pltpu.VMEM((4, 2, BLOCK, 128), bf16),
            pltpu.VMEM((4, 2) + piece, bf16),
            pltpu.VMEM((4, 2) + piece, bf16),
            pltpu.VMEM((3, 2) + piece, bf16),
            pltpu.VMEM((4,) + piece, bf16),
            pltpu.VMEM((2,) + piece, bf16),
            pltpu.VMEM((4,) + piece, bf16),
            pltpu.VMEM(piece, bf16),
            pltpu.VMEM((3,) + piece, bf16),
        ]
        + [pltpu.SemaphoreType.DMA((2,))] * 2
        + [pltpu.SemaphoreType.DMA((4,))] * 4,
        compiler_params=pltpu.CompilerParams(
            vmem_limit_bytes=VMEM_LIMIT, collective_id=6, has_side_effects=True
        ),
    )(terms)


def finish_kernel(
    dq_ref, dkv_ref, cos_ref, sin_ref, normed_ref, br_ref, rows_ref,
    ao, go,
    d_qkv, terms, s1, r1, s2, r2, loc,
):
    c, m = place()
    upper = m >= MP // 2
    t = jnp.where(upper, CTX - 1 - c, c)
    barrier = pltpu.get_barrier_semaphore()
    for k in range(1, MP):
        pl.semaphore_signal(
            barrier, inc=1, device_id=(t, lax.rem(m + k, MP)), device_id_type=MESH
        )
    for k in range(1, CTX):
        pl.semaphore_signal(
            barrier, inc=1, device_id=(lax.rem(c + k, CTX), m), device_id_type=MESH
        )

    @pl.when(upper)
    def _():
        pl.semaphore_signal(barrier, inc=1, device_id=(t, m), device_id_type=MESH)
        pl.semaphore_wait(barrier, MP + CTX - 1)

    @pl.when(jnp.logical_not(upper))
    def _():
        pl.semaphore_wait(barrier, MP + CTX - 2)

    low = lanes(TOK) < HEAD
    for i in range(MP):
        at = i * TOK
        part, inside = at // HALF, at % HALF
        columns = dq_ref[part]
        heads = jnp.concatenate(
            [
                columns[:HEAD, inside : inside + TOK],
                columns[:HEAD, HALF + inside : HALF + inside + TOK],
            ],
            axis=0,
        ).T
        cosine, sine = phase_rows(cos_ref, at, TOK), phase_rows(sin_ref, at, TOK)
        d_qkv[i, :, 0:128] = turn_back(heads * score_scale, cosine, sine).astype(bf16)
        dkv = dkv_ref[at : at + TOK]
        d_qkv[i, :, 128:256] = jnp.where(low, turn_back(dkv, cosine, sine), dkv).astype(bf16)

    own_a = pltpu.make_async_copy(d_qkv.at[m], ao.at[m], loc.at[1])
    a_copies, g_copies = [], []
    for k in range(MP):
        to = lax.rem(m + k, MP)
        target = (jnp.where(to >= MP // 2, CTX - 1 - c, c), to)
        a_copies.append(remote(d_qkv.at[to], ao.at[m], s1.at[k], r1.at[k], target))

    @pl.when(upper)
    def _():
        a_copies[0].start()

    @pl.when(jnp.logical_not(upper))
    def _():
        own_a.start()

    for k in range(1, MP):
        a_copies[k].start()
    grads = d_qkv[...].reshape(BLOCK, 256)
    columns = jnp.concatenate(
        [
            contract(grads, normed_ref[...], 0, 0),
            contract(rows_ref[...], br_ref[...], 0, 0),
        ],
        axis=0,
    )
    terms[...] = columns.T.astype(bf16).reshape(terms.shape)
    own_g = pltpu.make_async_copy(terms.at[c], go.at[c], loc.at[0])
    own_g.start()
    for k in range(1, CTX):
        to = lax.rem(c + k, CTX)
        copy = remote(terms.at[to], go.at[c], s2.at[k], r2.at[k], (to, m))
        copy.start()
        g_copies.append(copy)
    for k in range(1, MP):
        a_copies[k].wait()
    for copy in g_copies:
        copy.wait()
    own_g.wait()

    @pl.when(upper)
    def _():
        a_copies[0].wait()

    @pl.when(jnp.logical_not(upper))
    def _():
        own_a.wait()


def finish(dq, dkv, cosine, sine, normed, branch_rows, out_rows):
    return pl.pallas_call(
        finish_kernel,
        out_shape=[
            shape((MP, TOK, 256)),
            shape((CTX, 64, 384)),
        ],
        in_specs=[VM] * 7,
        out_specs=[ANY] * 2,
        scratch_shapes=[
            pltpu.VMEM((MP, TOK, 256), bf16),
            pltpu.VMEM((CTX, 64, 384), bf16),
        ]
        + [pltpu.SemaphoreType.DMA((n,)) for n in (MP, MP, CTX, CTX, 2)],
        compiler_params=pltpu.CompilerParams(
            vmem_limit_bytes=VMEM_LIMIT, collective_id=8, has_side_effects=True
        ),
    )(dq, dkv, cosine, sine, normed, branch_rows, out_rows)


def sums_kernel(
    small_ref, qg_ref, qw_ref, x_ref, gain_ref, hid_ref, w_ref, y_ref,
    out, ig_ref, wq_ref, wk_ref, wv_ref, wo_ref, y_out,
    terms, got, part, got2, s1, r1, s2, r2, loc,
):
    c, m = place()
    upper = m >= MP // 2
    move = remote(y_ref, y_out, s1.at[0], r1.at[0], (CTX - 1 - c, m))
    stay = pltpu.make_async_copy(y_ref, y_out, loc)
    peers = [(lax.rem(c + k, CTX), m) for k in range(1, CTX)]
    mates = [(c, lax.rem(m + k, MP)) for k in range(1, MP)]
    barrier = pltpu.get_barrier_semaphore()
    for target in peers + mates:
        pl.semaphore_signal(barrier, inc=1, device_id=target, device_id_type=MESH)
    grads = contract(qg_ref[0], qw_ref[0], 1, 1)
    for h in range(1, MP):
        grads = grads + contract(qg_ref[h], qw_ref[h], 1, 1)
    x = x_ref[...].astype(f32)
    inverse = lax.rsqrt(jnp.mean(x * x, axis=1, keepdims=True) + epsilon)
    scaled = x * inverse
    inner = grads * gain_ref[...]
    gain_grad = jnp.sum(grads * scaled, axis=0, keepdims=True)
    columns = jnp.broadcast_to(gain_grad, (128, 1024)).T
    terms[...] = jnp.where(lanes(1024) == 32, columns, small_ref[...]).reshape(terms.shape)
    pl.semaphore_wait(barrier, CTX - 1 + MP - 1)
    copies = []
    for k in range(1, CTX):
        to = lax.rem(c + k, CTX)
        copy = remote(terms.at[to], got.at[k], s1.at[k], r1.at[k], peers[k - 1])
        copy.start()
        copies.append(copy)

    @pl.when(upper)
    def _():
        move.start()

    @pl.when(jnp.logical_not(upper))
    def _():
        stay.start()

    ig = inverse * (inner - scaled * jnp.mean(inner * scaled, axis=1, keepdims=True))
    ig_ref[...] = (ig + hid_ref[...].astype(f32)).astype(bf16)
    weights = w_ref[0].astype(f32)
    for k in range(1, CTX):
        weights = weights + w_ref[k].astype(f32)
    wq_ref[...] = weights[:, :128]
    wk_ref[...] = weights[:, 128:192]
    wv_ref[...] = weights[:, 192:256]
    wo_ref[...] = weights[:, 256:].T
    total = terms[c]
    for copy in copies:
        copy.wait()
    for k in range(1, CTX):
        total = total + got[k]
    part[...] = total
    copies = []
    for k in range(1, MP):
        to = lax.rem(m + k, MP)
        copy = remote(part.at[to], got2.at[k], s2.at[k], r2.at[k], mates[k - 1])
        copy.start()
        copies.append(copy)
    last = part[m]
    for copy in copies:
        copy.wait()
    for k in range(1, MP):
        last = last + got2[k]
    out[...] = last

    @pl.when(upper)
    def _():
        move.wait()

    @pl.when(jnp.logical_not(upper))
    def _():
        stay.wait()


def last_sums(small, qkv_got, qkv_w_all, x, gain, hidden_grad, w_got, outputs):
    dims = (8, 128)
    return pl.pallas_call(
        sums_kernel,
        out_shape=[
            shape(dims, f32),
            shape((TOK, 1024)),
            shape((64, 128), f32),
            shape((64, 64), f32),
            shape((64, 64), f32),
            shape((128, 64), f32),
            shape((TOK, 1024)),
        ],
        in_specs=[VM] * 7 + [ANY],
        out_specs=[VM] * 6 + [ANY],
        scratch_shapes=[
            pltpu.VMEM((CTX, MP) + dims, f32),
            pltpu.VMEM((CTX, MP) + dims, f32),
            pltpu.VMEM((MP,) + dims, f32),
            pltpu.VMEM((MP,) + dims, f32),
            pltpu.SemaphoreType.DMA((CTX,)),
            pltpu.SemaphoreType.DMA((CTX,)),
            pltpu.SemaphoreType.DMA((MP,)),
            pltpu.SemaphoreType.DMA((MP,)),
            pltpu.SemaphoreType.DMA,
        ],
        compiler_params=pltpu.CompilerParams(
            vmem_limit_bytes=VMEM_LIMIT, collective_id=9, has_side_effects=True
        ),
    )(small, qkv_got, qkv_w_all, x, gain, hidden_grad, w_got, outputs)


def unit(index, first_half):
    second = index > first_half
    part = second.astype(jnp.int32)
    key_half = jnp.where(second, index - first_half - 1, index)
    odd = lax.rem(key_half, 2) == 1
    slot = jnp.where(odd, 2 * CTX - key_half, key_half)
    diagonal = jnp.logical_or(index == first_half, index == 2 * CTX)
    return part, slot, diagonal


def visible_mask(rows):
    key_at = lax.broadcasted_iota(jnp.int32, (HALF, rows), 0)
    query_at = lax.rem(lax.broadcasted_iota(jnp.int32, (HALF, rows), 1), HALF)
    return key_at <= query_at


def forward_kernel(
    q_ref, kv_ref, in_ref, qw_ref, rows_ref,
    out_ref, rows_out, lse_ref, in_all, qw_all, rows_all,
    best, total, summed, *sems,
):
    first_half = 2 * lax.axis_index("ctx")
    greet(ctx_neighbours() + mp_neighbours(), 7)
    weights_rings = [ctx_ring(in_ref, row_slots(in_all), sems[0:5])]
    rows_rings = [
        shared_ring(rows_ref, rows_all, sems[5:10]),
        shared_ring(qw_ref, qw_all, sems[10:15]),
    ]
    for ring in weights_rings + rows_rings:
        ring.start()
    best[...] = jnp.full(best.shape, -1e30, f32)
    total[...] = jnp.zeros(total.shape, f32)
    summed[...] = jnp.zeros(summed.shape, f32)

    def work(part, slot, masked):
        kv = kv_ref[slot]
        scores = contract(kv, q_ref[part], 1, 1)
        if masked:
            scores = jnp.where(visible_mask(scores.shape[1]), scores, -jnp.inf)
        old = best[part]
        new = jnp.maximum(old, jnp.max(scores, axis=0, keepdims=True))
        weights = jnp.exp2(scores * log2_e - new * log2_e)
        fading = jnp.exp2((old - new) * log2_e)
        total[part] = total[part] * fading + jnp.sum(weights, axis=0, keepdims=True)
        summed[part] = summed[part] * fading + contract(kv, weights.astype(bf16), 0, 0)
        best[part] = new

    def step(index, carry):
        part, slot, diagonal = unit(index, first_half)

        @pl.when(index == 11)
        def _():
            for ring in weights_rings:
                ring.relay_near()
                ring.relay_own()

        @pl.when(index == 16)
        def _():
            for ring in rows_rings:
                ring.relay_near()
                ring.relay_own()

        @pl.when(index == 24)
        def _():
            for ring in rows_rings:
                ring.relay_far()

        @pl.when(index == 25)
        def _():
            for ring in weights_rings:
                ring.relay_far()

        @pl.when(diagonal)
        def _():
            work(part, slot, True)

        @pl.when(jnp.logical_not(diagonal))
        def _():
            work(part, slot, False)

        return carry

    lax.fori_loop(0, 2 * CTX + 1, step, 0)
    for part in range(2):
        columns = summed[part][HEAD:, :] / total[part]
        heads = jnp.concatenate([columns[:, :HALF], columns[:, HALF:]], axis=0).T
        out_ref[part * HALF : part * HALF + HALF] = heads
        rows_out[part * HALF : part * HALF + HALF] = heads.astype(bf16)
        lse_ref[part] = best[part] + jnp.log(total[part])
    for ring in weights_rings + rows_rings:
        ring.finish()


def attention(q_rows, kv_all, w_in, qkv_w, out_rows_w):
    rows = q_rows.shape[1]
    return pl.pallas_call(
        forward_kernel,
        out_shape=[
            shape((BLOCK, 128), f32),
            shape((BLOCK, 128)),
            shape((2, 1, rows), f32),
            shape((4, 1024, 1024)),
            shape((MP,) + qkv_w.shape),
            shape((MP, TOK, 1024)),
        ],
        in_specs=[VM, VM, ANY, ANY, ANY],
        out_specs=[VM, VM, VM, ANY, ANY, ANY],
        scratch_shapes=[
            pltpu.VMEM((2, 1, rows), f32),
            pltpu.VMEM((2, 1, rows), f32),
            pltpu.VMEM((2, 2 * HEAD, rows), f32),
        ]
        + CTX_SEMS * 3,
        compiler_params=pltpu.CompilerParams(
            vmem_limit_bytes=VMEM_LIMIT, collective_id=10, has_side_effects=True
        ),
        cost_estimate=pl.CostEstimate(
            flops=33 * 4 * HALF * rows * 256, bytes_accessed=1 << 23, transcendentals=33 * HALF * rows
        ),
    )(q_rows, kv_all, w_in, qkv_w, out_rows_w)


def backward_kernel(
    q_ref, og_ref, att_ref, lse_ref, kv_ref, sum_0, pair_ref, br_ref, mixed_ref,
    dkv_ref, dq_ref, in_grad, out_grad, br_all, mixed_out,
    total, do_ref, delta_ref, own_a, own_b, got_a, got_b, sum_a, sum_b, last_0, last_a, last_b,
    *sems,
):
    c, m = place()
    first_half = 2 * c
    x, y = c // 4, lax.rem(c // 2, 2)
    peers = [(lax.rem(c + 4 * k, CTX), m) for k in range(1, 4)]
    across = (flip(c, 2), m)
    mates = [(c, lax.rem(m + k, MP)) for k in range(1, MP)]
    greet(peers + [across] + mates, 4 + MP - 1)
    sa, ra, sb, rb, sm, rm, loc = sems[:7]
    ring = mp_ring(br_ref, slots(br_all), sems[7:10])

    def first_copies():
        copies = [
            remote(
                pair_ref.at[pl.ds(0, 2), lax.rem(x + k, 4)],
                got_a.at[k - 1], sa.at[k], ra.at[k], peers[k - 1],
            )
            for k in range(1, 4)
        ]
        copies.append(remote(pair_ref.at[2, :, 1 - y], got_b, sa.at[0], ra.at[0], across))
        return copies

    def own_copies():
        return [
            pltpu.make_async_copy(pair_ref.at[pl.ds(0, 2), x], own_a, loc.at[1]),
            pltpu.make_async_copy(pair_ref.at[2, :, y], own_b, loc.at[2]),
        ]

    def sum_0_copy():
        return remote(sum_0.at[1 - y], last_0, sb.at[0], rb.at[0], across)

    def second_copies():
        copies = [
            remote(
                sum_b.at[lax.rem(x + k, 4)], last_b.at[k - 1], sb.at[k], rb.at[k], peers[k - 1]
            )
            for k in range(1, 4)
        ]
        copies.append(remote(sum_a.at[:, 1 - y], last_a, sb.at[4], rb.at[4], across))
        return copies

    def middle():
        for copy in first_copies() + own_copies():
            copy.wait()
        for e in range(2):
            for j in range(2):
                term = own_a[e, j].astype(f32)
                for k in range(3):
                    term = term + got_a[k, e, j].astype(f32)
                sum_a[e, j] = term.astype(bf16)
        for j in range(4):
            sum_b[j] = (own_b[j].astype(f32) + got_b[j].astype(f32)).astype(bf16)
        for copy in second_copies():
            copy.start()

    def mixed_copies():
        copies = []
        for k in range(1, MP):
            to = lax.rem(m + k, MP)
            copies.append(
                remote(mixed_ref.at[to], mixed_out.at[m], sm.at[k], rm.at[k], mates[k - 1])
            )
        return copies

    def own_mixed():
        return pltpu.make_async_copy(mixed_ref.at[m], mixed_out.at[m], loc.at[0])

    ring.start()
    for copy in first_copies() + own_copies() + [sum_0_copy()]:
        copy.start()
    low = lanes(HALF) < HEAD
    for part in range(2):
        rows = slice(part * HALF, part * HALF + HALF)
        grads = og_ref[rows].astype(f32)
        product = (grads * att_ref[rows]).T
        delta_ref[part, :, 0:HALF] = jnp.sum(product[:HEAD], axis=0, keepdims=True)
        delta_ref[part, :, HALF:] = jnp.sum(product[HEAD:], axis=0, keepdims=True)
        do_ref[part, 0:HALF] = jnp.where(low, 0.0, pltpu.roll(grads, HEAD, 1)).astype(bf16)
        do_ref[part, HALF:] = jnp.where(low, 0.0, grads).astype(bf16)
    dq_ref[...] = jnp.zeros(dq_ref.shape, f32)

    def clear(index, carry):
        total[index] = jnp.zeros(total.shape[1:], f32)
        return carry

    lax.fori_loop(0, 2 * CTX, clear, 0)

    def work(part, slot, masked):
        kv = kv_ref[slot]
        queries = q_ref[part]
        grads = do_ref[part]
        scores = contract(kv, queries, 1, 1)
        probs = jnp.exp2((scores - lse_ref[part]) * log2_e)
        if masked:
            probs = jnp.where(visible_mask(scores.shape[1]), probs, 0.0)
        prob_grad = contract(kv, grads, 1, 1)
        score_grad = (probs * (prob_grad - delta_ref[part])).astype(bf16)
        total[slot] += contract(probs.astype(bf16), grads, 1, 0) + contract(
            score_grad, queries, 1, 0
        )
        dq_ref[part] += contract(kv, score_grad, 0, 0)

    def step(index, carry):
        part, slot, diagonal = unit(index, first_half)

        @pl.when(index == 1)
        def _():
            own_mixed().start()
            for copy in mixed_copies():
                copy.start()

        @pl.when(index == 18)
        def _():
            ring.relay_near()
            ring.relay_own()

        @pl.when(index == 25)
        def _():
            middle()

        @pl.when(index == 27)
        def _():
            ring.relay_far()

        @pl.when(diagonal)
        def _():
            work(part, slot, True)

        @pl.when(jnp.logical_not(diagonal))
        def _():
            work(part, slot, False)

        return carry

    lax.fori_loop(0, 2 * CTX + 1, step, 0)

    def write(index, carry):
        dkv_ref[index] = total[index].astype(bf16)
        return carry

    lax.fori_loop(0, 2 * CTX, write, 0)
    ring.finish()
    sum_0_copy().wait()
    for copy in second_copies():
        copy.wait()

    def put(at, term):
        in_grad[at] = term[:, :1024]
        out_grad[at] = term[:, 1024:].T

    put(0, sum_0[y].astype(f32) + last_0[...].astype(f32))
    for e in range(2):
        put(1 + e, sum_a[e, y].astype(f32) + last_a[e].astype(f32))
    term = sum_b[x].astype(f32)
    for k in range(3):
        term = term + last_b[k].astype(f32)
    put(3, term)
    for copy in mixed_copies():
        copy.wait()
    own_mixed().wait()


def attention_back(
    q_rows, out_grad, attended, lse, kv_all, sum_first, pair, branch_grad, mixed
):
    rows = q_rows.shape[1]
    wide = pair.shape[-1]
    return pl.pallas_call(
        backward_kernel,
        out_shape=[
            shape(kv_all.shape, bf16),
            shape((2, 2 * HEAD, rows), f32),
            shape((4, 64, 1024), f32),
            shape((4, 512, 64), f32),
            shape((MP, TOK, 1024)),
            shape((MP, TOK, 1024)),
        ],
        in_specs=[VM] * 6 + [ANY] * 3,
        out_specs=[VM] * 4 + [ANY] * 2,
        scratch_shapes=[
            pltpu.VMEM(kv_all.shape, f32),
            pltpu.VMEM(q_rows.shape, bf16),
            pltpu.VMEM((2, 1, rows), f32),
            pltpu.VMEM((2, 2, 64, wide), bf16),
            pltpu.VMEM((4, 64, wide), bf16),
            pltpu.VMEM((3, 2, 2, 64, wide), bf16),
            pltpu.VMEM((4, 64, wide), bf16),
            pltpu.VMEM((2, 2, 64, wide), bf16),
            pltpu.VMEM((4, 64, wide), bf16),
            pltpu.VMEM((64, wide), bf16),
            pltpu.VMEM((2, 64, wide), bf16),
            pltpu.VMEM((3, 64, wide), bf16),
        ]
        + [pltpu.SemaphoreType.DMA((4,))] * 2
        + [pltpu.SemaphoreType.DMA((5,))] * 2
        + [pltpu.SemaphoreType.DMA((MP,))] * 2
        + [pltpu.SemaphoreType.DMA((3,))]
        + MP_SEMS,
        compiler_params=pltpu.CompilerParams(
            vmem_limit_bytes=VMEM_LIMIT, collective_id=11, has_side_effects=True
        ),
        cost_estimate=pl.CostEstimate(
            flops=33 * 10 * HALF * rows * 256, bytes_accessed=1 << 24, transcendentals=33 * HALF * rows
        ),
    )(q_rows, out_grad, attended, lse, kv_all, sum_first, pair, branch_grad, mixed)


def phases(positions, head_width):
    steps_up = jnp.arange(head_width // 2).astype(f32)
    frequency = rope_base ** (-2.0 * steps_up / head_width)
    angles = frequency[:, None] * positions.astype(f32)[None, :]
    return (jnp.cos(angles), jnp.sin(angles))


def normalize(values):
    inverse = lax.rsqrt(jnp.mean(values * values, axis=-1, keepdims=True) + epsilon)
    return (values * inverse, inverse)


def norm_back(grads, scaled, inverse, gain):
    inner = grads * gain
    return (
        inverse * (inner - scaled * jnp.mean(inner * scaled, axis=-1, keepdims=True)),
        jnp.sum(grads * scaled, axis=0),
    )


def swap_home(array):
    pairs = []
    for c in range(CTX):
        for m in range(MP):
            t = CTX - 1 - c if m >= MP // 2 else c
            pairs.append((c * MP + m, t * MP + m))
    return lax.ppermute(array, ("ctx", "mp"), pairs)


def body(
    layer_input,
    positions,
    expert_ids,
    attn_gain,
    w_query,
    w_key,
    w_value,
    w_attn_out,
    ffn_gain,
    router,
    w_in,
    w_out,
    cotangent,
):
    c, m = place()
    dy_swapped = swap_home(cotangent)
    own_positions = lax.dynamic_slice_in_dim(positions, m * TOK, TOK, 0)
    id_pack = jnp.concatenate(
        [expert_ids.T, own_positions[None, :], jnp.zeros((7, TOK), jnp.int32)], axis=0
    )
    w_pack = jnp.concatenate(
        [
            w_query,
            w_key,
            w_value,
            router,
            attn_gain[:, None],
            ffn_gain[:, None],
            jnp.zeros((64, 94), bf16),
            w_attn_out.T,
        ],
        axis=1,
    )
    x_all, id_all, w_all = comm_call(
        start_kernel,
        1,
        [layer_input, id_pack, w_pack],
        [
            shape((MP, TOK, 1024)),
            shape((MP, 16, TOK), jnp.int32),
            shape((CTX, 64, 512)),
        ],
        [2, 2, 2] + CTX_SEMS + MP_SEMS * 2,
        4 << 20,
    )
    inputs = x_all.reshape(BLOCK, 1024).astype(f32)
    ids = id_all[:, :8, :].transpose(1, 0, 2).reshape(8, BLOCK)
    places = id_all[:, 8, :].reshape(BLOCK)
    w_all = w_all.reshape(1024, 512)
    qkv_w = w_all[:, :256]
    router_w = w_all[:, 256:288]
    gain_one = w_all[:, 288].astype(f32)
    gain_two = w_all[:, 289].astype(f32)
    out_w = w_all[:, 384:].T

    cosine, sine = lax.optimization_barrier(phases(places, HEAD))
    normed, q_rows, kv_all, dy_all = keys_and_values(
        x_all.reshape(BLOCK, 1024), gain_one[None, :], qkv_w, cosine, sine, dy_swapped
    )
    kv_all = kv_all.reshape(2 * CTX, HALF, 128)
    attended, out_rows, lse, in_w, qkv_w_all, out_w_all = attention(
        q_rows, kv_all, w_in, qkv_w, out_w
    )
    dy_all = dy_all.reshape(BLOCK, 1024)
    rows_all, out_w_t = comm_call(
        gather_kernel,
        3,
        [out_rows, w_out.transpose(0, 2, 1)],
        [shape((MP, BLOCK, 128)), shape((4, 1024, 512))],
        MP_SEMS + CTX_SEMS,
        8 << 20,
    )
    branch = lax.dot_general(
        rows_all, out_w_all, (((0, 2), (0, 1)), ((), ())), preferred_element_type=f32
    )
    hidden = inputs + branch_scale * branch
    scaled_two, inverse_two = normalize(hidden)
    routed = (scaled_two * gain_two).astype(bf16)

    logits = contract(router_w, routed, 0, 1)
    experts = lax.broadcasted_iota(jnp.int32, (32, BLOCK), 0)
    member = jnp.any(ids[:, None, :] == experts[None], axis=0)
    chosen = jnp.where(member, logits, -jnp.inf)
    top_logit = jnp.max(chosen, axis=0, keepdims=True)
    powers = jnp.exp(chosen - top_logit)
    gates = powers / jnp.sum(powers, axis=0, keepdims=True)

    here = 4 * m + lax.broadcasted_iota(jnp.int32, (4, BLOCK), 0)
    selected = jnp.any(ids[:, None, :] == here[None], axis=0)
    earlier = (
        lax.broadcasted_iota(jnp.int32, (BLOCK, BLOCK), 0)
        <= lax.broadcasted_iota(jnp.int32, (BLOCK, BLOCK), 1)
    ).astype(bf16)
    counts = jnp.dot(selected.astype(bf16), earlier, preferred_element_type=f32)
    rank = jnp.where(selected, counts.astype(jnp.int32) - 1, -1)
    capacity = 288
    place_bool = rank[:, None, :] == lax.broadcasted_iota(jnp.int32, (4, capacity, BLOCK), 1)
    placing = place_bool.astype(bf16).reshape(4 * capacity, BLOCK)
    gates_here = lax.dynamic_slice_in_dim(gates, 4 * m, 4, 0)
    slot_gate = jnp.sum(jnp.where(place_bool, gates_here[:, None, :], 0.0), axis=2)

    incoming = jnp.dot(placing, routed, preferred_element_type=f32).astype(bf16)
    incoming = incoming.reshape(4, capacity, 1024)
    dy_rows = jnp.dot(placing, dy_all, preferred_element_type=f32).reshape(4, capacity, 1024)
    gate_up = jnp.einsum("esd,edf->esf", incoming, in_w, preferred_element_type=f32)
    gate_part, up_part = gate_up[..., :512], gate_up[..., 512:]
    squashed = jax.nn.sigmoid(gate_part)
    silu_part = gate_part * squashed
    active = (silu_part * up_part).astype(bf16)
    produced = jnp.einsum(
        "esf,edf->esd", active, out_w_t, preferred_element_type=f32
    ).astype(bf16)
    produced_f = produced.astype(f32)
    d_produced = (branch_scale * slot_gate[..., None] * dy_rows).astype(bf16)
    slot_share = branch_scale * jnp.sum(dy_rows * produced_f, axis=2)
    weighted = (slot_gate[..., None] * produced_f).astype(bf16).reshape(4 * capacity, 1024)
    mixed = branch_scale * contract(placing, weighted, 0, 0)
    mixed = mixed.astype(bf16).reshape(MP, TOK, 1024)

    d_active = jnp.einsum("esd,edf->esf", d_produced, out_w_t, preferred_element_type=f32)
    slope = squashed * (1.0 + gate_part * (1.0 - squashed))
    d_gate_up = jnp.concatenate(
        [d_active * up_part * slope, d_active * silu_part], axis=-1
    ).astype(bf16)
    d_gate_up = lax.optimization_barrier(d_gate_up)
    row_grads = jnp.einsum(
        "esf,edf->esd", d_gate_up, in_w, preferred_element_type=f32
    ).astype(bf16)
    row_grads = lax.optimization_barrier(row_grads)
    routed_terms = contract(placing, row_grads.reshape(4 * capacity, 1024), 0, 0)
    routed_terms = routed_terms.astype(bf16).reshape(MP, TOK, 1024)
    share = jnp.sum(jnp.where(place_bool, slot_share[:, :, None], 0.0), axis=1)
    share = jnp.pad(share.reshape(4, MP, TOK).transpose(1, 0, 2), ((0, 0), (0, 4), (0, 0)))
    routed_got, share_got, pair, sum_first = scatter_rows(
        routed_terms, share, d_produced, active, incoming, d_gate_up
    )

    def own_rows(array):
        return lax.dynamic_slice_in_dim(array, m * TOK, TOK, 0)

    hidden_own = own_rows(hidden)
    scaled_own, inverse_own = normalize(hidden_own)
    routed_own = (scaled_own * gain_two).astype(bf16).astype(f32)
    dy_own = own_rows(dy_all).astype(f32)
    gates_own = lax.dynamic_slice_in_dim(gates, m * TOK, TOK, 1)
    share_own = share_got[:, :4, :].reshape(32, TOK)
    logit_grad = gates_own * (
        share_own - jnp.sum(gates_own * share_own, axis=0, keepdims=True)
    )
    routed_grad = jnp.sum(routed_got.astype(f32), axis=0) + lax.dot_general(
        logit_grad,
        router_w.astype(f32),
        (((0,), (1,)), ((), ())),
        precision=highest,
        preferred_element_type=f32,
    )
    router_grad = lax.dot_general(
        routed_own,
        logit_grad,
        (((0,), (1,)), ((), ())),
        precision=highest,
        preferred_element_type=f32,
    )
    hidden_grad, gain_two_grad = norm_back(routed_grad, scaled_own, inverse_own, gain_two)
    hidden_grad = hidden_grad + dy_own
    branch_grad = (branch_scale * hidden_grad).astype(bf16)

    out_grad_terms = jnp.einsum(
        "td,hfd->htf", branch_grad, out_w_all, preferred_element_type=f32
    ).astype(bf16)
    out_grad, hidden_grad_home = comm_call(
        outputs_kernel,
        5,
        [out_grad_terms, hidden_grad.astype(bf16)],
        [shape((MP, TOK, 128)), shape((TOK, 1024))],
        [MP, MP, 2],
        1 << 20,
    )
    out_grad = out_grad.reshape(BLOCK, 128)

    dkv_terms, dq_cols, expert_in, expert_out, branch_rows, mixed_got = attention_back(
        q_rows, out_grad, attended, lse, kv_all, sum_first, pair, branch_grad, mixed
    )
    outputs = (hidden_own + jnp.sum(mixed_got.astype(f32), axis=0)).astype(bf16)
    dkv = keys_grad(dkv_terms.reshape(4, 2, 2, BLOCK, 128))
    qkv_got, w_got = finish(
        dq_cols,
        dkv,
        cosine,
        sine,
        normed,
        branch_rows.reshape(BLOCK, 1024),
        out_rows,
    )
    small = jnp.concatenate(
        [
            router_grad,
            jnp.zeros((1024, 1), f32),
            gain_two_grad[:, None],
            jnp.zeros((1024, 94), f32),
        ],
        axis=1,
    )
    sums, input_grad, query_grad, key_grad, value_grad, attn_out_grad, outputs = last_sums(
        small,
        qkv_got,
        qkv_w_all,
        layer_input,
        gain_one[None, :],
        hidden_grad_home,
        w_got,
        outputs,
    )
    return (
        outputs,
        input_grad,
        sums[:, 32],
        query_grad,
        key_grad,
        value_grad,
        attn_out_grad,
        sums[:, 33],
        sums[:, :32],
        expert_in,
        expert_out,
    )


def solution(mesh):
    placed = (
        P(("ctx", "mp"), None),
        P("ctx"),
        P(("ctx", "mp"), None),
        P("ctx"),
        P("ctx", "mp"),
        P("ctx", "mp"),
        P("ctx", "mp"),
        P("mp", "ctx"),
        P("ctx"),
        P("ctx", None),
        P("mp", "ctx", None),
        P("mp", None, "ctx"),
        P(("ctx", "mp"), None),
    )
    return jax.shard_map(
        body,
        mesh=mesh,
        in_specs=placed,
        out_specs=(
            P(("ctx", "mp"), None),
            P(("ctx", "mp"), None),
            P(("ctx", "mp")),
            P("ctx", "mp"),
            P("ctx", "mp"),
            P("ctx", "mp"),
            P("mp", "ctx"),
            P(("ctx", "mp")),
            P(("ctx", "mp"), None),
            P("mp", "ctx", None),
            P("mp", None, "ctx"),
        ),
        check_vma=False,
    )
```

```python
import functools

import jax
import jax.numpy as jnp
from jax import lax
from jax.experimental import pallas as pl
from jax.experimental.pallas import tpu as pltpu
from jax.sharding import PartitionSpec as P

MESH = pl.DeviceIdType.MESH
epsilon = 1e-06
branch_scale = 0.22
score_scale = 0.015625
rope_base = 10000.0
highest = lax.Precision.HIGHEST
log2_e = 1.4426950408889634
bf16 = jnp.bfloat16
f32 = jnp.float32
CTX, MP = 16, 8
HEAD = 64
TOK = 128
BLOCK = 1024
HALF = 512
ANY = pl.BlockSpec(memory_space=pl.ANY)
VM = pl.BlockSpec(memory_space=pltpu.VMEM)
VMEM_LIMIT = 56 * 1024 * 1024


def contract(left, right, left_dim, right_dim):
    return lax.dot_general(
        left, right, (((left_dim,), (right_dim,)), ((), ())), preferred_element_type=f32
    )


def place():
    return lax.axis_index("ctx"), lax.axis_index("mp")


def greet(signal_to, expected):
    barrier = pltpu.get_barrier_semaphore()
    for target in signal_to:
        pl.semaphore_signal(barrier, inc=1, device_id=target, device_id_type=MESH)
    pl.semaphore_wait(barrier, expected)


def remote(src, dst, send, recv, target):
    return pltpu.make_async_remote_copy(
        src_ref=src, dst_ref=dst, send_sem=send, recv_sem=recv,
        device_id=target, device_id_type=MESH,
    )


def comm_call(kernel, number, arrays, outs, sems, cost):
    return pl.pallas_call(
        kernel,
        out_shape=outs,
        in_specs=[ANY] * len(arrays),
        out_specs=[ANY] * len(outs),
        scratch_shapes=[
            pltpu.SemaphoreType.DMA((n,)) if isinstance(n, int) else n for n in sems
        ],
        compiler_params=pltpu.CompilerParams(collective_id=number, has_side_effects=True),
        cost_estimate=pl.CostEstimate(flops=0, bytes_accessed=cost, transcendentals=0),
    )(*arrays)


def shape(dims, kind=bf16):
    return jax.ShapeDtypeStruct(dims, kind)


def flip(index, stride):
    return index + stride - 2 * stride * lax.rem(index // stride, 2)


class Ring:
    def __init__(self, own, dst, index, spread, near, stride, target, sems, sibling=None):
        send, recv, loc = sems[:3]
        count = spread
        plus, minus = lax.rem(index + stride, count), lax.rem(index + count - stride, count)
        far = lax.rem(index + 2 * stride, count)
        near_of = lambda slot: flip(slot, near)
        me_near = near_of(index)

        def copy(src, place_of, at, to):
            return lambda: remote(src, place_of, send.at[at], recv.at[at], target(to))

        def relay(slot, part, at, to):
            return copy(dst(slot, part), dst(slot, part), at, to)

        self.own = None
        if own is not None:
            self.own = lambda: pltpu.make_async_copy(own, dst(index, None), loc)
        own = dst(index, None) if own is None else own
        self.to_near = copy(own, dst(index, None), 0, me_near)
        self.plus_own = copy(own, dst(index, None), 1, plus)
        self.minus_own = copy(own, dst(index, None), 2, minus)
        self.plus_near = relay(me_near, None, 3, plus)
        self.minus_near = relay(me_near, None, 4, minus)
        self.plus_far = relay(minus, 0, 5, plus)
        self.minus_far = relay(plus, 1, 6, minus)
        self.plus_far_near = relay(near_of(minus), 0, 7, plus)
        self.minus_far_near = relay(near_of(plus), 1, 8, minus)
        self.over = None
        if sibling is not None:
            send2, recv2 = sems[3:]
            parts = [
                (index, None),
                (me_near, None),
                (minus, None),
                (plus, None),
                (near_of(minus), None),
                (near_of(plus), None),
                (far, 0),
                (far, 1),
                (near_of(far), 0),
                (near_of(far), 1),
            ]

            def over(at):
                slot, part = parts[at]
                src = own if at == 0 else dst(slot, part)
                return remote(src, dst(slot, part), send2.at[at], recv2.at[at], sibling)

            self.over = over

    def cross(self, *numbers):
        if self.over is not None:
            for at in numbers:
                self.over(at).start()

    def start(self):
        if self.own is not None:
            self.own().start()
        for copy in (self.to_near, self.plus_own, self.minus_own):
            copy().start()
        self.cross(0)

    def relay_near(self):
        self.to_near().wait_recv()
        self.plus_near().start()
        self.minus_near().start()
        self.cross(1)

    def relay_own(self):
        self.plus_own().wait_recv()
        self.plus_far().start()
        self.minus_own().wait_recv()
        self.minus_far().start()
        self.cross(2, 3)

    def relay_far(self):
        self.plus_near().wait_recv()
        self.plus_far_near().start()
        self.minus_near().wait_recv()
        self.minus_far_near().start()
        self.cross(4, 5)

    def finish(self):
        last = (self.plus_far, self.minus_far, self.plus_far_near, self.minus_far_near)
        for number, copy in enumerate(last):
            copy().wait_recv()
            self.cross(6 + number)
        for copy in (
            self.to_near,
            self.plus_own,
            self.minus_own,
            self.plus_near,
            self.minus_near,
        ) + last:
            copy().wait_send()
        if self.over is not None:
            for at in range(10):
                self.over(at).wait()
        if self.own is not None:
            self.own().wait()


def mp_ring(own, dst, sems):
    c, m = place()
    return Ring(own, dst, m, MP, 1, 2, lambda slot: (c, slot), sems)


def shared_ring(own, out, sems):
    c, m = place()
    half = own.shape[0] // 2
    first = pl.multiple_of(lax.rem(c, 2) * half, half)

    def dst(slot, part):
        if part is None:
            return out.at[slot, pl.ds(first, half)]
        return out.at[slot, pl.ds(first + part * (half // 2), half // 2)]

    mine = own.at[pl.ds(first, half)]
    return Ring(mine, dst, m, MP, 1, 2, lambda slot: (c, slot), sems, (flip(c, 1), m))


def ctx_ring(own, dst, sems):
    c, m = place()
    return Ring(own, dst, c, CTX, 2, 4, lambda slot: (slot, m), sems, (flip(c, 1), m))


def mp_neighbours():
    c, m = place()
    return [(c, flip(m, 1)), (c, lax.rem(m + 2, MP)), (c, lax.rem(m + 6, MP))]


def ctx_neighbours():
    c, m = place()
    return [
        (flip(c, 2), m),
        (lax.rem(c + 4, CTX), m),
        (lax.rem(c + 12, CTX), m),
        (flip(c, 1), m),
    ]


def slots(ref):
    half = ref.shape[1] // 2

    def dst(slot, part):
        return ref.at[slot] if part is None else ref.at[slot, pl.ds(part * half, half)]

    return dst


def row_slots(ref):
    half = ref.shape[0] // 2

    def dst(slot, part):
        rows = pl.ds(pl.multiple_of(slot * 64, 64), 64)
        return ref.at[:, rows] if part is None else ref.at[pl.ds(part * half, half), rows]

    return dst


MP_SEMS = [pltpu.SemaphoreType.DMA((9,)), pltpu.SemaphoreType.DMA((9,)), pltpu.SemaphoreType.DMA]
CTX_SEMS = MP_SEMS + [pltpu.SemaphoreType.DMA((10,)), pltpu.SemaphoreType.DMA((10,))]


def start_kernel(x_ref, id_ref, w_ref, xo, ido, wo, s1, r1, loc, *sems):
    c, m = place()
    upper = m >= MP // 2
    opposite = (CTX - 1 - c, m)
    greet([opposite] + ctx_neighbours() + mp_neighbours(), 8)
    ring = ctx_ring(w_ref, slots(wo), sems[0:5])
    rings = [
        mp_ring(None, slots(xo), sems[5:8]),
        mp_ring(None, slots(ido), sems[8:11]),
    ]
    moves = [
        remote(x_ref, xo.at[m], s1.at[0], r1.at[0], opposite),
        remote(id_ref, ido.at[m], s1.at[1], r1.at[1], opposite),
    ]
    stays = [
        pltpu.make_async_copy(x_ref, xo.at[m], loc.at[0]),
        pltpu.make_async_copy(id_ref, ido.at[m], loc.at[1]),
    ]

    @pl.when(upper)
    def _():
        for copy in moves:
            copy.start()

    @pl.when(jnp.logical_not(upper))
    def _():
        for copy in stays:
            copy.start()

    ring.start()

    @pl.when(upper)
    def _():
        for copy in moves:
            copy.wait()

    @pl.when(jnp.logical_not(upper))
    def _():
        for copy in stays:
            copy.wait()

    for one in rings:
        one.start()
    ring.relay_near()
    ring.relay_own()
    for one in rings:
        one.relay_near()
        one.relay_own()
    ring.relay_far()
    for one in rings:
        one.relay_far()
    for one in rings:
        one.finish()
    ring.finish()


def lanes(rows):
    return lax.broadcasted_iota(jnp.int32, (rows, 128), 1)


def phase_rows(ref, at, rows):
    part = ref[:, at : at + rows]
    return jnp.concatenate([part] * 4, axis=0).T


def turn(values, cosine, sine):
    first = lax.rem(lanes(values.shape[0]), HEAD) < HEAD // 2
    turned = jnp.where(first, -pltpu.roll(values, 96, 1), pltpu.roll(values, 32, 1))
    return values * cosine + turned * sine


def turn_back(grads, cosine, sine):
    first = lax.rem(lanes(grads.shape[0]), HEAD) < HEAD // 2
    scaled = grads * sine
    turned = jnp.where(first, pltpu.roll(scaled, 96, 1), -pltpu.roll(scaled, 32, 1))
    return grads * cosine + turned


def keys_kernel(
    x_ref, gain_ref, w_ref, cos_ref, sin_ref, dy_ref,
    normed_ref, q_ref, kv_out, dy_out,
    kv_own, *sems,
):
    greet(ctx_neighbours() + mp_neighbours(), 7)
    ring = ctx_ring(kv_own, slots(kv_out), sems[:5])
    rows = mp_ring(dy_ref, slots(dy_out), sems[5:])
    rows.start()
    size = 256
    low = lanes(size) < HEAD
    for part in range(4):
        at = part * size
        block = slice(at, at + size)
        x = x_ref[block].astype(f32)
        inverse = lax.rsqrt(jnp.mean(x * x, axis=1, keepdims=True) + epsilon)
        normed = (x * inverse * gain_ref[...]).astype(bf16)
        normed_ref[block] = normed
        qkv = jnp.dot(normed, w_ref[...], preferred_element_type=f32)
        cosine, sine = phase_rows(cos_ref, at, size), phase_rows(sin_ref, at, size)
        queries = turn(qkv[:, :128], cosine, sine).astype(bf16).astype(f32) * score_scale
        half, place_in = part // 2, at % HALF
        q_ref[half, place_in : place_in + size] = jnp.where(low, queries, 0.0).astype(bf16)
        q_ref[half, HALF + place_in : HALF + place_in + size] = jnp.where(
            low, pltpu.roll(queries, HEAD, 1), 0.0
        ).astype(bf16)
        kv = qkv[:, 128:]
        kv_own[block] = jnp.where(low, turn(kv, cosine, sine), kv).astype(bf16)
    ring.start()
    rows.relay_near()
    rows.relay_own()
    ring.relay_near()
    ring.relay_own()
    rows.relay_far()
    ring.relay_far()
    rows.finish()
    ring.finish()


def keys_and_values(x_all, gain, qkv_w, cosine, sine, dy):
    return pl.pallas_call(
        keys_kernel,
        out_shape=[
            shape((BLOCK, 1024)),
            shape((2, 2 * HALF, 128)),
            shape((CTX, BLOCK, 128)),
            shape((MP, TOK, 1024)),
        ],
        in_specs=[VM] * 5 + [ANY],
        out_specs=[VM] * 2 + [ANY] * 2,
        scratch_shapes=[pltpu.VMEM((BLOCK, 128), bf16)] + CTX_SEMS + MP_SEMS,
        compiler_params=pltpu.CompilerParams(
            vmem_limit_bytes=VMEM_LIMIT, collective_id=2, has_side_effects=True
        ),
    )(x_all, gain, qkv_w, cosine, sine, dy)


def gather_kernel(a_ref, w_ref, out, w_out, *sems):
    greet(ctx_neighbours() + mp_neighbours(), 7)
    ring = mp_ring(a_ref, slots(out), sems[:3])
    weights = ctx_ring(w_ref, row_slots(w_out), sems[3:])
    ring.start()
    weights.start()
    ring.relay_near()
    ring.relay_own()
    weights.relay_near()
    weights.relay_own()
    ring.relay_far()
    weights.relay_far()
    ring.finish()
    weights.finish()


def scatter_kernel(
    a_ref, b_ref, dp_ref, act_ref, in_ref, dgu_ref,
    ao, bo, pair_ref, sum_ref,
    terms, theirs, got, own, s1, r1, s2, r2, s3, r3, s4, r4, loc,
):
    c, m = place()
    core = lax.rem(c, 2)
    x = c // 4
    sibling = (flip(c, 1), m)
    mates = [(c, lax.rem(m + k, MP)) for k in range(1, MP)]
    peers = [(lax.rem(c + 4 * k, CTX), m) for k in range(1, 4)]
    greet(mates + [sibling] + peers, MP + 3)
    own_a = pltpu.make_async_copy(a_ref.at[m], ao.at[m], loc.at[0])
    own_a.start()
    own_b = pltpu.make_async_copy(b_ref.at[m], bo.at[m], loc.at[1])
    own_b.start()
    copies = []
    for k in range(1, MP):
        to = lax.rem(m + k, MP)
        copies.append(remote(a_ref.at[to], ao.at[m], s1.at[k], r1.at[k], mates[k - 1]))
        copies.append(remote(b_ref.at[to], bo.at[m], s2.at[k], r2.at[k], mates[k - 1]))
    for copy in copies:
        copy.start()
    crossing = [
        remote(terms.at[1 - core, e], theirs.at[e], s3.at[e], r3.at[e], sibling)
        for e in range(4)
    ]
    first = [
        remote(own.at[lax.rem(x + k, 4)], got.at[k - 1], s4.at[k], r4.at[k], peers[k - 1])
        for k in range(1, 4)
    ]

    def join(e, put):
        crossing[e].wait()

        def add(chip, carry):
            put(
                chip,
                (terms[core, e, chip].astype(f32) + theirs[e, chip].astype(f32)).astype(bf16),
            )
            return carry

        lax.fori_loop(0, 8, add, 0)

    def put_own(chip, value):
        own[chip // 2, lax.rem(chip, 2)] = value

    def put_pair(e):
        def put(chip, value):
            pair_ref[e, chip // 2, lax.rem(chip, 2)] = value

        return put

    for e in range(4):
        gate_up_grads = dgu_ref[e]
        active = act_ref[e]

        def chunk(at, carry):
            columns = pl.ds(pl.multiple_of(at * 256, 256), 256)
            in_part = contract(in_ref[e, :, columns], gate_up_grads, 0, 0).astype(bf16)
            out_part = contract(dp_ref[e, :, columns], active, 0, 0).astype(bf16)
            for j in range(4):
                rows = slice(64 * j, 64 * j + 64)
                terms[j % 2, e, 2 * at + j // 2, :, 0:1024] = in_part[rows]
                terms[j % 2, e, 2 * at + j // 2, :, 1024:1536] = out_part[rows]
            return carry

        lax.fori_loop(0, 4, chunk, 0)
        crossing[e].start()
        if e == 1:
            join(0, put_own)
            for copy in first:
                copy.start()
    for e in range(1, 4):
        join(e, put_pair(e - 1))
    for copy in first:
        copy.wait()
    for j in range(2):
        term = own[x, j].astype(f32)
        for k in range(3):
            term = term + got[k, j].astype(f32)
        sum_ref[j] = term.astype(bf16)
    for copy in copies:
        copy.wait()
    own_a.wait()
    own_b.wait()


def scatter_rows(routed_terms, share, d_produced, active, incoming, d_gate_up):
    return pl.pallas_call(
        scatter_kernel,
        out_shape=[
            shape((MP, TOK, 1024)),
            shape((MP, 8, TOK), f32),
            shape((3, 4, 2, 64, 1536)),
            shape((2, 64, 1536)),
        ],
        in_specs=[ANY, ANY, VM, VM, VM, VM],
        out_specs=[ANY, ANY, VM, VM],
        scratch_shapes=[
            pltpu.VMEM((2, 4, 8, 64, 1536), bf16),
            pltpu.VMEM((4, 8, 64, 1536), bf16),
            pltpu.VMEM((3, 2, 64, 1536), bf16),
            pltpu.VMEM((4, 2, 64, 1536), bf16),
        ]
        + [pltpu.SemaphoreType.DMA((MP,))] * 4
        + [pltpu.SemaphoreType.DMA((4,))] * 4
        + [pltpu.SemaphoreType.DMA((2,))],
        compiler_params=pltpu.CompilerParams(
            vmem_limit_bytes=VMEM_LIMIT, collective_id=4, has_side_effects=True
        ),
    )(routed_terms, share, d_produced, active, incoming, d_gate_up)


def outputs_kernel(a_ref, ao, s1, r1, loc):
    c, m = place()
    mates = [(c, lax.rem(m + k, MP)) for k in range(1, MP)]
    greet(mates, MP - 1)
    own_a = pltpu.make_async_copy(a_ref.at[m], ao.at[m], loc.at[0])
    own_a.start()
    copies = []
    for k in range(1, MP):
        to = lax.rem(m + k, MP)
        copies.append(remote(a_ref.at[to], ao.at[m], s1.at[k], r1.at[k], mates[k - 1]))
    for copy in copies:
        copy.start()
    for copy in copies:
        copy.wait()
    own_a.wait()


def keys_grad_kernel(
    a_ref, out, theirs, pair_a, pair_b, got_a, got_b, sum_a, sum_b, last_a, last_b,
    s0, r0, s1, r1, s2, r2,
):
    c, m = place()
    core = lax.rem(c, 2)
    x, y = c // 4, lax.rem(c // 2, 2)
    sibling = (flip(c, 1), m)
    across = (flip(c, 2), m)
    peers = [(lax.rem(c + 4 * k, CTX), m) for k in range(1, 4)]
    greet(peers + [across, sibling], 5)
    low, high = pl.ds(0, HALF), pl.ds(HALF, HALF)
    crossing = [
        remote(
            a_ref.at[:, :, 1 - core, rows], theirs.at[:, :, rows], s0.at[at], r0.at[at], sibling
        )
        for at, rows in enumerate((high, low))
    ]
    for copy in crossing:
        copy.start()

    def add(a, b):
        return a.astype(f32) + b.astype(f32)

    crossing[0].wait()
    for i in range(4):
        for j in range(2):
            pair_b[i, j] = add(a_ref[i, j, core, high], theirs[i, j, high]).astype(bf16)
    first = [remote(pair_b.at[:, 1 - y], got_b, s1.at[0], r1.at[0], across)]
    first[0].start()
    crossing[1].wait()
    for i in range(4):
        for j in range(2):
            pair_a[i, j] = add(a_ref[i, j, core, low], theirs[i, j, low]).astype(bf16)
    for k in range(1, 4):
        copy = remote(
            pair_a.at[lax.rem(x + k, 4)], got_a.at[k - 1], s1.at[k], r1.at[k], peers[k - 1]
        )
        copy.start()
        first.append(copy)
    first[0].wait()
    for i in range(4):
        sum_b[i] = add(pair_b[i, y], got_b[i]).astype(bf16)
    second = []
    for k in range(1, 4):
        copy = remote(
            sum_b.at[lax.rem(x + k, 4)], last_b.at[k - 1], s2.at[k], r2.at[k], peers[k - 1]
        )
        copy.start()
        second.append(copy)
    for copy in first[1:]:
        copy.wait()
    for j in range(2):
        sum_a[j] = (add(pair_a[x, j], got_a[0, j]) + add(got_a[1, j], got_a[2, j])).astype(bf16)
    copy = remote(sum_a.at[1 - y], last_a, s2.at[0], r2.at[0], across)
    copy.start()
    second.append(copy)
    for copy in second:
        copy.wait()
    out[low] = add(sum_a[y], last_a[...])
    out[high] = add(sum_b[x], last_b[0]) + add(last_b[1], last_b[2])


def keys_grad(terms):
    piece = (HALF, 128)
    return pl.pallas_call(
        keys_grad_kernel,
        out_shape=shape((BLOCK, 128), f32),
        in_specs=[VM],
        out_specs=VM,
        scratch_shapes=[
            pltpu.VMEM((4, 2, BLOCK, 128), bf16),
            pltpu.VMEM((4, 2) + piece, bf16),
            pltpu.VMEM((4, 2) + piece, bf16),
            pltpu.VMEM((3, 2) + piece, bf16),
            pltpu.VMEM((4,) + piece, bf16),
            pltpu.VMEM((2,) + piece, bf16),
            pltpu.VMEM((4,) + piece, bf16),
            pltpu.VMEM(piece, bf16),
            pltpu.VMEM((3,) + piece, bf16),
        ]
        + [pltpu.SemaphoreType.DMA((2,))] * 2
        + [pltpu.SemaphoreType.DMA((4,))] * 4,
        compiler_params=pltpu.CompilerParams(
            vmem_limit_bytes=VMEM_LIMIT, collective_id=6, has_side_effects=True
        ),
    )(terms)


def finish_kernel(
    dq_ref, dkv_ref, cos_ref, sin_ref, normed_ref, br_ref, rows_ref,
    ao, go,
    d_qkv, terms, s1, r1, s2, r2, loc,
):
    c, m = place()
    upper = m >= MP // 2
    t = jnp.where(upper, CTX - 1 - c, c)
    barrier = pltpu.get_barrier_semaphore()
    for k in range(1, MP):
        pl.semaphore_signal(
            barrier, inc=1, device_id=(t, lax.rem(m + k, MP)), device_id_type=MESH
        )
    for k in range(1, CTX):
        pl.semaphore_signal(
            barrier, inc=1, device_id=(lax.rem(c + k, CTX), m), device_id_type=MESH
        )

    @pl.when(upper)
    def _():
        pl.semaphore_signal(barrier, inc=1, device_id=(t, m), device_id_type=MESH)
        pl.semaphore_wait(barrier, MP + CTX - 1)

    @pl.when(jnp.logical_not(upper))
    def _():
        pl.semaphore_wait(barrier, MP + CTX - 2)

    low = lanes(TOK) < HEAD
    for i in range(MP):
        at = i * TOK
        part, inside = at // HALF, at % HALF
        columns = dq_ref[part]
        heads = jnp.concatenate(
            [
                columns[:HEAD, inside : inside + TOK],
                columns[:HEAD, HALF + inside : HALF + inside + TOK],
            ],
            axis=0,
        ).T
        cosine, sine = phase_rows(cos_ref, at, TOK), phase_rows(sin_ref, at, TOK)
        d_qkv[i, :, 0:128] = turn_back(heads * score_scale, cosine, sine).astype(bf16)
        dkv = dkv_ref[at : at + TOK]
        d_qkv[i, :, 128:256] = jnp.where(low, turn_back(dkv, cosine, sine), dkv).astype(bf16)

    own_a = pltpu.make_async_copy(d_qkv.at[m], ao.at[m], loc.at[1])
    a_copies, g_copies = [], []
    for k in range(MP):
        to = lax.rem(m + k, MP)
        target = (jnp.where(to >= MP // 2, CTX - 1 - c, c), to)
        a_copies.append(remote(d_qkv.at[to], ao.at[m], s1.at[k], r1.at[k], target))

    @pl.when(upper)
    def _():
        a_copies[0].start()

    @pl.when(jnp.logical_not(upper))
    def _():
        own_a.start()

    for k in range(1, MP):
        a_copies[k].start()
    grads = d_qkv[...].reshape(BLOCK, 256)
    columns = jnp.concatenate(
        [
            contract(grads, normed_ref[...], 0, 0),
            contract(rows_ref[...], br_ref[...], 0, 0),
        ],
        axis=0,
    )
    terms[...] = columns.T.astype(bf16).reshape(terms.shape)
    own_g = pltpu.make_async_copy(terms.at[c], go.at[c], loc.at[0])
    own_g.start()
    for k in range(1, CTX):
        to = lax.rem(c + k, CTX)
        copy = remote(terms.at[to], go.at[c], s2.at[k], r2.at[k], (to, m))
        copy.start()
        g_copies.append(copy)
    for k in range(1, MP):
        a_copies[k].wait()
    for copy in g_copies:
        copy.wait()
    own_g.wait()

    @pl.when(upper)
    def _():
        a_copies[0].wait()

    @pl.when(jnp.logical_not(upper))
    def _():
        own_a.wait()


def finish(dq, dkv, cosine, sine, normed, branch_rows, out_rows):
    return pl.pallas_call(
        finish_kernel,
        out_shape=[
            shape((MP, TOK, 256)),
            shape((CTX, 64, 384)),
        ],
        in_specs=[VM] * 7,
        out_specs=[ANY] * 2,
        scratch_shapes=[
            pltpu.VMEM((MP, TOK, 256), bf16),
            pltpu.VMEM((CTX, 64, 384), bf16),
        ]
        + [pltpu.SemaphoreType.DMA((n,)) for n in (MP, MP, CTX, CTX, 2)],
        compiler_params=pltpu.CompilerParams(
            vmem_limit_bytes=VMEM_LIMIT, collective_id=8, has_side_effects=True
        ),
    )(dq, dkv, cosine, sine, normed, branch_rows, out_rows)


def sums_kernel(
    small_ref, qg_ref, qw_ref, x_ref, gain_ref, hid_ref, w_ref, y_ref,
    out, ig_ref, wq_ref, wk_ref, wv_ref, wo_ref, y_out,
    terms, got, part, got2, s1, r1, s2, r2, loc,
):
    c, m = place()
    upper = m >= MP // 2
    move = remote(y_ref, y_out, s1.at[0], r1.at[0], (CTX - 1 - c, m))
    stay = pltpu.make_async_copy(y_ref, y_out, loc)
    peers = [(lax.rem(c + k, CTX), m) for k in range(1, CTX)]
    mates = [(c, lax.rem(m + k, MP)) for k in range(1, MP)]
    barrier = pltpu.get_barrier_semaphore()
    for target in peers + mates:
        pl.semaphore_signal(barrier, inc=1, device_id=target, device_id_type=MESH)
    grads = contract(qg_ref[0], qw_ref[0], 1, 1)
    for h in range(1, MP):
        grads = grads + contract(qg_ref[h], qw_ref[h], 1, 1)
    x = x_ref[...].astype(f32)
    inverse = lax.rsqrt(jnp.mean(x * x, axis=1, keepdims=True) + epsilon)
    scaled = x * inverse
    inner = grads * gain_ref[...]
    gain_grad = jnp.sum(grads * scaled, axis=0, keepdims=True)
    columns = jnp.broadcast_to(gain_grad, (128, 1024)).T
    terms[...] = jnp.where(lanes(1024) == 32, columns, small_ref[...]).reshape(terms.shape)
    pl.semaphore_wait(barrier, CTX - 1 + MP - 1)
    copies = []
    for k in range(1, CTX):
        to = lax.rem(c + k, CTX)
        copy = remote(terms.at[to], got.at[k], s1.at[k], r1.at[k], peers[k - 1])
        copy.start()
        copies.append(copy)

    @pl.when(upper)
    def _():
        move.start()

    @pl.when(jnp.logical_not(upper))
    def _():
        stay.start()

    ig = inverse * (inner - scaled * jnp.mean(inner * scaled, axis=1, keepdims=True))
    ig_ref[...] = (ig + hid_ref[...].astype(f32)).astype(bf16)
    weights = w_ref[0].astype(f32)
    for k in range(1, CTX):
        weights = weights + w_ref[k].astype(f32)
    wq_ref[...] = weights[:, :128]
    wk_ref[...] = weights[:, 128:192]
    wv_ref[...] = weights[:, 192:256]
    wo_ref[...] = weights[:, 256:].T
    total = terms[c]
    for copy in copies:
        copy.wait()
    for k in range(1, CTX):
        total = total + got[k]
    part[...] = total
    copies = []
    for k in range(1, MP):
        to = lax.rem(m + k, MP)
        copy = remote(part.at[to], got2.at[k], s2.at[k], r2.at[k], mates[k - 1])
        copy.start()
        copies.append(copy)
    last = part[m]
    for copy in copies:
        copy.wait()
    for k in range(1, MP):
        last = last + got2[k]
    out[...] = last

    @pl.when(upper)
    def _():
        move.wait()

    @pl.when(jnp.logical_not(upper))
    def _():
        stay.wait()


def last_sums(small, qkv_got, qkv_w_all, x, gain, hidden_grad, w_got, outputs):
    dims = (8, 128)
    return pl.pallas_call(
        sums_kernel,
        out_shape=[
            shape(dims, f32),
            shape((TOK, 1024)),
            shape((64, 128), f32),
            shape((64, 64), f32),
            shape((64, 64), f32),
            shape((128, 64), f32),
            shape((TOK, 1024)),
        ],
        in_specs=[VM] * 7 + [ANY],
        out_specs=[VM] * 6 + [ANY],
        scratch_shapes=[
            pltpu.VMEM((CTX, MP) + dims, f32),
            pltpu.VMEM((CTX, MP) + dims, f32),
            pltpu.VMEM((MP,) + dims, f32),
            pltpu.VMEM((MP,) + dims, f32),
            pltpu.SemaphoreType.DMA((CTX,)),
            pltpu.SemaphoreType.DMA((CTX,)),
            pltpu.SemaphoreType.DMA((MP,)),
            pltpu.SemaphoreType.DMA((MP,)),
            pltpu.SemaphoreType.DMA,
        ],
        compiler_params=pltpu.CompilerParams(
            vmem_limit_bytes=VMEM_LIMIT, collective_id=9, has_side_effects=True
        ),
    )(small, qkv_got, qkv_w_all, x, gain, hidden_grad, w_got, outputs)


def unit(index, first_half):
    second = index > first_half
    part = second.astype(jnp.int32)
    key_half = jnp.where(second, index - first_half - 1, index)
    odd = lax.rem(key_half, 2) == 1
    slot = jnp.where(odd, 2 * CTX - key_half, key_half)
    diagonal = jnp.logical_or(index == first_half, index == 2 * CTX)
    return part, slot, diagonal


def visible_mask(rows):
    key_at = lax.broadcasted_iota(jnp.int32, (HALF, rows), 0)
    query_at = lax.rem(lax.broadcasted_iota(jnp.int32, (HALF, rows), 1), HALF)
    return key_at <= query_at


def forward_kernel(
    q_ref, kv_ref, in_ref, qw_ref, rows_ref,
    out_ref, rows_out, lse_ref, in_all, qw_all, rows_all,
    best, total, summed, *sems,
):
    first_half = 2 * lax.axis_index("ctx")
    greet(ctx_neighbours() + mp_neighbours(), 7)
    weights_rings = [ctx_ring(in_ref, row_slots(in_all), sems[0:5])]
    rows_rings = [
        shared_ring(rows_ref, rows_all, sems[5:10]),
        shared_ring(qw_ref, qw_all, sems[10:15]),
    ]
    for ring in weights_rings + rows_rings:
        ring.start()
    best[...] = jnp.full(best.shape, -1e30, f32)
    total[...] = jnp.zeros(total.shape, f32)
    summed[...] = jnp.zeros(summed.shape, f32)

    def work(part, slot, masked):
        kv = kv_ref[slot]
        scores = contract(kv, q_ref[part], 1, 1)
        if masked:
            scores = jnp.where(visible_mask(scores.shape[1]), scores, -jnp.inf)
        old = best[part]
        new = jnp.maximum(old, jnp.max(scores, axis=0, keepdims=True))
        weights = jnp.exp2(scores * log2_e - new * log2_e)
        fading = jnp.exp2((old - new) * log2_e)
        total[part] = total[part] * fading + jnp.sum(weights, axis=0, keepdims=True)
        summed[part] = summed[part] * fading + contract(kv, weights.astype(bf16), 0, 0)
        best[part] = new

    def step(index, carry):
        part, slot, diagonal = unit(index, first_half)

        @pl.when(index == 11)
        def _():
            for ring in weights_rings:
                ring.relay_near()
                ring.relay_own()

        @pl.when(index == 16)
        def _():
            for ring in rows_rings:
                ring.relay_near()
                ring.relay_own()

        @pl.when(index == 24)
        def _():
            for ring in rows_rings:
                ring.relay_far()

        @pl.when(index == 25)
        def _():
            for ring in weights_rings:
                ring.relay_far()

        @pl.when(diagonal)
        def _():
            work(part, slot, True)

        @pl.when(jnp.logical_not(diagonal))
        def _():
            work(part, slot, False)

        return carry

    lax.fori_loop(0, 2 * CTX + 1, step, 0)
    for part in range(2):
        columns = summed[part][HEAD:, :] / total[part]
        heads = jnp.concatenate([columns[:, :HALF], columns[:, HALF:]], axis=0).T
        out_ref[part * HALF : part * HALF + HALF] = heads
        rows_out[part * HALF : part * HALF + HALF] = heads.astype(bf16)
        lse_ref[part] = best[part] + jnp.log(total[part])
    for ring in weights_rings + rows_rings:
        ring.finish()


def attention(q_rows, kv_all, w_in, qkv_w, out_rows_w):
    rows = q_rows.shape[1]
    return pl.pallas_call(
        forward_kernel,
        out_shape=[
            shape((BLOCK, 128), f32),
            shape((BLOCK, 128)),
            shape((2, 1, rows), f32),
            shape((4, 1024, 1024)),
            shape((MP,) + qkv_w.shape),
            shape((MP, TOK, 1024)),
        ],
        in_specs=[VM, VM, ANY, ANY, ANY],
        out_specs=[VM, VM, VM, ANY, ANY, ANY],
        scratch_shapes=[
            pltpu.VMEM((2, 1, rows), f32),
            pltpu.VMEM((2, 1, rows), f32),
            pltpu.VMEM((2, 2 * HEAD, rows), f32),
        ]
        + CTX_SEMS * 3,
        compiler_params=pltpu.CompilerParams(
            vmem_limit_bytes=VMEM_LIMIT, collective_id=10, has_side_effects=True
        ),
        cost_estimate=pl.CostEstimate(
            flops=33 * 4 * HALF * rows * 256, bytes_accessed=1 << 23, transcendentals=33 * HALF * rows
        ),
    )(q_rows, kv_all, w_in, qkv_w, out_rows_w)


def backward_kernel(
    q_ref, og_ref, att_ref, lse_ref, kv_ref, sum_0, pair_ref, br_ref, mixed_ref, hid_ref,
    dkv_ref, dq_ref, in_grad, out_grad, br_all, mixed_out, hid_out,
    total, do_ref, delta_ref, own_a, own_b, got_a, got_b, sum_a, sum_b, last_0, last_a, last_b,
    *sems,
):
    c, m = place()
    first_half = 2 * c
    x, y = c // 4, lax.rem(c // 2, 2)
    peers = [(lax.rem(c + 4 * k, CTX), m) for k in range(1, 4)]
    across = (flip(c, 2), m)
    mates = [(c, lax.rem(m + k, MP)) for k in range(1, MP)]
    upper = m >= MP // 2
    opposite = (CTX - 1 - c, m)
    greet(peers + [across, opposite] + mates, 5 + MP - 1)
    sa, ra, sb, rb, sm, rm, loc = sems[:7]
    move = remote(hid_ref, hid_out, sm.at[0], rm.at[0], opposite)
    stay = pltpu.make_async_copy(hid_ref, hid_out, loc.at[3])
    ring = mp_ring(br_ref, slots(br_all), sems[7:10])

    def first_copies():
        copies = [
            remote(
                pair_ref.at[pl.ds(0, 2), lax.rem(x + k, 4)],
                got_a.at[k - 1], sa.at[k], ra.at[k], peers[k - 1],
            )
            for k in range(1, 4)
        ]
        copies.append(remote(pair_ref.at[2, :, 1 - y], got_b, sa.at[0], ra.at[0], across))
        return copies

    def own_copies():
        return [
            pltpu.make_async_copy(pair_ref.at[pl.ds(0, 2), x], own_a, loc.at[1]),
            pltpu.make_async_copy(pair_ref.at[2, :, y], own_b, loc.at[2]),
        ]

    def sum_0_copy():
        return remote(sum_0.at[1 - y], last_0, sb.at[0], rb.at[0], across)

    def second_copies():
        copies = [
            remote(
                sum_b.at[lax.rem(x + k, 4)], last_b.at[k - 1], sb.at[k], rb.at[k], peers[k - 1]
            )
            for k in range(1, 4)
        ]
        copies.append(remote(sum_a.at[:, 1 - y], last_a, sb.at[4], rb.at[4], across))
        return copies

    def middle():
        for copy in first_copies() + own_copies():
            copy.wait()
        for e in range(2):
            for j in range(2):
                term = own_a[e, j].astype(f32)
                for k in range(3):
                    term = term + got_a[k, e, j].astype(f32)
                sum_a[e, j] = term.astype(bf16)
        for j in range(4):
            sum_b[j] = (own_b[j].astype(f32) + got_b[j].astype(f32)).astype(bf16)
        for copy in second_copies():
            copy.start()

    def mixed_copies():
        copies = []
        for k in range(1, MP):
            to = lax.rem(m + k, MP)
            copies.append(
                remote(mixed_ref.at[to], mixed_out.at[m], sm.at[k], rm.at[k], mates[k - 1])
            )
        return copies

    def own_mixed():
        return pltpu.make_async_copy(mixed_ref.at[m], mixed_out.at[m], loc.at[0])

    ring.start()
    for copy in first_copies() + own_copies() + [sum_0_copy()]:
        copy.start()
    low = lanes(HALF) < HEAD
    for part in range(2):
        rows = slice(part * HALF, part * HALF + HALF)
        grads = og_ref[rows].astype(f32)
        product = (grads * att_ref[rows]).T
        delta_ref[part, :, 0:HALF] = jnp.sum(product[:HEAD], axis=0, keepdims=True)
        delta_ref[part, :, HALF:] = jnp.sum(product[HEAD:], axis=0, keepdims=True)
        do_ref[part, 0:HALF] = jnp.where(low, 0.0, pltpu.roll(grads, HEAD, 1)).astype(bf16)
        do_ref[part, HALF:] = jnp.where(low, 0.0, grads).astype(bf16)
    dq_ref[...] = jnp.zeros(dq_ref.shape, f32)

    def clear(index, carry):
        total[index] = jnp.zeros(total.shape[1:], f32)
        return carry

    lax.fori_loop(0, 2 * CTX, clear, 0)

    def work(part, slot, masked):
        kv = kv_ref[slot]
        queries = q_ref[part]
        grads = do_ref[part]
        scores = contract(kv, queries, 1, 1)
        probs = jnp.exp2((scores - lse_ref[part]) * log2_e)
        if masked:
            probs = jnp.where(visible_mask(scores.shape[1]), probs, 0.0)
        prob_grad = contract(kv, grads, 1, 1)
        score_grad = (probs * (prob_grad - delta_ref[part])).astype(bf16)
        total[slot] += contract(probs.astype(bf16), grads, 1, 0) + contract(
            score_grad, queries, 1, 0
        )
        dq_ref[part] += contract(kv, score_grad, 0, 0)

    def step(index, carry):
        part, slot, diagonal = unit(index, first_half)

        @pl.when(index == 1)
        def _():
            own_mixed().start()
            for copy in mixed_copies():
                copy.start()

        @pl.when(jnp.logical_and(index == 1, upper))
        def _():
            move.start()

        @pl.when(jnp.logical_and(index == 1, jnp.logical_not(upper)))
        def _():
            stay.start()

        @pl.when(index == 18)
        def _():
            ring.relay_near()
            ring.relay_own()

        @pl.when(index == 25)
        def _():
            middle()

        @pl.when(index == 27)
        def _():
            ring.relay_far()

        @pl.when(diagonal)
        def _():
            work(part, slot, True)

        @pl.when(jnp.logical_not(diagonal))
        def _():
            work(part, slot, False)

        return carry

    lax.fori_loop(0, 2 * CTX + 1, step, 0)

    def write(index, carry):
        dkv_ref[index] = total[index].astype(bf16)
        return carry

    lax.fori_loop(0, 2 * CTX, write, 0)
    ring.finish()
    sum_0_copy().wait()
    for copy in second_copies():
        copy.wait()

    def put(at, term):
        in_grad[at] = term[:, :1024]
        out_grad[at] = term[:, 1024:].T

    put(0, sum_0[y].astype(f32) + last_0[...].astype(f32))
    for e in range(2):
        put(1 + e, sum_a[e, y].astype(f32) + last_a[e].astype(f32))
    term = sum_b[x].astype(f32)
    for k in range(3):
        term = term + last_b[k].astype(f32)
    put(3, term)
    for copy in mixed_copies():
        copy.wait()
    own_mixed().wait()

    @pl.when(upper)
    def _():
        move.wait()

    @pl.when(jnp.logical_not(upper))
    def _():
        stay.wait()


def attention_back(
    q_rows, out_grad, attended, lse, kv_all, sum_first, pair, branch_grad, mixed, hidden_grad
):
    rows = q_rows.shape[1]
    wide = pair.shape[-1]
    return pl.pallas_call(
        backward_kernel,
        out_shape=[
            shape(kv_all.shape, bf16),
            shape((2, 2 * HEAD, rows), f32),
            shape((4, 64, 1024), f32),
            shape((4, 512, 64), f32),
            shape((MP, TOK, 1024)),
            shape((MP, TOK, 1024)),
            shape((TOK, 1024)),
        ],
        in_specs=[VM] * 6 + [ANY] * 4,
        out_specs=[VM] * 4 + [ANY] * 3,
        scratch_shapes=[
            pltpu.VMEM(kv_all.shape, f32),
            pltpu.VMEM(q_rows.shape, bf16),
            pltpu.VMEM((2, 1, rows), f32),
            pltpu.VMEM((2, 2, 64, wide), bf16),
            pltpu.VMEM((4, 64, wide), bf16),
            pltpu.VMEM((3, 2, 2, 64, wide), bf16),
            pltpu.VMEM((4, 64, wide), bf16),
            pltpu.VMEM((2, 2, 64, wide), bf16),
            pltpu.VMEM((4, 64, wide), bf16),
            pltpu.VMEM((64, wide), bf16),
            pltpu.VMEM((2, 64, wide), bf16),
            pltpu.VMEM((3, 64, wide), bf16),
        ]
        + [pltpu.SemaphoreType.DMA((4,))] * 2
        + [pltpu.SemaphoreType.DMA((5,))] * 2
        + [pltpu.SemaphoreType.DMA((MP,))] * 2
        + [pltpu.SemaphoreType.DMA((4,))]
        + MP_SEMS,
        compiler_params=pltpu.CompilerParams(
            vmem_limit_bytes=VMEM_LIMIT, collective_id=11, has_side_effects=True
        ),
        cost_estimate=pl.CostEstimate(
            flops=33 * 10 * HALF * rows * 256, bytes_accessed=1 << 24, transcendentals=33 * HALF * rows
        ),
    )(
        q_rows, out_grad, attended, lse, kv_all, sum_first, pair, branch_grad, mixed, hidden_grad
    )


def phases(positions, head_width):
    steps_up = jnp.arange(head_width // 2).astype(f32)
    frequency = rope_base ** (-2.0 * steps_up / head_width)
    angles = frequency[:, None] * positions.astype(f32)[None, :]
    return (jnp.cos(angles), jnp.sin(angles))


def normalize(values):
    inverse = lax.rsqrt(jnp.mean(values * values, axis=-1, keepdims=True) + epsilon)
    return (values * inverse, inverse)


def norm_back(grads, scaled, inverse, gain):
    inner = grads * gain
    return (
        inverse * (inner - scaled * jnp.mean(inner * scaled, axis=-1, keepdims=True)),
        jnp.sum(grads * scaled, axis=0),
    )


def swap_home(array):
    pairs = []
    for c in range(CTX):
        for m in range(MP):
            t = CTX - 1 - c if m >= MP // 2 else c
            pairs.append((c * MP + m, t * MP + m))
    return lax.ppermute(array, ("ctx", "mp"), pairs)


def body(
    layer_input,
    positions,
    expert_ids,
    attn_gain,
    w_query,
    w_key,
    w_value,
    w_attn_out,
    ffn_gain,
    router,
    w_in,
    w_out,
    cotangent,
):
    c, m = place()
    dy_swapped = swap_home(cotangent)
    own_positions = lax.dynamic_slice_in_dim(positions, m * TOK, TOK, 0)
    id_pack = jnp.concatenate(
        [expert_ids.T, own_positions[None, :], jnp.zeros((7, TOK), jnp.int32)], axis=0
    )
    w_pack = jnp.concatenate(
        [
            w_query,
            w_key,
            w_value,
            router,
            attn_gain[:, None],
            ffn_gain[:, None],
            jnp.zeros((64, 94), bf16),
            w_attn_out.T,
        ],
        axis=1,
    )
    x_all, id_all, w_all = comm_call(
        start_kernel,
        1,
        [layer_input, id_pack, w_pack],
        [
            shape((MP, TOK, 1024)),
            shape((MP, 16, TOK), jnp.int32),
            shape((CTX, 64, 512)),
        ],
        [2, 2, 2] + CTX_SEMS + MP_SEMS * 2,
        4 << 20,
    )
    inputs = x_all.reshape(BLOCK, 1024).astype(f32)
    ids = id_all[:, :8, :].transpose(1, 0, 2).reshape(8, BLOCK)
    places = id_all[:, 8, :].reshape(BLOCK)
    w_all = w_all.reshape(1024, 512)
    qkv_w = w_all[:, :256]
    router_w = w_all[:, 256:288]
    gain_one = w_all[:, 288].astype(f32)
    gain_two = w_all[:, 289].astype(f32)
    out_w = w_all[:, 384:].T

    cosine, sine = lax.optimization_barrier(phases(places, HEAD))
    normed, q_rows, kv_all, dy_all = keys_and_values(
        x_all.reshape(BLOCK, 1024), gain_one[None, :], qkv_w, cosine, sine, dy_swapped
    )
    kv_all = kv_all.reshape(2 * CTX, HALF, 128)
    attended, out_rows, lse, in_w, qkv_w_all, out_w_all = attention(
        q_rows, kv_all, w_in, qkv_w, out_w
    )
    dy_all = dy_all.reshape(BLOCK, 1024)
    rows_all, out_w_t = comm_call(
        gather_kernel,
        3,
        [out_rows, w_out.transpose(0, 2, 1)],
        [shape((MP, BLOCK, 128)), shape((4, 1024, 512))],
        MP_SEMS + CTX_SEMS,
        8 << 20,
    )
    branch = lax.dot_general(
        rows_all, out_w_all, (((0, 2), (0, 1)), ((), ())), preferred_element_type=f32
    )
    hidden = inputs + branch_scale * branch
    scaled_two, inverse_two = normalize(hidden)
    routed = (scaled_two * gain_two).astype(bf16)

    logits = contract(router_w, routed, 0, 1)
    experts = lax.broadcasted_iota(jnp.int32, (32, BLOCK), 0)
    member = jnp.any(ids[:, None, :] == experts[None], axis=0)
    chosen = jnp.where(member, logits, -jnp.inf)
    top_logit = jnp.max(chosen, axis=0, keepdims=True)
    powers = jnp.exp(chosen - top_logit)
    gates = powers / jnp.sum(powers, axis=0, keepdims=True)

    here = 4 * m + lax.broadcasted_iota(jnp.int32, (4, BLOCK), 0)
    selected = jnp.any(ids[:, None, :] == here[None], axis=0)
    earlier = (
        lax.broadcasted_iota(jnp.int32, (BLOCK, BLOCK), 0)
        <= lax.broadcasted_iota(jnp.int32, (BLOCK, BLOCK), 1)
    ).astype(bf16)
    counts = jnp.dot(selected.astype(bf16), earlier, preferred_element_type=f32)
    rank = jnp.where(selected, counts.astype(jnp.int32) - 1, -1)
    capacity = 288
    place_bool = rank[:, None, :] == lax.broadcasted_iota(jnp.int32, (4, capacity, BLOCK), 1)
    placing = place_bool.astype(bf16).reshape(4 * capacity, BLOCK)
    gates_here = lax.dynamic_slice_in_dim(gates, 4 * m, 4, 0)
    slot_gate = jnp.sum(jnp.where(place_bool, gates_here[:, None, :], 0.0), axis=2)

    incoming = jnp.dot(placing, routed, preferred_element_type=f32).astype(bf16)
    incoming = incoming.reshape(4, capacity, 1024)
    dy_rows = jnp.dot(placing, dy_all, preferred_element_type=f32).reshape(4, capacity, 1024)
    gate_up = jnp.einsum("esd,edf->esf", incoming, in_w, preferred_element_type=f32)
    gate_part, up_part = gate_up[..., :512], gate_up[..., 512:]
    squashed = jax.nn.sigmoid(gate_part)
    silu_part = gate_part * squashed
    active = (silu_part * up_part).astype(bf16)
    produced = jnp.einsum(
        "esf,edf->esd", active, out_w_t, preferred_element_type=f32
    ).astype(bf16)
    produced_f = produced.astype(f32)
    d_produced = (branch_scale * slot_gate[..., None] * dy_rows).astype(bf16)
    slot_share = branch_scale * jnp.sum(dy_rows * produced_f, axis=2)
    weighted = (slot_gate[..., None] * produced_f).astype(bf16).reshape(4 * capacity, 1024)
    mixed = branch_scale * contract(placing, weighted, 0, 0)
    mixed = mixed.astype(bf16).reshape(MP, TOK, 1024)

    d_active = jnp.einsum("esd,edf->esf", d_produced, out_w_t, preferred_element_type=f32)
    slope = squashed * (1.0 + gate_part * (1.0 - squashed))
    d_gate_up = jnp.concatenate(
        [d_active * up_part * slope, d_active * silu_part], axis=-1
    ).astype(bf16)
    d_gate_up = lax.optimization_barrier(d_gate_up)
    row_grads = jnp.einsum(
        "esf,edf->esd", d_gate_up, in_w, preferred_element_type=f32
    ).astype(bf16)
    row_grads = lax.optimization_barrier(row_grads)
    routed_terms = contract(placing, row_grads.reshape(4 * capacity, 1024), 0, 0)
    routed_terms = routed_terms.astype(bf16).reshape(MP, TOK, 1024)
    share = jnp.sum(jnp.where(place_bool, slot_share[:, :, None], 0.0), axis=1)
    share = jnp.pad(share.reshape(4, MP, TOK).transpose(1, 0, 2), ((0, 0), (0, 4), (0, 0)))
    routed_got, share_got, pair, sum_first = scatter_rows(
        routed_terms, share, d_produced, active, incoming, d_gate_up
    )

    def own_rows(array):
        return lax.dynamic_slice_in_dim(array, m * TOK, TOK, 0)

    hidden_own = own_rows(hidden)
    scaled_own, inverse_own = normalize(hidden_own)
    routed_own = (scaled_own * gain_two).astype(bf16).astype(f32)
    dy_own = own_rows(dy_all).astype(f32)
    gates_own = lax.dynamic_slice_in_dim(gates, m * TOK, TOK, 1)
    share_own = share_got[:, :4, :].reshape(32, TOK)
    logit_grad = gates_own * (
        share_own - jnp.sum(gates_own * share_own, axis=0, keepdims=True)
    )
    routed_grad = jnp.sum(routed_got.astype(f32), axis=0) + lax.dot_general(
        logit_grad,
        router_w.astype(f32),
        (((0,), (1,)), ((), ())),
        precision=highest,
        preferred_element_type=f32,
    )
    router_grad = lax.dot_general(
        routed_own,
        logit_grad,
        (((0,), (1,)), ((), ())),
        precision=highest,
        preferred_element_type=f32,
    )
    hidden_grad, gain_two_grad = norm_back(routed_grad, scaled_own, inverse_own, gain_two)
    hidden_grad = hidden_grad + dy_own
    branch_grad = (branch_scale * hidden_grad).astype(bf16)

    out_grad_terms = jnp.einsum(
        "td,hfd->htf", branch_grad, out_w_all, preferred_element_type=f32
    ).astype(bf16)
    (out_grad,) = comm_call(
        outputs_kernel, 5, [out_grad_terms], [shape((MP, TOK, 128))], [MP, MP, 1], 1 << 20
    )
    out_grad = out_grad.reshape(BLOCK, 128)

    dkv_terms, dq_cols, expert_in, expert_out, branch_rows, mixed_got, hidden_grad_home = (
        attention_back(
            q_rows, out_grad, attended, lse, kv_all, sum_first, pair, branch_grad, mixed,
            hidden_grad.astype(bf16),
        )
    )
    outputs = (hidden_own + jnp.sum(mixed_got.astype(f32), axis=0)).astype(bf16)
    dkv = keys_grad(dkv_terms.reshape(4, 2, 2, BLOCK, 128))
    qkv_got, w_got = finish(
        dq_cols,
        dkv,
        cosine,
        sine,
        normed,
        branch_rows.reshape(BLOCK, 1024),
        out_rows,
    )
    small = jnp.concatenate(
        [
            router_grad,
            jnp.zeros((1024, 1), f32),
            gain_two_grad[:, None],
            jnp.zeros((1024, 94), f32),
        ],
        axis=1,
    )
    sums, input_grad, query_grad, key_grad, value_grad, attn_out_grad, outputs = last_sums(
        small,
        qkv_got,
        qkv_w_all,
        layer_input,
        gain_one[None, :],
        hidden_grad_home,
        w_got,
        outputs,
    )
    return (
        outputs,
        input_grad,
        sums[:, 32],
        query_grad,
        key_grad,
        value_grad,
        attn_out_grad,
        sums[:, 33],
        sums[:, :32],
        expert_in,
        expert_out,
    )


def solution(mesh):
    placed = (
        P(("ctx", "mp"), None),
        P("ctx"),
        P(("ctx", "mp"), None),
        P("ctx"),
        P("ctx", "mp"),
        P("ctx", "mp"),
        P("ctx", "mp"),
        P("mp", "ctx"),
        P("ctx"),
        P("ctx", None),
        P("mp", "ctx", None),
        P("mp", None, "ctx"),
        P(("ctx", "mp"), None),
    )
    return jax.shard_map(
        body,
        mesh=mesh,
        in_specs=placed,
        out_specs=(
            P(("ctx", "mp"), None),
            P(("ctx", "mp"), None),
            P(("ctx", "mp")),
            P("ctx", "mp"),
            P("ctx", "mp"),
            P("ctx", "mp"),
            P("mp", "ctx"),
            P(("ctx", "mp")),
            P(("ctx", "mp"), None),
            P("mp", "ctx", None),
            P("mp", None, "ctx"),
        ),
        check_vma=False,
    )
```
